32 devices in a mesh: seq: 4 (over y, x), dp: 8 (over z, core).
Axes of the slice: x: 2, y: 2, z: 4, core: 2. Of those that a mesh axis runs over, the one named last changes fastest.
Arguments:
- queries: bfloat16 [8192, 1024], P(('dp', 'seq')), parts along dimension 0, may hold values from -6 to 6
- keys: bfloat16 [8192, 256], P(('dp', 'seq')), parts along dimension 0, may hold values from -6 to 6
- values: bfloat16 [8192, 256], P(('dp', 'seq')), parts along dimension 0, may hold values from -6 to 6
- out_grad: bfloat16 [8192, 1024], P(('dp', 'seq')), parts along dimension 0, may hold values from -6 to 6
- rand_blocks: int32 [128, 3], P('dp'), parts along dimension 0, may hold values from 0 to 15, as said below
- global_blocks: int32 [16], P('dp'), parts along dimension 0, may hold values from 0 to 15, as said below
Outputs:
- out: bfloat16 [8192, 1024], P(('dp', 'seq')), parts along dimension 0
- query_grad: bfloat16 [8192, 1024], P(('dp', 'seq')), parts along dimension 0
- key_grad: bfloat16 [8192, 256], P(('dp', 'seq')), parts along dimension 0
- value_grad: bfloat16 [8192, 256], P(('dp', 'seq')), parts along dimension 0
The draws below stay inside these ranges and needn't reach their ends.
There are 8 independent parts, one for each index of `dp`. The reference program is written for one: setup_inputs(seed, part) draws one part's arguments, and reference() takes and returns one part's arrays. A program takes and returns all parts, laid end to end along the dimension named above; each array names one. Nothing has to cross between parts.
Inputs may be any that keep to these rules, and one draw needn't show every extreme that they name: `rand_blocks`: block j lies on index j // 4 of seq. For each index r of seq, the 12 entries of rows r * 4 to (r + 1) * 4 - 1 together with the 2 global blocks name blocks of no index more than 4 times, and blocks of some index exactly 4 times. `global_blocks`: the global blocks lie on different indices of seq.
All inputs are finite; a program needn't handle non-finite values.
Results may differ from the reference program's by a relative error of at most 0.011.
Values may be sent and summed in bfloat16 or wider, within the bound.
No kernel may reach another device: no remote copies, remote signals or barrier semaphores. Data moves between devices by JAX's collectives and lax.ppermute only.
A program may use at most 64 MiB of HBM per device.

```python
import jax
import jax.numpy as jnp
from jax import lax

KVH = 2
HD = 128
BLOCK = 64
GLOB = 2
RAND = 3
QB = 4
GROUP = 4
QW = 1024
KW = 256
NB = 16
TOKENS = 1024
CAP = 4
N_SEQ = 4


def far_lists(key):
    cycle_size = NB // QB
    base = jax.random.fold_in(key, 11)
    owner_pick = jax.random.permutation(jax.random.fold_in(base, 1), cycle_size)[:GLOB]
    local_pick = jax.random.randint(jax.random.fold_in(base, 2), (GLOB,), 0, QB)
    global_ids = (owner_pick * QB + local_pick).astype(jnp.int32)
    slot_total = cycle_size * CAP
    reserved = jnp.zeros((slot_total,), jnp.int32).at[owner_pick * CAP].set(1)

    def one_device(sub_key):
        scores = jax.random.permutation(sub_key, slot_total)
        scores = scores + reserved * slot_total
        ordering = jnp.argsort(scores)
        chosen = ordering[:RAND * QB]
        owners = chosen // CAP
        local_ids = jax.random.randint(jax.random.fold_in(sub_key, 5), (RAND * QB,), 0, QB)
        return owners * QB + local_ids
    device_keys = jax.random.split(jax.random.fold_in(base, 3), cycle_size)
    rand_ids = jax.vmap(one_device)(device_keys).reshape(NB, RAND).astype(jnp.int32)
    return (rand_ids, global_ids)


def draw_rand_blocks(key, part):
    return far_lists(key)[0]


def draw_global_blocks(key, part):
    return far_lists(key)[1]


def base_field(key, columns):
    field = jnp.clip(jax.random.normal(jax.random.fold_in(key, 34), (TOKENS, columns), jnp.float32), -5.0, 5.0)
    return field


def draw_queries(key, part):
    field = base_field(jax.random.fold_in(key, 41), QW)
    return field.astype(jnp.bfloat16)


def draw_keys(key, part):
    field = base_field(jax.random.fold_in(key, 42), KW)
    return field.astype(jnp.bfloat16)


def block_levels(own_key, extent, shards, least, high):
    gain = 1.0
    for position, blocks in shards:
        draws = jax.random.uniform(jax.random.fold_in(jax.random.fold_in(own_key, 6), position), (blocks,), jnp.float32, least / len(shards), high / len(shards))
        gain = gain * jnp.repeat(jnp.exp(draws), extent[position] // blocks).reshape((-1,) + (1,) * (len(extent) - 1 - position))
    return gain


def gaussian(rng, extent, scale, most, cuts=(), kind=jnp.bfloat16):
    entries = scale * jax.random.normal(rng, extent, jnp.float32)
    if cuts:
        entries = entries * block_levels(rng, extent, cuts, -0.22, 0.18)
    return jnp.clip(entries, -most, most).astype(kind)


def setup_inputs(seed: int = 0, part: int = 0) -> dict:
    seeds = jax.random.split(jax.random.key(seed), 7)
    own_keys = jax.random.split(jax.random.fold_in(seeds[6], part), 7)
    queries = draw_queries(jax.random.fold_in(jax.random.fold_in(seeds[6], part), 71), part)
    keys = draw_keys(jax.random.fold_in(jax.random.fold_in(seeds[6], part), 71), part)
    values = gaussian(own_keys[2], (TOKENS, KW), 1.0, 6.0, ((0, 4),))
    out_grad = gaussian(own_keys[3], (TOKENS, QW), 1.0, 6.0, ((0, 4),))
    rand_blocks = draw_rand_blocks(jax.random.fold_in(jax.random.fold_in(seeds[6], part), 71), part)
    global_blocks = draw_global_blocks(jax.random.fold_in(jax.random.fold_in(seeds[6], part), 71), part)
    return dict(queries=queries, keys=keys, values=values, out_grad=out_grad, rand_blocks=rand_blocks, global_blocks=global_blocks)


def attend(inputs):
    query_block, key_set, grad_block = inputs
    rows = query_block.shape[0]
    scale = HD ** -0.5
    heads_q = query_block.astype(jnp.float32).reshape(rows, KVH, GROUP, HD)
    grads_q = grad_block.astype(jnp.float32).reshape(rows, KVH, GROUP, HD)
    keys_all = key_set[:, :, 0].astype(jnp.float32).reshape(-1, KVH, HD)
    values_all = key_set[:, :, 1].astype(jnp.float32).reshape(-1, KVH, HD)
    scores = jnp.einsum("qgjd,kgd->gjqk", heads_q, keys_all) * scale
    peak = jnp.max(scores, axis=-1, keepdims=True)
    expos = jnp.exp(scores - peak)
    probs = expos / jnp.sum(expos, axis=-1, keepdims=True)
    probs_b = probs.astype(jnp.bfloat16)
    attended = jnp.einsum("gjqk,kgd->qgjd", probs_b.astype(jnp.float32), values_all)
    delta = jnp.transpose(jnp.sum(grads_q * attended, axis=-1), (1, 2, 0))
    dprobs = jnp.einsum("qgjd,kgd->gjqk", grads_q, values_all)
    dscores = (probs * (dprobs - delta[..., None]) * scale).astype(jnp.bfloat16)
    qgrad = jnp.einsum("gjqk,kgd->qgjd", dscores.astype(jnp.float32), keys_all)
    key_part = jnp.einsum("gjqk,qgjd->kgd", dscores.astype(jnp.float32), heads_q)
    value_part = jnp.einsum("gjqk,qgjd->kgd", probs_b.astype(jnp.float32), grads_q)
    terms = jnp.stack([key_part.reshape(-1, KVH * HD), value_part.reshape(-1, KVH * HD)], axis=1)
    terms = terms.reshape(key_set.shape[0], rows, 2, KVH * HD)
    return (attended.reshape(rows, -1).astype(jnp.bfloat16), qgrad.reshape(rows, -1).astype(jnp.bfloat16), terms)


def reference(queries, keys, values, out_grad, rand_blocks, global_blocks):
    pair_blocks = jnp.stack([keys, values], axis=1).reshape(NB, BLOCK, 2, KW)
    query_blocks = queries.reshape(NB, BLOCK, QW)
    grad_blocks = out_grad.reshape(NB, BLOCK, QW)
    block_ids = jnp.arange(NB, dtype=jnp.int32)
    windows = (block_ids[:, None] + jnp.arange(-1, 2, dtype=jnp.int32)[None, :]) % NB
    key_lists = jnp.concatenate([windows.astype(jnp.int32), jnp.broadcast_to(global_blocks[None, :], (NB, GLOB)).astype(jnp.int32), rand_blocks.astype(jnp.int32)], axis=1)

    def per_block(inputs):
        query_block, grad_block, listing = inputs
        key_set = pair_blocks[listing]
        return attend((query_block, key_set, grad_block))

    out_blocks, qgrad_blocks, key_terms = lax.map(per_block, (query_blocks, grad_blocks, key_lists))
    window_terms = key_terms[:, :3].reshape(-1, BLOCK, 2, KW)
    total = jax.ops.segment_sum(window_terms, key_lists[:, :3].reshape(-1), num_segments=NB)
    rand_rounded = lax.optimization_barrier(key_terms[:, 3 + GLOB:].astype(jnp.bfloat16)).astype(jnp.float32)
    total = total + jax.ops.segment_sum(rand_rounded.reshape(-1, BLOCK, 2, KW), key_lists[:, 3 + GLOB:].reshape(-1), num_segments=NB)
    glob_sums = jnp.sum(key_terms[:, 3:3 + GLOB].reshape(N_SEQ, QB, GLOB, BLOCK, 2, KW), axis=1)
    glob_rounded = lax.optimization_barrier(glob_sums.astype(jnp.bfloat16)).astype(jnp.float32)
    glob_ids = jnp.broadcast_to(global_blocks[None, :], (N_SEQ, GLOB)).reshape(-1).astype(jnp.int32)
    total = total + jax.ops.segment_sum(glob_rounded.reshape(-1, BLOCK, 2, KW), glob_ids, num_segments=NB)
    out = out_blocks.reshape(TOKENS, QW)
    query_grad = qgrad_blocks.reshape(TOKENS, QW)
    key_grad = total[:, :, 0].reshape(TOKENS, KW).astype(jnp.bfloat16)
    value_grad = total[:, :, 1].reshape(TOKENS, KW).astype(jnp.bfloat16)
    return (out, query_grad, key_grad, value_grad)
```

```python
import functools

import jax
import jax.numpy as jnp
from jax import lax
from jax.experimental import pallas as pl
from jax.experimental.pallas import tpu as pltpu
from jax.sharding import PartitionSpec as P

KVH = 2
HD = 128
BLOCK = 64
GLOB = 2
RAND = 3
GROUP = 4
ENTRIES = 3 + GLOB + RAND
LOG2E = 1.4426950408889634
SCALE = HD ** (-0.5)


def attention_kernel(parts, table, *refs):
    count = len(parts)
    q_any, g_any = refs[:2]
    k_any = refs[2 : 2 + count]
    v_any = refs[2 + count : 2 + 2 * count]
    outs = refs[2 + 2 * count :]
    out_any, qgrad_any = outs[:2]
    grad_any = outs[2 : 2 + count]
    scratch = outs[2 + count :]
    q_ref, g_ref, k_pool, v_pool, dk_pool, dv_pool, out_ref, qgrad_ref = scratch[:8]
    grad_refs = scratch[8 : 8 + count]
    in_sem, out_sem = scratch[8 + count :]
    blocks_here = q_ref.shape[0] // BLOCK

    loads = []

    def load(source, target):
        copy = pltpu.make_async_copy(source, target, in_sem.at[len(loads)])
        copy.start()
        loads.append(copy)

    start = 0
    for i, blocks in enumerate(parts):
        load(k_any[i], k_pool.at[pl.ds(start * BLOCK, blocks * BLOCK)])
        load(v_any[i], v_pool.at[pl.ds(start * BLOCK, blocks * BLOCK)])
        start += blocks
    load(q_any, q_ref)
    load(g_any, g_ref)
    dk_pool[...] = jnp.zeros_like(dk_pool)
    dv_pool[...] = jnp.zeros_like(dv_pool)
    for copy in loads:
        copy.wait()

    stores = []

    def store(source, target):
        copy = pltpu.make_async_copy(source, target, out_sem.at[len(stores)])
        copy.start()
        stores.append(copy)

    nt = (((1,), (1,)), ((), ()))
    nn = (((1,), (0,)), ((), ()))
    tn = (((0,), (0,)), ((), ()))
    dot = functools.partial(lax.dot_general, preferred_element_type=jnp.float32)
    for b in range(blocks_here):
        rows = pl.ds(b * BLOCK, BLOCK)
        places = [pl.ds(pl.multiple_of(table[b, e] * BLOCK, BLOCK), BLOCK) for e in range(ENTRIES)]
        for h in range(KVH):
            cols = pl.ds(h * HD, HD)
            heads = [pl.ds((h * GROUP + j) * HD, HD) for j in range(GROUP)]
            ks = jnp.concatenate([k_pool[place, cols] for place in places], axis=0)
            vs = jnp.concatenate([v_pool[place, cols] for place in places], axis=0)
            qs = jnp.concatenate([q_ref[rows, head] for head in heads], axis=0)
            gs = jnp.concatenate([g_ref[rows, head] for head in heads], axis=0)
            scores = dot(ks, qs, nt)
            peak = jnp.max(scores, axis=0, keepdims=True)
            expos = jnp.exp2((scores - peak) * (SCALE * LOG2E))
            probs = expos * (1.0 / jnp.sum(expos, axis=0, keepdims=True))
            probs_b = probs.astype(jnp.bfloat16)
            dprobs = dot(vs, gs, nt)
            delta = jnp.sum(probs * dprobs, axis=0, keepdims=True)
            dscores = (probs * (dprobs - delta)).astype(jnp.bfloat16)
            attended = dot(probs_b, vs, tn).astype(jnp.bfloat16)
            qgrad = (dot(dscores, ks, tn) * SCALE).astype(jnp.bfloat16)
            for j in range(GROUP):
                out_ref[rows, heads[j]] = attended[j * BLOCK : (j + 1) * BLOCK]
                qgrad_ref[rows, heads[j]] = qgrad[j * BLOCK : (j + 1) * BLOCK]
            dk = dot(dscores, qs, nn)
            dv = dot(probs_b, gs, nn)
            for e in range(ENTRIES):
                dk_pool[places[e], cols] += dk[e * BLOCK : (e + 1) * BLOCK]
                dv_pool[places[e], cols] += dv[e * BLOCK : (e + 1) * BLOCK]
        store(out_ref.at[rows], out_any.at[rows])
        store(qgrad_ref.at[rows], qgrad_any.at[rows])

    width = k_pool.shape[1]
    start = 0
    for i, blocks in enumerate(parts):
        span = pl.ds(start * BLOCK, blocks * BLOCK)
        grad_refs[i][:, :width] = (dk_pool[span] * SCALE).astype(grad_refs[i].dtype)
        grad_refs[i][:, width:] = dv_pool[span].astype(grad_refs[i].dtype)
        store(grad_refs[i], grad_any[i])
        start += blocks
    for copy in stores:
        copy.wait()


def attend(table, queries, out_grad, keys, values):
    tok_rows, q_width = queries.shape
    width = keys[0].shape[1]
    parts = tuple(part.shape[0] // BLOCK for part in keys)
    pool_rows = sum(parts) * BLOCK
    grad_types = [jnp.float32] + [jnp.bfloat16] * (len(parts) - 1)
    grad_shapes = [
        jax.ShapeDtypeStruct((blocks * BLOCK, 2 * width), kind)
        for blocks, kind in zip(parts, grad_types)
    ]
    wide = jax.ShapeDtypeStruct((tok_rows, q_width), jnp.bfloat16)
    operands = [queries, out_grad, *keys, *values]
    anywhere = pl.BlockSpec(memory_space=pl.ANY)
    units = 6 * 2 * tok_rows * KVH * GROUP * ENTRIES * BLOCK * HD
    results = pl.pallas_call(
        functools.partial(attention_kernel, parts),
        out_shape=[wide, wide, *grad_shapes],
        in_specs=[pl.BlockSpec(memory_space=pltpu.SMEM)] + [anywhere] * len(operands),
        out_specs=[anywhere] * (2 + len(parts)),
        scratch_shapes=[
            pltpu.VMEM((tok_rows, q_width), jnp.bfloat16),
            pltpu.VMEM((tok_rows, q_width), jnp.bfloat16),
            pltpu.VMEM((pool_rows, width), jnp.bfloat16),
            pltpu.VMEM((pool_rows, width), jnp.bfloat16),
            pltpu.VMEM((pool_rows, width), jnp.float32),
            pltpu.VMEM((pool_rows, width), jnp.float32),
            pltpu.VMEM((tok_rows, q_width), jnp.bfloat16),
            pltpu.VMEM((tok_rows, q_width), jnp.bfloat16),
            *[pltpu.VMEM(shape.shape, shape.dtype) for shape in grad_shapes],
            pltpu.SemaphoreType.DMA((len(operands),)),
            pltpu.SemaphoreType.DMA((2 * (tok_rows // BLOCK) + len(parts),)),
        ],
        compiler_params=pltpu.CompilerParams(vmem_limit_bytes=32 * 2**20),
        cost_estimate=pl.CostEstimate(
            flops=units, bytes_accessed=6 * 2**20, transcendentals=units // (12 * HD)
        ),
    )(table, *operands)
    return results[0], results[1], results[2:]


def key_lists(rand_blocks, global_blocks, myself, blocks_here, total):
    mine = myself * blocks_here + jnp.arange(blocks_here, dtype=jnp.int32)
    window = (mine[:, None] + jnp.arange(-1, 2, dtype=jnp.int32)[None, :]) % total
    rand_mine = lax.dynamic_slice_in_dim(rand_blocks, myself * blocks_here, blocks_here, 0)
    spread = jnp.broadcast_to(global_blocks[None, :], (blocks_here, GLOB))
    return jnp.concatenate([window, spread, rand_mine], axis=1)


def dense_local(queries, keys, values, out_grad, rand_blocks, global_blocks):
    cycle_size = lax.axis_size("seq")
    myself = lax.axis_index("seq").astype(jnp.int32)
    blocks_here = queries.shape[0] // BLOCK
    width = keys.shape[1]

    def swap(array, offset):
        return lax.ppermute(array, "seq", [(i, i ^ offset) for i in range(cycle_size)])

    offsets = range(1, cycle_size)
    key_parts = [keys] + [swap(keys, offset) for offset in offsets]
    value_parts = [values] + [swap(values, offset) for offset in offsets]
    listed = key_lists(rand_blocks, global_blocks, myself, blocks_here, cycle_size * blocks_here)
    table = ((listed // blocks_here) ^ myself) * blocks_here + listed % blocks_here
    out, query_grad, grads = attend(table, queries, out_grad, key_parts, value_parts)
    total = grads[0]
    for offset in offsets:
        total = total + swap(grads[offset], offset).astype(jnp.float32)
    total = total.astype(jnp.bfloat16)
    return out, query_grad, total[:, :width], total[:, width:]


def sparse_local(queries, keys, values, out_grad, rand_blocks, global_blocks):
    cycle_size = lax.axis_size("seq")
    myself = lax.axis_index("seq").astype(jnp.int32)
    tok_rows, width = keys.shape
    blocks_here = tok_rows // BLOCK
    rand_total = RAND * blocks_here
    capacity = (rand_total + GLOB + cycle_size - 1) // cycle_size
    slot_total = cycle_size * capacity
    listed = jnp.concatenate(
        [
            rand_blocks.reshape(cycle_size, rand_total),
            jnp.broadcast_to(global_blocks[None, :], (cycle_size, GLOB)),
        ],
        axis=1,
    )
    entries = listed.shape[1]
    owners = listed // blocks_here
    local_slot = listed % blocks_here
    earlier = jnp.arange(entries)[None, :] < jnp.arange(entries)[:, None]
    same_owner = owners[:, :, None] == owners[:, None, :]
    ranking = jnp.sum(same_owner & earlier[None], axis=2)
    owners_mine = lax.dynamic_index_in_dim(owners, myself, 0, keepdims=False)
    ranking_mine = lax.dynamic_index_in_dim(ranking, myself, 0, keepdims=False)
    far_place = (blocks_here + 2 + owners_mine * capacity + ranking_mine).astype(jnp.int32)
    slot_ids = jnp.arange(slot_total)
    requester = slot_ids // capacity
    position = slot_ids % capacity
    matches = (owners[requester] == myself) & (ranking[requester] == position[:, None])
    source = jnp.sum(jnp.where(matches, local_slot[requester], 0), axis=1)

    up = [(i, (i + 1) % cycle_size) for i in range(cycle_size)]
    down = [(j, i) for i, j in up]
    pair = jnp.concatenate([keys, values], axis=1)
    before = lax.ppermute(pair[tok_rows - BLOCK :], "seq", up)
    after = lax.ppermute(pair[:BLOCK], "seq", down)
    outgoing = jnp.take(pair.reshape(blocks_here, BLOCK, 2 * width), source, axis=0)
    far = lax.all_to_all(outgoing, "seq", split_axis=0, concat_axis=0, tiled=True)
    others = [before, after, far.reshape(slot_total * BLOCK, 2 * width)]
    key_parts = [keys] + [part[:, :width] for part in others]
    value_parts = [values] + [part[:, width:] for part in others]

    here = jnp.arange(blocks_here, dtype=jnp.int32)[:, None]
    ahead = jnp.where(here == 0, blocks_here, here - 1)
    behind = jnp.where(here == blocks_here - 1, blocks_here + 1, here + 1)
    table = jnp.concatenate(
        [
            ahead,
            here,
            behind,
            jnp.broadcast_to(far_place[None, rand_total:], (blocks_here, GLOB)),
            far_place[:rand_total].reshape(blocks_here, RAND),
        ],
        axis=1,
    )
    out, query_grad, grads = attend(table, queries, out_grad, key_parts, value_parts)
    own, grad_before, grad_after, grad_far = grads
    own = own.reshape(blocks_here, BLOCK, 2 * width)
    last_rim = lax.ppermute(grad_before, "seq", down).astype(jnp.float32)
    first_rim = lax.ppermute(grad_after, "seq", up).astype(jnp.float32)
    returned = lax.all_to_all(
        grad_far.reshape(slot_total, BLOCK, 2 * width),
        "seq", split_axis=0, concat_axis=0, tiled=True,
    )
    landing = (source[:, None] == jnp.arange(blocks_here)[None, :]).astype(jnp.bfloat16)
    total = own + jnp.einsum("sq,sbx->qbx", landing, returned, preferred_element_type=jnp.float32)
    total = total.at[blocks_here - 1].add(last_rim).at[0].add(first_rim)
    total = total.reshape(tok_rows, 2 * width).astype(jnp.bfloat16)
    return out, query_grad, total[:, :width], total[:, width:]


def local(queries, keys, values, out_grad, rand_blocks, global_blocks):
    cycle_size = lax.axis_size("seq")
    blocks_here = queries.shape[0] // BLOCK
    capacity = (RAND * blocks_here + GLOB + cycle_size - 1) // cycle_size
    dense = capacity >= blocks_here and cycle_size & (cycle_size - 1) == 0
    plan = dense_local if dense else sparse_local
    return plan(queries, keys, values, out_grad, rand_blocks, global_blocks)


def solution(mesh):
    rows = P(("dp", "seq"), None)
    return jax.shard_map(
        local,
        mesh=mesh,
        in_specs=(rows, rows, rows, rows, P("dp", None), P("dp")),
        out_specs=(rows, rows, rows, rows),
        check_vma=False,
    )
```

```python
import functools

import jax
import jax.numpy as jnp
from jax import lax
from jax.experimental import pallas as pl
from jax.experimental.pallas import tpu as pltpu
from jax.sharding import PartitionSpec as P

KVH = 2
HD = 128
BLOCK = 64
GLOB = 2
RAND = 3
GROUP = 4
ENTRIES = 3 + GLOB + RAND
LOG2E = 1.4426950408889634
SCALE = HD ** (-0.5)


NN = (((1,), (0,)), ((), ()))
TN = (((0,), (0,)), ((), ()))
dot = functools.partial(lax.dot_general, preferred_element_type=jnp.float32)

KEYS = ENTRIES * BLOCK
ROWS = GROUP * BLOCK


def units(blocks_here):
    return [(b, h, b * KVH + h) for b in range(blocks_here) for h in range(KVH)]


def places_of(table, b):
    return [pl.ds(pl.multiple_of(table[b, e] * BLOCK, BLOCK), BLOCK) for e in range(ENTRIES)]


def picked(pool, places, h):
    return jnp.concatenate([pool[place, h * HD : (h + 1) * HD] for place in places], axis=0)


def unstack(ref, b, h, value):
    for j in range(GROUP):
        c = (h * GROUP + j) * HD
        ref[b * BLOCK : (b + 1) * BLOCK, c : c + HD] = value[j * BLOCK : (j + 1) * BLOCK]


def add_terms(pool, places, h, terms):
    for e, place in enumerate(places):
        pool[place, h * HD : (h + 1) * HD] += terms[e * BLOCK : (e + 1) * BLOCK]


def gather_pool(pool, parts):
    start = 0
    for part in parts:
        pool[start : start + part.shape[0]] = part[...]
        start += part.shape[0]


def split_pool(outs, pool, factor):
    start = 0
    for out in outs:
        total = pool[start : start + out.shape[0]]
        out[...] = (total if factor is None else total * factor).astype(out.dtype)
        start += out.shape[0]


def stage_kernel(q_any, g_any, k_any, v_any, *refs):
    q_rows, g_rows, q_cols, g_cols, k_ref, v_ref, q_ref, g_ref, sem = refs
    pairs = [(q_any, q_ref), (g_any, g_ref), (k_any, k_ref), (v_any, v_ref)]
    copies = [pltpu.make_async_copy(*pair, sem.at[i]) for i, pair in enumerate(pairs)]
    for copy in copies:
        copy.start()
    for copy, ref, rows, cols in ((copies[0], q_ref, q_rows, q_cols), (copies[1], g_ref, g_rows, g_cols)):
        copy.wait()
        for b, h, u in units(ref.shape[0] // BLOCK):
            heads = [(h * GROUP + j) * HD for j in range(GROUP)]
            unit = jnp.concatenate(
                [ref[b * BLOCK : (b + 1) * BLOCK, c : c + HD] for c in heads], axis=0
            )
            rows[u * ROWS : (u + 1) * ROWS] = unit
            cols[u * HD : (u + 1) * HD] = unit.T
    copies[2].wait()
    copies[3].wait()


def probs_kernel(count, table, q_cols, g_rows, *refs):
    parts = refs[:count]
    probs_ref, k_pool = refs[count : count + 2]
    dv_refs = refs[count + 2 : 2 * count + 2]
    dv_pool = refs[2 * count + 2]
    gather_pool(k_pool, parts)
    dv_pool[...] = jnp.zeros_like(dv_pool)
    for b, h, u in units(table.shape[0]):
        places = places_of(table, b)
        scores = dot(picked(k_pool, places, h), q_cols[u * HD : (u + 1) * HD], NN)
        peak = jnp.max(scores, axis=0, keepdims=True)
        expos = jnp.exp2((scores - peak) * (SCALE * LOG2E))
        probs = expos * (1.0 / jnp.sum(expos, axis=0, keepdims=True))
        probs_b = probs.astype(jnp.bfloat16)
        probs_ref[u * KEYS : (u + 1) * KEYS] = probs_b
        add_terms(dv_pool, places, h, dot(probs_b, g_rows[u * ROWS : (u + 1) * ROWS], NN))
    split_pool(dv_refs, dv_pool, None)


def dscores_kernel(count, table, q_rows, g_cols, probs_ref, *refs):
    parts = refs[:count]
    ds_ref, v_pool = refs[count : count + 2]
    dk_refs = refs[count + 2 : 2 * count + 2]
    dk_pool = refs[2 * count + 2]
    gather_pool(v_pool, parts)
    dk_pool[...] = jnp.zeros_like(dk_pool)
    for b, h, u in units(table.shape[0]):
        places = places_of(table, b)
        probs = probs_ref[u * KEYS : (u + 1) * KEYS].astype(jnp.float32)
        dprobs = dot(picked(v_pool, places, h), g_cols[u * HD : (u + 1) * HD], NN)
        delta = jnp.sum(probs * dprobs, axis=0, keepdims=True)
        dscores = (probs * (dprobs - delta)).astype(jnp.bfloat16)
        ds_ref[u * KEYS : (u + 1) * KEYS] = dscores
        add_terms(dk_pool, places, h, dot(dscores, q_rows[u * ROWS : (u + 1) * ROWS], NN))
    split_pool(dk_refs, dk_pool, SCALE)


def rows_kernel(table, probs_ref, ds_ref, k_pool, v_pool, out_ref, qgrad_ref):
    for b, h, u in units(out_ref.shape[0] // BLOCK):
        places = places_of(table, b)
        span = slice(u * KEYS, (u + 1) * KEYS)
        attended = dot(probs_ref[span], picked(v_pool, places, h), TN)
        unstack(out_ref, b, h, attended.astype(jnp.bfloat16))
        qgrad = dot(ds_ref[span], picked(k_pool, places, h), TN) * SCALE
        unstack(qgrad_ref, b, h, qgrad.astype(jnp.bfloat16))


def run_kernel(kernel, operands, in_specs, results, scratch, products):
    vmem = pl.BlockSpec(memory_space=pltpu.VMEM)
    flops = products * 2 * 4 * KVH * ROWS * KEYS * HD
    return pl.pallas_call(
        kernel,
        out_shape=[jax.ShapeDtypeStruct(shape, kind) for shape, kind in results],
        in_specs=in_specs + [vmem] * (len(operands) - len(in_specs)),
        out_specs=[vmem] * len(results),
        scratch_shapes=scratch,
        compiler_params=pltpu.CompilerParams(vmem_limit_bytes=32 * 2**20),
        cost_estimate=pl.CostEstimate(
            flops=flops, bytes_accessed=products * 2**20, transcendentals=0
        ),
    )(*operands)


def attend(table, queries, out_grad, keys, values, key_parts, value_parts, send):
    tok_rows, q_width = queries.shape
    width = keys.shape[1]
    half, full = jnp.bfloat16, jnp.float32
    unit_count = tok_rows // BLOCK * KVH
    rows, cols = ((unit_count * ROWS, HD), half), ((unit_count * HD, ROWS), half)
    narrow, wide = ((tok_rows, width), half), ((tok_rows, q_width), half)
    hbm = pl.BlockSpec(memory_space=pltpu.HBM)
    smem = pl.BlockSpec(memory_space=pltpu.SMEM)
    local = (queries, out_grad, keys, values)
    q_rows, g_rows, q_cols, g_cols, keys, values = run_kernel(
        stage_kernel,
        [pltpu.with_memory_space_constraint(array, pltpu.HBM) for array in local],
        [hbm] * 4,
        [rows, rows, cols, cols, narrow, narrow],
        [pltpu.VMEM(*wide), pltpu.VMEM(*wide), pltpu.SemaphoreType.DMA((4,))],
        1,
    )
    key_parts, value_parts = [keys, *key_parts], [values, *value_parts]
    count = len(key_parts)
    pool_rows = sum(part.shape[0] for part in key_parts)
    held = ((unit_count * KEYS, ROWS), half)
    sums = [(part.shape, half if i else full) for i, part in enumerate(key_parts)]
    scratch = [pltpu.VMEM((pool_rows, width), full)]
    pool = ((pool_rows, width), half)
    probs, k_pool, *dv = run_kernel(
        functools.partial(probs_kernel, count),
        (table, q_cols, g_rows, *key_parts),
        [smem], [held, pool, *sums], scratch, 2,
    )
    dv = send(dv)
    dscores, v_pool, *dk = run_kernel(
        functools.partial(dscores_kernel, count),
        (table, q_rows, g_cols, probs, *value_parts),
        [smem], [held, pool, *sums], scratch, 2,
    )
    dk = send(dk)
    dv[1], table = lax.optimization_barrier((dv[1], table))
    out, query_grad = run_kernel(
        rows_kernel, (table, probs, dscores, k_pool, v_pool), [smem], [wide, wide], [], 2
    )
    return out, query_grad, dk, dv


def key_lists(rand_blocks, global_blocks, myself, blocks_here, total):
    mine = myself * blocks_here + jnp.arange(blocks_here, dtype=jnp.int32)
    window = (mine[:, None] + jnp.arange(-1, 2, dtype=jnp.int32)[None, :]) % total
    rand_mine = lax.dynamic_slice_in_dim(rand_blocks, myself * blocks_here, blocks_here, 0)
    spread = jnp.broadcast_to(global_blocks[None, :], (blocks_here, GLOB))
    return jnp.concatenate([window, spread, rand_mine], axis=1)


def dense_local(queries, keys, values, out_grad, rand_blocks, global_blocks):
    cycle_size = lax.axis_size("seq")
    myself = lax.axis_index("seq").astype(jnp.int32)
    blocks_here = queries.shape[0] // BLOCK
    width = keys.shape[1]

    def swap(array, offset):
        return lax.ppermute(array, "seq", [(i, i ^ offset) for i in range(cycle_size)])

    offsets = range(1, cycle_size)
    key_parts = [swap(keys, offset) for offset in offsets]
    value_parts = [swap(values, offset) for offset in offsets]
    listed = key_lists(rand_blocks, global_blocks, myself, blocks_here, cycle_size * blocks_here)
    table = ((listed // blocks_here) ^ myself) * blocks_here + listed % blocks_here

    def send(grads):
        return [grads[0]] + [swap(grads[offset], offset) for offset in offsets]

    def total(grads):
        return sum(grad.astype(jnp.float32) for grad in grads).astype(jnp.bfloat16)

    out, query_grad, dk, dv = attend(
        table, queries, out_grad, keys, values, key_parts, value_parts, send
    )
    return out, query_grad, total(dk), total(dv)


def sparse_local(queries, keys, values, out_grad, rand_blocks, global_blocks):
    cycle_size = lax.axis_size("seq")
    myself = lax.axis_index("seq").astype(jnp.int32)
    tok_rows, width = keys.shape
    blocks_here = tok_rows // BLOCK
    rand_total = RAND * blocks_here
    capacity = (rand_total + GLOB + cycle_size - 1) // cycle_size
    slot_total = cycle_size * capacity
    listed = jnp.concatenate(
        [
            rand_blocks.reshape(cycle_size, rand_total),
            jnp.broadcast_to(global_blocks[None, :], (cycle_size, GLOB)),
        ],
        axis=1,
    )
    entries = listed.shape[1]
    owners = listed // blocks_here
    local_slot = listed % blocks_here
    earlier = jnp.arange(entries)[None, :] < jnp.arange(entries)[:, None]
    same_owner = owners[:, :, None] == owners[:, None, :]
    ranking = jnp.sum(same_owner & earlier[None], axis=2)
    owners_mine = lax.dynamic_index_in_dim(owners, myself, 0, keepdims=False)
    ranking_mine = lax.dynamic_index_in_dim(ranking, myself, 0, keepdims=False)
    far_place = (blocks_here + 2 + owners_mine * capacity + ranking_mine).astype(jnp.int32)
    slot_ids = jnp.arange(slot_total)
    requester = slot_ids // capacity
    position = slot_ids % capacity
    matches = (owners[requester] == myself) & (ranking[requester] == position[:, None])
    source = jnp.sum(jnp.where(matches, local_slot[requester], 0), axis=1)

    up = [(i, (i + 1) % cycle_size) for i in range(cycle_size)]
    down = [(j, i) for i, j in up]
    pair = jnp.concatenate([keys, values], axis=1)
    before = lax.ppermute(pair[tok_rows - BLOCK :], "seq", up)
    after = lax.ppermute(pair[:BLOCK], "seq", down)
    outgoing = jnp.take(pair.reshape(blocks_here, BLOCK, 2 * width), source, axis=0)
    far = lax.all_to_all(outgoing, "seq", split_axis=0, concat_axis=0, tiled=True)
    others = [before, after, far.reshape(slot_total * BLOCK, 2 * width)]
    key_parts = [part[:, :width] for part in others]
    value_parts = [part[:, width:] for part in others]

    here = jnp.arange(blocks_here, dtype=jnp.int32)[:, None]
    ahead = jnp.where(here == 0, blocks_here, here - 1)
    behind = jnp.where(here == blocks_here - 1, blocks_here + 1, here + 1)
    table = jnp.concatenate(
        [
            ahead,
            here,
            behind,
            jnp.broadcast_to(far_place[None, rand_total:], (blocks_here, GLOB)),
            far_place[:rand_total].reshape(blocks_here, RAND),
        ],
        axis=1,
    )
    landing = (source[:, None] == jnp.arange(blocks_here)[None, :]).astype(jnp.bfloat16)

    def send(grads):
        own, grad_before, grad_after, grad_far = grads
        last_rim = lax.ppermute(grad_before, "seq", down)
        first_rim = lax.ppermute(grad_after, "seq", up)
        returned = lax.all_to_all(
            grad_far.reshape(slot_total, BLOCK, width),
            "seq", split_axis=0, concat_axis=0, tiled=True,
        )
        return [own, last_rim, first_rim, returned]

    def total(grads):
        own, last_rim, first_rim, returned = grads
        landed = jnp.einsum("sq,sbx->qbx", landing, returned, preferred_element_type=jnp.float32)
        sums = own.reshape(blocks_here, BLOCK, width) + landed
        sums = sums.at[blocks_here - 1].add(last_rim.astype(jnp.float32))
        sums = sums.at[0].add(first_rim.astype(jnp.float32))
        return sums.reshape(tok_rows, width).astype(jnp.bfloat16)

    out, query_grad, dk, dv = attend(
        table, queries, out_grad, keys, values, key_parts, value_parts, send
    )
    return out, query_grad, total(dk), total(dv)


def local(queries, keys, values, out_grad, rand_blocks, global_blocks):
    cycle_size = lax.axis_size("seq")
    blocks_here = queries.shape[0] // BLOCK
    capacity = (RAND * blocks_here + GLOB + cycle_size - 1) // cycle_size
    dense = capacity >= blocks_here and cycle_size & (cycle_size - 1) == 0
    plan = dense_local if dense else sparse_local
    return plan(queries, keys, values, out_grad, rand_blocks, global_blocks)


def solution(mesh):
    rows = P(("dp", "seq"), None)
    return jax.shard_map(
        local,
        mesh=mesh,
        in_specs=(rows, rows, rows, rows, P("dp", None), P("dp")),
        out_specs=(rows, rows, rows, rows),
        check_vma=False,
    )
```

```python
import functools

import jax
import jax.numpy as jnp
from jax import lax
from jax.experimental import pallas as pl
from jax.experimental.pallas import tpu as pltpu
from jax.sharding import PartitionSpec as P

KVH = 2
HD = 128
BLOCK = 64
GLOB = 2
RAND = 3
GROUP = 4
ENTRIES = 3 + GLOB + RAND
LOG2E = 1.4426950408889634
SCALE = HD ** (-0.5)


NN = (((1,), (0,)), ((), ()))
TN = (((0,), (0,)), ((), ()))
dot = functools.partial(lax.dot_general, preferred_element_type=jnp.float32)

KEYS = ENTRIES * BLOCK
ROWS = GROUP * BLOCK


def units(blocks_here):
    return [(b, h, b * KVH + h) for b in range(blocks_here) for h in range(KVH)]


def places_of(table, b):
    return [pl.ds(pl.multiple_of(table[b, e] * BLOCK, BLOCK), BLOCK) for e in range(ENTRIES)]


def picked(pool, places, h):
    return jnp.concatenate([pool[place, h * HD : (h + 1) * HD] for place in places], axis=0)


def unstack(ref, b, h, value):
    for j in range(GROUP):
        c = (h * GROUP + j) * HD
        ref[b * BLOCK : (b + 1) * BLOCK, c : c + HD] = value[j * BLOCK : (j + 1) * BLOCK]


def add_terms(pool, places, h, terms):
    for e, place in enumerate(places):
        pool[place, h * HD : (h + 1) * HD] += terms[e * BLOCK : (e + 1) * BLOCK]


def pool_of(parts, pool):
    if len(parts) == 1:
        return parts[0]
    start = 0
    for part in parts:
        pool[start : start + part.shape[0]] = part[...]
        start += part.shape[0]
    return pool


def split_pool(outs, pool, factor):
    start = 0
    for out in outs:
        total = pool[start : start + out.shape[0]]
        out[...] = (total if factor is None else total * factor).astype(out.dtype)
        start += out.shape[0]


def stage_kernel(q_any, g_any, *refs):
    *plain, q_rows, g_rows, q_cols, g_cols = refs[:-3]
    q_ref, g_ref, sem = refs[-3:]
    half = len(plain) // 2
    pairs = [(q_any, q_ref), (g_any, g_ref), *zip(plain[:half], plain[half:])]
    copies = [pltpu.make_async_copy(*pair, sem.at[i]) for i, pair in enumerate(pairs)]
    for copy in copies:
        copy.start()
    for copy, ref, rows, cols in ((copies[0], q_ref, q_rows, q_cols), (copies[1], g_ref, g_rows, g_cols)):
        copy.wait()
        for b, h, u in units(ref.shape[0] // BLOCK):
            heads = [(h * GROUP + j) * HD for j in range(GROUP)]
            unit = jnp.concatenate(
                [ref[b * BLOCK : (b + 1) * BLOCK, c : c + HD] for c in heads], axis=0
            )
            rows[u * ROWS : (u + 1) * ROWS] = unit
            cols[u * HD : (u + 1) * HD] = unit.T
    for copy in copies[2:]:
        copy.wait()


def probs_kernel(count, table, grad_table, q_cols, g_rows, *refs):
    parts = refs[:count]
    probs_ref, k_pool, *dv_refs, dv_pool = refs[count:]
    k_pool = pool_of(parts, k_pool)
    dv_pool[...] = jnp.zeros_like(dv_pool)
    for b, h, u in units(table.shape[0]):
        scores = dot(picked(k_pool, places_of(table, b), h), q_cols[u * HD : (u + 1) * HD], NN)
        peak = jnp.max(scores, axis=0, keepdims=True)
        expos = jnp.exp2((scores - peak) * (SCALE * LOG2E))
        probs = expos * (1.0 / jnp.sum(expos, axis=0, keepdims=True))
        probs_b = probs.astype(jnp.bfloat16)
        probs_ref[u * KEYS : (u + 1) * KEYS] = probs_b
        terms = dot(probs_b, g_rows[u * ROWS : (u + 1) * ROWS], NN)
        add_terms(dv_pool, places_of(grad_table, b), h, terms)
    split_pool(dv_refs, dv_pool, None)


def dscores_kernel(count, table, grad_table, q_rows, g_cols, probs_ref, *refs):
    parts = refs[:count]
    ds_ref, v_pool, *dk_refs, dk_pool = refs[count:]
    v_pool = pool_of(parts, v_pool)
    dk_pool[...] = jnp.zeros_like(dk_pool)
    for b, h, u in units(table.shape[0]):
        probs = probs_ref[u * KEYS : (u + 1) * KEYS].astype(jnp.float32)
        dprobs = dot(picked(v_pool, places_of(table, b), h), g_cols[u * HD : (u + 1) * HD], NN)
        delta = jnp.sum(probs * dprobs, axis=0, keepdims=True)
        dscores = (probs * (dprobs - delta)).astype(jnp.bfloat16)
        ds_ref[u * KEYS : (u + 1) * KEYS] = dscores
        terms = dot(dscores, q_rows[u * ROWS : (u + 1) * ROWS], NN)
        add_terms(dk_pool, places_of(grad_table, b), h, terms)
    split_pool(dk_refs, dk_pool, SCALE)


def rows_kernel(table, probs_ref, ds_ref, k_pool, v_pool, out_ref, qgrad_ref):
    for b, h, u in units(out_ref.shape[0] // BLOCK):
        places = places_of(table, b)
        span = slice(u * KEYS, (u + 1) * KEYS)
        attended = dot(probs_ref[span], picked(v_pool, places, h), TN)
        unstack(out_ref, b, h, attended.astype(jnp.bfloat16))
        qgrad = dot(ds_ref[span], picked(k_pool, places, h), TN) * SCALE
        unstack(qgrad_ref, b, h, qgrad.astype(jnp.bfloat16))


def run_kernel(kernel, operands, in_specs, results, scratch, products):
    vmem = pl.BlockSpec(memory_space=pltpu.VMEM)
    flops = products * 2 * 4 * KVH * ROWS * KEYS * HD
    return pl.pallas_call(
        kernel,
        out_shape=[jax.ShapeDtypeStruct(shape, kind) for shape, kind in results],
        in_specs=in_specs + [vmem] * (len(operands) - len(in_specs)),
        out_specs=[vmem] * len(results),
        scratch_shapes=scratch,
        compiler_params=pltpu.CompilerParams(vmem_limit_bytes=32 * 2**20),
        cost_estimate=pl.CostEstimate(
            flops=flops, bytes_accessed=products * 2**20, transcendentals=0
        ),
    )(*operands)


def attend(table, grad_table, queries, out_grad, plain, key_parts, value_parts, grad_rows, send):
    tok_rows, q_width = queries.shape
    width = q_width // GROUP
    half, full = jnp.bfloat16, jnp.float32
    unit_count = tok_rows // BLOCK * KVH
    rows, cols = ((unit_count * ROWS, HD), half), ((unit_count * HD, ROWS), half)
    wide = ((tok_rows, q_width), half)
    hbm = pl.BlockSpec(memory_space=pltpu.HBM)
    smem = pl.BlockSpec(memory_space=pltpu.SMEM)
    mine = (queries, out_grad, *plain)
    *plain, q_rows, g_rows, q_cols, g_cols = run_kernel(
        stage_kernel,
        [pltpu.with_memory_space_constraint(array, pltpu.HBM) for array in mine],
        [hbm] * len(mine),
        [(array.shape, half) for array in plain] + [rows, rows, cols, cols],
        [pltpu.VMEM(*wide), pltpu.VMEM(*wide), pltpu.SemaphoreType.DMA((len(mine),))],
        1,
    )
    if plain:
        key_parts, value_parts = [plain[0], *key_parts], [plain[1], *value_parts]
    count = len(key_parts)
    pool_rows = sum(part.shape[0] for part in key_parts) if count > 1 else BLOCK
    held = ((unit_count * KEYS, ROWS), half)
    sums = [((size, width), half if i else full) for i, size in enumerate(grad_rows)]
    scratch = [pltpu.VMEM((sum(grad_rows), width), full)]
    pool = ((pool_rows, width), half)
    probs, k_pool, *dv = run_kernel(
        functools.partial(probs_kernel, count),
        (table, grad_table, q_cols, g_rows, *key_parts),
        [smem] * 2, [held, pool, *sums], scratch, 2,
    )
    dv = send(dv)
    dscores, v_pool, *dk = run_kernel(
        functools.partial(dscores_kernel, count),
        (table, grad_table, q_rows, g_cols, probs, *value_parts),
        [smem] * 2, [held, pool, *sums], scratch, 2,
    )
    dk = send(dk)
    dv[1], table = lax.optimization_barrier((dv[1], table))
    if count == 1:
        k_pool, v_pool = key_parts[0], value_parts[0]
    out, query_grad = run_kernel(
        rows_kernel, (table, probs, dscores, k_pool, v_pool), [smem], [wide, wide], [], 2
    )
    return out, query_grad, dk, dv


def key_lists(rand_blocks, global_blocks, myself, blocks_here, total):
    mine = myself * blocks_here + jnp.arange(blocks_here, dtype=jnp.int32)
    window = (mine[:, None] + jnp.arange(-1, 2, dtype=jnp.int32)[None, :]) % total
    rand_mine = lax.dynamic_slice_in_dim(rand_blocks, myself * blocks_here, blocks_here, 0)
    spread = jnp.broadcast_to(global_blocks[None, :], (blocks_here, GLOB))
    return jnp.concatenate([window, spread, rand_mine], axis=1)


def dense_local(queries, keys, values, out_grad, rand_blocks, global_blocks):
    cycle_size = lax.axis_size("seq")
    myself = lax.axis_index("seq").astype(jnp.int32)
    blocks_here = queries.shape[0] // BLOCK

    def swap(array, offset):
        return lax.ppermute(array, "seq", [(i, i ^ offset) for i in range(cycle_size)])

    offsets = range(1, cycle_size)
    key_pool = lax.all_gather(keys, "seq", tiled=True)
    value_pool = lax.all_gather(values, "seq", tiled=True)
    table = key_lists(rand_blocks, global_blocks, myself, blocks_here, cycle_size * blocks_here)
    grad_table = ((table // blocks_here) ^ myself) * blocks_here + table % blocks_here

    def send(grads):
        return [grads[0]] + [swap(grads[offset], offset) for offset in offsets]

    def total(grads):
        return sum(grad.astype(jnp.float32) for grad in grads).astype(jnp.bfloat16)

    out, query_grad, dk, dv = attend(
        table, grad_table, queries, out_grad, (), [key_pool], [value_pool],
        [keys.shape[0]] * cycle_size, send,
    )
    return out, query_grad, total(dk), total(dv)


def sparse_local(queries, keys, values, out_grad, rand_blocks, global_blocks):
    cycle_size = lax.axis_size("seq")
    myself = lax.axis_index("seq").astype(jnp.int32)
    tok_rows, width = keys.shape
    blocks_here = tok_rows // BLOCK
    rand_total = RAND * blocks_here
    capacity = (rand_total + GLOB + cycle_size - 1) // cycle_size
    slot_total = cycle_size * capacity
    listed = jnp.concatenate(
        [
            rand_blocks.reshape(cycle_size, rand_total),
            jnp.broadcast_to(global_blocks[None, :], (cycle_size, GLOB)),
        ],
        axis=1,
    )
    entries = listed.shape[1]
    owners = listed // blocks_here
    local_slot = listed % blocks_here
    earlier = jnp.arange(entries)[None, :] < jnp.arange(entries)[:, None]
    same_owner = owners[:, :, None] == owners[:, None, :]
    ranking = jnp.sum(same_owner & earlier[None], axis=2)
    owners_mine = lax.dynamic_index_in_dim(owners, myself, 0, keepdims=False)
    ranking_mine = lax.dynamic_index_in_dim(ranking, myself, 0, keepdims=False)
    far_place = (blocks_here + 2 + owners_mine * capacity + ranking_mine).astype(jnp.int32)
    slot_ids = jnp.arange(slot_total)
    requester = slot_ids // capacity
    position = slot_ids % capacity
    matches = (owners[requester] == myself) & (ranking[requester] == position[:, None])
    source = jnp.sum(jnp.where(matches, local_slot[requester], 0), axis=1)

    up = [(i, (i + 1) % cycle_size) for i in range(cycle_size)]
    down = [(j, i) for i, j in up]
    pair = jnp.concatenate([keys, values], axis=1)
    before = lax.ppermute(pair[tok_rows - BLOCK :], "seq", up)
    after = lax.ppermute(pair[:BLOCK], "seq", down)
    outgoing = jnp.take(pair.reshape(blocks_here, BLOCK, 2 * width), source, axis=0)
    far = lax.all_to_all(outgoing, "seq", split_axis=0, concat_axis=0, tiled=True)
    others = [before, after, far.reshape(slot_total * BLOCK, 2 * width)]
    key_parts = [part[:, :width] for part in others]
    value_parts = [part[:, width:] for part in others]

    here = jnp.arange(blocks_here, dtype=jnp.int32)[:, None]
    ahead = jnp.where(here == 0, blocks_here, here - 1)
    behind = jnp.where(here == blocks_here - 1, blocks_here + 1, here + 1)
    table = jnp.concatenate(
        [
            ahead,
            here,
            behind,
            jnp.broadcast_to(far_place[None, rand_total:], (blocks_here, GLOB)),
            far_place[:rand_total].reshape(blocks_here, RAND),
        ],
        axis=1,
    )
    landing = (source[:, None] == jnp.arange(blocks_here)[None, :]).astype(jnp.bfloat16)

    def send(grads):
        own, grad_before, grad_after, grad_far = grads
        last_rim = lax.ppermute(grad_before, "seq", down)
        first_rim = lax.ppermute(grad_after, "seq", up)
        returned = lax.all_to_all(
            grad_far.reshape(slot_total, BLOCK, width),
            "seq", split_axis=0, concat_axis=0, tiled=True,
        )
        return [own, last_rim, first_rim, returned]

    def total(grads):
        own, last_rim, first_rim, returned = grads
        landed = jnp.einsum("sq,sbx->qbx", landing, returned, preferred_element_type=jnp.float32)
        sums = own.reshape(blocks_here, BLOCK, width) + landed
        sums = sums.at[blocks_here - 1].add(last_rim.astype(jnp.float32))
        sums = sums.at[0].add(first_rim.astype(jnp.float32))
        return sums.reshape(tok_rows, width).astype(jnp.bfloat16)

    grad_rows = [tok_rows] + [part.shape[0] for part in key_parts]
    out, query_grad, dk, dv = attend(
        table, table, queries, out_grad, (keys, values), key_parts, value_parts, grad_rows, send
    )
    return out, query_grad, total(dk), total(dv)


def local(queries, keys, values, out_grad, rand_blocks, global_blocks):
    cycle_size = lax.axis_size("seq")
    blocks_here = queries.shape[0] // BLOCK
    capacity = (RAND * blocks_here + GLOB + cycle_size - 1) // cycle_size
    dense = capacity >= blocks_here and cycle_size & (cycle_size - 1) == 0
    plan = dense_local if dense else sparse_local
    return plan(queries, keys, values, out_grad, rand_blocks, global_blocks)


def solution(mesh):
    rows = P(("dp", "seq"), None)
    return jax.shard_map(
        local,
        mesh=mesh,
        in_specs=(rows, rows, rows, rows, P("dp", None), P("dp")),
        out_specs=(rows, rows, rows, rows),
        check_vma=False,
    )
```

```python
import functools

import jax
import jax.numpy as jnp
from jax import lax
from jax.experimental import pallas as pl
from jax.experimental.pallas import tpu as pltpu
from jax.sharding import PartitionSpec as P

KVH = 2
HD = 128
BLOCK = 64
GLOB = 2
RAND = 3
GROUP = 4
ENTRIES = 3 + GLOB + RAND
LOG2E = 1.4426950408889634
SCALE = HD ** (-0.5)


NN = (((1,), (0,)), ((), ()))
TN = (((0,), (0,)), ((), ()))
dot = functools.partial(lax.dot_general, preferred_element_type=jnp.float32)

KEYS = ENTRIES * BLOCK
ROWS = GROUP * BLOCK


def units(blocks_here):
    return [(b, h, b * KVH + h) for b in range(blocks_here) for h in range(KVH)]


def given_places(lists, blocks_here, b):
    return [lists[0][b, e] for e in range(ENTRIES)]


def dense_places(cycle_size, lists, blocks_here, b):
    rand_ref, glob_ref, me_ref = lists
    me = me_ref[0]

    def place(owner, local):
        return (owner ^ me) * blocks_here + local

    def far_place(block):
        return place(lax.div(block, blocks_here), lax.rem(block, blocks_here))

    window = [b - 1, b, b + 1]
    if b == 0:
        window[0] = place(lax.rem(me + cycle_size - 1, cycle_size), blocks_here - 1)
    if b == blocks_here - 1:
        window[2] = place(lax.rem(me + 1, cycle_size), 0)
    far = [glob_ref[i] for i in range(GLOB)] + [rand_ref[i, me * blocks_here + b] for i in range(RAND)]
    return window + [far_place(block) for block in far]


def spans(table, b):
    result = []
    for e in range(ENTRIES):
        near = b + e - 1
        if e < 3 and 0 <= near < table.shape[0]:
            result.append(pl.ds(near * BLOCK, BLOCK))
        else:
            result.append(pl.ds(pl.multiple_of(table[b, e] * BLOCK, BLOCK), BLOCK))
    return result


def picked(pool, places, h):
    return jnp.concatenate([pool[place, h * HD : (h + 1) * HD] for place in places], axis=0)


def unstack(ref, b, h, value):
    for j in range(GROUP):
        c = (h * GROUP + j) * HD
        ref[b * BLOCK : (b + 1) * BLOCK, c : c + HD] = value[j * BLOCK : (j + 1) * BLOCK]


def add_terms(pool, places, h, terms):
    for e, place in enumerate(places):
        pool[place, h * HD : (h + 1) * HD] += terms[e * BLOCK : (e + 1) * BLOCK]


def gather_pool(pool, parts):
    start = 0
    for part in parts:
        pool[start : start + part.shape[0]] = part[...]
        start += part.shape[0]


def split_pool(outs, pool, factor):
    start = 0
    for out in outs:
        total = pool[start : start + out.shape[0]]
        out[...] = (total if factor is None else total * factor).astype(out.dtype)
        start += out.shape[0]


def stage_kernel(locate, count, *refs):
    lists, refs = refs[:count], refs[count:]
    q_any, g_any, k_any, v_any, table, *refs = refs
    q_rows, g_rows, q_cols, g_cols, k_ref, v_ref, q_ref, g_ref, sem = refs
    pairs = [(q_any, q_ref), (g_any, g_ref), (k_any, k_ref), (v_any, v_ref)]
    copies = [pltpu.make_async_copy(*pair, sem.at[i]) for i, pair in enumerate(pairs)]
    for copy in copies:
        copy.start()
    for b in range(table.shape[0]):
        for e, place in enumerate(locate(lists, table.shape[0], b)):
            table[b, e] = jnp.int32(place)
    for copy, ref, rows, cols in ((copies[0], q_ref, q_rows, q_cols), (copies[1], g_ref, g_rows, g_cols)):
        copy.wait()
        for b, h, u in units(table.shape[0]):
            heads = [(h * GROUP + j) * HD for j in range(GROUP)]
            unit = jnp.concatenate(
                [ref[b * BLOCK : (b + 1) * BLOCK, c : c + HD] for c in heads], axis=0
            )
            rows[u * ROWS : (u + 1) * ROWS] = unit
            cols[u * HD : (u + 1) * HD] = unit.T
    copies[2].wait()
    copies[3].wait()


def probs_kernel(count, table, q_cols, g_rows, *refs):
    parts = refs[:count]
    probs_ref, k_pool, *dv_refs, dv_pool = refs[count:]
    gather_pool(k_pool, parts)
    dv_pool[...] = jnp.zeros_like(dv_pool)
    for b, h, u in units(table.shape[0]):
        places = spans(table, b)
        scores = dot(picked(k_pool, places, h), q_cols[u * HD : (u + 1) * HD], NN)
        peak = jnp.max(scores, axis=0, keepdims=True)
        expos = jnp.exp2((scores - peak) * (SCALE * LOG2E))
        probs = expos * (1.0 / jnp.sum(expos, axis=0, keepdims=True))
        probs_b = probs.astype(jnp.bfloat16)
        probs_ref[u * KEYS : (u + 1) * KEYS] = probs_b
        add_terms(dv_pool, places, h, dot(probs_b, g_rows[u * ROWS : (u + 1) * ROWS], NN))
    split_pool(dv_refs, dv_pool, None)


def dscores_kernel(count, table, q_rows, g_cols, probs_ref, *refs):
    parts = refs[:count]
    ds_ref, v_pool, *dk_refs, dk_pool = refs[count:]
    gather_pool(v_pool, parts)
    dk_pool[...] = jnp.zeros_like(dk_pool)
    for b, h, u in units(table.shape[0]):
        places = spans(table, b)
        probs = probs_ref[u * KEYS : (u + 1) * KEYS].astype(jnp.float32)
        dprobs = dot(picked(v_pool, places, h), g_cols[u * HD : (u + 1) * HD], NN)
        delta = jnp.sum(probs * dprobs, axis=0, keepdims=True)
        dscores = (probs * (dprobs - delta)).astype(jnp.bfloat16)
        ds_ref[u * KEYS : (u + 1) * KEYS] = dscores
        add_terms(dk_pool, places, h, dot(dscores, q_rows[u * ROWS : (u + 1) * ROWS], NN))
    split_pool(dk_refs, dk_pool, SCALE)


def rows_kernel(table, probs_ref, ds_ref, k_pool, v_pool, out_ref, qgrad_ref):
    for b, h, u in units(table.shape[0]):
        places = spans(table, b)
        span = slice(u * KEYS, (u + 1) * KEYS)
        attended = dot(probs_ref[span], picked(v_pool, places, h), TN)
        unstack(out_ref, b, h, attended.astype(jnp.bfloat16))
        qgrad = dot(ds_ref[span], picked(k_pool, places, h), TN) * SCALE
        unstack(qgrad_ref, b, h, qgrad.astype(jnp.bfloat16))


SMEM = pl.BlockSpec(memory_space=pltpu.SMEM)
HBM = pl.BlockSpec(memory_space=pltpu.HBM)
VMEM = pl.BlockSpec(memory_space=pltpu.VMEM)


def run_kernel(kernel, operands, in_specs, results, out_specs, scratch, products):
    flops = products * 2 * 4 * KVH * ROWS * KEYS * HD
    return pl.pallas_call(
        kernel,
        out_shape=[jax.ShapeDtypeStruct(shape, kind) for shape, kind in results],
        in_specs=in_specs + [VMEM] * (len(operands) - len(in_specs)),
        out_specs=out_specs + [VMEM] * (len(results) - len(out_specs)),
        scratch_shapes=scratch,
        compiler_params=pltpu.CompilerParams(vmem_limit_bytes=32 * 2**20),
        cost_estimate=pl.CostEstimate(
            flops=flops, bytes_accessed=products * 2**20, transcendentals=0
        ),
    )(*operands)


def stage(locate, lists, queries, out_grad, keys, values):
    blocks_here = queries.shape[0] // BLOCK
    half = jnp.bfloat16
    rows = ((blocks_here * KVH * ROWS, HD), half)
    cols = ((blocks_here * KVH * HD, ROWS), half)
    narrow, wide = (keys.shape, half), (queries.shape, half)
    mine = (queries, out_grad, keys, values)
    return run_kernel(
        functools.partial(stage_kernel, locate, len(lists)),
        [*lists, *(pltpu.with_memory_space_constraint(array, pltpu.HBM) for array in mine)],
        [SMEM] * len(lists) + [HBM] * 4,
        [((blocks_here, ENTRIES), jnp.int32), rows, rows, cols, cols, narrow, narrow],
        [SMEM],
        [pltpu.VMEM(*wide), pltpu.VMEM(*wide), pltpu.SemaphoreType.DMA((4,))],
        1,
    )


def attend(table, staged, key_parts, value_parts, send):
    q_rows, g_rows, q_cols, g_cols = staged
    tok_rows, width = key_parts[0].shape
    half, full = jnp.bfloat16, jnp.float32
    wide = ((tok_rows, GROUP * width), half)
    count = len(key_parts)
    pool_rows = sum(part.shape[0] for part in key_parts)
    held = ((table.shape[0] * KVH * KEYS, ROWS), half)
    sums = [(part.shape, half if i else full) for i, part in enumerate(key_parts)]
    scratch = [pltpu.VMEM((pool_rows, width), full)]
    pool = ((pool_rows, width), half)
    probs, k_pool, *dv = run_kernel(
        functools.partial(probs_kernel, count),
        (table, q_cols, g_rows, *key_parts),
        [SMEM], [held, pool, *sums], [], scratch, 2,
    )
    dv = send(dv)
    dscores, v_pool, *dk = run_kernel(
        functools.partial(dscores_kernel, count),
        (table, q_rows, g_cols, probs, *value_parts),
        [SMEM], [held, pool, *sums], [], scratch, 2,
    )
    dk = send(dk)
    dv[1], table = lax.optimization_barrier((dv[1], table))
    out, query_grad = run_kernel(
        rows_kernel, (table, probs, dscores, k_pool, v_pool), [SMEM], [wide, wide], [], [], 2
    )
    return out, query_grad, dk, dv


def dense_local(queries, keys, values, out_grad, rand_blocks, global_blocks):
    cycle_size = lax.axis_size("seq")
    myself = lax.axis_index("seq").astype(jnp.int32)

    def swap(array, offset):
        return lax.ppermute(array, "seq", [(i, i ^ offset) for i in range(cycle_size)])

    def send(grads):
        return [grads[0]] + [swap(grads[offset], offset) for offset in offsets]

    def total(grads):
        return sum(grad.astype(jnp.float32) for grad in grads).astype(jnp.bfloat16)

    offsets = range(1, cycle_size)
    key_parts = [swap(keys, offset) for offset in offsets]
    lists = [
        pltpu.with_memory_space_constraint(rand_blocks.T, pltpu.HBM),
        pltpu.with_memory_space_constraint(global_blocks, pltpu.HBM),
        myself[None],
    ]
    table, *staged, keys, values = stage(
        functools.partial(dense_places, cycle_size), lists, queries, out_grad, keys, values
    )
    value_parts = [swap(values, offset) for offset in offsets]
    out, query_grad, dk, dv = attend(
        table, staged, [keys, *key_parts], [values, *value_parts], send
    )
    return out, query_grad, total(dk), total(dv)


def sparse_local(queries, keys, values, out_grad, rand_blocks, global_blocks):
    cycle_size = lax.axis_size("seq")
    myself = lax.axis_index("seq").astype(jnp.int32)
    tok_rows, width = keys.shape
    blocks_here = tok_rows // BLOCK
    rand_total = RAND * blocks_here
    capacity = (rand_total + GLOB + cycle_size - 1) // cycle_size
    slot_total = cycle_size * capacity
    listed = jnp.concatenate(
        [
            rand_blocks.reshape(cycle_size, rand_total),
            jnp.broadcast_to(global_blocks[None, :], (cycle_size, GLOB)),
        ],
        axis=1,
    )
    entries = listed.shape[1]
    owners = listed // blocks_here
    local_slot = listed % blocks_here
    earlier = jnp.arange(entries)[None, :] < jnp.arange(entries)[:, None]
    same_owner = owners[:, :, None] == owners[:, None, :]
    ranking = jnp.sum(same_owner & earlier[None], axis=2)
    owners_mine = lax.dynamic_index_in_dim(owners, myself, 0, keepdims=False)
    ranking_mine = lax.dynamic_index_in_dim(ranking, myself, 0, keepdims=False)
    far_place = (blocks_here + 2 + owners_mine * capacity + ranking_mine).astype(jnp.int32)
    slot_ids = jnp.arange(slot_total)
    requester = slot_ids // capacity
    position = slot_ids % capacity
    matches = (owners[requester] == myself) & (ranking[requester] == position[:, None])
    source = jnp.sum(jnp.where(matches, local_slot[requester], 0), axis=1)

    up = [(i, (i + 1) % cycle_size) for i in range(cycle_size)]
    down = [(j, i) for i, j in up]
    pair = jnp.concatenate([keys, values], axis=1)
    before = lax.ppermute(pair[tok_rows - BLOCK :], "seq", up)
    after = lax.ppermute(pair[:BLOCK], "seq", down)
    outgoing = jnp.take(pair.reshape(blocks_here, BLOCK, 2 * width), source, axis=0)
    far = lax.all_to_all(outgoing, "seq", split_axis=0, concat_axis=0, tiled=True)
    others = [before, after, far.reshape(slot_total * BLOCK, 2 * width)]
    key_parts = [part[:, :width] for part in others]
    value_parts = [part[:, width:] for part in others]

    here = jnp.arange(blocks_here, dtype=jnp.int32)[:, None]
    ahead = jnp.where(here == 0, blocks_here, here - 1)
    behind = jnp.where(here == blocks_here - 1, blocks_here + 1, here + 1)
    table = jnp.concatenate(
        [
            ahead,
            here,
            behind,
            jnp.broadcast_to(far_place[None, rand_total:], (blocks_here, GLOB)),
            far_place[:rand_total].reshape(blocks_here, RAND),
        ],
        axis=1,
    )
    landing = (source[:, None] == jnp.arange(blocks_here)[None, :]).astype(jnp.bfloat16)

    def send(grads):
        own, grad_before, grad_after, grad_far = grads
        last_rim = lax.ppermute(grad_before, "seq", down)
        first_rim = lax.ppermute(grad_after, "seq", up)
        returned = lax.all_to_all(
            grad_far.reshape(slot_total, BLOCK, width),
            "seq", split_axis=0, concat_axis=0, tiled=True,
        )
        return [own, last_rim, first_rim, returned]

    def total(grads):
        own, last_rim, first_rim, returned = grads
        landed = jnp.einsum("sq,sbx->qbx", landing, returned, preferred_element_type=jnp.float32)
        sums = own.reshape(blocks_here, BLOCK, width) + landed
        sums = sums.at[blocks_here - 1].add(last_rim.astype(jnp.float32))
        sums = sums.at[0].add(first_rim.astype(jnp.float32))
        return sums.reshape(tok_rows, width).astype(jnp.bfloat16)

    table, *staged, keys, values = stage(
        given_places, (table,), queries, out_grad, keys, values
    )
    out, query_grad, dk, dv = attend(
        table, staged, [keys, *key_parts], [values, *value_parts], send
    )
    return out, query_grad, total(dk), total(dv)


def local(queries, keys, values, out_grad, rand_blocks, global_blocks):
    cycle_size = lax.axis_size("seq")
    blocks_here = queries.shape[0] // BLOCK
    capacity = (RAND * blocks_here + GLOB + cycle_size - 1) // cycle_size
    dense = capacity >= blocks_here and cycle_size & (cycle_size - 1) == 0
    plan = dense_local if dense else sparse_local
    return plan(queries, keys, values, out_grad, rand_blocks, global_blocks)


def solution(mesh):
    rows = P(("dp", "seq"), None)
    return jax.shard_map(
        local,
        mesh=mesh,
        in_specs=(rows, rows, rows, rows, P("dp", None), P("dp")),
        out_specs=(rows, rows, rows, rows),
        check_vma=False,
    )
```

```python
import functools

import jax
import jax.numpy as jnp
from jax import lax
from jax.experimental import pallas as pl
from jax.experimental.pallas import tpu as pltpu
from jax.sharding import PartitionSpec as P

KVH = 2
HD = 128
BLOCK = 64
GLOB = 2
RAND = 3
GROUP = 4
ENTRIES = 3 + GLOB + RAND
LOG2E = 1.4426950408889634
SCALE = HD ** (-0.5)


NN = (((1,), (0,)), ((), ()))
TN = (((0,), (0,)), ((), ()))
dot = functools.partial(lax.dot_general, preferred_element_type=jnp.float32)

KEYS = ENTRIES * BLOCK
ROWS = GROUP * BLOCK


def units(blocks_here):
    return [(b, h, b * KVH + h) for b in range(blocks_here) for h in range(KVH)]


def given_places(lists, blocks_here, b):
    return [lists[0][b, e] for e in range(ENTRIES)]


def dense_offsets(cycle_size, position):
    odd = position & 1
    offsets = list(range(cycle_size))
    offsets[1], offsets[2] = 1 + odd, 2 - odd
    return offsets


def dense_places(cycle_size, lists, blocks_here, b):
    rand_ref, glob_ref = lists
    me = lax.axis_index("seq").astype(jnp.int32)
    odd = lax.axis_index("dp").astype(jnp.int32) & 1

    def place(owner, local):
        offset = owner ^ me
        swapped = (odd == 1) & ((offset == 1) | (offset == 2))
        return jnp.where(swapped, 3 - offset, offset) * blocks_here + local

    def far_place(block):
        return place(lax.div(block, blocks_here), lax.rem(block, blocks_here))

    window = [b - 1, b, b + 1]
    if b == 0:
        window[0] = place(lax.rem(me + cycle_size - 1, cycle_size), blocks_here - 1)
    if b == blocks_here - 1:
        window[2] = place(lax.rem(me + 1, cycle_size), 0)
    far = [glob_ref[i] for i in range(GLOB)] + [rand_ref[i, me * blocks_here + b] for i in range(RAND)]
    return window + [far_place(block) for block in far]


def spans(table, b):
    result = []
    for e in range(ENTRIES):
        near = b + e - 1
        if e < 3 and 0 <= near < table.shape[0]:
            result.append(pl.ds(near * BLOCK, BLOCK))
        else:
            result.append(pl.ds(pl.multiple_of(table[b, e] * BLOCK, BLOCK), BLOCK))
    return result


def picked(pool, places, h):
    return jnp.concatenate([pool[place, h * HD : (h + 1) * HD] for place in places], axis=0)


def unstack(ref, b, h, value):
    for j in range(GROUP):
        c = (h * GROUP + j) * HD
        ref[b * BLOCK : (b + 1) * BLOCK, c : c + HD] = value[j * BLOCK : (j + 1) * BLOCK]


def add_terms(pool, places, h, terms):
    for e, place in enumerate(places):
        pool[place, h * HD : (h + 1) * HD] += terms[e * BLOCK : (e + 1) * BLOCK]


def gather_pool(pool, parts):
    start = 0
    for part in parts:
        pool[start : start + part.shape[0]] = part[...]
        start += part.shape[0]


def split_pool(outs, pool, factor):
    start = 0
    for out in outs:
        total = pool[start : start + out.shape[0]]
        out[...] = (total if factor is None else total * factor).astype(out.dtype)
        start += out.shape[0]


def stage_kernel(locate, count, *refs):
    sources, refs = refs[: count + 4], refs[count + 4 :]
    table, q_rows, g_rows, q_cols, g_cols, k_ref, v_ref, *refs = refs
    lists = refs[:count]
    q_ref, g_ref, sem = refs[count:]
    targets = [*lists, q_ref, g_ref, k_ref, v_ref]
    copies = [
        pltpu.make_async_copy(source, target, sem.at[i])
        for i, (source, target) in enumerate(zip(sources, targets))
    ]
    for copy in copies:
        copy.start()
    for copy in copies[:count]:
        copy.wait()
    copies = copies[count:]
    row = lax.broadcasted_iota(jnp.int32, table.shape, 0)
    column = lax.broadcasted_iota(jnp.int32, table.shape, 1)
    places = jnp.zeros(table.shape, jnp.int32)
    for b in range(table.shape[0]):
        for e, place in enumerate(locate(lists, table.shape[0], b)):
            places = jnp.where((row == b) & (column == e), place, places)
    table[...] = places
    for copy, ref, rows, cols in ((copies[0], q_ref, q_rows, q_cols), (copies[1], g_ref, g_rows, g_cols)):
        copy.wait()
        for b, h, u in units(table.shape[0]):
            heads = [(h * GROUP + j) * HD for j in range(GROUP)]
            unit = jnp.concatenate(
                [ref[b * BLOCK : (b + 1) * BLOCK, c : c + HD] for c in heads], axis=0
            )
            rows[u * ROWS : (u + 1) * ROWS] = unit
            cols[u * HD : (u + 1) * HD] = unit.T
    copies[2].wait()
    copies[3].wait()


def probs_kernel(count, table, q_cols, g_rows, *refs):
    parts = refs[:count]
    probs_ref, k_pool, *dv_refs, dv_pool = refs[count:]
    gather_pool(k_pool, parts)
    dv_pool[...] = jnp.zeros_like(dv_pool)
    for b, h, u in units(table.shape[0]):
        places = spans(table, b)
        scores = dot(picked(k_pool, places, h), q_cols[u * HD : (u + 1) * HD], NN)
        peak = jnp.max(scores, axis=0, keepdims=True)
        expos = jnp.exp2((scores - peak) * (SCALE * LOG2E))
        probs = expos * (1.0 / jnp.sum(expos, axis=0, keepdims=True))
        probs_b = probs.astype(jnp.bfloat16)
        probs_ref[u * KEYS : (u + 1) * KEYS] = probs_b
        add_terms(dv_pool, places, h, dot(probs_b, g_rows[u * ROWS : (u + 1) * ROWS], NN))
    split_pool(dv_refs, dv_pool, None)


def dscores_kernel(count, table, q_rows, g_cols, probs_ref, *refs):
    parts = refs[:count]
    ds_ref, v_pool, *dk_refs, dk_pool = refs[count:]
    gather_pool(v_pool, parts)
    dk_pool[...] = jnp.zeros_like(dk_pool)
    for b, h, u in units(table.shape[0]):
        places = spans(table, b)
        probs = probs_ref[u * KEYS : (u + 1) * KEYS].astype(jnp.float32)
        dprobs = dot(picked(v_pool, places, h), g_cols[u * HD : (u + 1) * HD], NN)
        delta = jnp.sum(probs * dprobs, axis=0, keepdims=True)
        dscores = (probs * (dprobs - delta)).astype(jnp.bfloat16)
        ds_ref[u * KEYS : (u + 1) * KEYS] = dscores
        add_terms(dk_pool, places, h, dot(dscores, q_rows[u * ROWS : (u + 1) * ROWS], NN))
    split_pool(dk_refs, dk_pool, SCALE)


def rows_kernel(table, probs_ref, ds_ref, k_pool, v_pool, out_ref, qgrad_ref):
    for b, h, u in units(table.shape[0]):
        places = spans(table, b)
        span = slice(u * KEYS, (u + 1) * KEYS)
        attended = dot(probs_ref[span], picked(v_pool, places, h), TN)
        unstack(out_ref, b, h, attended.astype(jnp.bfloat16))
        qgrad = dot(ds_ref[span], picked(k_pool, places, h), TN) * SCALE
        unstack(qgrad_ref, b, h, qgrad.astype(jnp.bfloat16))


SMEM = pl.BlockSpec(memory_space=pltpu.SMEM)
HBM = pl.BlockSpec(memory_space=pltpu.HBM)
VMEM = pl.BlockSpec(memory_space=pltpu.VMEM)


def run_kernel(kernel, operands, in_specs, results, scratch, products):
    flops = products * 2 * 4 * KVH * ROWS * KEYS * HD
    return pl.pallas_call(
        kernel,
        out_shape=[jax.ShapeDtypeStruct(shape, kind) for shape, kind in results],
        in_specs=in_specs + [VMEM] * (len(operands) - len(in_specs)),
        out_specs=[VMEM] * len(results),
        scratch_shapes=scratch,
        compiler_params=pltpu.CompilerParams(vmem_limit_bytes=32 * 2**20),
        cost_estimate=pl.CostEstimate(
            flops=flops, bytes_accessed=products * 2**20, transcendentals=0
        ),
    )(*operands)


def stage(locate, lists, queries, out_grad, keys, values):
    blocks_here = queries.shape[0] // BLOCK
    half = jnp.bfloat16
    rows = ((blocks_here * KVH * ROWS, HD), half)
    cols = ((blocks_here * KVH * HD, ROWS), half)
    narrow, wide = (keys.shape, half), (queries.shape, half)
    mine = (*lists, queries, out_grad, keys, values)
    return run_kernel(
        functools.partial(stage_kernel, locate, len(lists)),
        [pltpu.with_memory_space_constraint(array, pltpu.HBM) for array in mine],
        [HBM] * len(mine),
        [((blocks_here, ENTRIES), jnp.int32), rows, rows, cols, cols, narrow, narrow],
        [
            *[pltpu.SMEM(array.shape, array.dtype) for array in lists],
            pltpu.VMEM(*wide), pltpu.VMEM(*wide),
            pltpu.SemaphoreType.DMA((len(mine),)),
        ],
        1,
    )


def attend(table, staged, key_parts, value_parts, send):
    q_rows, g_rows, q_cols, g_cols = staged
    tok_rows, width = key_parts[0].shape
    half, full = jnp.bfloat16, jnp.float32
    wide = ((tok_rows, GROUP * width), half)
    count = len(key_parts)
    pool_rows = sum(part.shape[0] for part in key_parts)
    held = ((table.shape[0] * KVH * KEYS, ROWS), half)
    sums = [(part.shape, half if i else full) for i, part in enumerate(key_parts)]
    scratch = [pltpu.VMEM((pool_rows, width), full)]
    pool = ((pool_rows, width), half)
    probs, k_pool, *dv = run_kernel(
        functools.partial(probs_kernel, count),
        (table, q_cols, g_rows, *key_parts),
        [SMEM], [held, pool, *sums], scratch, 2,
    )
    dv = send(dv, None)
    dscores, v_pool, *dk = run_kernel(
        functools.partial(dscores_kernel, count),
        (table, q_rows, g_cols, probs, *value_parts),
        [SMEM], [held, pool, *sums], scratch, 2,
    )
    dk = send(dk, dv)
    dv[1], table = lax.optimization_barrier((dv[1], table))
    out, query_grad = run_kernel(
        rows_kernel, (table, probs, dscores, k_pool, v_pool), [SMEM], [wide, wide], [], 2
    )
    return out, query_grad, dk, dv


def dense_local(queries, keys, values, out_grad, rand_blocks, global_blocks):
    cycle_size = lax.axis_size("seq")
    positions = lax.axis_size("dp")

    def swap(array, part):
        pairs = []
        for position in range(positions):
            offset = dense_offsets(cycle_size, position)[part]
            pairs += [(i * positions + position, (i ^ offset) * positions + position) for i in range(cycle_size)]
        return lax.ppermute(array, ("seq", "dp"), pairs)

    def send(grads, earlier):
        sent = [grads[0]] + [None] * (cycle_size - 1)
        sent[-1] = swap(grads[-1], cycle_size - 1)
        near = grads[1:-1]
        if earlier is not None:
            near, earlier[1] = lax.optimization_barrier((near, earlier[1]))
        for part in range(1, cycle_size - 1):
            sent[part] = swap(near[part - 1], part)
        return sent

    def total(grads):
        return sum(grad.astype(jnp.float32) for grad in grads).astype(jnp.bfloat16)

    parts = range(1, cycle_size)
    key_parts = [swap(keys, part) for part in parts]
    table, *staged, keys, values = stage(
        functools.partial(dense_places, cycle_size), (rand_blocks.T, global_blocks),
        queries, out_grad, keys, values,
    )
    value_parts = [swap(values, part) for part in parts]
    out, query_grad, dk, dv = attend(
        table, staged, [keys, *key_parts], [values, *value_parts], send
    )
    return out, query_grad, total(dk), total(dv)


def sparse_local(queries, keys, values, out_grad, rand_blocks, global_blocks):
    cycle_size = lax.axis_size("seq")
    myself = lax.axis_index("seq").astype(jnp.int32)
    tok_rows, width = keys.shape
    blocks_here = tok_rows // BLOCK
    rand_total = RAND * blocks_here
    capacity = (rand_total + GLOB + cycle_size - 1) // cycle_size
    slot_total = cycle_size * capacity
    listed = jnp.concatenate(
        [
            rand_blocks.reshape(cycle_size, rand_total),
            jnp.broadcast_to(global_blocks[None, :], (cycle_size, GLOB)),
        ],
        axis=1,
    )
    entries = listed.shape[1]
    owners = listed // blocks_here
    local_slot = listed % blocks_here
    earlier = jnp.arange(entries)[None, :] < jnp.arange(entries)[:, None]
    same_owner = owners[:, :, None] == owners[:, None, :]
    ranking = jnp.sum(same_owner & earlier[None], axis=2)
    owners_mine = lax.dynamic_index_in_dim(owners, myself, 0, keepdims=False)
    ranking_mine = lax.dynamic_index_in_dim(ranking, myself, 0, keepdims=False)
    far_place = (blocks_here + 2 + owners_mine * capacity + ranking_mine).astype(jnp.int32)
    slot_ids = jnp.arange(slot_total)
    requester = slot_ids // capacity
    position = slot_ids % capacity
    matches = (owners[requester] == myself) & (ranking[requester] == position[:, None])
    source = jnp.sum(jnp.where(matches, local_slot[requester], 0), axis=1)

    up = [(i, (i + 1) % cycle_size) for i in range(cycle_size)]
    down = [(j, i) for i, j in up]
    pair = jnp.concatenate([keys, values], axis=1)
    before = lax.ppermute(pair[tok_rows - BLOCK :], "seq", up)
    after = lax.ppermute(pair[:BLOCK], "seq", down)
    outgoing = jnp.take(pair.reshape(blocks_here, BLOCK, 2 * width), source, axis=0)
    far = lax.all_to_all(outgoing, "seq", split_axis=0, concat_axis=0, tiled=True)
    others = [before, after, far.reshape(slot_total * BLOCK, 2 * width)]
    key_parts = [part[:, :width] for part in others]
    value_parts = [part[:, width:] for part in others]

    here = jnp.arange(blocks_here, dtype=jnp.int32)[:, None]
    ahead = jnp.where(here == 0, blocks_here, here - 1)
    behind = jnp.where(here == blocks_here - 1, blocks_here + 1, here + 1)
    table = jnp.concatenate(
        [
            ahead,
            here,
            behind,
            jnp.broadcast_to(far_place[None, rand_total:], (blocks_here, GLOB)),
            far_place[:rand_total].reshape(blocks_here, RAND),
        ],
        axis=1,
    )
    landing = (source[:, None] == jnp.arange(blocks_here)[None, :]).astype(jnp.bfloat16)

    def send(grads, earlier):
        own, grad_before, grad_after, grad_far = grads
        last_rim = lax.ppermute(grad_before, "seq", down)
        first_rim = lax.ppermute(grad_after, "seq", up)
        returned = lax.all_to_all(
            grad_far.reshape(slot_total, BLOCK, width),
            "seq", split_axis=0, concat_axis=0, tiled=True,
        )
        return [own, last_rim, first_rim, returned]

    def total(grads):
        own, last_rim, first_rim, returned = grads
        landed = jnp.einsum("sq,sbx->qbx", landing, returned, preferred_element_type=jnp.float32)
        sums = own.reshape(blocks_here, BLOCK, width) + landed
        sums = sums.at[blocks_here - 1].add(last_rim.astype(jnp.float32))
        sums = sums.at[0].add(first_rim.astype(jnp.float32))
        return sums.reshape(tok_rows, width).astype(jnp.bfloat16)

    table, *staged, keys, values = stage(
        given_places, (table,), queries, out_grad, keys, values
    )
    out, query_grad, dk, dv = attend(
        table, staged, [keys, *key_parts], [values, *value_parts], send
    )
    return out, query_grad, total(dk), total(dv)


def local(queries, keys, values, out_grad, rand_blocks, global_blocks):
    cycle_size = lax.axis_size("seq")
    blocks_here = queries.shape[0] // BLOCK
    capacity = (RAND * blocks_here + GLOB + cycle_size - 1) // cycle_size
    dense = capacity >= blocks_here and cycle_size == 4
    plan = dense_local if dense else sparse_local
    return plan(queries, keys, values, out_grad, rand_blocks, global_blocks)


def solution(mesh):
    rows = P(("dp", "seq"), None)
    return jax.shard_map(
        local,
        mesh=mesh,
        in_specs=(rows, rows, rows, rows, P("dp", None), P("dp")),
        out_specs=(rows, rows, rows, rows),
        check_vma=False,
    )
```

```python
import functools

import jax
import jax.numpy as jnp
from jax import lax
from jax.experimental import pallas as pl
from jax.experimental.pallas import tpu as pltpu
from jax.sharding import PartitionSpec as P

KVH = 2
HD = 128
BLOCK = 64
GLOB = 2
RAND = 3
GROUP = 4
ENTRIES = 3 + GLOB + RAND
LOG2E = 1.4426950408889634
SCALE = HD ** (-0.5)


NN = (((1,), (0,)), ((), ()))
TN = (((0,), (0,)), ((), ()))
dot = functools.partial(lax.dot_general, preferred_element_type=jnp.float32)

KEYS = ENTRIES * BLOCK
ROWS = GROUP * BLOCK


def units(blocks_here):
    return [(b, h, b * KVH + h) for b in range(blocks_here) for h in range(KVH)]


def given_places(lists, blocks_here, b):
    return [lists[0][b, e] for e in range(ENTRIES)]


def dense_offsets(cycle_size, position):
    odd = position & 1
    offsets = list(range(cycle_size))
    offsets[1], offsets[2] = 1 + odd, 2 - odd
    return offsets


def dense_places(cycle_size, lists, blocks_here, b):
    rand_ref, glob_ref = lists
    me = lax.axis_index("seq").astype(jnp.int32)
    odd = lax.axis_index("dp").astype(jnp.int32) & 1

    def place(owner, local):
        offset = owner ^ me
        swapped = (odd == 1) & ((offset == 1) | (offset == 2))
        return jnp.where(swapped, 3 - offset, offset) * blocks_here + local

    def far_place(block):
        return place(lax.div(block, blocks_here), lax.rem(block, blocks_here))

    window = [b - 1, b, b + 1]
    if b == 0:
        window[0] = place(lax.rem(me + cycle_size - 1, cycle_size), blocks_here - 1)
    if b == blocks_here - 1:
        window[2] = place(lax.rem(me + 1, cycle_size), 0)
    far = [glob_ref[i] for i in range(GLOB)] + [rand_ref[i, me * blocks_here + b] for i in range(RAND)]
    return window + [far_place(block) for block in far]


def spans(table, b):
    result = []
    for e in range(ENTRIES):
        near = b + e - 1
        if e < 3 and 0 <= near < table.shape[0]:
            result.append(pl.ds(near * BLOCK, BLOCK))
        else:
            result.append(pl.ds(pl.multiple_of(table[b, e] * BLOCK, BLOCK), BLOCK))
    return result


def picked(pool, places, h):
    return jnp.concatenate([pool[place, h * HD : (h + 1) * HD] for place in places], axis=0)


def unstack(ref, b, h, value):
    for j in range(GROUP):
        c = (h * GROUP + j) * HD
        ref[b * BLOCK : (b + 1) * BLOCK, c : c + HD] = value[j * BLOCK : (j + 1) * BLOCK]


def add_terms(pool, places, h, terms):
    for e, place in enumerate(places):
        pool[place, h * HD : (h + 1) * HD] += terms[e * BLOCK : (e + 1) * BLOCK]


def gather_pool(pool, parts):
    start = 0
    for part in parts:
        pool[start : start + part.shape[0]] = part[...]
        start += part.shape[0]


def split_pool(outs, pool, factor):
    start = 0
    for out in outs:
        total = pool[start : start + out.shape[0]]
        out[...] = (total if factor is None else total * factor).astype(out.dtype)
        start += out.shape[0]


def stage_kernel(locate, count, *refs):
    sources, refs = refs[: count + 4], refs[count + 4 :]
    table, q_rows, g_rows, q_cols, g_cols, k_ref, v_ref, *refs = refs
    lists = refs[:count]
    q_ref, g_ref, sem = refs[count:]
    targets = [*lists, q_ref, g_ref, k_ref, v_ref]
    copies = [
        pltpu.make_async_copy(source, target, sem.at[i])
        for i, (source, target) in enumerate(zip(sources, targets))
    ]
    for copy in copies:
        copy.start()
    for copy in copies[:count]:
        copy.wait()
    copies = copies[count:]
    row = lax.broadcasted_iota(jnp.int32, table.shape, 0)
    column = lax.broadcasted_iota(jnp.int32, table.shape, 1)
    places = jnp.zeros(table.shape, jnp.int32)
    for b in range(table.shape[0]):
        for e, place in enumerate(locate(lists, table.shape[0], b)):
            places = jnp.where((row == b) & (column == e), place, places)
    table[...] = places
    for copy, ref, rows, cols in ((copies[0], q_ref, q_rows, q_cols), (copies[1], g_ref, g_rows, g_cols)):
        copy.wait()
        for b, h, u in units(table.shape[0]):
            heads = [(h * GROUP + j) * HD for j in range(GROUP)]
            unit = jnp.concatenate(
                [ref[b * BLOCK : (b + 1) * BLOCK, c : c + HD] for c in heads], axis=0
            )
            rows[u * ROWS : (u + 1) * ROWS] = unit
            cols[u * HD : (u + 1) * HD] = unit.T
    copies[2].wait()
    copies[3].wait()


def probs_kernel(count, table, q_cols, g_rows, *refs):
    parts = refs[:count]
    probs_ref, k_pool, *dv_refs, dv_pool = refs[count:]
    gather_pool(k_pool, parts)
    dv_pool[...] = jnp.zeros_like(dv_pool)
    for b, h, u in units(table.shape[0]):
        places = spans(table, b)
        scores = dot(picked(k_pool, places, h), q_cols[u * HD : (u + 1) * HD], NN)
        peak = jnp.max(scores, axis=0, keepdims=True)
        expos = jnp.exp2((scores - peak) * (SCALE * LOG2E))
        probs = expos * (1.0 / jnp.sum(expos, axis=0, keepdims=True))
        probs_b = probs.astype(jnp.bfloat16)
        probs_ref[u * KEYS : (u + 1) * KEYS] = probs_b
        add_terms(dv_pool, places, h, dot(probs_b, g_rows[u * ROWS : (u + 1) * ROWS], NN))
    split_pool(dv_refs, dv_pool, None)


def dscores_kernel(count, table, q_rows, g_cols, probs_ref, *refs):
    parts = refs[:count]
    ds_ref, v_pool, *dk_refs, dk_pool = refs[count:]
    gather_pool(v_pool, parts)
    dk_pool[...] = jnp.zeros_like(dk_pool)
    for b, h, u in units(table.shape[0]):
        places = spans(table, b)
        probs = probs_ref[u * KEYS : (u + 1) * KEYS].astype(jnp.float32)
        dprobs = dot(picked(v_pool, places, h), g_cols[u * HD : (u + 1) * HD], NN)
        delta = jnp.sum(probs * dprobs, axis=0, keepdims=True)
        dscores = (probs * (dprobs - delta)).astype(jnp.bfloat16)
        ds_ref[u * KEYS : (u + 1) * KEYS] = dscores
        add_terms(dk_pool, places, h, dot(dscores, q_rows[u * ROWS : (u + 1) * ROWS], NN))
    split_pool(dk_refs, dk_pool, SCALE)


def rows_kernel(factor, table, weights_ref, pool, out_ref):
    for b, h, u in units(table.shape[0]):
        keys = picked(pool, spans(table, b), h)
        result = dot(weights_ref[u * KEYS : (u + 1) * KEYS], keys, TN)
        unstack(out_ref, b, h, (result if factor is None else result * factor).astype(out_ref.dtype))


SMEM = pl.BlockSpec(memory_space=pltpu.SMEM)
HBM = pl.BlockSpec(memory_space=pltpu.HBM)
VMEM = pl.BlockSpec(memory_space=pltpu.VMEM)


def run_kernel(kernel, operands, in_specs, results, scratch, products):
    flops = products * 2 * 4 * KVH * ROWS * KEYS * HD
    return pl.pallas_call(
        kernel,
        out_shape=[jax.ShapeDtypeStruct(shape, kind) for shape, kind in results],
        in_specs=in_specs + [VMEM] * (len(operands) - len(in_specs)),
        out_specs=[VMEM] * len(results),
        scratch_shapes=scratch,
        compiler_params=pltpu.CompilerParams(vmem_limit_bytes=32 * 2**20),
        cost_estimate=pl.CostEstimate(
            flops=flops, bytes_accessed=products * 2**20, transcendentals=0
        ),
    )(*operands)


def stage(locate, lists, queries, out_grad, keys, values):
    blocks_here = queries.shape[0] // BLOCK
    half = jnp.bfloat16
    rows = ((blocks_here * KVH * ROWS, HD), half)
    cols = ((blocks_here * KVH * HD, ROWS), half)
    narrow, wide = (keys.shape, half), (queries.shape, half)
    mine = (*lists, queries, out_grad, keys, values)
    return run_kernel(
        functools.partial(stage_kernel, locate, len(lists)),
        [pltpu.with_memory_space_constraint(array, pltpu.HBM) for array in mine],
        [HBM] * len(mine),
        [((blocks_here, ENTRIES), jnp.int32), rows, rows, cols, cols, narrow, narrow],
        [
            *[pltpu.SMEM(array.shape, array.dtype) for array in lists],
            pltpu.VMEM(*wide), pltpu.VMEM(*wide),
            pltpu.SemaphoreType.DMA((len(mine),)),
        ],
        1,
    )


def attend(table, staged, key_parts, value_parts, sums, send):
    q_rows, g_rows, q_cols, g_cols = staged
    tok_rows, width = key_parts[0].shape
    half, full = jnp.bfloat16, jnp.float32
    wide = ((tok_rows, GROUP * width), half)
    count = len(key_parts)
    pool_rows = sum(part.shape[0] for part in key_parts)
    held = ((table.shape[0] * KVH * KEYS, ROWS), half)
    sums = [((rows, width), kind) for rows, kind in sums]
    scratch = [pltpu.VMEM((pool_rows, width), full)]
    pool = ((pool_rows, width), half)
    probs, k_pool, *dv = run_kernel(
        functools.partial(probs_kernel, count),
        (table, q_cols, g_rows, *key_parts),
        [SMEM], [held, pool, *sums], scratch, 2,
    )
    dv, value_parts = lax.optimization_barrier((dv, value_parts))
    dv = send(dv)
    dscores, v_pool, *dk = run_kernel(
        functools.partial(dscores_kernel, count),
        (table, q_rows, g_cols, probs, *value_parts),
        [SMEM], [held, pool, *sums], scratch, 2,
    )
    dk = send(dk)
    dv[1], table = lax.optimization_barrier((dv[1], table))
    (out,) = run_kernel(
        functools.partial(rows_kernel, None), (table, probs, v_pool), [SMEM], [wide], [], 1
    )
    dk[1], out, table = lax.optimization_barrier((dk[1], out, table))
    (query_grad,) = run_kernel(
        functools.partial(rows_kernel, SCALE), (table, dscores, k_pool), [SMEM], [wide], [], 1
    )
    return out, query_grad, dk, dv


def dense_local(queries, keys, values, out_grad, rand_blocks, global_blocks):
    cycle_size = lax.axis_size("seq")
    positions = lax.axis_size("dp")

    def swap(array, part):
        pairs = []
        for position in range(positions):
            offset = dense_offsets(cycle_size, position)[part]
            pairs += [(i * positions + position, (i ^ offset) * positions + position) for i in range(cycle_size)]
        return lax.ppermute(array, ("seq", "dp"), pairs)

    def send(grads):
        kept, first = grads
        return [kept, swap(first, 2)]

    def total(grads):
        kept, received = grads
        mixed = kept + received.astype(jnp.float32)
        rows = mixed.shape[0] // 2
        returned = swap(mixed[rows:].astype(jnp.bfloat16), 1)
        return (mixed[:rows] + returned.astype(jnp.float32)).astype(jnp.bfloat16)

    def fetch(array):
        second, first = swap(array, 2), swap(array, 1)
        return [first, second, swap(second, 1)]

    key_parts = fetch(keys)
    table, *staged, keys, values = stage(
        functools.partial(dense_places, cycle_size), (rand_blocks.T, global_blocks),
        queries, out_grad, keys, values,
    )
    value_parts = fetch(values)
    sums = [(2 * keys.shape[0], jnp.float32), (2 * keys.shape[0], jnp.bfloat16)]
    out, query_grad, dk, dv = attend(
        table, staged, [keys, *key_parts], [values, *value_parts], sums, send
    )
    return out, query_grad, total(dk), total(dv)


def sparse_local(queries, keys, values, out_grad, rand_blocks, global_blocks):
    cycle_size = lax.axis_size("seq")
    myself = lax.axis_index("seq").astype(jnp.int32)
    tok_rows, width = keys.shape
    blocks_here = tok_rows // BLOCK
    rand_total = RAND * blocks_here
    capacity = (rand_total + GLOB + cycle_size - 1) // cycle_size
    slot_total = cycle_size * capacity
    listed = jnp.concatenate(
        [
            rand_blocks.reshape(cycle_size, rand_total),
            jnp.broadcast_to(global_blocks[None, :], (cycle_size, GLOB)),
        ],
        axis=1,
    )
    entries = listed.shape[1]
    owners = listed // blocks_here
    local_slot = listed % blocks_here
    earlier = jnp.arange(entries)[None, :] < jnp.arange(entries)[:, None]
    same_owner = owners[:, :, None] == owners[:, None, :]
    ranking = jnp.sum(same_owner & earlier[None], axis=2)
    owners_mine = lax.dynamic_index_in_dim(owners, myself, 0, keepdims=False)
    ranking_mine = lax.dynamic_index_in_dim(ranking, myself, 0, keepdims=False)
    far_place = (blocks_here + 2 + owners_mine * capacity + ranking_mine).astype(jnp.int32)
    slot_ids = jnp.arange(slot_total)
    requester = slot_ids // capacity
    position = slot_ids % capacity
    matches = (owners[requester] == myself) & (ranking[requester] == position[:, None])
    source = jnp.sum(jnp.where(matches, local_slot[requester], 0), axis=1)

    up = [(i, (i + 1) % cycle_size) for i in range(cycle_size)]
    down = [(j, i) for i, j in up]
    pair = jnp.concatenate([keys, values], axis=1)
    before = lax.ppermute(pair[tok_rows - BLOCK :], "seq", up)
    after = lax.ppermute(pair[:BLOCK], "seq", down)
    outgoing = jnp.take(pair.reshape(blocks_here, BLOCK, 2 * width), source, axis=0)
    far = lax.all_to_all(outgoing, "seq", split_axis=0, concat_axis=0, tiled=True)
    others = [before, after, far.reshape(slot_total * BLOCK, 2 * width)]
    key_parts = [part[:, :width] for part in others]
    value_parts = [part[:, width:] for part in others]

    here = jnp.arange(blocks_here, dtype=jnp.int32)[:, None]
    ahead = jnp.where(here == 0, blocks_here, here - 1)
    behind = jnp.where(here == blocks_here - 1, blocks_here + 1, here + 1)
    table = jnp.concatenate(
        [
            ahead,
            here,
            behind,
            jnp.broadcast_to(far_place[None, rand_total:], (blocks_here, GLOB)),
            far_place[:rand_total].reshape(blocks_here, RAND),
        ],
        axis=1,
    )
    landing = (source[:, None] == jnp.arange(blocks_here)[None, :]).astype(jnp.bfloat16)

    def send(grads):
        own, grad_before, grad_after, grad_far = grads
        last_rim = lax.ppermute(grad_before, "seq", down)
        first_rim = lax.ppermute(grad_after, "seq", up)
        returned = lax.all_to_all(
            grad_far.reshape(slot_total, BLOCK, width),
            "seq", split_axis=0, concat_axis=0, tiled=True,
        )
        return [own, last_rim, first_rim, returned]

    def total(grads):
        own, last_rim, first_rim, returned = grads
        landed = jnp.einsum("sq,sbx->qbx", landing, returned, preferred_element_type=jnp.float32)
        sums = own.reshape(blocks_here, BLOCK, width) + landed
        sums = sums.at[blocks_here - 1].add(last_rim.astype(jnp.float32))
        sums = sums.at[0].add(first_rim.astype(jnp.float32))
        return sums.reshape(tok_rows, width).astype(jnp.bfloat16)

    table, *staged, keys, values = stage(
        given_places, (table,), queries, out_grad, keys, values
    )
    sums = [(tok_rows, jnp.float32)] + [(part.shape[0], jnp.bfloat16) for part in key_parts]
    out, query_grad, dk, dv = attend(
        table, staged, [keys, *key_parts], [values, *value_parts], sums, send
    )
    return out, query_grad, total(dk), total(dv)


def local(queries, keys, values, out_grad, rand_blocks, global_blocks):
    cycle_size = lax.axis_size("seq")
    blocks_here = queries.shape[0] // BLOCK
    capacity = (RAND * blocks_here + GLOB + cycle_size - 1) // cycle_size
    dense = capacity >= blocks_here and cycle_size == 4
    plan = dense_local if dense else sparse_local
    return plan(queries, keys, values, out_grad, rand_blocks, global_blocks)


def solution(mesh):
    rows = P(("dp", "seq"), None)
    return jax.shard_map(
        local,
        mesh=mesh,
        in_specs=(rows, rows, rows, rows, P("dp", None), P("dp")),
        out_specs=(rows, rows, rows, rows),
        check_vma=False,
    )
```

```python
import functools

import jax
import jax.numpy as jnp
from jax import lax
from jax.experimental import pallas as pl
from jax.experimental.pallas import tpu as pltpu
from jax.sharding import PartitionSpec as P

KVH = 2
HD = 128
BLOCK = 64
GLOB = 2
RAND = 3
GROUP = 4
ENTRIES = 3 + GLOB + RAND
LOG2E = 1.4426950408889634
SCALE = HD ** (-0.5)


NN = (((1,), (0,)), ((), ()))
TN = (((0,), (0,)), ((), ()))
dot = functools.partial(lax.dot_general, preferred_element_type=jnp.float32)

KEYS = ENTRIES * BLOCK
ROWS = GROUP * BLOCK


def units(blocks_here):
    return [(b, h, b * KVH + h) for b in range(blocks_here) for h in range(KVH)]


def given_places(lists, blocks_here, b):
    return [lists[0][b, e] for e in range(ENTRIES)]


def dense_offsets(cycle_size, position):
    odd = position & 1
    offsets = list(range(cycle_size))
    offsets[1], offsets[2] = 1 + odd, 2 - odd
    return offsets


def dense_places(cycle_size, lists, blocks_here, b):
    rand_ref, glob_ref = lists
    me = lax.axis_index("seq").astype(jnp.int32)
    odd = lax.axis_index("dp").astype(jnp.int32) & 1

    def place(owner, local):
        offset = owner ^ me
        swapped = (odd == 1) & ((offset == 1) | (offset == 2))
        return jnp.where(swapped, 3 - offset, offset) * blocks_here + local

    def far_place(block):
        return place(lax.div(block, blocks_here), lax.rem(block, blocks_here))

    window = [b - 1, b, b + 1]
    if b == 0:
        window[0] = place(lax.rem(me + cycle_size - 1, cycle_size), blocks_here - 1)
    if b == blocks_here - 1:
        window[2] = place(lax.rem(me + 1, cycle_size), 0)
    far = [glob_ref[i] for i in range(GLOB)] + [rand_ref[i, me * blocks_here + b] for i in range(RAND)]
    return window + [far_place(block) for block in far]


def spans(table, b):
    result = []
    for e in range(ENTRIES):
        near = b + e - 1
        if e < 3 and 0 <= near < table.shape[0]:
            result.append(pl.ds(near * BLOCK, BLOCK))
        else:
            result.append(pl.ds(pl.multiple_of(table[b, e] * BLOCK, BLOCK), BLOCK))
    return result


def picked(pool, places, h):
    return jnp.concatenate([pool[place, h * HD : (h + 1) * HD] for place in places], axis=0)


def unstack(ref, b, h, value):
    for j in range(GROUP):
        c = (h * GROUP + j) * HD
        ref[b * BLOCK : (b + 1) * BLOCK, c : c + HD] = value[j * BLOCK : (j + 1) * BLOCK]


def add_terms(pool, places, h, terms):
    for e, place in enumerate(places):
        pool[place, h * HD : (h + 1) * HD] += terms[e * BLOCK : (e + 1) * BLOCK]


def gather_pool(pool, parts):
    start = 0
    for part in parts:
        pool[start : start + part.shape[0]] = part[...]
        start += part.shape[0]


def split_pool(outs, pool, factor):
    start = 0
    for out in outs:
        total = pool[start : start + out.shape[0]]
        out[...] = (total if factor is None else total * factor).astype(out.dtype)
        start += out.shape[0]


def stage_kernel(locate, count, *refs):
    sources, refs = refs[: count + 4], refs[count + 4 :]
    table, q_rows, g_rows, q_cols, g_cols, k_ref, v_ref, *refs = refs
    lists = refs[:count]
    q_ref, g_ref, sem = refs[count:]
    targets = [*lists, q_ref, g_ref, k_ref, v_ref]
    copies = [
        pltpu.make_async_copy(source, target, sem.at[i])
        for i, (source, target) in enumerate(zip(sources, targets))
    ]
    for copy in copies:
        copy.start()
    for copy in copies[:count]:
        copy.wait()
    copies = copies[count:]
    row = lax.broadcasted_iota(jnp.int32, table.shape, 0)
    column = lax.broadcasted_iota(jnp.int32, table.shape, 1)
    places = jnp.zeros(table.shape, jnp.int32)
    for b in range(table.shape[0]):
        for e, place in enumerate(locate(lists, table.shape[0], b)):
            places = jnp.where((row == b) & (column == e), place, places)
    table[...] = places
    for copy, ref, rows, cols in ((copies[0], q_ref, q_rows, q_cols), (copies[1], g_ref, g_rows, g_cols)):
        copy.wait()
        for b, h, u in units(table.shape[0]):
            heads = [(h * GROUP + j) * HD for j in range(GROUP)]
            unit = jnp.concatenate(
                [ref[b * BLOCK : (b + 1) * BLOCK, c : c + HD] for c in heads], axis=0
            )
            rows[u * ROWS : (u + 1) * ROWS] = unit
            cols[u * HD : (u + 1) * HD] = unit.T
    copies[2].wait()
    copies[3].wait()


def probs_kernel(count, table, q_cols, g_rows, *refs):
    parts = refs[:count]
    probs_ref, k_pool, *dv_refs, dv_pool = refs[count:]
    gather_pool(k_pool, parts)
    dv_pool[...] = jnp.zeros_like(dv_pool)
    for b, h, u in units(table.shape[0]):
        places = spans(table, b)
        scores = dot(picked(k_pool, places, h), q_cols[u * HD : (u + 1) * HD], NN)
        peak = jnp.max(scores, axis=0, keepdims=True)
        expos = jnp.exp2((scores - peak) * (SCALE * LOG2E))
        probs = expos * (1.0 / jnp.sum(expos, axis=0, keepdims=True))
        probs_b = probs.astype(jnp.bfloat16)
        probs_ref[u * KEYS : (u + 1) * KEYS] = probs_b
        add_terms(dv_pool, places, h, dot(probs_b, g_rows[u * ROWS : (u + 1) * ROWS], NN))
    split_pool(dv_refs, dv_pool, None)


def dscores_kernel(count, table, q_rows, g_cols, probs_ref, *refs):
    parts = refs[:count]
    ds_ref, v_pool, *dk_refs, dk_pool = refs[count:]
    gather_pool(v_pool, parts)
    dk_pool[...] = jnp.zeros_like(dk_pool)
    for b, h, u in units(table.shape[0]):
        places = spans(table, b)
        probs = probs_ref[u * KEYS : (u + 1) * KEYS].astype(jnp.float32)
        dprobs = dot(picked(v_pool, places, h), g_cols[u * HD : (u + 1) * HD], NN)
        delta = jnp.sum(probs * dprobs, axis=0, keepdims=True)
        dscores = (probs * (dprobs - delta)).astype(jnp.bfloat16)
        ds_ref[u * KEYS : (u + 1) * KEYS] = dscores
        add_terms(dk_pool, places, h, dot(dscores, q_rows[u * ROWS : (u + 1) * ROWS], NN))
    split_pool(dk_refs, dk_pool, SCALE)


def rows_kernel(table, probs_ref, ds_ref, k_pool, v_pool, out_ref, qgrad_ref):
    for b, h, u in units(table.shape[0]):
        places = spans(table, b)
        span = slice(u * KEYS, (u + 1) * KEYS)
        attended = dot(probs_ref[span], picked(v_pool, places, h), TN)
        unstack(out_ref, b, h, attended.astype(jnp.bfloat16))
        qgrad = dot(ds_ref[span], picked(k_pool, places, h), TN) * SCALE
        unstack(qgrad_ref, b, h, qgrad.astype(jnp.bfloat16))


SMEM = pl.BlockSpec(memory_space=pltpu.SMEM)
HBM = pl.BlockSpec(memory_space=pltpu.HBM)
VMEM = pl.BlockSpec(memory_space=pltpu.VMEM)


def run_kernel(kernel, operands, in_specs, results, scratch, products):
    flops = products * 2 * 4 * KVH * ROWS * KEYS * HD
    return pl.pallas_call(
        kernel,
        out_shape=[jax.ShapeDtypeStruct(shape, kind) for shape, kind in results],
        in_specs=in_specs + [VMEM] * (len(operands) - len(in_specs)),
        out_specs=[VMEM] * len(results),
        scratch_shapes=scratch,
        compiler_params=pltpu.CompilerParams(vmem_limit_bytes=32 * 2**20),
        cost_estimate=pl.CostEstimate(
            flops=flops, bytes_accessed=products * 2**20, transcendentals=0
        ),
    )(*operands)


def stage(locate, lists, queries, out_grad, keys, values):
    blocks_here = queries.shape[0] // BLOCK
    half = jnp.bfloat16
    rows = ((blocks_here * KVH * ROWS, HD), half)
    cols = ((blocks_here * KVH * HD, ROWS), half)
    narrow, wide = (keys.shape, half), (queries.shape, half)
    mine = (*lists, queries, out_grad, keys, values)
    return run_kernel(
        functools.partial(stage_kernel, locate, len(lists)),
        [pltpu.with_memory_space_constraint(array, pltpu.HBM) for array in mine],
        [HBM] * len(mine),
        [((blocks_here, ENTRIES), jnp.int32), rows, rows, cols, cols, narrow, narrow],
        [
            *[pltpu.SMEM(array.shape, array.dtype) for array in lists],
            pltpu.VMEM(*wide), pltpu.VMEM(*wide),
            pltpu.SemaphoreType.DMA((len(mine),)),
        ],
        1,
    )


def attend(table, staged, key_parts, value_parts, dk_sums, dv_sums, send_dk, send_dv):
    q_rows, g_rows, q_cols, g_cols = staged
    width = key_parts[0].shape[1]
    half, full = jnp.bfloat16, jnp.float32
    wide = ((table.shape[0] * BLOCK, GROUP * width), half)
    count = len(key_parts)
    pool_rows = sum(part.shape[0] for part in key_parts)
    held = ((table.shape[0] * KVH * KEYS, ROWS), half)
    scratch = [pltpu.VMEM((pool_rows, width), full)]
    pool = ((pool_rows, width), half)
    probs, k_pool, *dv = run_kernel(
        functools.partial(probs_kernel, count),
        (table, q_cols, g_rows, *key_parts),
        [SMEM], [held, pool, *(((rows, width), kind) for rows, kind in dv_sums)], scratch, 2,
    )
    dv, value_parts = lax.optimization_barrier((dv, value_parts))
    dv = send_dv(dv)
    dscores, v_pool, *dk = run_kernel(
        functools.partial(dscores_kernel, count),
        (table, q_rows, g_cols, probs, *value_parts),
        [SMEM], [held, pool, *(((rows, width), kind) for rows, kind in dk_sums)], scratch, 2,
    )
    dk = send_dk(dk)
    dv[1], table = lax.optimization_barrier((dv[1], table))
    out, query_grad = run_kernel(
        rows_kernel, (table, probs, dscores, k_pool, v_pool), [SMEM], [wide, wide], [], 2
    )
    dk[-1], query_grad = lax.optimization_barrier((dk[-1], query_grad))
    return out, query_grad, dk, dv


def dense_local(queries, keys, values, out_grad, rand_blocks, global_blocks):
    cycle_size = lax.axis_size("seq")
    positions = lax.axis_size("dp")

    def swap(array, part):
        pairs = []
        for position in range(positions):
            offset = dense_offsets(cycle_size, position)[part]
            pairs += [(i * positions + position, (i ^ offset) * positions + position) for i in range(cycle_size)]
        return lax.ppermute(array, ("seq", "dp"), pairs)

    def fetch(near, own):
        pair = jnp.concatenate([own, near], axis=0)
        return [pair, swap(pair, 2)]

    def send_dk(grads):
        own, first, second, far = grads
        return [own, swap(first, 1), swap(second, 2), swap(far, 3)]

    def send_dv(grads):
        kept, first = grads
        return [kept, swap(first, 2)]

    def total_dk(grads):
        return sum(grad.astype(jnp.float32) for grad in grads).astype(jnp.bfloat16)

    def total_dv(grads):
        kept, received = grads
        mixed = kept + received.astype(jnp.float32)
        returned = swap(mixed[rows:].astype(jnp.bfloat16), 1)
        return (mixed[:rows] + returned.astype(jnp.float32)).astype(jnp.bfloat16)

    rows = keys.shape[0]
    near_keys, near_values = swap(keys, 1), swap(values, 1)
    table, *staged, own_keys, own_values = stage(
        functools.partial(dense_places, cycle_size), (rand_blocks.T, global_blocks),
        queries, out_grad, keys, values,
    )
    half, full = jnp.bfloat16, jnp.float32
    out, query_grad, dk, dv = attend(
        table, staged, fetch(near_keys, own_keys), fetch(near_values, own_values),
        [(rows, full), (rows, half), (rows, half), (rows, half)],
        [(2 * rows, full), (2 * rows, half)], send_dk, send_dv,
    )
    return out, query_grad, total_dk(dk), total_dv(dv)


def sparse_local(queries, keys, values, out_grad, rand_blocks, global_blocks):
    cycle_size = lax.axis_size("seq")
    myself = lax.axis_index("seq").astype(jnp.int32)
    tok_rows, width = keys.shape
    blocks_here = tok_rows // BLOCK
    rand_total = RAND * blocks_here
    capacity = (rand_total + GLOB + cycle_size - 1) // cycle_size
    slot_total = cycle_size * capacity
    listed = jnp.concatenate(
        [
            rand_blocks.reshape(cycle_size, rand_total),
            jnp.broadcast_to(global_blocks[None, :], (cycle_size, GLOB)),
        ],
        axis=1,
    )
    entries = listed.shape[1]
    owners = listed // blocks_here
    local_slot = listed % blocks_here
    earlier = jnp.arange(entries)[None, :] < jnp.arange(entries)[:, None]
    same_owner = owners[:, :, None] == owners[:, None, :]
    ranking = jnp.sum(same_owner & earlier[None], axis=2)
    owners_mine = lax.dynamic_index_in_dim(owners, myself, 0, keepdims=False)
    ranking_mine = lax.dynamic_index_in_dim(ranking, myself, 0, keepdims=False)
    far_place = (blocks_here + 2 + owners_mine * capacity + ranking_mine).astype(jnp.int32)
    slot_ids = jnp.arange(slot_total)
    requester = slot_ids // capacity
    position = slot_ids % capacity
    matches = (owners[requester] == myself) & (ranking[requester] == position[:, None])
    source = jnp.sum(jnp.where(matches, local_slot[requester], 0), axis=1)

    up = [(i, (i + 1) % cycle_size) for i in range(cycle_size)]
    down = [(j, i) for i, j in up]
    pair = jnp.concatenate([keys, values], axis=1)
    before = lax.ppermute(pair[tok_rows - BLOCK :], "seq", up)
    after = lax.ppermute(pair[:BLOCK], "seq", down)
    outgoing = jnp.take(pair.reshape(blocks_here, BLOCK, 2 * width), source, axis=0)
    far = lax.all_to_all(outgoing, "seq", split_axis=0, concat_axis=0, tiled=True)
    others = [before, after, far.reshape(slot_total * BLOCK, 2 * width)]
    key_parts = [part[:, :width] for part in others]
    value_parts = [part[:, width:] for part in others]

    here = jnp.arange(blocks_here, dtype=jnp.int32)[:, None]
    ahead = jnp.where(here == 0, blocks_here, here - 1)
    behind = jnp.where(here == blocks_here - 1, blocks_here + 1, here + 1)
    table = jnp.concatenate(
        [
            ahead,
            here,
            behind,
            jnp.broadcast_to(far_place[None, rand_total:], (blocks_here, GLOB)),
            far_place[:rand_total].reshape(blocks_here, RAND),
        ],
        axis=1,
    )
    landing = (source[:, None] == jnp.arange(blocks_here)[None, :]).astype(jnp.bfloat16)

    def send(grads):
        own, grad_before, grad_after, grad_far = grads
        last_rim = lax.ppermute(grad_before, "seq", down)
        first_rim = lax.ppermute(grad_after, "seq", up)
        returned = lax.all_to_all(
            grad_far.reshape(slot_total, BLOCK, width),
            "seq", split_axis=0, concat_axis=0, tiled=True,
        )
        return [own, last_rim, first_rim, returned]

    def total(grads):
        own, last_rim, first_rim, returned = grads
        landed = jnp.einsum("sq,sbx->qbx", landing, returned, preferred_element_type=jnp.float32)
        sums = own.reshape(blocks_here, BLOCK, width) + landed
        sums = sums.at[blocks_here - 1].add(last_rim.astype(jnp.float32))
        sums = sums.at[0].add(first_rim.astype(jnp.float32))
        return sums.reshape(tok_rows, width).astype(jnp.bfloat16)

    table, *staged, keys, values = stage(
        given_places, (table,), queries, out_grad, keys, values
    )
    sums = [(tok_rows, jnp.float32)] + [(part.shape[0], jnp.bfloat16) for part in key_parts]
    out, query_grad, dk, dv = attend(
        table, staged, [keys, *key_parts], [values, *value_parts], sums, sums,
        send, send,
    )
    return out, query_grad, total(dk), total(dv)


def local(queries, keys, values, out_grad, rand_blocks, global_blocks):
    cycle_size = lax.axis_size("seq")
    blocks_here = queries.shape[0] // BLOCK
    capacity = (RAND * blocks_here + GLOB + cycle_size - 1) // cycle_size
    dense = capacity >= blocks_here and cycle_size == 4
    plan = dense_local if dense else sparse_local
    return plan(queries, keys, values, out_grad, rand_blocks, global_blocks)


def solution(mesh):
    rows = P(("dp", "seq"), None)
    return jax.shard_map(
        local,
        mesh=mesh,
        in_specs=(rows, rows, rows, rows, P("dp", None), P("dp")),
        out_specs=(rows, rows, rows, rows),
        check_vma=False,
    )
```

```python
import functools

import jax
import jax.numpy as jnp
from jax import lax
from jax.experimental import pallas as pl
from jax.experimental.pallas import tpu as pltpu
from jax.sharding import PartitionSpec as P

KVH = 2
HD = 128
BLOCK = 64
GLOB = 2
RAND = 3
GROUP = 4
ENTRIES = 3 + GLOB + RAND
LOG2E = 1.4426950408889634
SCALE = HD ** (-0.5)


NN = (((1,), (0,)), ((), ()))
TN = (((0,), (0,)), ((), ()))
dot = functools.partial(lax.dot_general, preferred_element_type=jnp.float32)

KEYS = ENTRIES * BLOCK
ROWS = GROUP * BLOCK


def units(blocks_here):
    return [(b, h, b * KVH + h) for b in range(blocks_here) for h in range(KVH)]


def given_places(lists, blocks_here, b):
    return [lists[0][b, e] for e in range(ENTRIES)]


def dense_offsets(cycle_size, position):
    odd = position & 1
    offsets = list(range(cycle_size))
    offsets[1], offsets[2] = 1 + odd, 2 - odd
    return offsets


def dense_places(cycle_size, lists, blocks_here, b):
    rand_ref, glob_ref = lists
    me = lax.axis_index("seq").astype(jnp.int32)
    odd = lax.axis_index("dp").astype(jnp.int32) & 1

    def place(owner, local):
        offset = owner ^ me
        swapped = (odd == 1) & ((offset == 1) | (offset == 2))
        return jnp.where(swapped, 3 - offset, offset) * blocks_here + local

    def far_place(block):
        return place(lax.div(block, blocks_here), lax.rem(block, blocks_here))

    window = [b - 1, b, b + 1]
    if b == 0:
        window[0] = place(lax.rem(me + cycle_size - 1, cycle_size), blocks_here - 1)
    if b == blocks_here - 1:
        window[2] = place(lax.rem(me + 1, cycle_size), 0)
    far = [glob_ref[i] for i in range(GLOB)] + [rand_ref[i, me * blocks_here + b] for i in range(RAND)]
    return window + [far_place(block) for block in far]


def spans(table, b):
    result = []
    for e in range(ENTRIES):
        near = b + e - 1
        if e < 3 and 0 <= near < table.shape[0]:
            result.append(pl.ds(near * BLOCK, BLOCK))
        else:
            result.append(pl.ds(pl.multiple_of(table[b, e] * BLOCK, BLOCK), BLOCK))
    return result


def picked(pool, places, h):
    return jnp.concatenate([pool[place, h * HD : (h + 1) * HD] for place in places], axis=0)


def unstack(ref, b, h, value):
    for j in range(GROUP):
        c = (h * GROUP + j) * HD
        ref[b * BLOCK : (b + 1) * BLOCK, c : c + HD] = value[j * BLOCK : (j + 1) * BLOCK]


def add_terms(pool, places, h, terms):
    for e, place in enumerate(places):
        pool[place, h * HD : (h + 1) * HD] += terms[e * BLOCK : (e + 1) * BLOCK]


def gather_pool(pool, parts):
    start = 0
    for part in parts:
        pool[start : start + part.shape[0]] = part[...]
        start += part.shape[0]


def split_pool(outs, pool, factor):
    start = 0
    for out in outs:
        total = pool[start : start + out.shape[0]]
        out[...] = (total if factor is None else total * factor).astype(out.dtype)
        start += out.shape[0]


def stage_kernel(locate, count, *refs):
    sources, refs = refs[: count + 4], refs[count + 4 :]
    table, q_rows, g_rows, q_cols, g_cols, k_ref, v_ref, *refs = refs
    lists = refs[:count]
    q_ref, g_ref, sem = refs[count:]
    targets = [*lists, q_ref, g_ref, k_ref, v_ref]
    copies = [
        pltpu.make_async_copy(source, target, sem.at[i])
        for i, (source, target) in enumerate(zip(sources, targets))
    ]
    for copy in copies:
        copy.start()
    for copy in copies[:count]:
        copy.wait()
    copies = copies[count:]
    row = lax.broadcasted_iota(jnp.int32, table.shape, 0)
    column = lax.broadcasted_iota(jnp.int32, table.shape, 1)
    places = jnp.zeros(table.shape, jnp.int32)
    for b in range(table.shape[0]):
        for e, place in enumerate(locate(lists, table.shape[0], b)):
            places = jnp.where((row == b) & (column == e), place, places)
    table[...] = places
    for copy, ref, rows, cols in ((copies[0], q_ref, q_rows, q_cols), (copies[1], g_ref, g_rows, g_cols)):
        copy.wait()
        for b, h, u in units(table.shape[0]):
            heads = [(h * GROUP + j) * HD for j in range(GROUP)]
            unit = jnp.concatenate(
                [ref[b * BLOCK : (b + 1) * BLOCK, c : c + HD] for c in heads], axis=0
            )
            rows[u * ROWS : (u + 1) * ROWS] = unit
            cols[u * HD : (u + 1) * HD] = unit.T
    copies[2].wait()
    copies[3].wait()


def probs_kernel(count, table, q_cols, g_rows, *refs):
    parts = refs[:count]
    probs_ref, k_pool, *dv_refs, dv_pool = refs[count:]
    gather_pool(k_pool, parts)
    dv_pool[...] = jnp.zeros_like(dv_pool)
    for b, h, u in units(table.shape[0]):
        places = spans(table, b)
        scores = dot(picked(k_pool, places, h), q_cols[u * HD : (u + 1) * HD], NN)
        peak = jnp.max(scores, axis=0, keepdims=True)
        expos = jnp.exp2((scores - peak) * (SCALE * LOG2E))
        probs = expos * (1.0 / jnp.sum(expos, axis=0, keepdims=True))
        probs_b = probs.astype(jnp.bfloat16)
        probs_ref[u * KEYS : (u + 1) * KEYS] = probs_b
        add_terms(dv_pool, places, h, dot(probs_b, g_rows[u * ROWS : (u + 1) * ROWS], NN))
    split_pool(dv_refs, dv_pool, None)


def dscores_kernel(count, carried, table, q_rows, g_cols, probs_ref, *refs):
    parts, refs = refs[:count], refs[count:]
    dv_refs, refs = refs[: len(carried)], refs[len(carried) :]
    ds_ref, v_pool, *dk_refs, dk_pool = refs
    gather_pool(v_pool, parts)
    dk_pool[...] = jnp.zeros_like(dk_pool)
    for i, dv_ref in zip(carried, dv_refs):
        dk_refs[i][parts[i].shape[0] :] = dv_ref[...]
    for b, h, u in units(table.shape[0]):
        places = spans(table, b)
        probs = probs_ref[u * KEYS : (u + 1) * KEYS].astype(jnp.float32)
        dprobs = dot(picked(v_pool, places, h), g_cols[u * HD : (u + 1) * HD], NN)
        delta = jnp.sum(probs * dprobs, axis=0, keepdims=True)
        dscores = (probs * (dprobs - delta)).astype(jnp.bfloat16)
        ds_ref[u * KEYS : (u + 1) * KEYS] = dscores
        add_terms(dk_pool, places, h, dot(dscores, q_rows[u * ROWS : (u + 1) * ROWS], NN))
    split_pool([ref.at[: part.shape[0]] for ref, part in zip(dk_refs, parts)], dk_pool, SCALE)


def rows_kernel(table, probs_ref, ds_ref, k_pool, v_pool, out_ref, qgrad_ref):
    for b, h, u in units(table.shape[0]):
        places = spans(table, b)
        span = slice(u * KEYS, (u + 1) * KEYS)
        attended = dot(probs_ref[span], picked(v_pool, places, h), TN)
        unstack(out_ref, b, h, attended.astype(jnp.bfloat16))
        qgrad = dot(ds_ref[span], picked(k_pool, places, h), TN) * SCALE
        unstack(qgrad_ref, b, h, qgrad.astype(jnp.bfloat16))


SMEM = pl.BlockSpec(memory_space=pltpu.SMEM)
HBM = pl.BlockSpec(memory_space=pltpu.HBM)
VMEM = pl.BlockSpec(memory_space=pltpu.VMEM)


def run_kernel(kernel, operands, in_specs, results, scratch, products):
    flops = products * 2 * 4 * KVH * ROWS * KEYS * HD
    return pl.pallas_call(
        kernel,
        out_shape=[jax.ShapeDtypeStruct(shape, kind) for shape, kind in results],
        in_specs=in_specs + [VMEM] * (len(operands) - len(in_specs)),
        out_specs=[VMEM] * len(results),
        scratch_shapes=scratch,
        compiler_params=pltpu.CompilerParams(vmem_limit_bytes=32 * 2**20),
        cost_estimate=pl.CostEstimate(
            flops=flops, bytes_accessed=products * 2**20, transcendentals=0
        ),
    )(*operands)


def stage(locate, lists, queries, out_grad, keys, values):
    blocks_here = queries.shape[0] // BLOCK
    half = jnp.bfloat16
    rows = ((blocks_here * KVH * ROWS, HD), half)
    cols = ((blocks_here * KVH * HD, ROWS), half)
    narrow, wide = (keys.shape, half), (queries.shape, half)
    mine = (*lists, queries, out_grad, keys, values)
    return run_kernel(
        functools.partial(stage_kernel, locate, len(lists)),
        [pltpu.with_memory_space_constraint(array, pltpu.HBM) for array in mine],
        [HBM] * len(mine),
        [((blocks_here, ENTRIES), jnp.int32), rows, rows, cols, cols, narrow, narrow],
        [
            *[pltpu.SMEM(array.shape, array.dtype) for array in lists],
            pltpu.VMEM(*wide), pltpu.VMEM(*wide),
            pltpu.SemaphoreType.DMA((len(mine),)),
        ],
        1,
    )


def attend(table, staged, key_parts, value_parts, carried, send):
    q_rows, g_rows, q_cols, g_cols = staged
    width = key_parts[0].shape[1]
    half, full = jnp.bfloat16, jnp.float32
    wide = ((table.shape[0] * BLOCK, GROUP * width), half)
    count = len(key_parts)
    pool_rows = sum(part.shape[0] for part in key_parts)
    held = ((table.shape[0] * KVH * KEYS, ROWS), half)
    scratch = [pltpu.VMEM((pool_rows, width), full)]
    pool = ((pool_rows, width), half)
    rows = [part.shape[0] for part in key_parts]
    kinds = [full] + [half] * (count - 1)
    probs, k_pool, *dv = run_kernel(
        functools.partial(probs_kernel, count),
        (table, q_cols, g_rows, *key_parts),
        [SMEM], [held, pool, *(((rows[i], width), kinds[i]) for i in range(count))], scratch, 2,
    )
    sums = {i: send(i, dv[i]) for i in range(1, count) if i not in carried}
    dscores, v_pool, *dk = run_kernel(
        functools.partial(dscores_kernel, count, carried),
        (table, q_rows, g_cols, probs, *value_parts, *(dv[i] for i in carried)),
        [SMEM],
        [held, pool, *(((rows[i] * (1 + (i in carried)), width), kinds[i]) for i in range(count))],
        scratch, 2,
    )
    for i in sums:
        sums[i], dk[-1] = lax.optimization_barrier((sums[i], dk[-1]))
    dk = dk[:1] + [send(i, dk[i]) for i in range(1, count)]
    for i in sums:
        sums[i], table = lax.optimization_barrier((sums[i], table))
    out, query_grad = run_kernel(
        rows_kernel, (table, probs, dscores, k_pool, v_pool), [SMEM], [wide, wide], [], 2
    )
    dk[-1], query_grad = lax.optimization_barrier((dk[-1], query_grad))
    return out, query_grad, [(dk[i], sums.get(i)) for i in range(count)]


def dense_local(queries, keys, values, out_grad, rand_blocks, global_blocks):
    cycle_size = lax.axis_size("seq")
    positions = lax.axis_size("dp")

    def swap(array, part):
        pairs = []
        for position in range(positions):
            offset = dense_offsets(cycle_size, position)[part]
            pairs += [(i * positions + position, (i ^ offset) * positions + position) for i in range(cycle_size)]
        return lax.ppermute(array, ("seq", "dp"), pairs)

    def send(part, sums):
        return swap(sums, part)

    parts = range(1, cycle_size)
    key_parts = [swap(keys, part) for part in parts]
    table, *staged, keys, values = stage(
        functools.partial(dense_places, cycle_size), (rand_blocks.T, global_blocks),
        queries, out_grad, keys, values,
    )
    value_parts = [swap(values, part) for part in parts]
    out, query_grad, sums = attend(
        table, staged, [keys, *key_parts], [values, *value_parts], (0, 1, 2), send
    )
    sums[3] = (jnp.concatenate(sums[3], axis=0), None)
    total = sum(part.astype(jnp.float32) for part, _ in sums).astype(jnp.bfloat16)
    return out, query_grad, total[: keys.shape[0]], total[keys.shape[0] :]


def sparse_local(queries, keys, values, out_grad, rand_blocks, global_blocks):
    cycle_size = lax.axis_size("seq")
    myself = lax.axis_index("seq").astype(jnp.int32)
    tok_rows, width = keys.shape
    blocks_here = tok_rows // BLOCK
    rand_total = RAND * blocks_here
    capacity = (rand_total + GLOB + cycle_size - 1) // cycle_size
    slot_total = cycle_size * capacity
    listed = jnp.concatenate(
        [
            rand_blocks.reshape(cycle_size, rand_total),
            jnp.broadcast_to(global_blocks[None, :], (cycle_size, GLOB)),
        ],
        axis=1,
    )
    entries = listed.shape[1]
    owners = listed // blocks_here
    local_slot = listed % blocks_here
    earlier = jnp.arange(entries)[None, :] < jnp.arange(entries)[:, None]
    same_owner = owners[:, :, None] == owners[:, None, :]
    ranking = jnp.sum(same_owner & earlier[None], axis=2)
    owners_mine = lax.dynamic_index_in_dim(owners, myself, 0, keepdims=False)
    ranking_mine = lax.dynamic_index_in_dim(ranking, myself, 0, keepdims=False)
    far_place = (blocks_here + 2 + owners_mine * capacity + ranking_mine).astype(jnp.int32)
    slot_ids = jnp.arange(slot_total)
    requester = slot_ids // capacity
    position = slot_ids % capacity
    matches = (owners[requester] == myself) & (ranking[requester] == position[:, None])
    source = jnp.sum(jnp.where(matches, local_slot[requester], 0), axis=1)

    up = [(i, (i + 1) % cycle_size) for i in range(cycle_size)]
    down = [(j, i) for i, j in up]
    pair = jnp.concatenate([keys, values], axis=1)
    before = lax.ppermute(pair[tok_rows - BLOCK :], "seq", up)
    after = lax.ppermute(pair[:BLOCK], "seq", down)
    outgoing = jnp.take(pair.reshape(blocks_here, BLOCK, 2 * width), source, axis=0)
    far = lax.all_to_all(outgoing, "seq", split_axis=0, concat_axis=0, tiled=True)
    others = [before, after, far.reshape(slot_total * BLOCK, 2 * width)]
    key_parts = [part[:, :width] for part in others]
    value_parts = [part[:, width:] for part in others]

    here = jnp.arange(blocks_here, dtype=jnp.int32)[:, None]
    ahead = jnp.where(here == 0, blocks_here, here - 1)
    behind = jnp.where(here == blocks_here - 1, blocks_here + 1, here + 1)
    table = jnp.concatenate(
        [
            ahead,
            here,
            behind,
            jnp.broadcast_to(far_place[None, rand_total:], (blocks_here, GLOB)),
            far_place[:rand_total].reshape(blocks_here, RAND),
        ],
        axis=1,
    )
    landing = (source[:, None] == jnp.arange(blocks_here)[None, :]).astype(jnp.bfloat16)

    def send(part, sums):
        if part < 3:
            return lax.ppermute(sums, "seq", (down, up)[part - 1])
        return lax.all_to_all(
            sums.reshape(slot_total, BLOCK, width), "seq", split_axis=0, concat_axis=0, tiled=True
        )

    def total(own, last_rim, first_rim, returned):
        landed = jnp.einsum("sq,sbx->qbx", landing, returned, preferred_element_type=jnp.float32)
        sums = own.reshape(blocks_here, BLOCK, width) + landed
        sums = sums.at[blocks_here - 1].add(last_rim.astype(jnp.float32))
        sums = sums.at[0].add(first_rim.astype(jnp.float32))
        return sums.reshape(tok_rows, width).astype(jnp.bfloat16)

    table, *staged, keys, values = stage(
        given_places, (table,), queries, out_grad, keys, values
    )
    out, query_grad, sums = attend(
        table, staged, [keys, *key_parts], [values, *value_parts], (0,), send
    )
    dk, dv = [part for part, _ in sums], [part for _, part in sums]
    dk[0], dv[0] = dk[0][:tok_rows], dk[0][tok_rows:]
    return out, query_grad, total(*dk), total(*dv)


def local(queries, keys, values, out_grad, rand_blocks, global_blocks):
    cycle_size = lax.axis_size("seq")
    blocks_here = queries.shape[0] // BLOCK
    capacity = (RAND * blocks_here + GLOB + cycle_size - 1) // cycle_size
    dense = capacity >= blocks_here and cycle_size == 4
    plan = dense_local if dense else sparse_local
    return plan(queries, keys, values, out_grad, rand_blocks, global_blocks)


def solution(mesh):
    rows = P(("dp", "seq"), None)
    return jax.shard_map(
        local,
        mesh=mesh,
        in_specs=(rows, rows, rows, rows, P("dp", None), P("dp")),
        out_specs=(rows, rows, rows, rows),
        check_vma=False,
    )
```

```python
import functools

import jax
import jax.numpy as jnp
from jax import lax
from jax.experimental import pallas as pl
from jax.experimental.pallas import tpu as pltpu
from jax.sharding import PartitionSpec as P

KVH = 2
HD = 128
BLOCK = 64
GLOB = 2
RAND = 3
GROUP = 4
ENTRIES = 3 + GLOB + RAND
LOG2E = 1.4426950408889634
SCALE = HD ** (-0.5)


NN = (((1,), (0,)), ((), ()))
TN = (((0,), (0,)), ((), ()))
dot = functools.partial(lax.dot_general, preferred_element_type=jnp.float32)

KEYS = ENTRIES * BLOCK
ROWS = GROUP * BLOCK


def units(blocks_here):
    return [(b, h, b * KVH + h) for b in range(blocks_here) for h in range(KVH)]


def given_places(lists, blocks_here, b):
    return [lists[0][b, e] for e in range(ENTRIES)]


def dense_offsets(cycle_size, position):
    odd = position & 1
    offsets = list(range(cycle_size))
    offsets[1], offsets[2] = 1 + odd, 2 - odd
    return offsets


def dense_places(cycle_size, lists, blocks_here, b):
    rand_ref, glob_ref = lists
    me = lax.axis_index("seq").astype(jnp.int32)
    odd = lax.axis_index("dp").astype(jnp.int32) & 1

    def place(owner, local):
        offset = owner ^ me
        swapped = (odd == 1) & ((offset == 1) | (offset == 2))
        return jnp.where(swapped, 3 - offset, offset) * blocks_here + local

    def far_place(block):
        return place(lax.div(block, blocks_here), lax.rem(block, blocks_here))

    window = [b - 1, b, b + 1]
    if b == 0:
        window[0] = place(lax.rem(me + cycle_size - 1, cycle_size), blocks_here - 1)
    if b == blocks_here - 1:
        window[2] = place(lax.rem(me + 1, cycle_size), 0)
    far = [glob_ref[i] for i in range(GLOB)] + [rand_ref[i, me * blocks_here + b] for i in range(RAND)]
    return window + [far_place(block) for block in far]


def dense_owners(cycle_size):
    me = lax.axis_index("seq").astype(jnp.int32)
    odd = lax.axis_index("dp").astype(jnp.int32) & 1
    return [me ^ (i if i in (0, 3) else jnp.where(odd == 1, 3 - i, i)) for i in range(cycle_size)]


def exchanged(array, owners, i):
    rows = array.shape[0] // len(owners)
    return array.at[pl.ds(pl.multiple_of(owners[i] * rows, BLOCK), rows)]


def spans(table, b):
    result = []
    for e in range(ENTRIES):
        near = b + e - 1
        if e < 3 and 0 <= near < table.shape[0]:
            result.append(pl.ds(near * BLOCK, BLOCK))
        else:
            result.append(pl.ds(pl.multiple_of(table[b, e] * BLOCK, BLOCK), BLOCK))
    return result


def picked(pool, places, h):
    return jnp.concatenate([pool[place, h * HD : (h + 1) * HD] for place in places], axis=0)


def unstack(ref, b, h, value):
    for j in range(GROUP):
        c = (h * GROUP + j) * HD
        ref[b * BLOCK : (b + 1) * BLOCK, c : c + HD] = value[j * BLOCK : (j + 1) * BLOCK]


def add_terms(pool, places, h, terms):
    for e, place in enumerate(places):
        pool[place, h * HD : (h + 1) * HD] += terms[e * BLOCK : (e + 1) * BLOCK]


def gather_pool(pool, parts):
    start = 0
    for part in parts:
        pool[start : start + part.shape[0]] = part[...]
        start += part.shape[0]


def split_pool(outs, pool, factor):
    start = 0
    for out in outs:
        total = pool[start : start + out.shape[0]]
        out[...] = (total if factor is None else total * factor).astype(out.dtype)
        start += out.shape[0]


def stage_kernel(locate, count, copies_of_v, *refs):
    sources, refs = refs[: count + 4], refs[count + 4 :]
    table, q_rows, g_rows, q_cols, g_cols, k_ref, v_ref, *refs = refs
    v_all, refs = (refs[:1], refs[1:]) if copies_of_v else ([], refs)
    lists = refs[:count]
    q_ref, g_ref, sem = refs[count:]
    targets = [*lists, q_ref, g_ref, k_ref, v_ref]
    copies = [
        pltpu.make_async_copy(source, target, sem.at[i])
        for i, (source, target) in enumerate(zip(sources, targets))
    ]
    for copy in copies:
        copy.start()
    for copy in copies[:count]:
        copy.wait()
    copies = copies[count:]
    row = lax.broadcasted_iota(jnp.int32, table.shape, 0)
    column = lax.broadcasted_iota(jnp.int32, table.shape, 1)
    places = jnp.zeros(table.shape, jnp.int32)
    for b in range(table.shape[0]):
        for e, place in enumerate(locate(lists, table.shape[0], b)):
            places = jnp.where((row == b) & (column == e), place, places)
    table[...] = places
    for copy, ref, rows, cols in ((copies[0], q_ref, q_rows, q_cols), (copies[1], g_ref, g_rows, g_cols)):
        copy.wait()
        for b, h, u in units(table.shape[0]):
            heads = [(h * GROUP + j) * HD for j in range(GROUP)]
            unit = jnp.concatenate(
                [ref[b * BLOCK : (b + 1) * BLOCK, c : c + HD] for c in heads], axis=0
            )
            rows[u * ROWS : (u + 1) * ROWS] = unit
            cols[u * HD : (u + 1) * HD] = unit.T
    copies[2].wait()
    copies[3].wait()
    if v_all:
        for i in range(copies_of_v):
            v_all[0][i * v_ref.shape[0] : (i + 1) * v_ref.shape[0]] = v_ref[...]


def probs_kernel(count, find_owners, table, q_cols, g_rows, *refs):
    parts = refs[:count]
    probs_ref, k_pool, *dv_refs, dv_pool = refs[count:]
    gather_pool(k_pool, parts)
    if find_owners:
        owners = find_owners()
        dv_refs = [exchanged(dv_refs[0], owners, i) for i in range(len(owners))]
    dv_pool[...] = jnp.zeros_like(dv_pool)
    for b, h, u in units(table.shape[0]):
        places = spans(table, b)
        scores = dot(picked(k_pool, places, h), q_cols[u * HD : (u + 1) * HD], NN)
        peak = jnp.max(scores, axis=0, keepdims=True)
        expos = jnp.exp2((scores - peak) * (SCALE * LOG2E))
        probs = expos * (1.0 / jnp.sum(expos, axis=0, keepdims=True))
        probs_b = probs.astype(jnp.bfloat16)
        probs_ref[u * KEYS : (u + 1) * KEYS] = probs_b
        add_terms(dv_pool, places, h, dot(probs_b, g_rows[u * ROWS : (u + 1) * ROWS], NN))
    split_pool(dv_refs, dv_pool, None)


def dscores_kernel(count, find_owners, table, q_rows, g_cols, probs_ref, *refs):
    parts = refs[:count]
    ds_ref, v_pool, *dk_refs, dk_pool = refs[count:]
    if find_owners:
        owners = find_owners()
        dk_refs = [exchanged(dk_refs[0], owners, i) for i in range(len(owners))]
        parts = [exchanged(parts[0], owners, i) for i in range(len(owners))]
    gather_pool(v_pool, parts)
    dk_pool[...] = jnp.zeros_like(dk_pool)
    for b, h, u in units(table.shape[0]):
        places = spans(table, b)
        probs = probs_ref[u * KEYS : (u + 1) * KEYS].astype(jnp.float32)
        dprobs = dot(picked(v_pool, places, h), g_cols[u * HD : (u + 1) * HD], NN)
        delta = jnp.sum(probs * dprobs, axis=0, keepdims=True)
        dscores = (probs * (dprobs - delta)).astype(jnp.bfloat16)
        ds_ref[u * KEYS : (u + 1) * KEYS] = dscores
        add_terms(dk_pool, places, h, dot(dscores, q_rows[u * ROWS : (u + 1) * ROWS], NN))
    split_pool(dk_refs, dk_pool, SCALE)


def rows_kernel(table, probs_ref, ds_ref, k_pool, v_pool, out_ref, qgrad_ref):
    for b, h, u in units(table.shape[0]):
        places = spans(table, b)
        span = slice(u * KEYS, (u + 1) * KEYS)
        attended = dot(probs_ref[span], picked(v_pool, places, h), TN)
        unstack(out_ref, b, h, attended.astype(jnp.bfloat16))
        qgrad = dot(ds_ref[span], picked(k_pool, places, h), TN) * SCALE
        unstack(qgrad_ref, b, h, qgrad.astype(jnp.bfloat16))


SMEM = pl.BlockSpec(memory_space=pltpu.SMEM)
HBM = pl.BlockSpec(memory_space=pltpu.HBM)
VMEM = pl.BlockSpec(memory_space=pltpu.VMEM)


def run_kernel(kernel, operands, in_specs, results, scratch, products):
    flops = products * 2 * 4 * KVH * ROWS * KEYS * HD
    return pl.pallas_call(
        kernel,
        out_shape=[jax.ShapeDtypeStruct(shape, kind) for shape, kind in results],
        in_specs=in_specs + [VMEM] * (len(operands) - len(in_specs)),
        out_specs=[VMEM] * len(results),
        scratch_shapes=scratch,
        compiler_params=pltpu.CompilerParams(vmem_limit_bytes=32 * 2**20),
        cost_estimate=pl.CostEstimate(
            flops=flops, bytes_accessed=products * 2**20, transcendentals=0
        ),
    )(*operands)


def stage(locate, lists, queries, out_grad, keys, values, copies_of_v=0):
    blocks_here = queries.shape[0] // BLOCK
    half = jnp.bfloat16
    rows = ((blocks_here * KVH * ROWS, HD), half)
    cols = ((blocks_here * KVH * HD, ROWS), half)
    narrow, wide = (keys.shape, half), (queries.shape, half)
    mine = (*lists, queries, out_grad, keys, values)
    return run_kernel(
        functools.partial(stage_kernel, locate, len(lists), copies_of_v),
        [pltpu.with_memory_space_constraint(array, pltpu.HBM) for array in mine],
        [HBM] * len(mine),
        [((blocks_here, ENTRIES), jnp.int32), rows, rows, cols, cols, narrow, narrow]
        + [((copies_of_v * keys.shape[0], keys.shape[1]), half)] * (copies_of_v > 0),
        [
            *[pltpu.SMEM(array.shape, array.dtype) for array in lists],
            pltpu.VMEM(*wide), pltpu.VMEM(*wide),
            pltpu.SemaphoreType.DMA((len(mine),)),
        ],
        1,
    )


def attend(table, staged, key_parts, value_parts, sums, find_owners, send):
    q_rows, g_rows, q_cols, g_cols = staged
    width = key_parts[0].shape[1]
    half, full = jnp.bfloat16, jnp.float32
    wide = ((table.shape[0] * BLOCK, GROUP * width), half)
    pool_rows = sum(part.shape[0] for part in key_parts)
    held = ((table.shape[0] * KVH * KEYS, ROWS), half)
    sums = [((rows, width), kind) for rows, kind in sums]
    scratch = [pltpu.VMEM((pool_rows, width), full)]
    pool = ((pool_rows, width), half)
    probs, k_pool, *dv = run_kernel(
        functools.partial(probs_kernel, len(key_parts), find_owners),
        (table, q_cols, g_rows, *key_parts),
        [SMEM], [held, pool, *sums], scratch, 2,
    )
    dv = send(dv)
    dscores, v_pool, *dk = run_kernel(
        functools.partial(dscores_kernel, len(value_parts), find_owners),
        (table, q_rows, g_cols, probs, *value_parts),
        [SMEM], [held, pool, *sums], scratch, 2,
    )
    dk = send(dk)
    out, query_grad = run_kernel(
        rows_kernel, (table, probs, dscores, k_pool, v_pool), [SMEM], [wide, wide], [], 2
    )
    dk[-1], query_grad = lax.optimization_barrier((dk[-1], query_grad))
    return out, query_grad, dk, dv


def dense_local(queries, keys, values, out_grad, rand_blocks, global_blocks):
    cycle_size = lax.axis_size("seq")
    positions = lax.axis_size("dp")

    def swap(array, part):
        pairs = []
        for position in range(positions):
            offset = dense_offsets(cycle_size, position)[part]
            pairs += [(i * positions + position, (i ^ offset) * positions + position) for i in range(cycle_size)]
        return lax.ppermute(array, ("seq", "dp"), pairs)

    def exchange(array):
        array = array.reshape(cycle_size, keys.shape[0], keys.shape[1])
        return lax.all_to_all(array, "seq", split_axis=0, concat_axis=0, tiled=True)

    def send(grads):
        return [exchange(grads[0])]

    def total(grads):
        return jnp.sum(grads[0].astype(jnp.float32), axis=0).astype(jnp.bfloat16)

    parts = range(1, cycle_size)
    key_parts = [swap(keys, part) for part in parts]
    table, *staged, own_keys, _, all_values = stage(
        functools.partial(dense_places, cycle_size), (rand_blocks.T, global_blocks),
        queries, out_grad, keys, values, cycle_size,
    )
    value_pool = exchange(all_values).reshape(all_values.shape)
    out, query_grad, dk, dv = attend(
        table, staged, [own_keys, *key_parts], [value_pool],
        [(cycle_size * keys.shape[0], jnp.bfloat16)],
        functools.partial(dense_owners, cycle_size), send,
    )
    return out, query_grad, total(dk), total(dv)


def sparse_local(queries, keys, values, out_grad, rand_blocks, global_blocks):
    cycle_size = lax.axis_size("seq")
    myself = lax.axis_index("seq").astype(jnp.int32)
    tok_rows, width = keys.shape
    blocks_here = tok_rows // BLOCK
    rand_total = RAND * blocks_here
    capacity = (rand_total + GLOB + cycle_size - 1) // cycle_size
    slot_total = cycle_size * capacity
    listed = jnp.concatenate(
        [
            rand_blocks.reshape(cycle_size, rand_total),
            jnp.broadcast_to(global_blocks[None, :], (cycle_size, GLOB)),
        ],
        axis=1,
    )
    entries = listed.shape[1]
    owners = listed // blocks_here
    local_slot = listed % blocks_here
    earlier = jnp.arange(entries)[None, :] < jnp.arange(entries)[:, None]
    same_owner = owners[:, :, None] == owners[:, None, :]
    ranking = jnp.sum(same_owner & earlier[None], axis=2)
    owners_mine = lax.dynamic_index_in_dim(owners, myself, 0, keepdims=False)
    ranking_mine = lax.dynamic_index_in_dim(ranking, myself, 0, keepdims=False)
    far_place = (blocks_here + 2 + owners_mine * capacity + ranking_mine).astype(jnp.int32)
    slot_ids = jnp.arange(slot_total)
    requester = slot_ids // capacity
    position = slot_ids % capacity
    matches = (owners[requester] == myself) & (ranking[requester] == position[:, None])
    source = jnp.sum(jnp.where(matches, local_slot[requester], 0), axis=1)

    up = [(i, (i + 1) % cycle_size) for i in range(cycle_size)]
    down = [(j, i) for i, j in up]
    pair = jnp.concatenate([keys, values], axis=1)
    before = lax.ppermute(pair[tok_rows - BLOCK :], "seq", up)
    after = lax.ppermute(pair[:BLOCK], "seq", down)
    outgoing = jnp.take(pair.reshape(blocks_here, BLOCK, 2 * width), source, axis=0)
    far = lax.all_to_all(outgoing, "seq", split_axis=0, concat_axis=0, tiled=True)
    others = [before, after, far.reshape(slot_total * BLOCK, 2 * width)]
    key_parts = [part[:, :width] for part in others]
    value_parts = [part[:, width:] for part in others]

    here = jnp.arange(blocks_here, dtype=jnp.int32)[:, None]
    ahead = jnp.where(here == 0, blocks_here, here - 1)
    behind = jnp.where(here == blocks_here - 1, blocks_here + 1, here + 1)
    table = jnp.concatenate(
        [
            ahead,
            here,
            behind,
            jnp.broadcast_to(far_place[None, rand_total:], (blocks_here, GLOB)),
            far_place[:rand_total].reshape(blocks_here, RAND),
        ],
        axis=1,
    )
    landing = (source[:, None] == jnp.arange(blocks_here)[None, :]).astype(jnp.bfloat16)

    def send(grads):
        own, grad_before, grad_after, grad_far = grads
        last_rim = lax.ppermute(grad_before, "seq", down)
        first_rim = lax.ppermute(grad_after, "seq", up)
        returned = lax.all_to_all(
            grad_far.reshape(slot_total, BLOCK, width),
            "seq", split_axis=0, concat_axis=0, tiled=True,
        )
        return [own, last_rim, first_rim, returned]

    def total(grads):
        own, last_rim, first_rim, returned = grads
        landed = jnp.einsum("sq,sbx->qbx", landing, returned, preferred_element_type=jnp.float32)
        sums = own.reshape(blocks_here, BLOCK, width) + landed
        sums = sums.at[blocks_here - 1].add(last_rim.astype(jnp.float32))
        sums = sums.at[0].add(first_rim.astype(jnp.float32))
        return sums.reshape(tok_rows, width).astype(jnp.bfloat16)

    table, *staged, keys, values = stage(
        given_places, (table,), queries, out_grad, keys, values
    )
    sums = [(tok_rows, jnp.float32)] + [(part.shape[0], jnp.bfloat16) for part in key_parts]
    out, query_grad, dk, dv = attend(
        table, staged, [keys, *key_parts], [values, *value_parts], sums, None, send
    )
    return out, query_grad, total(dk), total(dv)


def local(queries, keys, values, out_grad, rand_blocks, global_blocks):
    cycle_size = lax.axis_size("seq")
    blocks_here = queries.shape[0] // BLOCK
    capacity = (RAND * blocks_here + GLOB + cycle_size - 1) // cycle_size
    dense = capacity >= blocks_here and cycle_size == 4
    plan = dense_local if dense else sparse_local
    return plan(queries, keys, values, out_grad, rand_blocks, global_blocks)


def solution(mesh):
    rows = P(("dp", "seq"), None)
    return jax.shard_map(
        local,
        mesh=mesh,
        in_specs=(rows, rows, rows, rows, P("dp", None), P("dp")),
        out_specs=(rows, rows, rows, rows),
        check_vma=False,
    )
```

```python
import functools

import jax
import jax.numpy as jnp
from jax import lax
from jax.experimental import pallas as pl
from jax.experimental.pallas import tpu as pltpu
from jax.sharding import PartitionSpec as P

KVH = 2
HD = 128
BLOCK = 64
GLOB = 2
RAND = 3
GROUP = 4
ENTRIES = 3 + GLOB + RAND
LOG2E = 1.4426950408889634
SCALE = HD ** (-0.5)


NN = (((1,), (0,)), ((), ()))
TN = (((0,), (0,)), ((), ()))
dot = functools.partial(lax.dot_general, preferred_element_type=jnp.float32)

KEYS = ENTRIES * BLOCK
ROWS = GROUP * BLOCK


def units(blocks_here):
    return [(b, h, b * KVH + h) for b in range(blocks_here) for h in range(KVH)]


def given_places(lists, blocks_here, b):
    return [lists[0][b, e] for e in range(ENTRIES)]


def dense_offsets(cycle_size, position):
    odd = position & 1
    offsets = list(range(cycle_size))
    offsets[1], offsets[2] = 1 + odd, 2 - odd
    return offsets


def dense_places(cycle_size, lists, blocks_here, b):
    rand_ref, glob_ref = lists
    me = lax.axis_index("seq").astype(jnp.int32)
    odd = lax.axis_index("dp").astype(jnp.int32) & 1

    def place(owner, local):
        offset = owner ^ me
        swapped = (odd == 1) & ((offset == 1) | (offset == 2))
        return jnp.where(swapped, 3 - offset, offset) * blocks_here + local

    def far_place(block):
        return place(lax.div(block, blocks_here), lax.rem(block, blocks_here))

    window = [b - 1, b, b + 1]
    if b == 0:
        window[0] = place(lax.rem(me + cycle_size - 1, cycle_size), blocks_here - 1)
    if b == blocks_here - 1:
        window[2] = place(lax.rem(me + 1, cycle_size), 0)
    far = [glob_ref[i] for i in range(GLOB)] + [rand_ref[i, me * blocks_here + b] for i in range(RAND)]
    return window + [far_place(block) for block in far]


def spans(table, b):
    result = []
    for e in range(ENTRIES):
        near = b + e - 1
        if e < 3 and 0 <= near < table.shape[0]:
            result.append(pl.ds(near * BLOCK, BLOCK))
        else:
            result.append(pl.ds(pl.multiple_of(table[b, e] * BLOCK, BLOCK), BLOCK))
    return result


def picked(pool, places, h):
    return jnp.concatenate([pool[place, h * HD : (h + 1) * HD] for place in places], axis=0)


def unstack(ref, b, h, value):
    for j in range(GROUP):
        c = (h * GROUP + j) * HD
        ref[b * BLOCK : (b + 1) * BLOCK, c : c + HD] = value[j * BLOCK : (j + 1) * BLOCK]


def add_terms(pool, places, h, terms):
    for e, place in enumerate(places):
        pool[place, h * HD : (h + 1) * HD] += terms[e * BLOCK : (e + 1) * BLOCK]


def gather_pool(pool, parts):
    start = 0
    for part in parts:
        pool[start : start + part.shape[0]] = part[...]
        start += part.shape[0]


def split_pool(outs, pool, factor):
    start = 0
    for out in outs:
        total = pool[start : start + out.shape[0]]
        out[...] = (total if factor is None else total * factor).astype(out.dtype)
        start += out.shape[0]


def stage_kernel(locate, count, *refs):
    sources, refs = refs[: count + 4], refs[count + 4 :]
    table, q_rows, g_rows, q_cols, g_cols, k_ref, v_ref, *refs = refs
    lists = refs[:count]
    q_ref, g_ref, sem = refs[count:]
    targets = [*lists, q_ref, g_ref, k_ref, v_ref]
    copies = [
        pltpu.make_async_copy(source, target, sem.at[i])
        for i, (source, target) in enumerate(zip(sources, targets))
    ]
    for copy in copies:
        copy.start()
    for copy in copies[:count]:
        copy.wait()
    copies = copies[count:]
    row = lax.broadcasted_iota(jnp.int32, table.shape, 0)
    column = lax.broadcasted_iota(jnp.int32, table.shape, 1)
    places = jnp.zeros(table.shape, jnp.int32)
    for b in range(table.shape[0]):
        for e, place in enumerate(locate(lists, table.shape[0], b)):
            places = jnp.where((row == b) & (column == e), place, places)
    table[...] = places
    for copy, ref, rows, cols in ((copies[0], q_ref, q_rows, q_cols), (copies[1], g_ref, g_rows, g_cols)):
        copy.wait()
        for b, h, u in units(table.shape[0]):
            heads = [(h * GROUP + j) * HD for j in range(GROUP)]
            unit = jnp.concatenate(
                [ref[b * BLOCK : (b + 1) * BLOCK, c : c + HD] for c in heads], axis=0
            )
            rows[u * ROWS : (u + 1) * ROWS] = unit
            cols[u * HD : (u + 1) * HD] = unit.T
    copies[2].wait()
    copies[3].wait()


def probs_kernel(count, table, q_cols, g_rows, *refs):
    parts = refs[:count]
    probs_ref, k_pool, *dv_refs, dv_pool = refs[count:]
    gather_pool(k_pool, parts)
    dv_pool[...] = jnp.zeros_like(dv_pool)
    for b, h, u in units(table.shape[0]):
        places = spans(table, b)
        scores = dot(picked(k_pool, places, h), q_cols[u * HD : (u + 1) * HD], NN)
        peak = jnp.max(scores, axis=0, keepdims=True)
        expos = jnp.exp2((scores - peak) * (SCALE * LOG2E))
        probs = expos * (1.0 / jnp.sum(expos, axis=0, keepdims=True))
        probs_b = probs.astype(jnp.bfloat16)
        probs_ref[u * KEYS : (u + 1) * KEYS] = probs_b
        add_terms(dv_pool, places, h, dot(probs_b, g_rows[u * ROWS : (u + 1) * ROWS], NN))
    split_pool(dv_refs, dv_pool, None)


def dscores_kernel(count, table, q_rows, g_cols, probs_ref, *refs):
    parts = refs[:count]
    ds_ref, v_pool, *dk_refs, dk_pool = refs[count:]
    gather_pool(v_pool, parts)
    dk_pool[...] = jnp.zeros_like(dk_pool)
    for b, h, u in units(table.shape[0]):
        places = spans(table, b)
        probs = probs_ref[u * KEYS : (u + 1) * KEYS].astype(jnp.float32)
        dprobs = dot(picked(v_pool, places, h), g_cols[u * HD : (u + 1) * HD], NN)
        delta = jnp.sum(probs * dprobs, axis=0, keepdims=True)
        dscores = (probs * (dprobs - delta)).astype(jnp.bfloat16)
        ds_ref[u * KEYS : (u + 1) * KEYS] = dscores
        add_terms(dk_pool, places, h, dot(dscores, q_rows[u * ROWS : (u + 1) * ROWS], NN))
    split_pool(dk_refs, dk_pool, SCALE)


def rows_kernel(table, probs_ref, ds_ref, k_pool, v_pool, out_ref, qgrad_ref):
    for b, h, u in units(table.shape[0]):
        places = spans(table, b)
        span = slice(u * KEYS, (u + 1) * KEYS)
        attended = dot(probs_ref[span], picked(v_pool, places, h), TN)
        unstack(out_ref, b, h, attended.astype(jnp.bfloat16))
        qgrad = dot(ds_ref[span], picked(k_pool, places, h), TN) * SCALE
        unstack(qgrad_ref, b, h, qgrad.astype(jnp.bfloat16))


SMEM = pl.BlockSpec(memory_space=pltpu.SMEM)
HBM = pl.BlockSpec(memory_space=pltpu.HBM)
VMEM = pl.BlockSpec(memory_space=pltpu.VMEM)


def run_kernel(kernel, operands, in_specs, results, scratch, products):
    flops = products * 2 * 4 * KVH * ROWS * KEYS * HD
    return pl.pallas_call(
        kernel,
        out_shape=[jax.ShapeDtypeStruct(shape, kind) for shape, kind in results],
        in_specs=in_specs + [VMEM] * (len(operands) - len(in_specs)),
        out_specs=[VMEM] * len(results),
        scratch_shapes=scratch,
        compiler_params=pltpu.CompilerParams(vmem_limit_bytes=32 * 2**20),
        cost_estimate=pl.CostEstimate(
            flops=flops, bytes_accessed=products * 2**20, transcendentals=0
        ),
    )(*operands)


def stage(locate, lists, queries, out_grad, keys, values):
    blocks_here = queries.shape[0] // BLOCK
    half = jnp.bfloat16
    rows = ((blocks_here * KVH * ROWS, HD), half)
    cols = ((blocks_here * KVH * HD, ROWS), half)
    narrow, wide = (keys.shape, half), (queries.shape, half)
    mine = (*lists, queries, out_grad, keys, values)
    return run_kernel(
        functools.partial(stage_kernel, locate, len(lists)),
        [pltpu.with_memory_space_constraint(array, pltpu.HBM) for array in mine],
        [HBM] * len(mine),
        [((blocks_here, ENTRIES), jnp.int32), rows, rows, cols, cols, narrow, narrow],
        [
            *[pltpu.SMEM(array.shape, array.dtype) for array in lists],
            pltpu.VMEM(*wide), pltpu.VMEM(*wide),
            pltpu.SemaphoreType.DMA((len(mine),)),
        ],
        1,
    )


def attend(table, staged, key_parts, value_parts, send):
    q_rows, g_rows, q_cols, g_cols = staged
    tok_rows, width = key_parts[0].shape
    half, full = jnp.bfloat16, jnp.float32
    wide = ((tok_rows, GROUP * width), half)
    count = len(key_parts)
    pool_rows = sum(part.shape[0] for part in key_parts)
    held = ((table.shape[0] * KVH * KEYS, ROWS), half)
    sums = [(part.shape, half if i else full) for i, part in enumerate(key_parts)]
    scratch = [pltpu.VMEM((pool_rows, width), full)]
    pool = ((pool_rows, width), half)
    probs, k_pool, *dv = run_kernel(
        functools.partial(probs_kernel, count),
        (table, q_cols, g_rows, *key_parts),
        [SMEM], [held, pool, *sums], scratch, 2,
    )
    dv, value_parts = lax.optimization_barrier((dv, value_parts))
    dv = send(dv, None)
    dscores, v_pool, *dk = run_kernel(
        functools.partial(dscores_kernel, count),
        (table, q_rows, g_cols, probs, *value_parts),
        [SMEM], [held, pool, *sums], scratch, 2,
    )
    dk = send(dk, dv)
    dv[1], table = lax.optimization_barrier((dv[1], table))
    out, query_grad = run_kernel(
        rows_kernel, (table, probs, dscores, k_pool, v_pool), [SMEM], [wide, wide], [], 2
    )
    return out, query_grad, dk, dv


def dense_local(queries, keys, values, out_grad, rand_blocks, global_blocks):
    cycle_size = lax.axis_size("seq")
    positions = lax.axis_size("dp")

    def swap(array, part):
        pairs = []
        for position in range(positions):
            offset = dense_offsets(cycle_size, position)[part]
            pairs += [(i * positions + position, (i ^ offset) * positions + position) for i in range(cycle_size)]
        return lax.ppermute(array, ("seq", "dp"), pairs)

    def send(grads, earlier):
        sent = [grads[0]] + [None] * (cycle_size - 1)
        sent[-1] = swap(grads[-1], cycle_size - 1)
        near = grads[1:-1]
        if earlier is not None:
            near, earlier[1] = lax.optimization_barrier((near, earlier[1]))
        for part in range(1, cycle_size - 1):
            sent[part] = swap(near[part - 1], part)
        return sent

    def total(grads):
        return sum(grad.astype(jnp.float32) for grad in grads).astype(jnp.bfloat16)

    def fetch(array):
        second, first = swap(array, 2), swap(array, 1)
        return [first, second, swap(second, 1)]

    key_parts = fetch(keys)
    table, *staged, keys, values = stage(
        functools.partial(dense_places, cycle_size), (rand_blocks.T, global_blocks),
        queries, out_grad, keys, values,
    )
    late_values, key_parts[0] = lax.optimization_barrier((values, key_parts[0]))
    value_parts = fetch(late_values)
    out, query_grad, dk, dv = attend(
        table, staged, [keys, *key_parts], [values, *value_parts], send
    )
    return out, query_grad, total(dk), total(dv)


def sparse_local(queries, keys, values, out_grad, rand_blocks, global_blocks):
    cycle_size = lax.axis_size("seq")
    myself = lax.axis_index("seq").astype(jnp.int32)
    tok_rows, width = keys.shape
    blocks_here = tok_rows // BLOCK
    rand_total = RAND * blocks_here
    capacity = (rand_total + GLOB + cycle_size - 1) // cycle_size
    slot_total = cycle_size * capacity
    listed = jnp.concatenate(
        [
            rand_blocks.reshape(cycle_size, rand_total),
            jnp.broadcast_to(global_blocks[None, :], (cycle_size, GLOB)),
        ],
        axis=1,
    )
    entries = listed.shape[1]
    owners = listed // blocks_here
    local_slot = listed % blocks_here
    earlier = jnp.arange(entries)[None, :] < jnp.arange(entries)[:, None]
    same_owner = owners[:, :, None] == owners[:, None, :]
    ranking = jnp.sum(same_owner & earlier[None], axis=2)
    owners_mine = lax.dynamic_index_in_dim(owners, myself, 0, keepdims=False)
    ranking_mine = lax.dynamic_index_in_dim(ranking, myself, 0, keepdims=False)
    far_place = (blocks_here + 2 + owners_mine * capacity + ranking_mine).astype(jnp.int32)
    slot_ids = jnp.arange(slot_total)
    requester = slot_ids // capacity
    position = slot_ids % capacity
    matches = (owners[requester] == myself) & (ranking[requester] == position[:, None])
    source = jnp.sum(jnp.where(matches, local_slot[requester], 0), axis=1)

    up = [(i, (i + 1) % cycle_size) for i in range(cycle_size)]
    down = [(j, i) for i, j in up]
    pair = jnp.concatenate([keys, values], axis=1)
    before = lax.ppermute(pair[tok_rows - BLOCK :], "seq", up)
    after = lax.ppermute(pair[:BLOCK], "seq", down)
    outgoing = jnp.take(pair.reshape(blocks_here, BLOCK, 2 * width), source, axis=0)
    far = lax.all_to_all(outgoing, "seq", split_axis=0, concat_axis=0, tiled=True)
    others = [before, after, far.reshape(slot_total * BLOCK, 2 * width)]
    key_parts = [part[:, :width] for part in others]
    value_parts = [part[:, width:] for part in others]

    here = jnp.arange(blocks_here, dtype=jnp.int32)[:, None]
    ahead = jnp.where(here == 0, blocks_here, here - 1)
    behind = jnp.where(here == blocks_here - 1, blocks_here + 1, here + 1)
    table = jnp.concatenate(
        [
            ahead,
            here,
            behind,
            jnp.broadcast_to(far_place[None, rand_total:], (blocks_here, GLOB)),
            far_place[:rand_total].reshape(blocks_here, RAND),
        ],
        axis=1,
    )
    landing = (source[:, None] == jnp.arange(blocks_here)[None, :]).astype(jnp.bfloat16)

    def send(grads, earlier):
        own, grad_before, grad_after, grad_far = grads
        last_rim = lax.ppermute(grad_before, "seq", down)
        first_rim = lax.ppermute(grad_after, "seq", up)
        returned = lax.all_to_all(
            grad_far.reshape(slot_total, BLOCK, width),
            "seq", split_axis=0, concat_axis=0, tiled=True,
        )
        return [own, last_rim, first_rim, returned]

    def total(grads):
        own, last_rim, first_rim, returned = grads
        landed = jnp.einsum("sq,sbx->qbx", landing, returned, preferred_element_type=jnp.float32)
        sums = own.reshape(blocks_here, BLOCK, width) + landed
        sums = sums.at[blocks_here - 1].add(last_rim.astype(jnp.float32))
        sums = sums.at[0].add(first_rim.astype(jnp.float32))
        return sums.reshape(tok_rows, width).astype(jnp.bfloat16)

    table, *staged, keys, values = stage(
        given_places, (table,), queries, out_grad, keys, values
    )
    out, query_grad, dk, dv = attend(
        table, staged, [keys, *key_parts], [values, *value_parts], send
    )
    return out, query_grad, total(dk), total(dv)


def local(queries, keys, values, out_grad, rand_blocks, global_blocks):
    cycle_size = lax.axis_size("seq")
    blocks_here = queries.shape[0] // BLOCK
    capacity = (RAND * blocks_here + GLOB + cycle_size - 1) // cycle_size
    dense = capacity >= blocks_here and cycle_size == 4
    plan = dense_local if dense else sparse_local
    return plan(queries, keys, values, out_grad, rand_blocks, global_blocks)


def solution(mesh):
    rows = P(("dp", "seq"), None)
    return jax.shard_map(
        local,
        mesh=mesh,
        in_specs=(rows, rows, rows, rows, P("dp", None), P("dp")),
        out_specs=(rows, rows, rows, rows),
        check_vma=False,
    )
```

```python
import functools

import jax
import jax.numpy as jnp
from jax import lax
from jax.experimental import pallas as pl
from jax.experimental.pallas import tpu as pltpu
from jax.sharding import PartitionSpec as P

KVH = 2
HD = 128
BLOCK = 64
GLOB = 2
RAND = 3
GROUP = 4
ENTRIES = 3 + GLOB + RAND
LOG2E = 1.4426950408889634
SCALE = HD ** (-0.5)


NN = (((1,), (0,)), ((), ()))
TN = (((0,), (0,)), ((), ()))
dot = functools.partial(lax.dot_general, preferred_element_type=jnp.float32)

KEYS = ENTRIES * BLOCK
CHUNK = 128
FACTOR = SCALE * LOG2E
ROWS = GROUP * BLOCK


def units(blocks_here):
    return [(b, h, b * KVH + h) for b in range(blocks_here) for h in range(KVH)]


def given_places(lists, blocks_here, b):
    return [lists[0][b, e] for e in range(ENTRIES)]


def dense_offsets(cycle_size, position):
    odd = position & 1
    offsets = list(range(cycle_size))
    offsets[1], offsets[2] = 1 + odd, 2 - odd
    return offsets


def dense_places(cycle_size, lists, blocks_here, b):
    rand_ref, glob_ref = lists
    me = lax.axis_index("seq").astype(jnp.int32)
    odd = lax.axis_index("dp").astype(jnp.int32) & 1

    def place(owner, local):
        offset = owner ^ me
        swapped = (odd == 1) & ((offset == 1) | (offset == 2))
        return jnp.where(swapped, 3 - offset, offset) * blocks_here + local

    def far_place(block):
        return place(lax.div(block, blocks_here), lax.rem(block, blocks_here))

    window = [b - 1, b, b + 1]
    if b == 0:
        window[0] = place(lax.rem(me + cycle_size - 1, cycle_size), blocks_here - 1)
    if b == blocks_here - 1:
        window[2] = place(lax.rem(me + 1, cycle_size), 0)
    far = [glob_ref[i] for i in range(GLOB)] + [rand_ref[i, me * blocks_here + b] for i in range(RAND)]
    return window + [far_place(block) for block in far]


def spans(table, b):
    result = []
    for e in range(ENTRIES):
        near = b + e - 1
        if e < 3 and 0 <= near < table.shape[0]:
            result.append(pl.ds(near * BLOCK, BLOCK))
        else:
            result.append(pl.ds(pl.multiple_of(table[b, e] * BLOCK, BLOCK), BLOCK))
    return result


def picked(pool, places, h):
    return jnp.concatenate([pool[place, h * HD : (h + 1) * HD] for place in places], axis=0)


def unstack(ref, b, h, value):
    for j in range(GROUP):
        c = (h * GROUP + j) * HD
        ref[b * BLOCK : (b + 1) * BLOCK, c : c + HD] = value[j * BLOCK : (j + 1) * BLOCK]


def add_terms(pool, places, h, terms):
    for e, place in enumerate(places):
        pool[place, h * HD : (h + 1) * HD] += terms[e * BLOCK : (e + 1) * BLOCK]


def gather_pool(pool, parts):
    start = 0
    for part in parts:
        pool[start : start + part.shape[0]] = part[...]
        start += part.shape[0]


def split_pool(outs, pool, factor):
    start = 0
    for out in outs:
        total = pool[start : start + out.shape[0]]
        out[...] = (total if factor is None else total * factor).astype(out.dtype)
        start += out.shape[0]


def stage_kernel(locate, count, *refs):
    sources, refs = refs[: count + 4], refs[count + 4 :]
    table, q_rows, g_rows, q_cols, g_cols, k_ref, v_ref, *refs = refs
    lists = refs[:count]
    q_ref, g_ref, sem = refs[count:]
    targets = [*lists, q_ref, g_ref, k_ref, v_ref]
    copies = [
        pltpu.make_async_copy(source, target, sem.at[i])
        for i, (source, target) in enumerate(zip(sources, targets))
    ]
    for copy in copies:
        copy.start()
    for copy in copies[:count]:
        copy.wait()
    copies = copies[count:]
    row = lax.broadcasted_iota(jnp.int32, table.shape, 0)
    column = lax.broadcasted_iota(jnp.int32, table.shape, 1)
    places = jnp.zeros(table.shape, jnp.int32)
    for b in range(table.shape[0]):
        for e, place in enumerate(locate(lists, table.shape[0], b)):
            places = jnp.where((row == b) & (column == e), place, places)
    table[...] = places
    for copy, ref, rows, cols in ((copies[0], q_ref, q_rows, q_cols), (copies[1], g_ref, g_rows, g_cols)):
        copy.wait()
        for b, h, u in units(table.shape[0]):
            heads = [(h * GROUP + j) * HD for j in range(GROUP)]
            unit = jnp.concatenate(
                [ref[b * BLOCK : (b + 1) * BLOCK, c : c + HD] for c in heads], axis=0
            )
            rows[u * ROWS : (u + 1) * ROWS] = unit
            cols[u * HD : (u + 1) * HD] = unit.T
    copies[2].wait()
    copies[3].wait()


def probs_kernel(count, table_any, q_cols, g_rows, *refs):
    parts = refs[:count]
    probs_ref, k_pool, *dv_refs, dv_pool, table, sem = refs[count:]
    copy = pltpu.make_async_copy(table_any, table, sem)
    copy.start()
    gather_pool(k_pool, parts)
    dv_pool[...] = jnp.zeros_like(dv_pool)
    copy.wait()
    for b, h, u in units(table.shape[0]):
        places = spans(table, b)
        scores = dot(picked(k_pool, places, h), q_cols[u * HD : (u + 1) * HD], NN)
        chunks = [scores[i : i + CHUNK] for i in range(0, KEYS, CHUNK)]
        peaks = [jnp.max(chunk, axis=0, keepdims=True) for chunk in chunks]
        expos = [jnp.exp2((chunk - peak) * FACTOR) for chunk, peak in zip(chunks, peaks)]
        peak = functools.reduce(jnp.maximum, peaks)
        scales = [jnp.exp2((own - peak) * FACTOR) for own in peaks]
        norm = 1.0 / sum(jnp.sum(e, axis=0, keepdims=True) * r for e, r in zip(expos, scales))
        probs = [(e * (r * norm)).astype(jnp.bfloat16) for e, r in zip(expos, scales)]
        probs_b = jnp.concatenate(probs, axis=0)
        probs_ref[u * KEYS : (u + 1) * KEYS] = probs_b
        add_terms(dv_pool, places, h, dot(probs_b, g_rows[u * ROWS : (u + 1) * ROWS], NN))
    split_pool(dv_refs, dv_pool, None)


def dscores_kernel(count, table_any, q_rows, g_cols, probs_ref, *refs):
    parts = refs[:count]
    ds_ref, v_pool, *dk_refs, dk_pool, table, sem = refs[count:]
    copy = pltpu.make_async_copy(table_any, table, sem)
    copy.start()
    gather_pool(v_pool, parts)
    dk_pool[...] = jnp.zeros_like(dk_pool)
    copy.wait()
    for b, h, u in units(table.shape[0]):
        places = spans(table, b)
        probs = probs_ref[u * KEYS : (u + 1) * KEYS].astype(jnp.float32)
        dprobs = dot(picked(v_pool, places, h), g_cols[u * HD : (u + 1) * HD], NN)
        delta = jnp.sum(probs * dprobs, axis=0, keepdims=True)
        dscores = (probs * (dprobs - delta)).astype(jnp.bfloat16)
        ds_ref[u * KEYS : (u + 1) * KEYS] = dscores
        add_terms(dk_pool, places, h, dot(dscores, q_rows[u * ROWS : (u + 1) * ROWS], NN))
    split_pool(dk_refs, dk_pool, SCALE)


def rows_kernel(table, probs_ref, ds_ref, k_pool, v_pool, out_any, qgrad_any, out_ref, qgrad_ref, sem):
    copies = []
    for b in range(table.shape[0]):
        places = spans(table, b)
        for h in range(KVH):
            span = slice((b * KVH + h) * KEYS, (b * KVH + h + 1) * KEYS)
            attended = dot(probs_ref[span], picked(v_pool, places, h), TN)
            unstack(out_ref, b, h, attended.astype(jnp.bfloat16))
            qgrad = dot(ds_ref[span], picked(k_pool, places, h), TN) * SCALE
            unstack(qgrad_ref, b, h, qgrad.astype(jnp.bfloat16))
        rows = pl.ds(b * BLOCK, BLOCK)
        for ref, target in ((out_ref, out_any), (qgrad_ref, qgrad_any)):
            copies.append(pltpu.make_async_copy(ref.at[rows], target.at[rows], sem.at[len(copies)]))
            copies[-1].start()
    for copy in copies:
        copy.wait()


SMEM = pl.BlockSpec(memory_space=pltpu.SMEM)
HBM = pl.BlockSpec(memory_space=pltpu.HBM)
VMEM = pl.BlockSpec(memory_space=pltpu.VMEM)


def run_kernel(kernel, operands, in_specs, results, scratch, products, out_spec=VMEM):
    flops = products * 2 * 4 * KVH * ROWS * KEYS * HD
    return pl.pallas_call(
        kernel,
        out_shape=[jax.ShapeDtypeStruct(shape, kind) for shape, kind in results],
        in_specs=in_specs + [VMEM] * (len(operands) - len(in_specs)),
        out_specs=[out_spec] * len(results),
        scratch_shapes=scratch,
        compiler_params=pltpu.CompilerParams(vmem_limit_bytes=32 * 2**20),
        cost_estimate=pl.CostEstimate(
            flops=flops, bytes_accessed=products * 2**20, transcendentals=0
        ),
    )(*operands)


def stage(locate, lists, queries, out_grad, keys, values):
    blocks_here = queries.shape[0] // BLOCK
    half = jnp.bfloat16
    rows = ((blocks_here * KVH * ROWS, HD), half)
    cols = ((blocks_here * KVH * HD, ROWS), half)
    narrow, wide = (keys.shape, half), (queries.shape, half)
    mine = (*lists, queries, out_grad, keys, values)
    return run_kernel(
        functools.partial(stage_kernel, locate, len(lists)),
        [pltpu.with_memory_space_constraint(array, pltpu.HBM) for array in mine],
        [HBM] * len(mine),
        [((blocks_here, ENTRIES), jnp.int32), rows, rows, cols, cols, narrow, narrow],
        [
            *[pltpu.SMEM(array.shape, array.dtype) for array in lists],
            pltpu.VMEM(*wide), pltpu.VMEM(*wide),
            pltpu.SemaphoreType.DMA((len(mine),)),
        ],
        1,
    )


def attend(table, staged, key_parts, value_parts, send):
    q_rows, g_rows, q_cols, g_cols = staged
    tok_rows, width = key_parts[0].shape
    half, full = jnp.bfloat16, jnp.float32
    wide = ((tok_rows, GROUP * width), half)
    count = len(key_parts)
    pool_rows = sum(part.shape[0] for part in key_parts)
    held = ((table.shape[0] * KVH * KEYS, ROWS), half)
    sums = [(part.shape, half if i else full) for i, part in enumerate(key_parts)]
    scratch = [
        pltpu.VMEM((pool_rows, width), full),
        pltpu.SMEM(table.shape, jnp.int32),
        pltpu.SemaphoreType.DMA(()),
    ]
    pool = ((pool_rows, width), half)
    probs, k_pool, *dv = run_kernel(
        functools.partial(probs_kernel, count),
        (table, q_cols, g_rows, *key_parts),
        [], [held, pool, *sums], scratch, 2,
    )
    dv = send(dv, None)
    dscores, v_pool, *dk = run_kernel(
        functools.partial(dscores_kernel, count),
        (table, q_rows, g_cols, probs, *value_parts),
        [], [held, pool, *sums], scratch, 2,
    )
    dk = send(dk, dv)
    dv[1], table = lax.optimization_barrier((dv[1], table))
    out, query_grad = run_kernel(
        rows_kernel, (table, probs, dscores, k_pool, v_pool), [SMEM], [wide, wide],
        [pltpu.VMEM(*wide)] * 2 + [pltpu.SemaphoreType.DMA((2 * table.shape[0],))], 2, HBM,
    )
    dv[2:], dk[-1], query_grad = lax.optimization_barrier((dv[2:], dk[-1], query_grad))
    return out, query_grad, dk, dv


def dense_local(queries, keys, values, out_grad, rand_blocks, global_blocks):
    cycle_size = lax.axis_size("seq")
    positions = lax.axis_size("dp")

    def swap(array, part):
        pairs = []
        for position in range(positions):
            offset = dense_offsets(cycle_size, position)[part]
            pairs += [(i * positions + position, (i ^ offset) * positions + position) for i in range(cycle_size)]
        return lax.ppermute(array, ("seq", "dp"), pairs)

    def send(grads, earlier):
        sent = [grads[0]] + [None] * (cycle_size - 1)
        sent[-1] = swap(grads[-1], cycle_size - 1)
        near = grads[1:-1]
        if earlier is not None:
            near, earlier[1] = lax.optimization_barrier((near, earlier[1]))
        for part in range(1, cycle_size - 1):
            sent[part] = swap(near[part - 1], part)
        return sent

    def total(grads):
        return sum(grad.astype(jnp.float32) for grad in grads).astype(jnp.bfloat16)

    parts = range(1, cycle_size)
    key_parts = [swap(keys, part) for part in parts]
    table, *staged, keys, values = stage(
        functools.partial(dense_places, cycle_size), (rand_blocks.T, global_blocks),
        queries, out_grad, keys, values,
    )
    value_parts = [swap(values, part) for part in parts]
    out, query_grad, dk, dv = attend(
        table, staged, [keys, *key_parts], [values, *value_parts], send
    )
    return out, query_grad, total(dk), total(dv)


def sparse_local(queries, keys, values, out_grad, rand_blocks, global_blocks):
    cycle_size = lax.axis_size("seq")
    myself = lax.axis_index("seq").astype(jnp.int32)
    tok_rows, width = keys.shape
    blocks_here = tok_rows // BLOCK
    rand_total = RAND * blocks_here
    capacity = (rand_total + GLOB + cycle_size - 1) // cycle_size
    slot_total = cycle_size * capacity
    listed = jnp.concatenate(
        [
            rand_blocks.reshape(cycle_size, rand_total),
            jnp.broadcast_to(global_blocks[None, :], (cycle_size, GLOB)),
        ],
        axis=1,
    )
    entries = listed.shape[1]
    owners = listed // blocks_here
    local_slot = listed % blocks_here
    earlier = jnp.arange(entries)[None, :] < jnp.arange(entries)[:, None]
    same_owner = owners[:, :, None] == owners[:, None, :]
    ranking = jnp.sum(same_owner & earlier[None], axis=2)
    owners_mine = lax.dynamic_index_in_dim(owners, myself, 0, keepdims=False)
    ranking_mine = lax.dynamic_index_in_dim(ranking, myself, 0, keepdims=False)
    far_place = (blocks_here + 2 + owners_mine * capacity + ranking_mine).astype(jnp.int32)
    slot_ids = jnp.arange(slot_total)
    requester = slot_ids // capacity
    position = slot_ids % capacity
    matches = (owners[requester] == myself) & (ranking[requester] == position[:, None])
    source = jnp.sum(jnp.where(matches, local_slot[requester], 0), axis=1)

    up = [(i, (i + 1) % cycle_size) for i in range(cycle_size)]
    down = [(j, i) for i, j in up]
    pair = jnp.concatenate([keys, values], axis=1)
    before = lax.ppermute(pair[tok_rows - BLOCK :], "seq", up)
    after = lax.ppermute(pair[:BLOCK], "seq", down)
    outgoing = jnp.take(pair.reshape(blocks_here, BLOCK, 2 * width), source, axis=0)
    far = lax.all_to_all(outgoing, "seq", split_axis=0, concat_axis=0, tiled=True)
    others = [before, after, far.reshape(slot_total * BLOCK, 2 * width)]
    key_parts = [part[:, :width] for part in others]
    value_parts = [part[:, width:] for part in others]

    here = jnp.arange(blocks_here, dtype=jnp.int32)[:, None]
    ahead = jnp.where(here == 0, blocks_here, here - 1)
    behind = jnp.where(here == blocks_here - 1, blocks_here + 1, here + 1)
    table = jnp.concatenate(
        [
            ahead,
            here,
            behind,
            jnp.broadcast_to(far_place[None, rand_total:], (blocks_here, GLOB)),
            far_place[:rand_total].reshape(blocks_here, RAND),
        ],
        axis=1,
    )
    landing = (source[:, None] == jnp.arange(blocks_here)[None, :]).astype(jnp.bfloat16)

    def send(grads, earlier):
        own, grad_before, grad_after, grad_far = grads
        last_rim = lax.ppermute(grad_before, "seq", down)
        first_rim = lax.ppermute(grad_after, "seq", up)
        returned = lax.all_to_all(
            grad_far.reshape(slot_total, BLOCK, width),
            "seq", split_axis=0, concat_axis=0, tiled=True,
        )
        return [own, last_rim, first_rim, returned]

    def total(grads):
        own, last_rim, first_rim, returned = grads
        landed = jnp.einsum("sq,sbx->qbx", landing, returned, preferred_element_type=jnp.float32)
        sums = own.reshape(blocks_here, BLOCK, width) + landed
        sums = sums.at[blocks_here - 1].add(last_rim.astype(jnp.float32))
        sums = sums.at[0].add(first_rim.astype(jnp.float32))
        return sums.reshape(tok_rows, width).astype(jnp.bfloat16)

    table, *staged, keys, values = stage(
        given_places, (table,), queries, out_grad, keys, values
    )
    out, query_grad, dk, dv = attend(
        table, staged, [keys, *key_parts], [values, *value_parts], send
    )
    return out, query_grad, total(dk), total(dv)


def local(queries, keys, values, out_grad, rand_blocks, global_blocks):
    cycle_size = lax.axis_size("seq")
    blocks_here = queries.shape[0] // BLOCK
    capacity = (RAND * blocks_here + GLOB + cycle_size - 1) // cycle_size
    dense = capacity >= blocks_here and cycle_size == 4
    plan = dense_local if dense else sparse_local
    return plan(queries, keys, values, out_grad, rand_blocks, global_blocks)


def solution(mesh):
    rows = P(("dp", "seq"), None)
    return jax.shard_map(
        local,
        mesh=mesh,
        in_specs=(rows, rows, rows, rows, P("dp", None), P("dp")),
        out_specs=(rows, rows, rows, rows),
        check_vma=False,
    )
```

```python
import functools

import jax
import jax.numpy as jnp
from jax import lax
from jax.experimental import pallas as pl
from jax.experimental.pallas import tpu as pltpu
from jax.sharding import PartitionSpec as P

KVH = 2
HD = 128
BLOCK = 64
GLOB = 2
RAND = 3
GROUP = 4
ENTRIES = 3 + GLOB + RAND
LOG2E = 1.4426950408889634
SCALE = HD ** (-0.5)


NN = (((1,), (0,)), ((), ()))
TN = (((0,), (0,)), ((), ()))
dot = functools.partial(lax.dot_general, preferred_element_type=jnp.float32)

KEYS = ENTRIES * BLOCK
CHUNK = 128
FACTOR = SCALE * LOG2E
ROWS = GROUP * BLOCK


def units(blocks_here):
    return [(b, h, b * KVH + h) for b in range(blocks_here) for h in range(KVH)]


def given_places(lists, blocks_here, b):
    return [lists[0][b, e] for e in range(ENTRIES)]


def dense_offsets(cycle_size, position):
    odd = position & 1
    offsets = list(range(cycle_size))
    offsets[1], offsets[2] = 1 + odd, 2 - odd
    return offsets


def dense_places(cycle_size, lists, blocks_here, b):
    rand_ref, glob_ref = lists
    me = lax.axis_index("seq").astype(jnp.int32)
    odd = lax.axis_index("dp").astype(jnp.int32) & 1

    def place(owner, local):
        offset = owner ^ me
        swapped = (odd == 1) & ((offset == 1) | (offset == 2))
        return jnp.where(swapped, 3 - offset, offset) * blocks_here + local

    def far_place(block):
        return place(lax.div(block, blocks_here), lax.rem(block, blocks_here))

    window = [b - 1, b, b + 1]
    if b == 0:
        window[0] = place(lax.rem(me + cycle_size - 1, cycle_size), blocks_here - 1)
    if b == blocks_here - 1:
        window[2] = place(lax.rem(me + 1, cycle_size), 0)
    far = [glob_ref[i] for i in range(GLOB)] + [rand_ref[i, me * blocks_here + b] for i in range(RAND)]
    return window + [far_place(block) for block in far]


def spans(table, b):
    result = []
    for e in range(ENTRIES):
        near = b + e - 1
        if e < 3 and 0 <= near < table.shape[0]:
            result.append(pl.ds(near * BLOCK, BLOCK))
        else:
            result.append(pl.ds(pl.multiple_of(table[b, e] * BLOCK, BLOCK), BLOCK))
    return result


def picked(pool, places, h):
    return jnp.concatenate([pool[place, h * HD : (h + 1) * HD] for place in places], axis=0)


def unstack(ref, b, h, value):
    for j in range(GROUP):
        c = (h * GROUP + j) * HD
        ref[b * BLOCK : (b + 1) * BLOCK, c : c + HD] = value[j * BLOCK : (j + 1) * BLOCK]


def add_terms(pool, fixed, places, b, h, terms, count, touched):
    cols = slice(h * HD, (h + 1) * HD)
    for e, place in enumerate(places):
        term = terms[e * BLOCK : (e + 1) * BLOCK]
        near = b + e - 1
        if e >= 3 + GLOB:
            pool[place, cols] += term
            continue
        if e >= 3:
            slot = count + 2 + e - 3
        else:
            slot = count if near < 0 else count + 1 if near == count else near
        rows = slice(slot * BLOCK, (slot + 1) * BLOCK)
        fixed[rows, cols] = fixed[rows, cols] + term if (slot, h) in touched else term
        touched.add((slot, h))


def join_terms(pool, fixed, table):
    count = table.shape[0]
    pool[: count * BLOCK] += fixed[: count * BLOCK]
    first, last = spans(table, 0), spans(table, count - 1)
    for i, place in enumerate([first[0], last[2], *first[3 : 3 + GLOB]]):
        pool[place, :] += fixed[(count + i) * BLOCK : (count + i + 1) * BLOCK]


def gather_pool(pool, parts):
    start = 0
    for part in parts:
        pool[start : start + part.shape[0]] = part[...]
        start += part.shape[0]


def split_pool(outs, pool, factor):
    start = 0
    for out in outs:
        total = pool[start : start + out.shape[0]]
        out[...] = (total if factor is None else total * factor).astype(out.dtype)
        start += out.shape[0]


def stage_kernel(locate, count, *refs):
    sources, refs = refs[: count + 4], refs[count + 4 :]
    table, q_rows, g_rows, q_cols, g_cols, k_ref, v_ref, *refs = refs
    lists = refs[:count]
    q_ref, g_ref, sem = refs[count:]
    targets = [*lists, q_ref, g_ref, k_ref, v_ref]
    copies = [
        pltpu.make_async_copy(source, target, sem.at[i])
        for i, (source, target) in enumerate(zip(sources, targets))
    ]
    for copy in copies:
        copy.start()
    for copy in copies[:count]:
        copy.wait()
    copies = copies[count:]
    row = lax.broadcasted_iota(jnp.int32, table.shape, 0)
    column = lax.broadcasted_iota(jnp.int32, table.shape, 1)
    places = jnp.zeros(table.shape, jnp.int32)
    for b in range(table.shape[0]):
        for e, place in enumerate(locate(lists, table.shape[0], b)):
            places = jnp.where((row == b) & (column == e), place, places)
    table[...] = places
    for copy, ref, rows, cols in ((copies[0], q_ref, q_rows, q_cols), (copies[1], g_ref, g_rows, g_cols)):
        copy.wait()
        for b, h, u in units(table.shape[0]):
            heads = [(h * GROUP + j) * HD for j in range(GROUP)]
            unit = jnp.concatenate(
                [ref[b * BLOCK : (b + 1) * BLOCK, c : c + HD] for c in heads], axis=0
            )
            rows[u * ROWS : (u + 1) * ROWS] = unit
            cols[u * HD : (u + 1) * HD] = unit.T
    copies[2].wait()
    copies[3].wait()


def over_units(table, begin, finish):
    todo = None
    for b, h, u in units(table.shape[0]):
        begun = begin(b, h, u)
        if todo is not None:
            finish(*todo)
        todo = (b, h, u, *begun)
    finish(*todo)


def probs_kernel(count, table_any, q_cols, g_rows, *refs):
    parts = refs[:count]
    probs_ref, k_pool, *dv_refs, dv_pool, fixed, table, sem = refs[count:]
    copy = pltpu.make_async_copy(table_any, table, sem)
    copy.start()
    gather_pool(k_pool, parts)
    dv_pool[...] = jnp.zeros_like(dv_pool)
    copy.wait()
    touched = set()

    def begin(b, h, u):
        places = spans(table, b)
        return places, dot(picked(k_pool, places, h), q_cols[u * HD : (u + 1) * HD], NN)

    def finish(b, h, u, places, scores):
        chunks = [scores[i : i + CHUNK] for i in range(0, KEYS, CHUNK)]
        peaks = [jnp.max(chunk, axis=0, keepdims=True) for chunk in chunks]
        expos = [jnp.exp2((chunk - peak) * FACTOR) for chunk, peak in zip(chunks, peaks)]
        peak = functools.reduce(jnp.maximum, peaks)
        scales = [jnp.exp2((own - peak) * FACTOR) for own in peaks]
        norm = 1.0 / sum(jnp.sum(e, axis=0, keepdims=True) * r for e, r in zip(expos, scales))
        probs = [(e * (r * norm)).astype(jnp.bfloat16) for e, r in zip(expos, scales)]
        probs_b = jnp.concatenate(probs, axis=0)
        probs_ref[u * KEYS : (u + 1) * KEYS] = probs_b
        terms = dot(probs_b, g_rows[u * ROWS : (u + 1) * ROWS], NN)
        add_terms(dv_pool, fixed, places, b, h, terms, table.shape[0], touched)

    over_units(table, begin, finish)
    join_terms(dv_pool, fixed, table)
    split_pool(dv_refs, dv_pool, None)


def dscores_kernel(count, table_any, q_rows, g_cols, probs_ref, *refs):
    parts = refs[:count]
    ds_ref, v_pool, *dk_refs, dk_pool, fixed, table, sem = refs[count:]
    copy = pltpu.make_async_copy(table_any, table, sem)
    copy.start()
    gather_pool(v_pool, parts)
    dk_pool[...] = jnp.zeros_like(dk_pool)
    copy.wait()
    touched = set()

    def begin(b, h, u):
        places = spans(table, b)
        return places, dot(picked(v_pool, places, h), g_cols[u * HD : (u + 1) * HD], NN)

    def finish(b, h, u, places, dprobs):
        probs = probs_ref[u * KEYS : (u + 1) * KEYS].astype(jnp.float32)
        delta = jnp.sum(probs * dprobs, axis=0, keepdims=True)
        dscores = (probs * (dprobs - delta)).astype(jnp.bfloat16)
        ds_ref[u * KEYS : (u + 1) * KEYS] = dscores
        terms = dot(dscores, q_rows[u * ROWS : (u + 1) * ROWS], NN)
        add_terms(dk_pool, fixed, places, b, h, terms, table.shape[0], touched)

    over_units(table, begin, finish)
    join_terms(dk_pool, fixed, table)
    split_pool(dk_refs, dk_pool, SCALE)


def rows_kernel(table, probs_ref, ds_ref, k_pool, v_pool, out_any, qgrad_any, out_ref, qgrad_ref, sem):
    copies = []
    for b in range(table.shape[0]):
        places = spans(table, b)
        for h in range(KVH):
            span = slice((b * KVH + h) * KEYS, (b * KVH + h + 1) * KEYS)
            attended = dot(probs_ref[span], picked(v_pool, places, h), TN)
            unstack(out_ref, b, h, attended.astype(jnp.bfloat16))
            qgrad = dot(ds_ref[span], picked(k_pool, places, h), TN) * SCALE
            unstack(qgrad_ref, b, h, qgrad.astype(jnp.bfloat16))
        rows = pl.ds(b * BLOCK, BLOCK)
        for ref, target in ((out_ref, out_any), (qgrad_ref, qgrad_any)):
            copies.append(pltpu.make_async_copy(ref.at[rows], target.at[rows], sem.at[len(copies)]))
            copies[-1].start()
    for copy in copies:
        copy.wait()


SMEM = pl.BlockSpec(memory_space=pltpu.SMEM)
HBM = pl.BlockSpec(memory_space=pltpu.HBM)
VMEM = pl.BlockSpec(memory_space=pltpu.VMEM)


def run_kernel(kernel, operands, in_specs, results, scratch, products, out_spec=VMEM):
    flops = products * 2 * 4 * KVH * ROWS * KEYS * HD
    return pl.pallas_call(
        kernel,
        out_shape=[jax.ShapeDtypeStruct(shape, kind) for shape, kind in results],
        in_specs=in_specs + [VMEM] * (len(operands) - len(in_specs)),
        out_specs=[out_spec] * len(results),
        scratch_shapes=scratch,
        compiler_params=pltpu.CompilerParams(vmem_limit_bytes=32 * 2**20),
        cost_estimate=pl.CostEstimate(
            flops=flops, bytes_accessed=products * 2**20, transcendentals=0
        ),
    )(*operands)


def stage(locate, lists, queries, out_grad, keys, values):
    blocks_here = queries.shape[0] // BLOCK
    half = jnp.bfloat16
    rows = ((blocks_here * KVH * ROWS, HD), half)
    cols = ((blocks_here * KVH * HD, ROWS), half)
    narrow, wide = (keys.shape, half), (queries.shape, half)
    mine = (*lists, queries, out_grad, keys, values)
    return run_kernel(
        functools.partial(stage_kernel, locate, len(lists)),
        [pltpu.with_memory_space_constraint(array, pltpu.HBM) for array in mine],
        [HBM] * len(mine),
        [((blocks_here, ENTRIES), jnp.int32), rows, rows, cols, cols, narrow, narrow],
        [
            *[pltpu.SMEM(array.shape, array.dtype) for array in lists],
            pltpu.VMEM(*wide), pltpu.VMEM(*wide),
            pltpu.SemaphoreType.DMA((len(mine),)),
        ],
        1,
    )


def attend(table, staged, key_parts, value_parts, send):
    q_rows, g_rows, q_cols, g_cols = staged
    tok_rows, width = key_parts[0].shape
    half, full = jnp.bfloat16, jnp.float32
    wide = ((tok_rows, GROUP * width), half)
    count = len(key_parts)
    pool_rows = sum(part.shape[0] for part in key_parts)
    held = ((table.shape[0] * KVH * KEYS, ROWS), half)
    sums = [(part.shape, half if i else full) for i, part in enumerate(key_parts)]
    scratch = [
        pltpu.VMEM((pool_rows, width), full),
        pltpu.VMEM(((table.shape[0] + 2 + GLOB) * BLOCK, width), full),
        pltpu.SMEM(table.shape, jnp.int32),
        pltpu.SemaphoreType.DMA(()),
    ]
    pool = ((pool_rows, width), half)
    probs, k_pool, *dv = run_kernel(
        functools.partial(probs_kernel, count),
        (table, q_cols, g_rows, *key_parts),
        [], [held, pool, *sums], scratch, 2,
    )
    dv = send(dv, None)
    dscores, v_pool, *dk = run_kernel(
        functools.partial(dscores_kernel, count),
        (table, q_rows, g_cols, probs, *value_parts),
        [], [held, pool, *sums], scratch, 2,
    )
    dk = send(dk, dv)
    dv[1], table = lax.optimization_barrier((dv[1], table))
    out, query_grad = run_kernel(
        rows_kernel, (table, probs, dscores, k_pool, v_pool), [SMEM], [wide, wide],
        [pltpu.VMEM(*wide)] * 2 + [pltpu.SemaphoreType.DMA((2 * table.shape[0],))], 2, HBM,
    )
    dv[2:], dk[-1], query_grad = lax.optimization_barrier((dv[2:], dk[-1], query_grad))
    return out, query_grad, dk, dv


def dense_local(queries, keys, values, out_grad, rand_blocks, global_blocks):
    cycle_size = lax.axis_size("seq")
    positions = lax.axis_size("dp")

    def swap(array, part):
        pairs = []
        for position in range(positions):
            offset = dense_offsets(cycle_size, position)[part]
            pairs += [(i * positions + position, (i ^ offset) * positions + position) for i in range(cycle_size)]
        return lax.ppermute(array, ("seq", "dp"), pairs)

    def send(grads, earlier):
        sent = [grads[0]] + [None] * (cycle_size - 1)
        sent[-1] = swap(grads[-1], cycle_size - 1)
        near = grads[1:-1]
        if earlier is not None:
            near, earlier[1] = lax.optimization_barrier((near, earlier[1]))
        for part in range(1, cycle_size - 1):
            sent[part] = swap(near[part - 1], part)
        return sent

    def total(grads):
        return sum(grad.astype(jnp.float32) for grad in grads).astype(jnp.bfloat16)

    parts = range(1, cycle_size)
    key_parts = [swap(keys, part) for part in parts]
    table, *staged, keys, values = stage(
        functools.partial(dense_places, cycle_size), (rand_blocks.T, global_blocks),
        queries, out_grad, keys, values,
    )
    value_parts = [swap(values, part) for part in parts]
    out, query_grad, dk, dv = attend(
        table, staged, [keys, *key_parts], [values, *value_parts], send
    )
    return out, query_grad, total(dk), total(dv)


def sparse_local(queries, keys, values, out_grad, rand_blocks, global_blocks):
    cycle_size = lax.axis_size("seq")
    myself = lax.axis_index("seq").astype(jnp.int32)
    tok_rows, width = keys.shape
    blocks_here = tok_rows // BLOCK
    rand_total = RAND * blocks_here
    capacity = (rand_total + GLOB + cycle_size - 1) // cycle_size
    slot_total = cycle_size * capacity
    listed = jnp.concatenate(
        [
            rand_blocks.reshape(cycle_size, rand_total),
            jnp.broadcast_to(global_blocks[None, :], (cycle_size, GLOB)),
        ],
        axis=1,
    )
    entries = listed.shape[1]
    owners = listed // blocks_here
    local_slot = listed % blocks_here
    earlier = jnp.arange(entries)[None, :] < jnp.arange(entries)[:, None]
    same_owner = owners[:, :, None] == owners[:, None, :]
    ranking = jnp.sum(same_owner & earlier[None], axis=2)
    owners_mine = lax.dynamic_index_in_dim(owners, myself, 0, keepdims=False)
    ranking_mine = lax.dynamic_index_in_dim(ranking, myself, 0, keepdims=False)
    far_place = (blocks_here + 2 + owners_mine * capacity + ranking_mine).astype(jnp.int32)
    slot_ids = jnp.arange(slot_total)
    requester = slot_ids // capacity
    position = slot_ids % capacity
    matches = (owners[requester] == myself) & (ranking[requester] == position[:, None])
    source = jnp.sum(jnp.where(matches, local_slot[requester], 0), axis=1)

    up = [(i, (i + 1) % cycle_size) for i in range(cycle_size)]
    down = [(j, i) for i, j in up]
    pair = jnp.concatenate([keys, values], axis=1)
    before = lax.ppermute(pair[tok_rows - BLOCK :], "seq", up)
    after = lax.ppermute(pair[:BLOCK], "seq", down)
    outgoing = jnp.take(pair.reshape(blocks_here, BLOCK, 2 * width), source, axis=0)
    far = lax.all_to_all(outgoing, "seq", split_axis=0, concat_axis=0, tiled=True)
    others = [before, after, far.reshape(slot_total * BLOCK, 2 * width)]
    key_parts = [part[:, :width] for part in others]
    value_parts = [part[:, width:] for part in others]

    here = jnp.arange(blocks_here, dtype=jnp.int32)[:, None]
    ahead = jnp.where(here == 0, blocks_here, here - 1)
    behind = jnp.where(here == blocks_here - 1, blocks_here + 1, here + 1)
    table = jnp.concatenate(
        [
            ahead,
            here,
            behind,
            jnp.broadcast_to(far_place[None, rand_total:], (blocks_here, GLOB)),
            far_place[:rand_total].reshape(blocks_here, RAND),
        ],
        axis=1,
    )
    landing = (source[:, None] == jnp.arange(blocks_here)[None, :]).astype(jnp.bfloat16)

    def send(grads, earlier):
        own, grad_before, grad_after, grad_far = grads
        last_rim = lax.ppermute(grad_before, "seq", down)
        first_rim = lax.ppermute(grad_after, "seq", up)
        returned = lax.all_to_all(
            grad_far.reshape(slot_total, BLOCK, width),
            "seq", split_axis=0, concat_axis=0, tiled=True,
        )
        return [own, last_rim, first_rim, returned]

    def total(grads):
        own, last_rim, first_rim, returned = grads
        landed = jnp.einsum("sq,sbx->qbx", landing, returned, preferred_element_type=jnp.float32)
        sums = own.reshape(blocks_here, BLOCK, width) + landed
        sums = sums.at[blocks_here - 1].add(last_rim.astype(jnp.float32))
        sums = sums.at[0].add(first_rim.astype(jnp.float32))
        return sums.reshape(tok_rows, width).astype(jnp.bfloat16)

    table, *staged, keys, values = stage(
        given_places, (table,), queries, out_grad, keys, values
    )
    out, query_grad, dk, dv = attend(
        table, staged, [keys, *key_parts], [values, *value_parts], send
    )
    return out, query_grad, total(dk), total(dv)


def local(queries, keys, values, out_grad, rand_blocks, global_blocks):
    cycle_size = lax.axis_size("seq")
    blocks_here = queries.shape[0] // BLOCK
    capacity = (RAND * blocks_here + GLOB + cycle_size - 1) // cycle_size
    dense = capacity >= blocks_here and cycle_size == 4
    plan = dense_local if dense else sparse_local
    return plan(queries, keys, values, out_grad, rand_blocks, global_blocks)


def solution(mesh):
    rows = P(("dp", "seq"), None)
    return jax.shard_map(
        local,
        mesh=mesh,
        in_specs=(rows, rows, rows, rows, P("dp", None), P("dp")),
        out_specs=(rows, rows, rows, rows),
        check_vma=False,
    )
```

```python
import functools

import jax
import jax.numpy as jnp
from jax import lax
from jax.experimental import pallas as pl
from jax.experimental.pallas import tpu as pltpu
from jax.sharding import PartitionSpec as P

KVH = 2
HD = 128
BLOCK = 64
GLOB = 2
RAND = 3
GROUP = 4
ENTRIES = 3 + GLOB + RAND
LOG2E = 1.4426950408889634
SCALE = HD ** (-0.5)


NN = (((1,), (0,)), ((), ()))
TN = (((0,), (0,)), ((), ()))
dot = functools.partial(lax.dot_general, preferred_element_type=jnp.float32)

KEYS = ENTRIES * BLOCK
CHUNK = 128
FACTOR = SCALE * LOG2E
ROWS = GROUP * BLOCK


def units(blocks_here):
    return [(b, h, b * KVH + h) for b in range(blocks_here) for h in range(KVH)]


def given_places(lists, blocks_here, b):
    return [lists[0][b, e] for e in range(ENTRIES)]


def dense_offsets(cycle_size, position):
    odd = position & 1
    offsets = list(range(cycle_size))
    offsets[1], offsets[2] = 1 + odd, 2 - odd
    return offsets


def dense_places(cycle_size, lists, blocks_here, b):
    rand_ref, glob_ref = lists
    me = lax.axis_index("seq").astype(jnp.int32)
    odd = lax.axis_index("dp").astype(jnp.int32) & 1

    def place(owner, local):
        offset = owner ^ me
        swapped = (odd == 1) & ((offset == 1) | (offset == 2))
        return jnp.where(swapped, 3 - offset, offset) * blocks_here + local

    def far_place(block):
        return place(lax.div(block, blocks_here), lax.rem(block, blocks_here))

    window = [b - 1, b, b + 1]
    if b == 0:
        window[0] = place(lax.rem(me + cycle_size - 1, cycle_size), blocks_here - 1)
    if b == blocks_here - 1:
        window[2] = place(lax.rem(me + 1, cycle_size), 0)
    far = [glob_ref[i] for i in range(GLOB)] + [rand_ref[i, me * blocks_here + b] for i in range(RAND)]
    return window + [far_place(block) for block in far]


def spans(table, b):
    result = []
    for e in range(ENTRIES):
        near = b + e - 1
        if e < 3 and 0 <= near < table.shape[0]:
            result.append(pl.ds(near * BLOCK, BLOCK))
        else:
            result.append(pl.ds(pl.multiple_of(table[b, e] * BLOCK, BLOCK), BLOCK))
    return result


def picked(pool, places, h):
    return jnp.concatenate([pool[place, h * HD : (h + 1) * HD] for place in places], axis=0)


def unstack(ref, b, h, value):
    for j in range(GROUP):
        c = (h * GROUP + j) * HD
        ref[b * BLOCK : (b + 1) * BLOCK, c : c + HD] = value[j * BLOCK : (j + 1) * BLOCK]


def add_terms(pool, places, h, terms):
    for e, place in enumerate(places):
        pool[place, h * HD : (h + 1) * HD] += terms[e * BLOCK : (e + 1) * BLOCK]


def gather_pool(pool, parts):
    start = 0
    for part in parts:
        pool[start : start + part.shape[0]] = part[...]
        start += part.shape[0]


def split_pool(outs, pool, factor):
    start = 0
    for out in outs:
        total = pool[start : start + out.shape[0]]
        out[...] = (total if factor is None else total * factor).astype(out.dtype)
        start += out.shape[0]


def stage_kernel(locate, count, *refs):
    sources, refs = refs[: count + 4], refs[count + 4 :]
    table, q_rows, g_rows, q_cols, g_cols, k_ref, v_ref, *refs = refs
    lists = refs[:count]
    q_ref, g_ref, sem = refs[count:]
    targets = [*lists, q_ref, g_ref, k_ref, v_ref]
    copies = [
        pltpu.make_async_copy(source, target, sem.at[i])
        for i, (source, target) in enumerate(zip(sources, targets))
    ]
    for copy in copies:
        copy.start()
    for copy in copies[:count]:
        copy.wait()
    copies = copies[count:]
    row = lax.broadcasted_iota(jnp.int32, table.shape, 0)
    column = lax.broadcasted_iota(jnp.int32, table.shape, 1)
    places = jnp.zeros(table.shape, jnp.int32)
    for b in range(table.shape[0]):
        for e, place in enumerate(locate(lists, table.shape[0], b)):
            places = jnp.where((row == b) & (column == e), place, places)
    table[...] = places
    for copy, ref, rows, cols in ((copies[0], q_ref, q_rows, q_cols), (copies[1], g_ref, g_rows, g_cols)):
        copy.wait()
        for b, h, u in units(table.shape[0]):
            heads = [(h * GROUP + j) * HD for j in range(GROUP)]
            unit = jnp.concatenate(
                [ref[b * BLOCK : (b + 1) * BLOCK, c : c + HD] for c in heads], axis=0
            )
            rows[u * ROWS : (u + 1) * ROWS] = unit
            cols[u * HD : (u + 1) * HD] = unit.T
    copies[2].wait()
    copies[3].wait()


def probs_kernel(count, table_any, q_cols, g_rows, *refs):
    parts = refs[:count][::-1]
    probs_ref, k_pool, *dv_refs, dv_pool, table, sem = refs[count:]
    copy = pltpu.make_async_copy(table_any, table, sem)
    copy.start()
    gather_pool(k_pool, parts)
    dv_pool[...] = jnp.zeros_like(dv_pool)
    copy.wait()
    for b, h, u in units(table.shape[0]):
        places = spans(table, b)
        scores = dot(picked(k_pool, places, h), q_cols[u * HD : (u + 1) * HD], NN)
        chunks = [scores[i : i + CHUNK] for i in range(0, KEYS, CHUNK)]
        peaks = [jnp.max(chunk, axis=0, keepdims=True) for chunk in chunks]
        expos = [jnp.exp2((chunk - peak) * FACTOR) for chunk, peak in zip(chunks, peaks)]
        peak = functools.reduce(jnp.maximum, peaks)
        scales = [jnp.exp2((own - peak) * FACTOR) for own in peaks]
        norm = 1.0 / sum(jnp.sum(e, axis=0, keepdims=True) * r for e, r in zip(expos, scales))
        probs = [(e * (r * norm)).astype(jnp.bfloat16) for e, r in zip(expos, scales)]
        probs_b = jnp.concatenate(probs, axis=0)
        probs_ref[u * KEYS : (u + 1) * KEYS] = probs_b
        add_terms(dv_pool, places, h, dot(probs_b, g_rows[u * ROWS : (u + 1) * ROWS], NN))
    split_pool(dv_refs, dv_pool, None)


def dscores_kernel(count, table_any, q_rows, g_cols, probs_ref, *refs):
    parts = refs[:count][::-1]
    ds_ref, v_pool, *dk_refs, dk_pool, table, sem = refs[count:]
    copy = pltpu.make_async_copy(table_any, table, sem)
    copy.start()
    gather_pool(v_pool, parts)
    dk_pool[...] = jnp.zeros_like(dk_pool)
    copy.wait()
    for b, h, u in units(table.shape[0]):
        places = spans(table, b)
        probs = probs_ref[u * KEYS : (u + 1) * KEYS].astype(jnp.float32)
        dprobs = dot(picked(v_pool, places, h), g_cols[u * HD : (u + 1) * HD], NN)
        delta = jnp.sum(probs * dprobs, axis=0, keepdims=True)
        dscores = (probs * (dprobs - delta)).astype(jnp.bfloat16)
        ds_ref[u * KEYS : (u + 1) * KEYS] = dscores
        add_terms(dk_pool, places, h, dot(dscores, q_rows[u * ROWS : (u + 1) * ROWS], NN))
    split_pool(dk_refs, dk_pool, SCALE)


def rows_kernel(table, probs_ref, ds_ref, k_pool, v_pool, out_any, qgrad_any, out_ref, qgrad_ref, sem):
    copies = []
    for b in range(table.shape[0]):
        places = spans(table, b)
        for h in range(KVH):
            span = slice((b * KVH + h) * KEYS, (b * KVH + h + 1) * KEYS)
            attended = dot(probs_ref[span], picked(v_pool, places, h), TN)
            unstack(out_ref, b, h, attended.astype(jnp.bfloat16))
            qgrad = dot(ds_ref[span], picked(k_pool, places, h), TN) * SCALE
            unstack(qgrad_ref, b, h, qgrad.astype(jnp.bfloat16))
        rows = pl.ds(b * BLOCK, BLOCK)
        for ref, target in ((out_ref, out_any), (qgrad_ref, qgrad_any)):
            copies.append(pltpu.make_async_copy(ref.at[rows], target.at[rows], sem.at[len(copies)]))
            copies[-1].start()
    for copy in copies:
        copy.wait()


SMEM = pl.BlockSpec(memory_space=pltpu.SMEM)
HBM = pl.BlockSpec(memory_space=pltpu.HBM)
VMEM = pl.BlockSpec(memory_space=pltpu.VMEM)


def run_kernel(kernel, operands, in_specs, results, scratch, products, out_spec=VMEM):
    flops = products * 2 * 4 * KVH * ROWS * KEYS * HD
    return pl.pallas_call(
        kernel,
        out_shape=[jax.ShapeDtypeStruct(shape, kind) for shape, kind in results],
        in_specs=in_specs + [VMEM] * (len(operands) - len(in_specs)),
        out_specs=[out_spec] * len(results),
        scratch_shapes=scratch,
        compiler_params=pltpu.CompilerParams(vmem_limit_bytes=32 * 2**20),
        cost_estimate=pl.CostEstimate(
            flops=flops, bytes_accessed=products * 2**20, transcendentals=0
        ),
    )(*operands)


def stage(locate, lists, queries, out_grad, keys, values):
    blocks_here = queries.shape[0] // BLOCK
    half = jnp.bfloat16
    rows = ((blocks_here * KVH * ROWS, HD), half)
    cols = ((blocks_here * KVH * HD, ROWS), half)
    narrow, wide = (keys.shape, half), (queries.shape, half)
    mine = (*lists, queries, out_grad, keys, values)
    return run_kernel(
        functools.partial(stage_kernel, locate, len(lists)),
        [pltpu.with_memory_space_constraint(array, pltpu.HBM) for array in mine],
        [HBM] * len(mine),
        [((blocks_here, ENTRIES), jnp.int32), rows, rows, cols, cols, narrow, narrow],
        [
            *[pltpu.SMEM(array.shape, array.dtype) for array in lists],
            pltpu.VMEM(*wide), pltpu.VMEM(*wide),
            pltpu.SemaphoreType.DMA((len(mine),)),
        ],
        1,
    )


def attend(table, staged, key_parts, value_parts, send):
    q_rows, g_rows, q_cols, g_cols = staged
    tok_rows, width = key_parts[0].shape
    half, full = jnp.bfloat16, jnp.float32
    wide = ((tok_rows, GROUP * width), half)
    count = len(key_parts)
    pool_rows = sum(part.shape[0] for part in key_parts)
    held = ((table.shape[0] * KVH * KEYS, ROWS), half)
    sums = [(part.shape, half if i else full) for i, part in enumerate(key_parts)]
    scratch = [
        pltpu.VMEM((pool_rows, width), full),
        pltpu.SMEM(table.shape, jnp.int32),
        pltpu.SemaphoreType.DMA(()),
    ]
    pool = ((pool_rows, width), half)
    probs, k_pool, *dv = run_kernel(
        functools.partial(probs_kernel, count),
        (table, q_cols, g_rows, *key_parts[::-1]),
        [], [held, pool, *sums], scratch, 2,
    )
    dv = send(dv, None)
    dscores, v_pool, *dk = run_kernel(
        functools.partial(dscores_kernel, count),
        (table, q_rows, g_cols, probs, *value_parts[::-1]),
        [], [held, pool, *sums], scratch, 2,
    )
    dk = send(dk, dv)
    dv[1], table = lax.optimization_barrier((dv[1], table))
    out, query_grad = run_kernel(
        rows_kernel, (table, probs, dscores, k_pool, v_pool), [SMEM], [wide, wide],
        [pltpu.VMEM(*wide)] * 2 + [pltpu.SemaphoreType.DMA((2 * table.shape[0],))], 2, HBM,
    )
    dv[2:], dk[-1], query_grad = lax.optimization_barrier((dv[2:], dk[-1], query_grad))
    return out, query_grad, dk, dv


def dense_local(queries, keys, values, out_grad, rand_blocks, global_blocks):
    cycle_size = lax.axis_size("seq")
    positions = lax.axis_size("dp")

    def swap(array, part):
        pairs = []
        for position in range(positions):
            offset = dense_offsets(cycle_size, position)[part]
            pairs += [(i * positions + position, (i ^ offset) * positions + position) for i in range(cycle_size)]
        return lax.ppermute(array, ("seq", "dp"), pairs)

    def send(grads, earlier):
        sent = [grads[0]] + [None] * (cycle_size - 1)
        sent[-1] = swap(grads[-1], cycle_size - 1)
        near = grads[1:-1]
        if earlier is not None:
            near, earlier[1] = lax.optimization_barrier((near, earlier[1]))
        for part in range(1, cycle_size - 1):
            sent[part] = swap(near[part - 1], part)
        return sent

    def total(grads):
        return sum(grad.astype(jnp.float32) for grad in grads).astype(jnp.bfloat16)

    parts = range(1, cycle_size)
    key_parts = [swap(keys, part) for part in parts]
    table, *staged, keys, values = stage(
        functools.partial(dense_places, cycle_size), (rand_blocks.T, global_blocks),
        queries, out_grad, keys, values,
    )
    value_parts = [swap(values, part) for part in parts]
    out, query_grad, dk, dv = attend(
        table, staged, [keys, *key_parts], [values, *value_parts], send
    )
    return out, query_grad, total(dk), total(dv)


def sparse_local(queries, keys, values, out_grad, rand_blocks, global_blocks):
    cycle_size = lax.axis_size("seq")
    myself = lax.axis_index("seq").astype(jnp.int32)
    tok_rows, width = keys.shape
    blocks_here = tok_rows // BLOCK
    rand_total = RAND * blocks_here
    capacity = (rand_total + GLOB + cycle_size - 1) // cycle_size
    slot_total = cycle_size * capacity
    listed = jnp.concatenate(
        [
            rand_blocks.reshape(cycle_size, rand_total),
            jnp.broadcast_to(global_blocks[None, :], (cycle_size, GLOB)),
        ],
        axis=1,
    )
    entries = listed.shape[1]
    owners = listed // blocks_here
    local_slot = listed % blocks_here
    earlier = jnp.arange(entries)[None, :] < jnp.arange(entries)[:, None]
    same_owner = owners[:, :, None] == owners[:, None, :]
    ranking = jnp.sum(same_owner & earlier[None], axis=2)
    owners_mine = lax.dynamic_index_in_dim(owners, myself, 0, keepdims=False)
    ranking_mine = lax.dynamic_index_in_dim(ranking, myself, 0, keepdims=False)
    far_place = (blocks_here + 2 + owners_mine * capacity + ranking_mine).astype(jnp.int32)
    slot_ids = jnp.arange(slot_total)
    requester = slot_ids // capacity
    position = slot_ids % capacity
    matches = (owners[requester] == myself) & (ranking[requester] == position[:, None])
    source = jnp.sum(jnp.where(matches, local_slot[requester], 0), axis=1)

    up = [(i, (i + 1) % cycle_size) for i in range(cycle_size)]
    down = [(j, i) for i, j in up]
    pair = jnp.concatenate([keys, values], axis=1)
    before = lax.ppermute(pair[tok_rows - BLOCK :], "seq", up)
    after = lax.ppermute(pair[:BLOCK], "seq", down)
    outgoing = jnp.take(pair.reshape(blocks_here, BLOCK, 2 * width), source, axis=0)
    far = lax.all_to_all(outgoing, "seq", split_axis=0, concat_axis=0, tiled=True)
    others = [before, after, far.reshape(slot_total * BLOCK, 2 * width)]
    key_parts = [part[:, :width] for part in others]
    value_parts = [part[:, width:] for part in others]

    here = jnp.arange(blocks_here, dtype=jnp.int32)[:, None]
    ahead = jnp.where(here == 0, blocks_here, here - 1)
    behind = jnp.where(here == blocks_here - 1, blocks_here + 1, here + 1)
    table = jnp.concatenate(
        [
            ahead,
            here,
            behind,
            jnp.broadcast_to(far_place[None, rand_total:], (blocks_here, GLOB)),
            far_place[:rand_total].reshape(blocks_here, RAND),
        ],
        axis=1,
    )
    landing = (source[:, None] == jnp.arange(blocks_here)[None, :]).astype(jnp.bfloat16)

    def send(grads, earlier):
        own, grad_before, grad_after, grad_far = grads
        last_rim = lax.ppermute(grad_before, "seq", down)
        first_rim = lax.ppermute(grad_after, "seq", up)
        returned = lax.all_to_all(
            grad_far.reshape(slot_total, BLOCK, width),
            "seq", split_axis=0, concat_axis=0, tiled=True,
        )
        return [own, last_rim, first_rim, returned]

    def total(grads):
        own, last_rim, first_rim, returned = grads
        landed = jnp.einsum("sq,sbx->qbx", landing, returned, preferred_element_type=jnp.float32)
        sums = own.reshape(blocks_here, BLOCK, width) + landed
        sums = sums.at[blocks_here - 1].add(last_rim.astype(jnp.float32))
        sums = sums.at[0].add(first_rim.astype(jnp.float32))
        return sums.reshape(tok_rows, width).astype(jnp.bfloat16)

    table, *staged, keys, values = stage(
        given_places, (table,), queries, out_grad, keys, values
    )
    out, query_grad, dk, dv = attend(
        table, staged, [keys, *key_parts], [values, *value_parts], send
    )
    return out, query_grad, total(dk), total(dv)


def local(queries, keys, values, out_grad, rand_blocks, global_blocks):
    cycle_size = lax.axis_size("seq")
    blocks_here = queries.shape[0] // BLOCK
    capacity = (RAND * blocks_here + GLOB + cycle_size - 1) // cycle_size
    dense = capacity >= blocks_here and cycle_size == 4
    plan = dense_local if dense else sparse_local
    return plan(queries, keys, values, out_grad, rand_blocks, global_blocks)


def solution(mesh):
    rows = P(("dp", "seq"), None)
    return jax.shard_map(
        local,
        mesh=mesh,
        in_specs=(rows, rows, rows, rows, P("dp", None), P("dp")),
        out_specs=(rows, rows, rows, rows),
        check_vma=False,
    )
```

```python
import functools

import jax
import jax.numpy as jnp
from jax import lax
from jax.experimental import pallas as pl
from jax.experimental.pallas import tpu as pltpu
from jax.sharding import PartitionSpec as P

KVH = 2
HD = 128
BLOCK = 64
GLOB = 2
RAND = 3
GROUP = 4
ENTRIES = 3 + GLOB + RAND
LOG2E = 1.4426950408889634
SCALE = HD ** (-0.5)


NN = (((1,), (0,)), ((), ()))
TN = (((0,), (0,)), ((), ()))
dot = functools.partial(lax.dot_general, preferred_element_type=jnp.float32)

KEYS = ENTRIES * BLOCK
CHUNK = 128
FACTOR = SCALE * LOG2E
ROWS = GROUP * BLOCK


def units(blocks_here):
    return [(b, h, b * KVH + h) for b in range(blocks_here) for h in range(KVH)]


def given_places(lists, blocks_here, b):
    return [lists[0][b, e] for e in range(ENTRIES)]


def dense_offsets(cycle_size, position):
    odd = position & 1
    offsets = list(range(cycle_size))
    offsets[1], offsets[2] = 1 + odd, 2 - odd
    return offsets


def dense_places(cycle_size, lists, blocks_here, b):
    rand_ref, glob_ref = lists
    me = lax.axis_index("seq").astype(jnp.int32)
    odd = lax.axis_index("dp").astype(jnp.int32) & 1

    def place(owner, local):
        offset = owner ^ me
        swapped = (odd == 1) & ((offset == 1) | (offset == 2))
        return jnp.where(swapped, 3 - offset, offset) * blocks_here + local

    def far_place(block):
        return place(lax.div(block, blocks_here), lax.rem(block, blocks_here))

    window = [b - 1, b, b + 1]
    if b == 0:
        window[0] = place(lax.rem(me + cycle_size - 1, cycle_size), blocks_here - 1)
    if b == blocks_here - 1:
        window[2] = place(lax.rem(me + 1, cycle_size), 0)
    far = [glob_ref[i] for i in range(GLOB)] + [rand_ref[i, me * blocks_here + b] for i in range(RAND)]
    return window + [far_place(block) for block in far]


def spans(table, b):
    result = []
    for e in range(ENTRIES):
        near = b + e - 1
        if e < 3 and 0 <= near < table.shape[0]:
            result.append(pl.ds(near * BLOCK, BLOCK))
        else:
            result.append(pl.ds(pl.multiple_of(table[b, e] * BLOCK, BLOCK), BLOCK))
    return result


def picked(pool, places, h):
    return jnp.concatenate([pool[place, h * HD : (h + 1) * HD] for place in places], axis=0)


def unstack(ref, b, h, value):
    for j in range(GROUP):
        c = (h * GROUP + j) * HD
        ref[b * BLOCK : (b + 1) * BLOCK, c : c + HD] = value[j * BLOCK : (j + 1) * BLOCK]


def add_terms(pool, places, h, terms):
    for e, place in enumerate(places):
        pool[place, h * HD : (h + 1) * HD] += terms[e * BLOCK : (e + 1) * BLOCK]


def gather_pool(pool, parts):
    start = 0
    for part in parts:
        pool[start : start + part.shape[0]] = part[...]
        start += part.shape[0]


def split_pool(outs, pool, factor):
    start = 0
    for out in outs:
        total = pool[start : start + out.shape[0]]
        out[...] = (total if factor is None else total * factor).astype(out.dtype)
        start += out.shape[0]


def stage_kernel(locate, count, *refs):
    sources, refs = refs[: count + 4], refs[count + 4 :]
    table, q_rows, g_rows, q_cols, g_cols, k_ref, v_ref, *refs = refs
    lists = refs[:count]
    q_ref, g_ref, sem = refs[count:]
    targets = [*lists, q_ref, g_ref, k_ref, v_ref]
    copies = [
        pltpu.make_async_copy(source, target, sem.at[i])
        for i, (source, target) in enumerate(zip(sources, targets))
    ]
    for copy in copies:
        copy.start()
    for copy in copies[: count + 2]:
        copy.wait()
    for b in range(table.shape[0]):
        for e, place in enumerate(locate(lists, table.shape[0], b)):
            table[b, e] = jnp.int32(place)
    for ref, rows, cols in ((q_ref, q_rows, q_cols), (g_ref, g_rows, g_cols)):
        for b, h, u in units(table.shape[0]):
            heads = [(h * GROUP + j) * HD for j in range(GROUP)]
            unit = jnp.concatenate(
                [ref[b * BLOCK : (b + 1) * BLOCK, c : c + HD] for c in heads], axis=0
            )
            rows[u * ROWS : (u + 1) * ROWS] = unit
            cols[u * HD : (u + 1) * HD] = unit.T
    for copy in copies[count + 2 :]:
        copy.wait()


def probs_kernel(count, table, q_cols, g_rows, *refs):
    parts = refs[:count][::-1]
    probs_ref, k_pool, *dv_refs, dv_pool = refs[count:]
    gather_pool(k_pool, parts)
    dv_pool[...] = jnp.zeros_like(dv_pool)
    for b, h, u in units(table.shape[0]):
        places = spans(table, b)
        scores = dot(picked(k_pool, places, h), q_cols[u * HD : (u + 1) * HD], NN)
        chunks = [scores[i : i + CHUNK] for i in range(0, KEYS, CHUNK)]
        peaks = [jnp.max(chunk, axis=0, keepdims=True) for chunk in chunks]
        expos = [jnp.exp2((chunk - peak) * FACTOR) for chunk, peak in zip(chunks, peaks)]
        peak = functools.reduce(jnp.maximum, peaks)
        scales = [jnp.exp2((own - peak) * FACTOR) for own in peaks]
        norm = 1.0 / sum(jnp.sum(e, axis=0, keepdims=True) * r for e, r in zip(expos, scales))
        probs = [(e * (r * norm)).astype(jnp.bfloat16) for e, r in zip(expos, scales)]
        probs_b = jnp.concatenate(probs, axis=0)
        probs_ref[u * KEYS : (u + 1) * KEYS] = probs_b
        add_terms(dv_pool, places, h, dot(probs_b, g_rows[u * ROWS : (u + 1) * ROWS], NN))
    split_pool(dv_refs, dv_pool, None)


def dscores_kernel(count, table, q_rows, g_cols, probs_ref, *refs):
    parts = refs[:count][::-1]
    ds_ref, v_pool, *dk_refs, dk_pool = refs[count:]
    gather_pool(v_pool, parts)
    dk_pool[...] = jnp.zeros_like(dk_pool)
    for b, h, u in units(table.shape[0]):
        places = spans(table, b)
        probs = probs_ref[u * KEYS : (u + 1) * KEYS].astype(jnp.float32)
        dprobs = dot(picked(v_pool, places, h), g_cols[u * HD : (u + 1) * HD], NN)
        delta = jnp.sum(probs * dprobs, axis=0, keepdims=True)
        dscores = (probs * (dprobs - delta)).astype(jnp.bfloat16)
        ds_ref[u * KEYS : (u + 1) * KEYS] = dscores
        add_terms(dk_pool, places, h, dot(dscores, q_rows[u * ROWS : (u + 1) * ROWS], NN))
    split_pool(dk_refs, dk_pool, SCALE)


def rows_kernel(table, probs_ref, ds_ref, k_pool, v_pool, out_any, qgrad_any, out_ref, qgrad_ref, sem):
    copies = []
    for b in range(table.shape[0]):
        places = spans(table, b)
        for h in range(KVH):
            span = slice((b * KVH + h) * KEYS, (b * KVH + h + 1) * KEYS)
            attended = dot(probs_ref[span], picked(v_pool, places, h), TN)
            unstack(out_ref, b, h, attended.astype(jnp.bfloat16))
            qgrad = dot(ds_ref[span], picked(k_pool, places, h), TN) * SCALE
            unstack(qgrad_ref, b, h, qgrad.astype(jnp.bfloat16))
        rows = pl.ds(b * BLOCK, BLOCK)
        for ref, target in ((out_ref, out_any), (qgrad_ref, qgrad_any)):
            copies.append(pltpu.make_async_copy(ref.at[rows], target.at[rows], sem.at[len(copies)]))
            copies[-1].start()
    for copy in copies:
        copy.wait()


SMEM = pl.BlockSpec(memory_space=pltpu.SMEM)
HBM = pl.BlockSpec(memory_space=pltpu.HBM)
VMEM = pl.BlockSpec(memory_space=pltpu.VMEM)


def run_kernel(kernel, operands, in_specs, results, scratch, products, out_spec=VMEM):
    flops = products * 2 * 4 * KVH * ROWS * KEYS * HD
    return pl.pallas_call(
        kernel,
        out_shape=[
            result if hasattr(result, "memory_space") else jax.ShapeDtypeStruct(*result)
            for result in results
        ],
        in_specs=in_specs + [VMEM] * (len(operands) - len(in_specs)),
        out_specs=[SMEM if hasattr(result, "memory_space") else out_spec for result in results],
        scratch_shapes=scratch,
        compiler_params=pltpu.CompilerParams(vmem_limit_bytes=32 * 2**20),
        cost_estimate=pl.CostEstimate(
            flops=flops, bytes_accessed=products * 2**20, transcendentals=0
        ),
    )(*operands)


def stage(locate, lists, queries, out_grad, keys, values):
    blocks_here = queries.shape[0] // BLOCK
    half = jnp.bfloat16
    rows = ((blocks_here * KVH * ROWS, HD), half)
    cols = ((blocks_here * KVH * HD, ROWS), half)
    narrow, wide = (keys.shape, half), (queries.shape, half)
    mine = (*lists, queries, out_grad, keys, values)
    return run_kernel(
        functools.partial(stage_kernel, locate, len(lists)),
        [pltpu.with_memory_space_constraint(array, pltpu.HBM) for array in mine],
        [HBM] * len(mine),
        [pltpu.SMEM((blocks_here, ENTRIES), jnp.int32), rows, rows, cols, cols, narrow, narrow],
        [
            *[pltpu.SMEM(array.shape, array.dtype) for array in lists],
            pltpu.VMEM(*wide), pltpu.VMEM(*wide),
            pltpu.SemaphoreType.DMA((len(mine),)),
        ],
        1,
    )


def attend(table, staged, key_parts, value_parts, send):
    q_rows, g_rows, q_cols, g_cols = staged
    tok_rows, width = key_parts[0].shape
    half, full = jnp.bfloat16, jnp.float32
    wide = ((tok_rows, GROUP * width), half)
    count = len(key_parts)
    pool_rows = sum(part.shape[0] for part in key_parts)
    held = ((table.shape[0] * KVH * KEYS, ROWS), half)
    sums = [(part.shape, half if i else full) for i, part in enumerate(key_parts)]
    scratch = [pltpu.VMEM((pool_rows, width), full)]
    pool = ((pool_rows, width), half)
    probs, k_pool, *dv = run_kernel(
        functools.partial(probs_kernel, count),
        (table, q_cols, g_rows, *key_parts[::-1]),
        [SMEM], [held, pool, *sums], scratch, 2,
    )
    dv = send(dv, None)
    dscores, v_pool, *dk = run_kernel(
        functools.partial(dscores_kernel, count),
        (table, q_rows, g_cols, probs, *value_parts[::-1]),
        [SMEM], [held, pool, *sums], scratch, 2,
    )
    dk = send(dk, dv)
    dv[1], table = lax.optimization_barrier((dv[1], table))
    out, query_grad = run_kernel(
        rows_kernel, (table, probs, dscores, k_pool, v_pool), [SMEM], [wide, wide],
        [pltpu.VMEM(*wide)] * 2 + [pltpu.SemaphoreType.DMA((2 * table.shape[0],))], 2, HBM,
    )
    dv[2:], dk[-1], query_grad = lax.optimization_barrier((dv[2:], dk[-1], query_grad))
    return out, query_grad, dk, dv


def dense_local(queries, keys, values, out_grad, rand_blocks, global_blocks):
    cycle_size = lax.axis_size("seq")
    positions = lax.axis_size("dp")

    def swap(array, part):
        pairs = []
        for position in range(positions):
            offset = dense_offsets(cycle_size, position)[part]
            pairs += [(i * positions + position, (i ^ offset) * positions + position) for i in range(cycle_size)]
        return lax.ppermute(array, ("seq", "dp"), pairs)

    def send(grads, earlier):
        sent = [grads[0]] + [None] * (cycle_size - 1)
        sent[-1] = swap(grads[-1], cycle_size - 1)
        near = grads[1:-1]
        if earlier is not None:
            near, earlier[1] = lax.optimization_barrier((near, earlier[1]))
        for part in range(1, cycle_size - 1):
            sent[part] = swap(near[part - 1], part)
        return sent

    def total(grads):
        return sum(grad.astype(jnp.float32) for grad in grads).astype(jnp.bfloat16)

    parts = range(1, cycle_size)
    key_parts = [swap(keys, part) for part in parts]
    table, *staged, keys, values = stage(
        functools.partial(dense_places, cycle_size), (rand_blocks.T, global_blocks),
        queries, out_grad, keys, values,
    )
    value_parts = [swap(values, part) for part in parts]
    out, query_grad, dk, dv = attend(
        table, staged, [keys, *key_parts], [values, *value_parts], send
    )
    return out, query_grad, total(dk), total(dv)


def sparse_local(queries, keys, values, out_grad, rand_blocks, global_blocks):
    cycle_size = lax.axis_size("seq")
    myself = lax.axis_index("seq").astype(jnp.int32)
    tok_rows, width = keys.shape
    blocks_here = tok_rows // BLOCK
    rand_total = RAND * blocks_here
    capacity = (rand_total + GLOB + cycle_size - 1) // cycle_size
    slot_total = cycle_size * capacity
    listed = jnp.concatenate(
        [
            rand_blocks.reshape(cycle_size, rand_total),
            jnp.broadcast_to(global_blocks[None, :], (cycle_size, GLOB)),
        ],
        axis=1,
    )
    entries = listed.shape[1]
    owners = listed // blocks_here
    local_slot = listed % blocks_here
    earlier = jnp.arange(entries)[None, :] < jnp.arange(entries)[:, None]
    same_owner = owners[:, :, None] == owners[:, None, :]
    ranking = jnp.sum(same_owner & earlier[None], axis=2)
    owners_mine = lax.dynamic_index_in_dim(owners, myself, 0, keepdims=False)
    ranking_mine = lax.dynamic_index_in_dim(ranking, myself, 0, keepdims=False)
    far_place = (blocks_here + 2 + owners_mine * capacity + ranking_mine).astype(jnp.int32)
    slot_ids = jnp.arange(slot_total)
    requester = slot_ids // capacity
    position = slot_ids % capacity
    matches = (owners[requester] == myself) & (ranking[requester] == position[:, None])
    source = jnp.sum(jnp.where(matches, local_slot[requester], 0), axis=1)

    up = [(i, (i + 1) % cycle_size) for i in range(cycle_size)]
    down = [(j, i) for i, j in up]
    pair = jnp.concatenate([keys, values], axis=1)
    before = lax.ppermute(pair[tok_rows - BLOCK :], "seq", up)
    after = lax.ppermute(pair[:BLOCK], "seq", down)
    outgoing = jnp.take(pair.reshape(blocks_here, BLOCK, 2 * width), source, axis=0)
    far = lax.all_to_all(outgoing, "seq", split_axis=0, concat_axis=0, tiled=True)
    others = [before, after, far.reshape(slot_total * BLOCK, 2 * width)]
    key_parts = [part[:, :width] for part in others]
    value_parts = [part[:, width:] for part in others]

    here = jnp.arange(blocks_here, dtype=jnp.int32)[:, None]
    ahead = jnp.where(here == 0, blocks_here, here - 1)
    behind = jnp.where(here == blocks_here - 1, blocks_here + 1, here + 1)
    table = jnp.concatenate(
        [
            ahead,
            here,
            behind,
            jnp.broadcast_to(far_place[None, rand_total:], (blocks_here, GLOB)),
            far_place[:rand_total].reshape(blocks_here, RAND),
        ],
        axis=1,
    )
    landing = (source[:, None] == jnp.arange(blocks_here)[None, :]).astype(jnp.bfloat16)

    def send(grads, earlier):
        own, grad_before, grad_after, grad_far = grads
        last_rim = lax.ppermute(grad_before, "seq", down)
        first_rim = lax.ppermute(grad_after, "seq", up)
        returned = lax.all_to_all(
            grad_far.reshape(slot_total, BLOCK, width),
            "seq", split_axis=0, concat_axis=0, tiled=True,
        )
        return [own, last_rim, first_rim, returned]

    def total(grads):
        own, last_rim, first_rim, returned = grads
        landed = jnp.einsum("sq,sbx->qbx", landing, returned, preferred_element_type=jnp.float32)
        sums = own.reshape(blocks_here, BLOCK, width) + landed
        sums = sums.at[blocks_here - 1].add(last_rim.astype(jnp.float32))
        sums = sums.at[0].add(first_rim.astype(jnp.float32))
        return sums.reshape(tok_rows, width).astype(jnp.bfloat16)

    table, *staged, keys, values = stage(
        given_places, (table,), queries, out_grad, keys, values
    )
    out, query_grad, dk, dv = attend(
        table, staged, [keys, *key_parts], [values, *value_parts], send
    )
    return out, query_grad, total(dk), total(dv)


def local(queries, keys, values, out_grad, rand_blocks, global_blocks):
    cycle_size = lax.axis_size("seq")
    blocks_here = queries.shape[0] // BLOCK
    capacity = (RAND * blocks_here + GLOB + cycle_size - 1) // cycle_size
    dense = capacity >= blocks_here and cycle_size == 4
    plan = dense_local if dense else sparse_local
    return plan(queries, keys, values, out_grad, rand_blocks, global_blocks)


def solution(mesh):
    rows = P(("dp", "seq"), None)
    return jax.shard_map(
        local,
        mesh=mesh,
        in_specs=(rows, rows, rows, rows, P("dp", None), P("dp")),
        out_specs=(rows, rows, rows, rows),
        check_vma=False,
    )
```

```python
import functools

import jax
import jax.numpy as jnp
from jax import lax
from jax.experimental import pallas as pl
from jax.experimental.pallas import tpu as pltpu
from jax.sharding import PartitionSpec as P

KVH = 2
HD = 128
BLOCK = 64
GLOB = 2
RAND = 3
GROUP = 4
ENTRIES = 3 + GLOB + RAND
LOG2E = 1.4426950408889634
SCALE = HD ** (-0.5)


NN = (((1,), (0,)), ((), ()))
TN = (((0,), (0,)), ((), ()))
dot = functools.partial(lax.dot_general, preferred_element_type=jnp.float32)

KEYS = ENTRIES * BLOCK
CHUNK = 128
FACTOR = SCALE * LOG2E
ROWS = GROUP * BLOCK


def units(blocks_here):
    return [(b, h, b * KVH + h) for b in range(blocks_here) for h in range(KVH)]


def given_places(lists, blocks_here, b):
    return [lists[0][b, e] for e in range(ENTRIES)]


def dense_offsets(cycle_size, position):
    odd = position & 1
    offsets = list(range(cycle_size))
    offsets[1], offsets[2] = 1 + odd, 2 - odd
    return offsets


def dense_places(cycle_size, lists, blocks_here, b):
    rand_ref, glob_ref = lists
    me = lax.axis_index("seq").astype(jnp.int32)
    odd = lax.axis_index("dp").astype(jnp.int32) & 1

    def place(owner, local):
        offset = owner ^ me
        swapped = (odd == 1) & ((offset == 1) | (offset == 2))
        return jnp.where(swapped, 3 - offset, offset) * blocks_here + local

    def far_place(block):
        return place(lax.div(block, blocks_here), lax.rem(block, blocks_here))

    window = [b - 1, b, b + 1]
    if b == 0:
        window[0] = place(lax.rem(me + cycle_size - 1, cycle_size), blocks_here - 1)
    if b == blocks_here - 1:
        window[2] = place(lax.rem(me + 1, cycle_size), 0)
    far = [glob_ref[i] for i in range(GLOB)] + [rand_ref[i, me * blocks_here + b] for i in range(RAND)]
    return window + [far_place(block) for block in far]


def spans(table, b):
    result = []
    for e in range(ENTRIES):
        near = b + e - 1
        if e < 3 and 0 <= near < table.shape[0]:
            result.append(pl.ds(near * BLOCK, BLOCK))
        else:
            result.append(pl.ds(pl.multiple_of(table[b, e] * BLOCK, BLOCK), BLOCK))
    return result


def picked(pool, places, h):
    return jnp.concatenate([pool[place, h * HD : (h + 1) * HD] for place in places], axis=0)


def unstack(ref, b, h, value):
    for j in range(GROUP):
        c = (h * GROUP + j) * HD
        ref[b * BLOCK : (b + 1) * BLOCK, c : c + HD] = value[j * BLOCK : (j + 1) * BLOCK]


def add_terms(pool, places, h, terms):
    for e, place in enumerate(places):
        pool[place, h * HD : (h + 1) * HD] += terms[e * BLOCK : (e + 1) * BLOCK]


def gather_pool(pool, parts):
    start = 0
    for part in parts:
        pool[start : start + part.shape[0]] = part[...]
        start += part.shape[0]


def split_pool(outs, pool, factor):
    start = 0
    for out in outs:
        total = pool[start : start + out.shape[0]]
        out[...] = (total if factor is None else total * factor).astype(out.dtype)
        start += out.shape[0]


def stage_kernel(locate, count, *refs):
    sources, refs = refs[: count + 4], refs[count + 4 :]
    table, q_rows, g_rows, q_cols, g_cols, k_ref, v_ref, *refs = refs
    lists = refs[:count]
    q_ref, g_ref, sem = refs[count:]
    targets = [*lists, q_ref, g_ref, k_ref, v_ref]
    copies = [
        pltpu.make_async_copy(source, target, sem.at[i])
        for i, (source, target) in enumerate(zip(sources, targets))
    ]
    for copy in copies:
        copy.start()
    for copy in copies[: count + 2]:
        copy.wait()
    for b in range(table.shape[0]):
        for e, place in enumerate(locate(lists, table.shape[0], b)):
            table[b, e] = jnp.int32(place)
    for ref, rows, cols in ((q_ref, q_rows, q_cols), (g_ref, g_rows, g_cols)):
        for b, h, u in units(table.shape[0]):
            heads = [(h * GROUP + j) * HD for j in range(GROUP)]
            unit = jnp.concatenate(
                [ref[b * BLOCK : (b + 1) * BLOCK, c : c + HD] for c in heads], axis=0
            )
            rows[u * ROWS : (u + 1) * ROWS] = unit
            cols[u * HD : (u + 1) * HD] = unit.T
    for copy in copies[count + 2 :]:
        copy.wait()


def probs_kernel(count, table, q_cols, g_rows, *refs):
    parts = refs[:count][::-1]
    probs_ref, k_pool, *dv_refs, dv_pool = refs[count:]
    gather_pool(k_pool, parts)
    dv_pool[...] = jnp.zeros_like(dv_pool)
    for b, h, u in units(table.shape[0]):
        places = spans(table, b)
        scores = dot(picked(k_pool, places, h), q_cols[u * HD : (u + 1) * HD], NN)
        chunks = [scores[i : i + CHUNK] for i in range(0, KEYS, CHUNK)]
        peaks = [jnp.max(chunk, axis=0, keepdims=True) for chunk in chunks]
        expos = [jnp.exp2((chunk - peak) * FACTOR) for chunk, peak in zip(chunks, peaks)]
        peak = functools.reduce(jnp.maximum, peaks)
        scales = [jnp.exp2((own - peak) * FACTOR) for own in peaks]
        norm = 1.0 / sum(jnp.sum(e, axis=0, keepdims=True) * r for e, r in zip(expos, scales))
        probs = [(e * (r * norm)).astype(jnp.bfloat16) for e, r in zip(expos, scales)]
        probs_b = jnp.concatenate(probs, axis=0)
        probs_ref[u * KEYS : (u + 1) * KEYS] = probs_b
        add_terms(dv_pool, places, h, dot(probs_b, g_rows[u * ROWS : (u + 1) * ROWS], NN))
    split_pool(dv_refs, dv_pool, None)


def dscores_kernel(count, table, q_rows, g_cols, probs_ref, *refs):
    parts = refs[:count][::-1]
    ds_ref, v_pool, *dk_refs, dk_pool = refs[count:]
    gather_pool(v_pool, parts)
    dk_pool[...] = jnp.zeros_like(dk_pool)
    for b, h, u in units(table.shape[0]):
        places = spans(table, b)
        probs = probs_ref[u * KEYS : (u + 1) * KEYS].astype(jnp.float32)
        dprobs = dot(picked(v_pool, places, h), g_cols[u * HD : (u + 1) * HD], NN)
        delta = jnp.sum(probs * dprobs, axis=0, keepdims=True)
        dscores = (probs * (dprobs - delta)).astype(jnp.bfloat16)
        ds_ref[u * KEYS : (u + 1) * KEYS] = dscores
        add_terms(dk_pool, places, h, dot(dscores, q_rows[u * ROWS : (u + 1) * ROWS], NN))
    split_pool(dk_refs, dk_pool, SCALE)


def rows_kernel(table, probs_ref, ds_ref, k_pool, v_pool, out_any, qgrad_any, out_ref, qgrad_ref, sem):
    copies = []
    for b in range(table.shape[0]):
        places = spans(table, b)
        for h in range(KVH):
            span = slice((b * KVH + h) * KEYS, (b * KVH + h + 1) * KEYS)
            attended = dot(probs_ref[span], picked(v_pool, places, h), TN)
            unstack(out_ref, b, h, attended.astype(jnp.bfloat16))
            qgrad = dot(ds_ref[span], picked(k_pool, places, h), TN) * SCALE
            unstack(qgrad_ref, b, h, qgrad.astype(jnp.bfloat16))
        rows = pl.ds(b * BLOCK, BLOCK)
        for ref, target in ((out_ref, out_any), (qgrad_ref, qgrad_any)):
            copies.append(pltpu.make_async_copy(ref.at[rows], target.at[rows], sem.at[len(copies)]))
            copies[-1].start()
    for copy in copies:
        copy.wait()


SMEM = pl.BlockSpec(memory_space=pltpu.SMEM)
HBM = pl.BlockSpec(memory_space=pltpu.HBM)
VMEM = pl.BlockSpec(memory_space=pltpu.VMEM)


def run_kernel(kernel, operands, in_specs, results, scratch, products, out_spec=VMEM):
    flops = products * 2 * 4 * KVH * ROWS * KEYS * HD
    return pl.pallas_call(
        kernel,
        out_shape=[
            result if hasattr(result, "memory_space") else jax.ShapeDtypeStruct(*result)
            for result in results
        ],
        in_specs=in_specs + [VMEM] * (len(operands) - len(in_specs)),
        out_specs=[SMEM if hasattr(result, "memory_space") else out_spec for result in results],
        scratch_shapes=scratch,
        compiler_params=pltpu.CompilerParams(vmem_limit_bytes=32 * 2**20),
        cost_estimate=pl.CostEstimate(
            flops=flops, bytes_accessed=products * 2**20, transcendentals=0
        ),
    )(*operands)


def stage(locate, lists, queries, out_grad, keys, values):
    blocks_here = queries.shape[0] // BLOCK
    half = jnp.bfloat16
    rows = ((blocks_here * KVH * ROWS, HD), half)
    cols = ((blocks_here * KVH * HD, ROWS), half)
    narrow, wide = (keys.shape, half), (queries.shape, half)
    mine = (*lists, queries, out_grad, keys, values)
    return run_kernel(
        functools.partial(stage_kernel, locate, len(lists)),
        [pltpu.with_memory_space_constraint(array, pltpu.HBM) for array in mine],
        [HBM] * len(mine),
        [pltpu.SMEM((blocks_here, ENTRIES), jnp.int32), rows, rows, cols, cols, narrow, narrow],
        [
            *[pltpu.SMEM(array.shape, array.dtype) for array in lists],
            pltpu.VMEM(*wide), pltpu.VMEM(*wide),
            pltpu.SemaphoreType.DMA((len(mine),)),
        ],
        1,
    )


def attend(table, staged, key_parts, value_parts, send_dk, send_dv, relay, kept):
    q_rows, g_rows, q_cols, g_cols = staged
    tok_rows, width = key_parts[0].shape
    half, full = jnp.bfloat16, jnp.float32
    wide = ((tok_rows, GROUP * width), half)
    count = len(key_parts)
    pool_rows = sum(part.shape[0] for part in key_parts)
    held = ((table.shape[0] * KVH * KEYS, ROWS), half)
    dk_sums = [(part.shape, half if i else full) for i, part in enumerate(key_parts)]
    dv_sums = [(part.shape, half if i >= kept else full) for i, part in enumerate(key_parts)]
    scratch = [pltpu.VMEM((pool_rows, width), full)]
    pool = ((pool_rows, width), half)
    probs, k_pool, *dv = run_kernel(
        functools.partial(probs_kernel, count),
        (table, q_cols, g_rows, *key_parts[::-1]),
        [SMEM], [held, pool, *dv_sums], scratch, 2,
    )
    dv = send_dv(dv)
    dscores, v_pool, *dk = run_kernel(
        functools.partial(dscores_kernel, count),
        (table, q_rows, g_cols, probs, *value_parts[::-1]),
        [SMEM], [held, pool, *dk_sums], scratch, 2,
    )
    dk = send_dk(dk, dv)
    dv[-1], table = lax.optimization_barrier((dv[-1], table))
    dv = relay(dv)
    out, query_grad = run_kernel(
        rows_kernel, (table, probs, dscores, k_pool, v_pool), [SMEM], [wide, wide],
        [pltpu.VMEM(*wide)] * 2 + [pltpu.SemaphoreType.DMA((2 * table.shape[0],))], 2, HBM,
    )
    dv[2:], dk[-1], query_grad = lax.optimization_barrier((dv[2:], dk[-1], query_grad))
    return out, query_grad, dk, dv


def dense_local(queries, keys, values, out_grad, rand_blocks, global_blocks):
    cycle_size = lax.axis_size("seq")
    positions = lax.axis_size("dp")

    def swap(array, part):
        pairs = []
        for position in range(positions):
            offset = dense_offsets(cycle_size, position)[part]
            pairs += [(i * positions + position, (i ^ offset) * positions + position) for i in range(cycle_size)]
        return lax.ppermute(array, ("seq", "dp"), pairs)

    def send_dk(grads, earlier):
        own, first, second, far = grads
        far = swap(far, 3)
        (first, second), earlier[-1] = lax.optimization_barrier(((first, second), earlier[-1]))
        return [own, swap(first, 1), swap(second, 2), far]

    def send_dv(grads):
        own, first, second, far = grads
        far = swap(far, 2)
        return [own, first, swap(second, 2), far]

    def relay(grads):
        own, first, second, far = grads
        return [own, swap((first + far.astype(jnp.float32)).astype(jnp.bfloat16), 1), second]

    def total(grads):
        return sum(grad.astype(jnp.float32) for grad in grads).astype(jnp.bfloat16)

    parts = range(1, cycle_size)
    key_parts = [swap(keys, part) for part in parts]
    table, *staged, keys, values = stage(
        functools.partial(dense_places, cycle_size), (rand_blocks.T, global_blocks),
        queries, out_grad, keys, values,
    )
    value_parts = [swap(values, part) for part in parts]
    out, query_grad, dk, dv = attend(
        table, staged, [keys, *key_parts], [values, *value_parts], send_dk, send_dv, relay, 2
    )
    return out, query_grad, total(dk), total(dv)


def sparse_local(queries, keys, values, out_grad, rand_blocks, global_blocks):
    cycle_size = lax.axis_size("seq")
    myself = lax.axis_index("seq").astype(jnp.int32)
    tok_rows, width = keys.shape
    blocks_here = tok_rows // BLOCK
    rand_total = RAND * blocks_here
    capacity = (rand_total + GLOB + cycle_size - 1) // cycle_size
    slot_total = cycle_size * capacity
    listed = jnp.concatenate(
        [
            rand_blocks.reshape(cycle_size, rand_total),
            jnp.broadcast_to(global_blocks[None, :], (cycle_size, GLOB)),
        ],
        axis=1,
    )
    entries = listed.shape[1]
    owners = listed // blocks_here
    local_slot = listed % blocks_here
    earlier = jnp.arange(entries)[None, :] < jnp.arange(entries)[:, None]
    same_owner = owners[:, :, None] == owners[:, None, :]
    ranking = jnp.sum(same_owner & earlier[None], axis=2)
    owners_mine = lax.dynamic_index_in_dim(owners, myself, 0, keepdims=False)
    ranking_mine = lax.dynamic_index_in_dim(ranking, myself, 0, keepdims=False)
    far_place = (blocks_here + 2 + owners_mine * capacity + ranking_mine).astype(jnp.int32)
    slot_ids = jnp.arange(slot_total)
    requester = slot_ids // capacity
    position = slot_ids % capacity
    matches = (owners[requester] == myself) & (ranking[requester] == position[:, None])
    source = jnp.sum(jnp.where(matches, local_slot[requester], 0), axis=1)

    up = [(i, (i + 1) % cycle_size) for i in range(cycle_size)]
    down = [(j, i) for i, j in up]
    pair = jnp.concatenate([keys, values], axis=1)
    before = lax.ppermute(pair[tok_rows - BLOCK :], "seq", up)
    after = lax.ppermute(pair[:BLOCK], "seq", down)
    outgoing = jnp.take(pair.reshape(blocks_here, BLOCK, 2 * width), source, axis=0)
    far = lax.all_to_all(outgoing, "seq", split_axis=0, concat_axis=0, tiled=True)
    others = [before, after, far.reshape(slot_total * BLOCK, 2 * width)]
    key_parts = [part[:, :width] for part in others]
    value_parts = [part[:, width:] for part in others]

    here = jnp.arange(blocks_here, dtype=jnp.int32)[:, None]
    ahead = jnp.where(here == 0, blocks_here, here - 1)
    behind = jnp.where(here == blocks_here - 1, blocks_here + 1, here + 1)
    table = jnp.concatenate(
        [
            ahead,
            here,
            behind,
            jnp.broadcast_to(far_place[None, rand_total:], (blocks_here, GLOB)),
            far_place[:rand_total].reshape(blocks_here, RAND),
        ],
        axis=1,
    )
    landing = (source[:, None] == jnp.arange(blocks_here)[None, :]).astype(jnp.bfloat16)

    def send(grads, earlier=None):
        own, grad_before, grad_after, grad_far = grads
        last_rim = lax.ppermute(grad_before, "seq", down)
        first_rim = lax.ppermute(grad_after, "seq", up)
        returned = lax.all_to_all(
            grad_far.reshape(slot_total, BLOCK, width),
            "seq", split_axis=0, concat_axis=0, tiled=True,
        )
        return [own, last_rim, first_rim, returned]

    def total(grads):
        own, last_rim, first_rim, returned = grads
        landed = jnp.einsum("sq,sbx->qbx", landing, returned, preferred_element_type=jnp.float32)
        sums = own.reshape(blocks_here, BLOCK, width) + landed
        sums = sums.at[blocks_here - 1].add(last_rim.astype(jnp.float32))
        sums = sums.at[0].add(first_rim.astype(jnp.float32))
        return sums.reshape(tok_rows, width).astype(jnp.bfloat16)

    table, *staged, keys, values = stage(
        given_places, (table,), queries, out_grad, keys, values
    )
    out, query_grad, dk, dv = attend(
        table, staged, [keys, *key_parts], [values, *value_parts], send, send, lambda dv: dv, 1
    )
    return out, query_grad, total(dk), total(dv)


def local(queries, keys, values, out_grad, rand_blocks, global_blocks):
    cycle_size = lax.axis_size("seq")
    blocks_here = queries.shape[0] // BLOCK
    capacity = (RAND * blocks_here + GLOB + cycle_size - 1) // cycle_size
    dense = capacity >= blocks_here and cycle_size == 4
    plan = dense_local if dense else sparse_local
    return plan(queries, keys, values, out_grad, rand_blocks, global_blocks)


def solution(mesh):
    rows = P(("dp", "seq"), None)
    return jax.shard_map(
        local,
        mesh=mesh,
        in_specs=(rows, rows, rows, rows, P("dp", None), P("dp")),
        out_specs=(rows, rows, rows, rows),
        check_vma=False,
    )
```

```python
import functools

import jax
import jax.numpy as jnp
from jax import lax
from jax.experimental import pallas as pl
from jax.experimental.pallas import tpu as pltpu
from jax.sharding import PartitionSpec as P

KVH = 2
HD = 128
BLOCK = 64
GLOB = 2
RAND = 3
GROUP = 4
ENTRIES = 3 + GLOB + RAND
LOG2E = 1.4426950408889634
SCALE = HD ** (-0.5)


NN = (((1,), (0,)), ((), ()))
TN = (((0,), (0,)), ((), ()))
dot = functools.partial(lax.dot_general, preferred_element_type=jnp.float32)

KEYS = ENTRIES * BLOCK
CHUNK = 128
FACTOR = SCALE * LOG2E
ROWS = GROUP * BLOCK


def units(blocks_here):
    return [(b, h, b * KVH + h) for b in range(blocks_here) for h in range(KVH)]


def given_places(lists, blocks_here, b):
    return [lists[0][b, e] for e in range(ENTRIES)]


def dense_offsets(cycle_size, position):
    odd = position & 1
    offsets = list(range(cycle_size))
    offsets[1], offsets[2] = 1 + odd, 2 - odd
    return offsets


def dense_places(cycle_size, lists, blocks_here, b):
    rand_ref, glob_ref = lists
    me = lax.axis_index("seq").astype(jnp.int32)
    odd = lax.axis_index("dp").astype(jnp.int32) & 1

    def place(owner, local):
        offset = owner ^ me
        swapped = (odd == 1) & ((offset == 1) | (offset == 2))
        return jnp.where(swapped, 3 - offset, offset) * blocks_here + local

    def far_place(block):
        return place(lax.div(block, blocks_here), lax.rem(block, blocks_here))

    window = [b - 1, b, b + 1]
    if b == 0:
        window[0] = place(lax.rem(me + cycle_size - 1, cycle_size), blocks_here - 1)
    if b == blocks_here - 1:
        window[2] = place(lax.rem(me + 1, cycle_size), 0)
    far = [glob_ref[i] for i in range(GLOB)] + [rand_ref[i, me * blocks_here + b] for i in range(RAND)]
    return window + [far_place(block) for block in far]


def spans(table, b):
    result = []
    for e in range(ENTRIES):
        near = b + e - 1
        if e < 3 and 0 <= near < table.shape[0]:
            result.append(pl.ds(near * BLOCK, BLOCK))
        else:
            result.append(pl.ds(pl.multiple_of(table[b, e] * BLOCK, BLOCK), BLOCK))
    return result


def picked(pool, places, h):
    return jnp.concatenate([pool[place, h * HD : (h + 1) * HD] for place in places], axis=0)


def unstack(ref, b, h, value):
    for j in range(GROUP):
        c = (h * GROUP + j) * HD
        ref[b * BLOCK : (b + 1) * BLOCK, c : c + HD] = value[j * BLOCK : (j + 1) * BLOCK]


def add_terms(pool, places, h, terms):
    for e, place in enumerate(places):
        pool[place, h * HD : (h + 1) * HD] += terms[e * BLOCK : (e + 1) * BLOCK]


def gather_pool(pool, parts):
    start = 0
    for part in parts:
        pool[start : start + part.shape[0]] = part[...]
        start += part.shape[0]


def split_pool(outs, pool, factor):
    start = 0
    for out in outs:
        total = pool[start : start + out.shape[0]]
        out[...] = (total if factor is None else total * factor).astype(out.dtype)
        start += out.shape[0]


def stage_kernel(locate, count, *refs):
    sources, refs = refs[: count + 4], refs[count + 4 :]
    table, q_rows, g_rows, q_cols, g_cols, k_ref, v_ref, *refs = refs
    lists = refs[:count]
    q_ref, g_ref, sem = refs[count:]
    targets = [*lists, q_ref, g_ref, k_ref, v_ref]
    copies = [
        pltpu.make_async_copy(source, target, sem.at[i])
        for i, (source, target) in enumerate(zip(sources, targets))
    ]
    for copy in copies:
        copy.start()
    for copy in copies[: count + 2]:
        copy.wait()
    for b in range(table.shape[0]):
        for e, place in enumerate(locate(lists, table.shape[0], b)):
            table[b, e] = jnp.int32(place)
    for ref, rows, cols in ((q_ref, q_rows, q_cols), (g_ref, g_rows, g_cols)):
        for b, h, u in units(table.shape[0]):
            heads = [(h * GROUP + j) * HD for j in range(GROUP)]
            unit = jnp.concatenate(
                [ref[b * BLOCK : (b + 1) * BLOCK, c : c + HD] for c in heads], axis=0
            )
            rows[u * ROWS : (u + 1) * ROWS] = unit
            cols[u * HD : (u + 1) * HD] = unit.T
    for copy in copies[count + 2 :]:
        copy.wait()


def probs_kernel(count, table, q_cols, g_rows, *refs):
    parts = refs[:count][::-1]
    probs_ref, k_pool, *dv_refs, dv_pool = refs[count:]
    gather_pool(k_pool, parts)
    dv_pool[...] = jnp.zeros_like(dv_pool)
    for b, h, u in units(table.shape[0]):
        places = spans(table, b)
        scores = dot(picked(k_pool, places, h), q_cols[u * HD : (u + 1) * HD], NN)
        chunks = [scores[i : i + CHUNK] for i in range(0, KEYS, CHUNK)]
        peaks = [jnp.max(chunk, axis=0, keepdims=True) for chunk in chunks]
        expos = [jnp.exp2((chunk - peak) * FACTOR) for chunk, peak in zip(chunks, peaks)]
        peak = functools.reduce(jnp.maximum, peaks)
        scales = [jnp.exp2((own - peak) * FACTOR) for own in peaks]
        norm = 1.0 / sum(jnp.sum(e, axis=0, keepdims=True) * r for e, r in zip(expos, scales))
        probs = [(e * (r * norm)).astype(jnp.bfloat16) for e, r in zip(expos, scales)]
        probs_b = jnp.concatenate(probs, axis=0)
        probs_ref[u * KEYS : (u + 1) * KEYS] = probs_b
        add_terms(dv_pool, places, h, dot(probs_b, g_rows[u * ROWS : (u + 1) * ROWS], NN))
    split_pool(dv_refs, dv_pool, None)


def dscores_kernel(count, table, q_rows, g_cols, probs_ref, *refs):
    parts = refs[:count]
    ds_ref, v_pool, *dk_refs, dk_pool = refs[count:]
    gather_pool(v_pool, parts)
    dk_pool[...] = jnp.zeros_like(dk_pool)
    for b, h, u in units(table.shape[0]):
        places = spans(table, b)
        probs = probs_ref[u * KEYS : (u + 1) * KEYS].astype(jnp.float32)
        dprobs = dot(picked(v_pool, places, h), g_cols[u * HD : (u + 1) * HD], NN)
        delta = jnp.sum(probs * dprobs, axis=0, keepdims=True)
        dscores = (probs * (dprobs - delta)).astype(jnp.bfloat16)
        ds_ref[u * KEYS : (u + 1) * KEYS] = dscores
        add_terms(dk_pool, places, h, dot(dscores, q_rows[u * ROWS : (u + 1) * ROWS], NN))
    split_pool(dk_refs, dk_pool, SCALE)


def rows_kernel(table, probs_ref, ds_ref, k_pool, v_pool, out_any, qgrad_any, out_ref, qgrad_ref, sem):
    copies = []
    for b in range(table.shape[0]):
        places = spans(table, b)
        for h in range(KVH):
            span = slice((b * KVH + h) * KEYS, (b * KVH + h + 1) * KEYS)
            attended = dot(probs_ref[span], picked(v_pool, places, h), TN)
            unstack(out_ref, b, h, attended.astype(jnp.bfloat16))
            qgrad = dot(ds_ref[span], picked(k_pool, places, h), TN) * SCALE
            unstack(qgrad_ref, b, h, qgrad.astype(jnp.bfloat16))
        rows = pl.ds(b * BLOCK, BLOCK)
        for ref, target in ((out_ref, out_any), (qgrad_ref, qgrad_any)):
            copies.append(pltpu.make_async_copy(ref.at[rows], target.at[rows], sem.at[len(copies)]))
            copies[-1].start()
    for copy in copies:
        copy.wait()


SMEM = pl.BlockSpec(memory_space=pltpu.SMEM)
HBM = pl.BlockSpec(memory_space=pltpu.HBM)
VMEM = pl.BlockSpec(memory_space=pltpu.VMEM)


def run_kernel(kernel, operands, in_specs, results, scratch, products, out_spec=VMEM):
    flops = products * 2 * 4 * KVH * ROWS * KEYS * HD
    return pl.pallas_call(
        kernel,
        out_shape=[
            result if hasattr(result, "memory_space") else jax.ShapeDtypeStruct(*result)
            for result in results
        ],
        in_specs=in_specs + [VMEM] * (len(operands) - len(in_specs)),
        out_specs=[SMEM if hasattr(result, "memory_space") else out_spec for result in results],
        scratch_shapes=scratch,
        compiler_params=pltpu.CompilerParams(vmem_limit_bytes=32 * 2**20),
        cost_estimate=pl.CostEstimate(
            flops=flops, bytes_accessed=products * 2**20, transcendentals=0
        ),
    )(*operands)


def stage(locate, lists, queries, out_grad, keys, values):
    blocks_here = queries.shape[0] // BLOCK
    half = jnp.bfloat16
    rows = ((blocks_here * KVH * ROWS, HD), half)
    cols = ((blocks_here * KVH * HD, ROWS), half)
    narrow, wide = (keys.shape, half), (queries.shape, half)
    mine = (*lists, queries, out_grad, keys, values)
    return run_kernel(
        functools.partial(stage_kernel, locate, len(lists)),
        [pltpu.with_memory_space_constraint(array, pltpu.HBM) for array in mine],
        [HBM] * len(mine),
        [pltpu.SMEM((blocks_here, ENTRIES), jnp.int32), rows, rows, cols, cols, narrow, narrow],
        [
            *[pltpu.SMEM(array.shape, array.dtype) for array in lists],
            pltpu.VMEM(*wide), pltpu.VMEM(*wide),
            pltpu.SemaphoreType.DMA((len(mine),)),
        ],
        1,
    )


def attend(table, staged, key_parts, value_parts, send):
    q_rows, g_rows, q_cols, g_cols = staged
    tok_rows, width = key_parts[0].shape
    half, full = jnp.bfloat16, jnp.float32
    wide = ((tok_rows, GROUP * width), half)
    count = len(key_parts)
    pool_rows = sum(part.shape[0] for part in key_parts)
    held = ((table.shape[0] * KVH * KEYS, ROWS), half)
    sums = [(part.shape, half if i else full) for i, part in enumerate(key_parts)]
    scratch = [pltpu.VMEM((pool_rows, width), full)]
    pool = ((pool_rows, width), half)
    probs, k_pool, *dv = run_kernel(
        functools.partial(probs_kernel, count),
        (table, q_cols, g_rows, *key_parts[::-1]),
        [SMEM], [held, pool, *sums], scratch, 2,
    )
    dv = send(dv, None)
    dscores, v_pool, *dk = run_kernel(
        functools.partial(dscores_kernel, count),
        (table, q_rows, g_cols, probs, *value_parts),
        [SMEM], [held, pool, *sums], scratch, 2,
    )
    dk = send(dk, dv)
    dv[1], table = lax.optimization_barrier((dv[1], table))
    out, query_grad = run_kernel(
        rows_kernel, (table, probs, dscores, k_pool, v_pool), [SMEM], [wide, wide],
        [pltpu.VMEM(*wide)] * 2 + [pltpu.SemaphoreType.DMA((2 * table.shape[0],))], 2, HBM,
    )
    dv[2:], dk[-1], query_grad = lax.optimization_barrier((dv[2:], dk[-1], query_grad))
    return out, query_grad, dk, dv


def dense_local(queries, keys, values, out_grad, rand_blocks, global_blocks):
    cycle_size = lax.axis_size("seq")
    positions = lax.axis_size("dp")

    def swap(array, part):
        pairs = []
        for position in range(positions):
            offset = dense_offsets(cycle_size, position)[part]
            pairs += [(i * positions + position, (i ^ offset) * positions + position) for i in range(cycle_size)]
        return lax.ppermute(array, ("seq", "dp"), pairs)

    def send(grads, earlier):
        sent = [grads[0]] + [None] * (cycle_size - 1)
        sent[-1] = swap(grads[-1], cycle_size - 1)
        near = grads[1:-1]
        if earlier is not None:
            near, earlier[1] = lax.optimization_barrier((near, earlier[1]))
        for part in range(1, cycle_size - 1):
            sent[part] = swap(near[part - 1], part)
        return sent

    def total(grads):
        return sum(grad.astype(jnp.float32) for grad in grads).astype(jnp.bfloat16)

    parts = range(1, cycle_size)
    key_parts = [swap(keys, part) for part in parts]
    table, *staged, keys, values = stage(
        functools.partial(dense_places, cycle_size), (rand_blocks.T, global_blocks),
        queries, out_grad, keys, values,
    )
    value_parts = [swap(values, part) for part in parts]
    out, query_grad, dk, dv = attend(
        table, staged, [keys, *key_parts], [values, *value_parts], send
    )
    return out, query_grad, total(dk), total(dv)


def sparse_local(queries, keys, values, out_grad, rand_blocks, global_blocks):
    cycle_size = lax.axis_size("seq")
    myself = lax.axis_index("seq").astype(jnp.int32)
    tok_rows, width = keys.shape
    blocks_here = tok_rows // BLOCK
    rand_total = RAND * blocks_here
    capacity = (rand_total + GLOB + cycle_size - 1) // cycle_size
    slot_total = cycle_size * capacity
    listed = jnp.concatenate(
        [
            rand_blocks.reshape(cycle_size, rand_total),
            jnp.broadcast_to(global_blocks[None, :], (cycle_size, GLOB)),
        ],
        axis=1,
    )
    entries = listed.shape[1]
    owners = listed // blocks_here
    local_slot = listed % blocks_here
    earlier = jnp.arange(entries)[None, :] < jnp.arange(entries)[:, None]
    same_owner = owners[:, :, None] == owners[:, None, :]
    ranking = jnp.sum(same_owner & earlier[None], axis=2)
    owners_mine = lax.dynamic_index_in_dim(owners, myself, 0, keepdims=False)
    ranking_mine = lax.dynamic_index_in_dim(ranking, myself, 0, keepdims=False)
    far_place = (blocks_here + 2 + owners_mine * capacity + ranking_mine).astype(jnp.int32)
    slot_ids = jnp.arange(slot_total)
    requester = slot_ids // capacity
    position = slot_ids % capacity
    matches = (owners[requester] == myself) & (ranking[requester] == position[:, None])
    source = jnp.sum(jnp.where(matches, local_slot[requester], 0), axis=1)

    up = [(i, (i + 1) % cycle_size) for i in range(cycle_size)]
    down = [(j, i) for i, j in up]
    pair = jnp.concatenate([keys, values], axis=1)
    before = lax.ppermute(pair[tok_rows - BLOCK :], "seq", up)
    after = lax.ppermute(pair[:BLOCK], "seq", down)
    outgoing = jnp.take(pair.reshape(blocks_here, BLOCK, 2 * width), source, axis=0)
    far = lax.all_to_all(outgoing, "seq", split_axis=0, concat_axis=0, tiled=True)
    others = [before, after, far.reshape(slot_total * BLOCK, 2 * width)]
    key_parts = [part[:, :width] for part in others]
    value_parts = [part[:, width:] for part in others]

    here = jnp.arange(blocks_here, dtype=jnp.int32)[:, None]
    ahead = jnp.where(here == 0, blocks_here, here - 1)
    behind = jnp.where(here == blocks_here - 1, blocks_here + 1, here + 1)
    table = jnp.concatenate(
        [
            ahead,
            here,
            behind,
            jnp.broadcast_to(far_place[None, rand_total:], (blocks_here, GLOB)),
            far_place[:rand_total].reshape(blocks_here, RAND),
        ],
        axis=1,
    )
    landing = (source[:, None] == jnp.arange(blocks_here)[None, :]).astype(jnp.bfloat16)

    def send(grads, earlier):
        own, grad_before, grad_after, grad_far = grads
        last_rim = lax.ppermute(grad_before, "seq", down)
        first_rim = lax.ppermute(grad_after, "seq", up)
        returned = lax.all_to_all(
            grad_far.reshape(slot_total, BLOCK, width),
            "seq", split_axis=0, concat_axis=0, tiled=True,
        )
        return [own, last_rim, first_rim, returned]

    def total(grads):
        own, last_rim, first_rim, returned = grads
        landed = jnp.einsum("sq,sbx->qbx", landing, returned, preferred_element_type=jnp.float32)
        sums = own.reshape(blocks_here, BLOCK, width) + landed
        sums = sums.at[blocks_here - 1].add(last_rim.astype(jnp.float32))
        sums = sums.at[0].add(first_rim.astype(jnp.float32))
        return sums.reshape(tok_rows, width).astype(jnp.bfloat16)

    table, *staged, keys, values = stage(
        given_places, (table,), queries, out_grad, keys, values
    )
    out, query_grad, dk, dv = attend(
        table, staged, [keys, *key_parts], [values, *value_parts], send
    )
    return out, query_grad, total(dk), total(dv)


def local(queries, keys, values, out_grad, rand_blocks, global_blocks):
    cycle_size = lax.axis_size("seq")
    blocks_here = queries.shape[0] // BLOCK
    capacity = (RAND * blocks_here + GLOB + cycle_size - 1) // cycle_size
    dense = capacity >= blocks_here and cycle_size == 4
    plan = dense_local if dense else sparse_local
    return plan(queries, keys, values, out_grad, rand_blocks, global_blocks)


def solution(mesh):
    rows = P(("dp", "seq"), None)
    return jax.shard_map(
        local,
        mesh=mesh,
        in_specs=(rows, rows, rows, rows, P("dp", None), P("dp")),
        out_specs=(rows, rows, rows, rows),
        check_vma=False,
    )
```

```python
import functools

import jax
import jax.numpy as jnp
from jax import lax
from jax.experimental import pallas as pl
from jax.experimental.pallas import tpu as pltpu
from jax.sharding import PartitionSpec as P

KVH = 2
HD = 128
BLOCK = 64
GLOB = 2
RAND = 3
GROUP = 4
ENTRIES = 3 + GLOB + RAND
LOG2E = 1.4426950408889634
SCALE = HD ** (-0.5)


NN = (((1,), (0,)), ((), ()))
TN = (((0,), (0,)), ((), ()))
dot = functools.partial(lax.dot_general, preferred_element_type=jnp.float32)

KEYS = ENTRIES * BLOCK
CHUNK = 128
FACTOR = SCALE * LOG2E
ROWS = GROUP * BLOCK


def units(blocks_here):
    return [(b, h, b * KVH + h) for b in range(blocks_here) for h in range(KVH)]


def given_places(lists, blocks_here, b):
    return [lists[0][b, e] for e in range(ENTRIES)]


def dense_offsets(cycle_size, position):
    odd = position & 1
    offsets = list(range(cycle_size))
    offsets[1], offsets[2] = 1 + odd, 2 - odd
    return offsets


def dense_places(cycle_size, lists, blocks_here, b):
    rand_ref, glob_ref = lists
    me = lax.axis_index("seq").astype(jnp.int32)
    odd = lax.axis_index("dp").astype(jnp.int32) & 1

    def place(owner, local):
        offset = owner ^ me
        swapped = (odd == 1) & ((offset == 1) | (offset == 2))
        return jnp.where(swapped, 3 - offset, offset) * blocks_here + local

    def far_place(block):
        return place(lax.div(block, blocks_here), lax.rem(block, blocks_here))

    window = [b - 1, b, b + 1]
    if b == 0:
        window[0] = place(lax.rem(me + cycle_size - 1, cycle_size), blocks_here - 1)
    if b == blocks_here - 1:
        window[2] = place(lax.rem(me + 1, cycle_size), 0)
    far = [glob_ref[i] for i in range(GLOB)] + [rand_ref[i, me * blocks_here + b] for i in range(RAND)]
    return window + [far_place(block) for block in far]


def spans(table, b):
    result = []
    for e in range(ENTRIES):
        near = b + e - 1
        if e < 3 and 0 <= near < table.shape[0]:
            result.append(pl.ds(near * BLOCK, BLOCK))
        else:
            result.append(pl.ds(pl.multiple_of(table[b, e] * BLOCK, BLOCK), BLOCK))
    return result


def picked(pool, places, h):
    return jnp.concatenate([pool[place, h * HD : (h + 1) * HD] for place in places], axis=0)


def unstack(ref, b, h, value):
    for j in range(GROUP):
        c = (h * GROUP + j) * HD
        ref[b * BLOCK : (b + 1) * BLOCK, c : c + HD] = value[j * BLOCK : (j + 1) * BLOCK]


def add_terms(pool, places, h, terms):
    for e, place in enumerate(places):
        pool[place, h * HD : (h + 1) * HD] += terms[e * BLOCK : (e + 1) * BLOCK]


def gather_pool(pool, parts):
    start = 0
    for part in parts:
        pool[start : start + part.shape[0]] = part[...]
        start += part.shape[0]


def split_pool(outs, pool, factor):
    start = 0
    for out in outs:
        total = pool[start : start + out.shape[0]]
        out[...] = (total if factor is None else total * factor).astype(out.dtype)
        start += out.shape[0]


def stage_kernel(locate, count, *refs):
    sources, refs = refs[: count + 4], refs[count + 4 :]
    table, q_rows, g_rows, q_cols, g_cols, k_ref, v_ref, *refs = refs
    lists = refs[:count]
    q_ref, g_ref, sem = refs[count:]
    targets = [*lists, q_ref, g_ref, k_ref, v_ref]
    copies = [
        pltpu.make_async_copy(source, target, sem.at[i])
        for i, (source, target) in enumerate(zip(sources, targets))
    ]
    for copy in copies:
        copy.start()
    for copy in copies[: count + 2]:
        copy.wait()
    for b in range(table.shape[0]):
        for e, place in enumerate(locate(lists, table.shape[0], b)):
            table[b, e] = jnp.int32(place)
    for ref, rows, cols in ((q_ref, q_rows, q_cols), (g_ref, g_rows, g_cols)):
        for b, h, u in units(table.shape[0]):
            heads = [(h * GROUP + j) * HD for j in range(GROUP)]
            unit = jnp.concatenate(
                [ref[b * BLOCK : (b + 1) * BLOCK, c : c + HD] for c in heads], axis=0
            )
            rows[u * ROWS : (u + 1) * ROWS] = unit
            cols[u * HD : (u + 1) * HD] = unit.T
    for copy in copies[count + 2 :]:
        copy.wait()


def probs_kernel(count, table, q_cols, g_rows, *refs):
    parts = refs[:count][::-1]
    probs_ref, k_pool, *dv_refs, dv_pool = refs[count:]
    gather_pool(k_pool, parts)
    dv_pool[...] = jnp.zeros_like(dv_pool)
    for b, h, u in units(table.shape[0]):
        places = spans(table, b)
        scores = dot(picked(k_pool, places, h), q_cols[u * HD : (u + 1) * HD], NN)
        chunks = [scores[i : i + CHUNK] for i in range(0, KEYS, CHUNK)]
        peaks = [jnp.max(chunk, axis=0, keepdims=True) for chunk in chunks]
        expos = [jnp.exp2((chunk - peak) * FACTOR) for chunk, peak in zip(chunks, peaks)]
        peak = functools.reduce(jnp.maximum, peaks)
        scales = [jnp.exp2((own - peak) * FACTOR) for own in peaks]
        norm = 1.0 / sum(jnp.sum(e, axis=0, keepdims=True) * r for e, r in zip(expos, scales))
        probs = [(e * (r * norm)).astype(jnp.bfloat16) for e, r in zip(expos, scales)]
        probs_b = jnp.concatenate(probs, axis=0)
        probs_ref[u * KEYS : (u + 1) * KEYS] = probs_b
        add_terms(dv_pool, places, h, dot(probs_b, g_rows[u * ROWS : (u + 1) * ROWS], NN))
    split_pool(dv_refs, dv_pool, None)


def dscores_kernel(count, table, q_rows, g_cols, probs_ref, *refs):
    parts = refs[:count][::-1]
    ds_ref, v_pool, *dk_refs, dk_pool = refs[count:]
    gather_pool(v_pool, parts)
    dk_pool[...] = jnp.zeros_like(dk_pool)
    for b, h, u in units(table.shape[0]):
        places = spans(table, b)
        probs = probs_ref[u * KEYS : (u + 1) * KEYS].astype(jnp.float32)
        dprobs = dot(picked(v_pool, places, h), g_cols[u * HD : (u + 1) * HD], NN)
        delta = jnp.sum(probs * dprobs, axis=0, keepdims=True)
        dscores = (probs * (dprobs - delta)).astype(jnp.bfloat16)
        ds_ref[u * KEYS : (u + 1) * KEYS] = dscores
        add_terms(dk_pool, places, h, dot(dscores, q_rows[u * ROWS : (u + 1) * ROWS], NN))
    split_pool(dk_refs, dk_pool, SCALE)


def rows_kernel(table, probs_ref, ds_ref, k_pool, v_pool, out_any, qgrad_any, out_ref, qgrad_ref, sem):
    copies = []
    for b in range(table.shape[0]):
        places = spans(table, b)
        for h in range(KVH):
            span = slice((b * KVH + h) * KEYS, (b * KVH + h + 1) * KEYS)
            attended = dot(probs_ref[span], picked(v_pool, places, h), TN)
            unstack(out_ref, b, h, attended.astype(jnp.bfloat16))
            qgrad = dot(ds_ref[span], picked(k_pool, places, h), TN) * SCALE
            unstack(qgrad_ref, b, h, qgrad.astype(jnp.bfloat16))
        rows = pl.ds(b * BLOCK, BLOCK)
        for ref, target in ((out_ref, out_any), (qgrad_ref, qgrad_any)):
            copies.append(pltpu.make_async_copy(ref.at[rows], target.at[rows], sem.at[len(copies)]))
            copies[-1].start()
    for copy in copies:
        copy.wait()


SMEM = pl.BlockSpec(memory_space=pltpu.SMEM)
HBM = pl.BlockSpec(memory_space=pltpu.HBM)
VMEM = pl.BlockSpec(memory_space=pltpu.VMEM)


def run_kernel(kernel, operands, in_specs, results, scratch, products, out_spec=VMEM):
    flops = products * 2 * 4 * KVH * ROWS * KEYS * HD
    return pl.pallas_call(
        kernel,
        out_shape=[
            result if hasattr(result, "memory_space") else jax.ShapeDtypeStruct(*result)
            for result in results
        ],
        in_specs=in_specs + [VMEM] * (len(operands) - len(in_specs)),
        out_specs=[SMEM if hasattr(result, "memory_space") else out_spec for result in results],
        scratch_shapes=scratch,
        compiler_params=pltpu.CompilerParams(vmem_limit_bytes=32 * 2**20),
        cost_estimate=pl.CostEstimate(
            flops=flops, bytes_accessed=products * 2**20, transcendentals=0
        ),
    )(*operands)


def stage(locate, lists, queries, out_grad, keys, values):
    blocks_here = queries.shape[0] // BLOCK
    half = jnp.bfloat16
    rows = ((blocks_here * KVH * ROWS, HD), half)
    cols = ((blocks_here * KVH * HD, ROWS), half)
    narrow, wide = (keys.shape, half), (queries.shape, half)
    mine = (*lists, queries, out_grad, keys, values)
    return run_kernel(
        functools.partial(stage_kernel, locate, len(lists)),
        [pltpu.with_memory_space_constraint(array, pltpu.HBM) for array in mine],
        [HBM] * len(mine),
        [pltpu.SMEM((blocks_here, ENTRIES), jnp.int32), rows, rows, cols, cols, narrow, narrow],
        [
            *[pltpu.SMEM(array.shape, array.dtype) for array in lists],
            pltpu.VMEM(*wide), pltpu.VMEM(*wide),
            pltpu.SemaphoreType.DMA((len(mine),)),
        ],
        1,
    )


def attend(table, staged, key_parts, value_parts, send, relay=None):
    q_rows, g_rows, q_cols, g_cols = staged
    tok_rows, width = key_parts[0].shape
    half, full = jnp.bfloat16, jnp.float32
    wide = ((tok_rows, GROUP * width), half)
    count = len(key_parts)
    pool_rows = sum(part.shape[0] for part in key_parts)
    held = ((table.shape[0] * KVH * KEYS, ROWS), half)
    sums = [(part.shape, half if i else full) for i, part in enumerate(key_parts)]
    scratch = [pltpu.VMEM((pool_rows, width), full)]
    pool = ((pool_rows, width), half)
    probs, k_pool, *dv = run_kernel(
        functools.partial(probs_kernel, count),
        (table, q_cols, g_rows, *key_parts[::-1]),
        [SMEM], [held, pool, *sums], scratch, 2,
    )
    if relay is not None:
        dv[0], near = lax.optimization_barrier((dv[0], value_parts[1]))
        value_parts = [value_parts[0], near, *value_parts[2:], relay(near)]
    dv = send(dv, None)
    dscores, v_pool, *dk = run_kernel(
        functools.partial(dscores_kernel, count),
        (table, q_rows, g_cols, probs, *value_parts[::-1]),
        [SMEM], [held, pool, *sums], scratch, 2,
    )
    dk = send(dk, dv)
    dv[1], table = lax.optimization_barrier((dv[1], table))
    out, query_grad = run_kernel(
        rows_kernel, (table, probs, dscores, k_pool, v_pool), [SMEM], [wide, wide],
        [pltpu.VMEM(*wide)] * 2 + [pltpu.SemaphoreType.DMA((2 * table.shape[0],))], 2, HBM,
    )
    dv[2:], dk[-1], query_grad = lax.optimization_barrier((dv[2:], dk[-1], query_grad))
    return out, query_grad, dk, dv


def dense_local(queries, keys, values, out_grad, rand_blocks, global_blocks):
    cycle_size = lax.axis_size("seq")
    positions = lax.axis_size("dp")

    def swap(array, part):
        pairs = []
        for position in range(positions):
            offset = dense_offsets(cycle_size, position)[part]
            pairs += [(i * positions + position, (i ^ offset) * positions + position) for i in range(cycle_size)]
        return lax.ppermute(array, ("seq", "dp"), pairs)

    def send(grads, earlier):
        sent = [grads[0]] + [None] * (cycle_size - 1)
        sent[-1] = swap(grads[-1], cycle_size - 1)
        near = grads[1:-1]
        if earlier is not None:
            near, earlier[1] = lax.optimization_barrier((near, earlier[1]))
        for part in range(1, cycle_size - 1):
            sent[part] = swap(near[part - 1], part)
        return sent

    def total(grads):
        return sum(grad.astype(jnp.float32) for grad in grads).astype(jnp.bfloat16)

    parts = range(1, cycle_size)
    key_parts = [swap(keys, part) for part in parts]
    table, *staged, keys, values = stage(
        functools.partial(dense_places, cycle_size), (rand_blocks.T, global_blocks),
        queries, out_grad, keys, values,
    )
    value_parts = [swap(values, 1), swap(values, 2)]
    out, query_grad, dk, dv = attend(
        table, staged, [keys, *key_parts], [values, *value_parts], send,
        functools.partial(swap, part=2),
    )
    return out, query_grad, total(dk), total(dv)


def sparse_local(queries, keys, values, out_grad, rand_blocks, global_blocks):
    cycle_size = lax.axis_size("seq")
    myself = lax.axis_index("seq").astype(jnp.int32)
    tok_rows, width = keys.shape
    blocks_here = tok_rows // BLOCK
    rand_total = RAND * blocks_here
    capacity = (rand_total + GLOB + cycle_size - 1) // cycle_size
    slot_total = cycle_size * capacity
    listed = jnp.concatenate(
        [
            rand_blocks.reshape(cycle_size, rand_total),
            jnp.broadcast_to(global_blocks[None, :], (cycle_size, GLOB)),
        ],
        axis=1,
    )
    entries = listed.shape[1]
    owners = listed // blocks_here
    local_slot = listed % blocks_here
    earlier = jnp.arange(entries)[None, :] < jnp.arange(entries)[:, None]
    same_owner = owners[:, :, None] == owners[:, None, :]
    ranking = jnp.sum(same_owner & earlier[None], axis=2)
    owners_mine = lax.dynamic_index_in_dim(owners, myself, 0, keepdims=False)
    ranking_mine = lax.dynamic_index_in_dim(ranking, myself, 0, keepdims=False)
    far_place = (blocks_here + 2 + owners_mine * capacity + ranking_mine).astype(jnp.int32)
    slot_ids = jnp.arange(slot_total)
    requester = slot_ids // capacity
    position = slot_ids % capacity
    matches = (owners[requester] == myself) & (ranking[requester] == position[:, None])
    source = jnp.sum(jnp.where(matches, local_slot[requester], 0), axis=1)

    up = [(i, (i + 1) % cycle_size) for i in range(cycle_size)]
    down = [(j, i) for i, j in up]
    pair = jnp.concatenate([keys, values], axis=1)
    before = lax.ppermute(pair[tok_rows - BLOCK :], "seq", up)
    after = lax.ppermute(pair[:BLOCK], "seq", down)
    outgoing = jnp.take(pair.reshape(blocks_here, BLOCK, 2 * width), source, axis=0)
    far = lax.all_to_all(outgoing, "seq", split_axis=0, concat_axis=0, tiled=True)
    others = [before, after, far.reshape(slot_total * BLOCK, 2 * width)]
    key_parts = [part[:, :width] for part in others]
    value_parts = [part[:, width:] for part in others]

    here = jnp.arange(blocks_here, dtype=jnp.int32)[:, None]
    ahead = jnp.where(here == 0, blocks_here, here - 1)
    behind = jnp.where(here == blocks_here - 1, blocks_here + 1, here + 1)
    table = jnp.concatenate(
        [
            ahead,
            here,
            behind,
            jnp.broadcast_to(far_place[None, rand_total:], (blocks_here, GLOB)),
            far_place[:rand_total].reshape(blocks_here, RAND),
        ],
        axis=1,
    )
    landing = (source[:, None] == jnp.arange(blocks_here)[None, :]).astype(jnp.bfloat16)

    def send(grads, earlier):
        own, grad_before, grad_after, grad_far = grads
        last_rim = lax.ppermute(grad_before, "seq", down)
        first_rim = lax.ppermute(grad_after, "seq", up)
        returned = lax.all_to_all(
            grad_far.reshape(slot_total, BLOCK, width),
            "seq", split_axis=0, concat_axis=0, tiled=True,
        )
        return [own, last_rim, first_rim, returned]

    def total(grads):
        own, last_rim, first_rim, returned = grads
        landed = jnp.einsum("sq,sbx->qbx", landing, returned, preferred_element_type=jnp.float32)
        sums = own.reshape(blocks_here, BLOCK, width) + landed
        sums = sums.at[blocks_here - 1].add(last_rim.astype(jnp.float32))
        sums = sums.at[0].add(first_rim.astype(jnp.float32))
        return sums.reshape(tok_rows, width).astype(jnp.bfloat16)

    table, *staged, keys, values = stage(
        given_places, (table,), queries, out_grad, keys, values
    )
    out, query_grad, dk, dv = attend(
        table, staged, [keys, *key_parts], [values, *value_parts], send
    )
    return out, query_grad, total(dk), total(dv)


def local(queries, keys, values, out_grad, rand_blocks, global_blocks):
    cycle_size = lax.axis_size("seq")
    blocks_here = queries.shape[0] // BLOCK
    capacity = (RAND * blocks_here + GLOB + cycle_size - 1) // cycle_size
    dense = capacity >= blocks_here and cycle_size == 4
    plan = dense_local if dense else sparse_local
    return plan(queries, keys, values, out_grad, rand_blocks, global_blocks)


def solution(mesh):
    rows = P(("dp", "seq"), None)
    return jax.shard_map(
        local,
        mesh=mesh,
        in_specs=(rows, rows, rows, rows, P("dp", None), P("dp")),
        out_specs=(rows, rows, rows, rows),
        check_vma=False,
    )
```

```python
import functools

import jax
import jax.numpy as jnp
from jax import lax
from jax.experimental import pallas as pl
from jax.experimental.pallas import tpu as pltpu
from jax.sharding import PartitionSpec as P

KVH = 2
HD = 128
BLOCK = 64
GLOB = 2
RAND = 3
GROUP = 4
ENTRIES = 3 + GLOB + RAND
LOG2E = 1.4426950408889634
SCALE = HD ** (-0.5)


NN = (((1,), (0,)), ((), ()))
TN = (((0,), (0,)), ((), ()))
dot = functools.partial(lax.dot_general, preferred_element_type=jnp.float32)

KEYS = ENTRIES * BLOCK
CHUNK = 128
FACTOR = SCALE * LOG2E
ROWS = GROUP * BLOCK


def units(blocks_here):
    return [(b, h, b * KVH + h) for b in range(blocks_here) for h in range(KVH)]


def given_places(lists, blocks_here, b):
    return [lists[0][b, e] for e in range(ENTRIES)]


def dense_offsets(cycle_size, position):
    odd = position & 1
    offsets = list(range(cycle_size))
    offsets[1], offsets[2] = 2 - odd, 1 + odd
    return offsets


def dense_places(cycle_size, lists, blocks_here, b):
    rand_ref, glob_ref = lists
    me = lax.axis_index("seq").astype(jnp.int32)
    odd = lax.axis_index("dp").astype(jnp.int32) & 1

    def place(owner, local):
        offset = owner ^ me
        swapped = (odd == 0) & ((offset == 1) | (offset == 2))
        return jnp.where(swapped, 3 - offset, offset) * blocks_here + local

    def far_place(block):
        return place(lax.div(block, blocks_here), lax.rem(block, blocks_here))

    window = [b - 1, b, b + 1]
    if b == 0:
        window[0] = place(lax.rem(me + cycle_size - 1, cycle_size), blocks_here - 1)
    if b == blocks_here - 1:
        window[2] = place(lax.rem(me + 1, cycle_size), 0)
    far = [glob_ref[i] for i in range(GLOB)] + [rand_ref[i, me * blocks_here + b] for i in range(RAND)]
    return window + [far_place(block) for block in far]


def spans(table, b):
    result = []
    for e in range(ENTRIES):
        near = b + e - 1
        if e < 3 and 0 <= near < table.shape[0]:
            result.append(pl.ds(near * BLOCK, BLOCK))
        else:
            result.append(pl.ds(pl.multiple_of(table[b, e] * BLOCK, BLOCK), BLOCK))
    return result


def picked(pool, places, h):
    return jnp.concatenate([pool[place, h * HD : (h + 1) * HD] for place in places], axis=0)


def unstack(ref, b, h, value):
    for j in range(GROUP):
        c = (h * GROUP + j) * HD
        ref[b * BLOCK : (b + 1) * BLOCK, c : c + HD] = value[j * BLOCK : (j + 1) * BLOCK]


def add_terms(pool, places, h, terms):
    for e, place in enumerate(places):
        pool[place, h * HD : (h + 1) * HD] += terms[e * BLOCK : (e + 1) * BLOCK]


def gather_pool(pool, parts):
    start = 0
    for part in parts:
        pool[start : start + part.shape[0]] = part[...]
        start += part.shape[0]


def split_pool(outs, pool, factor):
    start = 0
    for out in outs:
        total = pool[start : start + out.shape[0]]
        out[...] = (total if factor is None else total * factor).astype(out.dtype)
        start += out.shape[0]


def stage_kernel(locate, count, *refs):
    sources, refs = refs[: count + 4], refs[count + 4 :]
    table, q_rows, g_rows, q_cols, g_cols, k_ref, v_ref, *refs = refs
    lists = refs[:count]
    q_ref, g_ref, sem = refs[count:]
    targets = [*lists, q_ref, g_ref, k_ref, v_ref]
    copies = [
        pltpu.make_async_copy(source, target, sem.at[i])
        for i, (source, target) in enumerate(zip(sources, targets))
    ]
    for copy in copies:
        copy.start()
    for copy in copies[: count + 2]:
        copy.wait()
    for b in range(table.shape[0]):
        for e, place in enumerate(locate(lists, table.shape[0], b)):
            table[b, e] = jnp.int32(place)
    for ref, rows, cols in ((q_ref, q_rows, q_cols), (g_ref, g_rows, g_cols)):
        for b, h, u in units(table.shape[0]):
            heads = [(h * GROUP + j) * HD for j in range(GROUP)]
            unit = jnp.concatenate(
                [ref[b * BLOCK : (b + 1) * BLOCK, c : c + HD] for c in heads], axis=0
            )
            rows[u * ROWS : (u + 1) * ROWS] = unit
            cols[u * HD : (u + 1) * HD] = unit.T
    for copy in copies[count + 2 :]:
        copy.wait()


def probs_kernel(count, table, q_cols, g_rows, *refs):
    parts = refs[:count][::-1]
    probs_ref, k_pool, *dv_refs, dv_pool = refs[count:]
    gather_pool(k_pool, parts)
    dv_pool[...] = jnp.zeros_like(dv_pool)
    for b, h, u in units(table.shape[0]):
        places = spans(table, b)
        scores = dot(picked(k_pool, places, h), q_cols[u * HD : (u + 1) * HD], NN)
        chunks = [scores[i : i + CHUNK] for i in range(0, KEYS, CHUNK)]
        peaks = [jnp.max(chunk, axis=0, keepdims=True) for chunk in chunks]
        expos = [jnp.exp2((chunk - peak) * FACTOR) for chunk, peak in zip(chunks, peaks)]
        peak = functools.reduce(jnp.maximum, peaks)
        scales = [jnp.exp2((own - peak) * FACTOR) for own in peaks]
        norm = 1.0 / sum(jnp.sum(e, axis=0, keepdims=True) * r for e, r in zip(expos, scales))
        probs = [(e * (r * norm)).astype(jnp.bfloat16) for e, r in zip(expos, scales)]
        probs_b = jnp.concatenate(probs, axis=0)
        probs_ref[u * KEYS : (u + 1) * KEYS] = probs_b
        add_terms(dv_pool, places, h, dot(probs_b, g_rows[u * ROWS : (u + 1) * ROWS], NN))
    split_pool(dv_refs, dv_pool, None)


def dscores_kernel(count, table, q_rows, g_cols, probs_ref, *refs):
    parts = refs[:count][::-1]
    ds_ref, v_pool, *dk_refs, dk_pool = refs[count:]
    gather_pool(v_pool, parts)
    dk_pool[...] = jnp.zeros_like(dk_pool)
    for b, h, u in units(table.shape[0]):
        places = spans(table, b)
        probs = probs_ref[u * KEYS : (u + 1) * KEYS].astype(jnp.float32)
        dprobs = dot(picked(v_pool, places, h), g_cols[u * HD : (u + 1) * HD], NN)
        delta = jnp.sum(probs * dprobs, axis=0, keepdims=True)
        dscores = (probs * (dprobs - delta)).astype(jnp.bfloat16)
        ds_ref[u * KEYS : (u + 1) * KEYS] = dscores
        add_terms(dk_pool, places, h, dot(dscores, q_rows[u * ROWS : (u + 1) * ROWS], NN))
    split_pool(dk_refs, dk_pool, SCALE)


def rows_kernel(table, probs_ref, ds_ref, k_pool, v_pool, out_any, qgrad_any, out_ref, qgrad_ref, sem):
    copies = []
    for b in range(table.shape[0]):
        places = spans(table, b)
        for h in range(KVH):
            span = slice((b * KVH + h) * KEYS, (b * KVH + h + 1) * KEYS)
            attended = dot(probs_ref[span], picked(v_pool, places, h), TN)
            unstack(out_ref, b, h, attended.astype(jnp.bfloat16))
            qgrad = dot(ds_ref[span], picked(k_pool, places, h), TN) * SCALE
            unstack(qgrad_ref, b, h, qgrad.astype(jnp.bfloat16))
        rows = pl.ds(b * BLOCK, BLOCK)
        for ref, target in ((out_ref, out_any), (qgrad_ref, qgrad_any)):
            copies.append(pltpu.make_async_copy(ref.at[rows], target.at[rows], sem.at[len(copies)]))
            copies[-1].start()
    for copy in copies:
        copy.wait()


SMEM = pl.BlockSpec(memory_space=pltpu.SMEM)
HBM = pl.BlockSpec(memory_space=pltpu.HBM)
VMEM = pl.BlockSpec(memory_space=pltpu.VMEM)


def run_kernel(kernel, operands, in_specs, results, scratch, products, out_spec=VMEM):
    flops = products * 2 * 4 * KVH * ROWS * KEYS * HD
    return pl.pallas_call(
        kernel,
        out_shape=[
            result if hasattr(result, "memory_space") else jax.ShapeDtypeStruct(*result)
            for result in results
        ],
        in_specs=in_specs + [VMEM] * (len(operands) - len(in_specs)),
        out_specs=[SMEM if hasattr(result, "memory_space") else out_spec for result in results],
        scratch_shapes=scratch,
        compiler_params=pltpu.CompilerParams(vmem_limit_bytes=32 * 2**20),
        cost_estimate=pl.CostEstimate(
            flops=flops, bytes_accessed=products * 2**20, transcendentals=0
        ),
    )(*operands)


def stage(locate, lists, queries, out_grad, keys, values):
    blocks_here = queries.shape[0] // BLOCK
    half = jnp.bfloat16
    rows = ((blocks_here * KVH * ROWS, HD), half)
    cols = ((blocks_here * KVH * HD, ROWS), half)
    narrow, wide = (keys.shape, half), (queries.shape, half)
    mine = (*lists, queries, out_grad, keys, values)
    return run_kernel(
        functools.partial(stage_kernel, locate, len(lists)),
        [pltpu.with_memory_space_constraint(array, pltpu.HBM) for array in mine],
        [HBM] * len(mine),
        [pltpu.SMEM((blocks_here, ENTRIES), jnp.int32), rows, rows, cols, cols, narrow, narrow],
        [
            *[pltpu.SMEM(array.shape, array.dtype) for array in lists],
            pltpu.VMEM(*wide), pltpu.VMEM(*wide),
            pltpu.SemaphoreType.DMA((len(mine),)),
        ],
        1,
    )


def attend(table, staged, key_parts, value_parts, send):
    q_rows, g_rows, q_cols, g_cols = staged
    tok_rows, width = key_parts[0].shape
    half, full = jnp.bfloat16, jnp.float32
    wide = ((tok_rows, GROUP * width), half)
    count = len(key_parts)
    pool_rows = sum(part.shape[0] for part in key_parts)
    held = ((table.shape[0] * KVH * KEYS, ROWS), half)
    sums = [(part.shape, half if i else full) for i, part in enumerate(key_parts)]
    scratch = [pltpu.VMEM((pool_rows, width), full)]
    pool = ((pool_rows, width), half)
    probs, k_pool, *dv = run_kernel(
        functools.partial(probs_kernel, count),
        (table, q_cols, g_rows, *key_parts[::-1]),
        [SMEM], [held, pool, *sums], scratch, 2,
    )
    dv = send(dv, None)
    dscores, v_pool, *dk = run_kernel(
        functools.partial(dscores_kernel, count),
        (table, q_rows, g_cols, probs, *value_parts[::-1]),
        [SMEM], [held, pool, *sums], scratch, 2,
    )
    dk = send(dk, dv)
    dv[1], table = lax.optimization_barrier((dv[1], table))
    out, query_grad = run_kernel(
        rows_kernel, (table, probs, dscores, k_pool, v_pool), [SMEM], [wide, wide],
        [pltpu.VMEM(*wide)] * 2 + [pltpu.SemaphoreType.DMA((2 * table.shape[0],))], 2, HBM,
    )
    dv[2:], dk[-1], query_grad = lax.optimization_barrier((dv[2:], dk[-1], query_grad))
    return out, query_grad, dk, dv


def dense_local(queries, keys, values, out_grad, rand_blocks, global_blocks):
    cycle_size = lax.axis_size("seq")
    positions = lax.axis_size("dp")

    def swap(array, part):
        pairs = []
        for position in range(positions):
            offset = dense_offsets(cycle_size, position)[part]
            pairs += [(i * positions + position, (i ^ offset) * positions + position) for i in range(cycle_size)]
        return lax.ppermute(array, ("seq", "dp"), pairs)

    def send(grads, earlier):
        sent = [grads[0]] + [None] * (cycle_size - 1)
        sent[-1] = swap(grads[-1], cycle_size - 1)
        near = grads[1:-1]
        if earlier is not None:
            near, earlier[1] = lax.optimization_barrier((near, earlier[1]))
        for part in range(1, cycle_size - 1):
            sent[part] = swap(near[part - 1], part)
        return sent

    def total(grads):
        return sum(grad.astype(jnp.float32) for grad in grads).astype(jnp.bfloat16)

    parts = range(1, cycle_size)
    key_parts = [swap(keys, part) for part in parts]
    table, *staged, keys, values = stage(
        functools.partial(dense_places, cycle_size), (rand_blocks.T, global_blocks),
        queries, out_grad, keys, values,
    )
    value_parts = [swap(values, part) for part in parts]
    out, query_grad, dk, dv = attend(
        table, staged, [keys, *key_parts], [values, *value_parts], send
    )
    return out, query_grad, total(dk), total(dv)


def sparse_local(queries, keys, values, out_grad, rand_blocks, global_blocks):
    cycle_size = lax.axis_size("seq")
    myself = lax.axis_index("seq").astype(jnp.int32)
    tok_rows, width = keys.shape
    blocks_here = tok_rows // BLOCK
    rand_total = RAND * blocks_here
    capacity = (rand_total + GLOB + cycle_size - 1) // cycle_size
    slot_total = cycle_size * capacity
    listed = jnp.concatenate(
        [
            rand_blocks.reshape(cycle_size, rand_total),
            jnp.broadcast_to(global_blocks[None, :], (cycle_size, GLOB)),
        ],
        axis=1,
    )
    entries = listed.shape[1]
    owners = listed // blocks_here
    local_slot = listed % blocks_here
    earlier = jnp.arange(entries)[None, :] < jnp.arange(entries)[:, None]
    same_owner = owners[:, :, None] == owners[:, None, :]
    ranking = jnp.sum(same_owner & earlier[None], axis=2)
    owners_mine = lax.dynamic_index_in_dim(owners, myself, 0, keepdims=False)
    ranking_mine = lax.dynamic_index_in_dim(ranking, myself, 0, keepdims=False)
    far_place = (blocks_here + 2 + owners_mine * capacity + ranking_mine).astype(jnp.int32)
    slot_ids = jnp.arange(slot_total)
    requester = slot_ids // capacity
    position = slot_ids % capacity
    matches = (owners[requester] == myself) & (ranking[requester] == position[:, None])
    source = jnp.sum(jnp.where(matches, local_slot[requester], 0), axis=1)

    up = [(i, (i + 1) % cycle_size) for i in range(cycle_size)]
    down = [(j, i) for i, j in up]
    pair = jnp.concatenate([keys, values], axis=1)
    before = lax.ppermute(pair[tok_rows - BLOCK :], "seq", up)
    after = lax.ppermute(pair[:BLOCK], "seq", down)
    outgoing = jnp.take(pair.reshape(blocks_here, BLOCK, 2 * width), source, axis=0)
    far = lax.all_to_all(outgoing, "seq", split_axis=0, concat_axis=0, tiled=True)
    others = [before, after, far.reshape(slot_total * BLOCK, 2 * width)]
    key_parts = [part[:, :width] for part in others]
    value_parts = [part[:, width:] for part in others]

    here = jnp.arange(blocks_here, dtype=jnp.int32)[:, None]
    ahead = jnp.where(here == 0, blocks_here, here - 1)
    behind = jnp.where(here == blocks_here - 1, blocks_here + 1, here + 1)
    table = jnp.concatenate(
        [
            ahead,
            here,
            behind,
            jnp.broadcast_to(far_place[None, rand_total:], (blocks_here, GLOB)),
            far_place[:rand_total].reshape(blocks_here, RAND),
        ],
        axis=1,
    )
    landing = (source[:, None] == jnp.arange(blocks_here)[None, :]).astype(jnp.bfloat16)

    def send(grads, earlier):
        own, grad_before, grad_after, grad_far = grads
        last_rim = lax.ppermute(grad_before, "seq", down)
        first_rim = lax.ppermute(grad_after, "seq", up)
        returned = lax.all_to_all(
            grad_far.reshape(slot_total, BLOCK, width),
            "seq", split_axis=0, concat_axis=0, tiled=True,
        )
        return [own, last_rim, first_rim, returned]

    def total(grads):
        own, last_rim, first_rim, returned = grads
        landed = jnp.einsum("sq,sbx->qbx", landing, returned, preferred_element_type=jnp.float32)
        sums = own.reshape(blocks_here, BLOCK, width) + landed
        sums = sums.at[blocks_here - 1].add(last_rim.astype(jnp.float32))
        sums = sums.at[0].add(first_rim.astype(jnp.float32))
        return sums.reshape(tok_rows, width).astype(jnp.bfloat16)

    table, *staged, keys, values = stage(
        given_places, (table,), queries, out_grad, keys, values
    )
    out, query_grad, dk, dv = attend(
        table, staged, [keys, *key_parts], [values, *value_parts], send
    )
    return out, query_grad, total(dk), total(dv)


def local(queries, keys, values, out_grad, rand_blocks, global_blocks):
    cycle_size = lax.axis_size("seq")
    blocks_here = queries.shape[0] // BLOCK
    capacity = (RAND * blocks_here + GLOB + cycle_size - 1) // cycle_size
    dense = capacity >= blocks_here and cycle_size == 4
    plan = dense_local if dense else sparse_local
    return plan(queries, keys, values, out_grad, rand_blocks, global_blocks)


def solution(mesh):
    rows = P(("dp", "seq"), None)
    return jax.shard_map(
        local,
        mesh=mesh,
        in_specs=(rows, rows, rows, rows, P("dp", None), P("dp")),
        out_specs=(rows, rows, rows, rows),
        check_vma=False,
    )
```

```python
import functools

import jax
import jax.numpy as jnp
from jax import lax
from jax.experimental import pallas as pl
from jax.experimental.pallas import tpu as pltpu
from jax.sharding import PartitionSpec as P

KVH = 2
HD = 128
BLOCK = 64
GLOB = 2
RAND = 3
GROUP = 4
ENTRIES = 3 + GLOB + RAND
LOG2E = 1.4426950408889634
SCALE = HD ** (-0.5)


NN = (((1,), (0,)), ((), ()))
TN = (((0,), (0,)), ((), ()))
dot = functools.partial(lax.dot_general, preferred_element_type=jnp.float32)

KEYS = ENTRIES * BLOCK
CHUNK = 128
FACTOR = SCALE * LOG2E
ROWS = GROUP * BLOCK


def units(blocks_here):
    return [(b, h, b * KVH + h) for b in range(blocks_here) for h in range(KVH)]


def given_places(lists, blocks_here, b):
    return [lists[0][b, e] for e in range(ENTRIES)]


def dense_offsets(cycle_size, position):
    odd = position & 1
    offsets = list(range(cycle_size))
    offsets[1], offsets[2] = 1 + odd, 2 - odd
    return offsets


def dense_places(cycle_size, lists, blocks_here, b):
    rand_ref, glob_ref = lists
    me = lax.axis_index("seq").astype(jnp.int32)
    odd = lax.axis_index("dp").astype(jnp.int32) & 1

    def place(owner, local):
        offset = owner ^ me
        swapped = (odd == 1) & ((offset == 1) | (offset == 2))
        return jnp.where(swapped, 3 - offset, offset) * blocks_here + local

    def far_place(block):
        return place(lax.div(block, blocks_here), lax.rem(block, blocks_here))

    window = [b - 1, b, b + 1]
    if b == 0:
        window[0] = place(lax.rem(me + cycle_size - 1, cycle_size), blocks_here - 1)
    if b == blocks_here - 1:
        window[2] = place(lax.rem(me + 1, cycle_size), 0)
    far = [glob_ref[i] for i in range(GLOB)] + [rand_ref[i, me * blocks_here + b] for i in range(RAND)]
    return window + [far_place(block) for block in far]


def spans(table, b):
    result = []
    for e in range(ENTRIES):
        near = b + e - 1
        if e < 3 and 0 <= near < table.shape[0]:
            result.append(pl.ds(near * BLOCK, BLOCK))
        else:
            result.append(pl.ds(pl.multiple_of(table[b, e] * BLOCK, BLOCK), BLOCK))
    return result


def picked(pool, places, h):
    return jnp.concatenate([pool[place, h * HD : (h + 1) * HD] for place in places], axis=0)


def unstack(ref, b, h, value):
    for j in range(GROUP):
        c = (h * GROUP + j) * HD
        ref[b * BLOCK : (b + 1) * BLOCK, c : c + HD] = value[j * BLOCK : (j + 1) * BLOCK]


def add_terms(pool, places, h, terms):
    for e, place in enumerate(places):
        pool[place, h * HD : (h + 1) * HD] += terms[e * BLOCK : (e + 1) * BLOCK]


def gather_pool(pool, parts):
    start = 0
    for part in parts:
        pool[start : start + part.shape[0]] = part[...]
        start += part.shape[0]


def split_pool(outs, pool, factor):
    start = 0
    for out in outs:
        total = pool[start : start + out.shape[0]]
        out[...] = (total if factor is None else total * factor).astype(out.dtype)
        start += out.shape[0]


def stage_kernel(locate, count, *refs):
    sources, refs = refs[: count + 4], refs[count + 4 :]
    table, q_rows, g_rows, q_cols, g_cols, dv_pool, dk_pool, k_ref, v_ref, *refs = refs
    lists = refs[:count]
    q_ref, g_ref, sem = refs[count:]
    targets = [*lists, q_ref, g_ref, k_ref, v_ref]
    copies = [
        pltpu.make_async_copy(source, target, sem.at[i])
        for i, (source, target) in enumerate(zip(sources, targets))
    ]
    for copy in copies:
        copy.start()
    dv_pool[...] = jnp.zeros_like(dv_pool)
    dk_pool[...] = jnp.zeros_like(dk_pool)
    for copy in copies[: count + 2]:
        copy.wait()
    for b in range(table.shape[0]):
        for e, place in enumerate(locate(lists, table.shape[0], b)):
            table[b, e] = jnp.int32(place)
    for ref, rows, cols in ((q_ref, q_rows, q_cols), (g_ref, g_rows, g_cols)):
        for b, h, u in units(table.shape[0]):
            heads = [(h * GROUP + j) * HD for j in range(GROUP)]
            unit = jnp.concatenate(
                [ref[b * BLOCK : (b + 1) * BLOCK, c : c + HD] for c in heads], axis=0
            )
            rows[u * ROWS : (u + 1) * ROWS] = unit
            cols[u * HD : (u + 1) * HD] = unit.T
    for copy in copies[count + 2 :]:
        copy.wait()


def probs_kernel(count, table, q_cols, g_rows, cleared, *refs):
    parts = refs[:count][::-1]
    probs_ref, k_pool, dv_pool, *dv_refs = refs[count:]
    gather_pool(k_pool, parts)
    for b, h, u in units(table.shape[0]):
        places = spans(table, b)
        scores = dot(picked(k_pool, places, h), q_cols[u * HD : (u + 1) * HD], NN)
        chunks = [scores[i : i + CHUNK] for i in range(0, KEYS, CHUNK)]
        peaks = [jnp.max(chunk, axis=0, keepdims=True) for chunk in chunks]
        expos = [jnp.exp2((chunk - peak) * FACTOR) for chunk, peak in zip(chunks, peaks)]
        peak = functools.reduce(jnp.maximum, peaks)
        scales = [jnp.exp2((own - peak) * FACTOR) for own in peaks]
        norm = 1.0 / sum(jnp.sum(e, axis=0, keepdims=True) * r for e, r in zip(expos, scales))
        probs = [(e * (r * norm)).astype(jnp.bfloat16) for e, r in zip(expos, scales)]
        probs_b = jnp.concatenate(probs, axis=0)
        probs_ref[u * KEYS : (u + 1) * KEYS] = probs_b
        add_terms(dv_pool, places, h, dot(probs_b, g_rows[u * ROWS : (u + 1) * ROWS], NN))
    split_pool(dv_refs, dv_pool, None)


def dscores_kernel(count, table, q_rows, g_cols, probs_ref, cleared, *refs):
    parts = refs[:count][::-1]
    ds_ref, v_pool, dk_pool, *dk_refs = refs[count:]
    gather_pool(v_pool, parts)
    for b, h, u in units(table.shape[0]):
        places = spans(table, b)
        probs = probs_ref[u * KEYS : (u + 1) * KEYS].astype(jnp.float32)
        dprobs = dot(picked(v_pool, places, h), g_cols[u * HD : (u + 1) * HD], NN)
        delta = jnp.sum(probs * dprobs, axis=0, keepdims=True)
        dscores = (probs * (dprobs - delta)).astype(jnp.bfloat16)
        ds_ref[u * KEYS : (u + 1) * KEYS] = dscores
        add_terms(dk_pool, places, h, dot(dscores, q_rows[u * ROWS : (u + 1) * ROWS], NN))
    split_pool(dk_refs, dk_pool, SCALE)


def rows_kernel(table, probs_ref, ds_ref, k_pool, v_pool, out_any, qgrad_any, out_ref, qgrad_ref, sem):
    copies = []
    for b in range(table.shape[0]):
        places = spans(table, b)
        for h in range(KVH):
            span = slice((b * KVH + h) * KEYS, (b * KVH + h + 1) * KEYS)
            attended = dot(probs_ref[span], picked(v_pool, places, h), TN)
            unstack(out_ref, b, h, attended.astype(jnp.bfloat16))
            qgrad = dot(ds_ref[span], picked(k_pool, places, h), TN) * SCALE
            unstack(qgrad_ref, b, h, qgrad.astype(jnp.bfloat16))
        rows = pl.ds(b * BLOCK, BLOCK)
        for ref, target in ((out_ref, out_any), (qgrad_ref, qgrad_any)):
            copies.append(pltpu.make_async_copy(ref.at[rows], target.at[rows], sem.at[len(copies)]))
            copies[-1].start()
    for copy in copies:
        copy.wait()


SMEM = pl.BlockSpec(memory_space=pltpu.SMEM)
HBM = pl.BlockSpec(memory_space=pltpu.HBM)
VMEM = pl.BlockSpec(memory_space=pltpu.VMEM)


def run_kernel(kernel, operands, in_specs, results, scratch, products, out_spec=VMEM, aliases={}):
    flops = products * 2 * 4 * KVH * ROWS * KEYS * HD
    return pl.pallas_call(
        kernel,
        out_shape=[
            result if hasattr(result, "memory_space") else jax.ShapeDtypeStruct(*result)
            for result in results
        ],
        in_specs=in_specs + [VMEM] * (len(operands) - len(in_specs)),
        out_specs=[SMEM if hasattr(result, "memory_space") else out_spec for result in results],
        scratch_shapes=scratch,
        input_output_aliases=aliases,
        compiler_params=pltpu.CompilerParams(vmem_limit_bytes=32 * 2**20),
        cost_estimate=pl.CostEstimate(
            flops=flops, bytes_accessed=products * 2**20, transcendentals=0
        ),
    )(*operands)


def stage(locate, lists, queries, out_grad, keys, values, pool_rows):
    blocks_here = queries.shape[0] // BLOCK
    half = jnp.bfloat16
    rows = ((blocks_here * KVH * ROWS, HD), half)
    cols = ((blocks_here * KVH * HD, ROWS), half)
    narrow, wide = (keys.shape, half), (queries.shape, half)
    cleared = ((pool_rows, keys.shape[1]), jnp.float32)
    mine = (*lists, queries, out_grad, keys, values)
    return run_kernel(
        functools.partial(stage_kernel, locate, len(lists)),
        [pltpu.with_memory_space_constraint(array, pltpu.HBM) for array in mine],
        [HBM] * len(mine),
        [
            pltpu.SMEM((blocks_here, ENTRIES), jnp.int32),
            rows, rows, cols, cols, cleared, cleared, narrow, narrow,
        ],
        [
            *[pltpu.SMEM(array.shape, array.dtype) for array in lists],
            pltpu.VMEM(*wide), pltpu.VMEM(*wide),
            pltpu.SemaphoreType.DMA((len(mine),)),
        ],
        1,
    )


def attend(table, staged, key_parts, value_parts, send):
    q_rows, g_rows, q_cols, g_cols, dv_pool, dk_pool = staged
    tok_rows, width = key_parts[0].shape
    half, full = jnp.bfloat16, jnp.float32
    wide = ((tok_rows, GROUP * width), half)
    count = len(key_parts)
    pool_rows = sum(part.shape[0] for part in key_parts)
    held = ((table.shape[0] * KVH * KEYS, ROWS), half)
    sums = [(part.shape, half if i else full) for i, part in enumerate(key_parts)]
    pool, cleared = ((pool_rows, width), half), ((pool_rows, width), full)
    probs, k_pool, _, *dv = run_kernel(
        functools.partial(probs_kernel, count),
        (table, q_cols, g_rows, dv_pool, *key_parts[::-1]),
        [SMEM], [held, pool, cleared, *sums], [], 2, aliases={3: 2},
    )
    dv = send(dv, None)
    dscores, v_pool, _, *dk = run_kernel(
        functools.partial(dscores_kernel, count),
        (table, q_rows, g_cols, probs, dk_pool, *value_parts[::-1]),
        [SMEM], [held, pool, cleared, *sums], [], 2, aliases={4: 2},
    )
    dk = send(dk, dv)
    dv[1], table = lax.optimization_barrier((dv[1], table))
    out, query_grad = run_kernel(
        rows_kernel, (table, probs, dscores, k_pool, v_pool), [SMEM], [wide, wide],
        [pltpu.VMEM(*wide)] * 2 + [pltpu.SemaphoreType.DMA((2 * table.shape[0],))], 2, HBM,
    )
    dv[2:], dk[-1], query_grad = lax.optimization_barrier((dv[2:], dk[-1], query_grad))
    return out, query_grad, dk, dv


def dense_local(queries, keys, values, out_grad, rand_blocks, global_blocks):
    cycle_size = lax.axis_size("seq")
    positions = lax.axis_size("dp")

    def swap(array, part):
        pairs = []
        for position in range(positions):
            offset = dense_offsets(cycle_size, position)[part]
            pairs += [(i * positions + position, (i ^ offset) * positions + position) for i in range(cycle_size)]
        return lax.ppermute(array, ("seq", "dp"), pairs)

    def send(grads, earlier):
        sent = [grads[0]] + [None] * (cycle_size - 1)
        sent[-1] = swap(grads[-1], cycle_size - 1)
        near = grads[1:-1]
        if earlier is not None:
            near, earlier[1] = lax.optimization_barrier((near, earlier[1]))
        for part in range(1, cycle_size - 1):
            sent[part] = swap(near[part - 1], part)
        return sent

    def total(grads):
        return sum(grad.astype(jnp.float32) for grad in grads).astype(jnp.bfloat16)

    parts = range(1, cycle_size)
    key_parts = [swap(keys, part) for part in parts]
    table, *staged, keys, values = stage(
        functools.partial(dense_places, cycle_size), (rand_blocks.T, global_blocks),
        queries, out_grad, keys, values, cycle_size * keys.shape[0],
    )
    value_parts = [swap(values, part) for part in parts]
    out, query_grad, dk, dv = attend(
        table, staged, [keys, *key_parts], [values, *value_parts], send
    )
    return out, query_grad, total(dk), total(dv)


def sparse_local(queries, keys, values, out_grad, rand_blocks, global_blocks):
    cycle_size = lax.axis_size("seq")
    myself = lax.axis_index("seq").astype(jnp.int32)
    tok_rows, width = keys.shape
    blocks_here = tok_rows // BLOCK
    rand_total = RAND * blocks_here
    capacity = (rand_total + GLOB + cycle_size - 1) // cycle_size
    slot_total = cycle_size * capacity
    listed = jnp.concatenate(
        [
            rand_blocks.reshape(cycle_size, rand_total),
            jnp.broadcast_to(global_blocks[None, :], (cycle_size, GLOB)),
        ],
        axis=1,
    )
    entries = listed.shape[1]
    owners = listed // blocks_here
    local_slot = listed % blocks_here
    earlier = jnp.arange(entries)[None, :] < jnp.arange(entries)[:, None]
    same_owner = owners[:, :, None] == owners[:, None, :]
    ranking = jnp.sum(same_owner & earlier[None], axis=2)
    owners_mine = lax.dynamic_index_in_dim(owners, myself, 0, keepdims=False)
    ranking_mine = lax.dynamic_index_in_dim(ranking, myself, 0, keepdims=False)
    far_place = (blocks_here + 2 + owners_mine * capacity + ranking_mine).astype(jnp.int32)
    slot_ids = jnp.arange(slot_total)
    requester = slot_ids // capacity
    position = slot_ids % capacity
    matches = (owners[requester] == myself) & (ranking[requester] == position[:, None])
    source = jnp.sum(jnp.where(matches, local_slot[requester], 0), axis=1)

    up = [(i, (i + 1) % cycle_size) for i in range(cycle_size)]
    down = [(j, i) for i, j in up]
    pair = jnp.concatenate([keys, values], axis=1)
    before = lax.ppermute(pair[tok_rows - BLOCK :], "seq", up)
    after = lax.ppermute(pair[:BLOCK], "seq", down)
    outgoing = jnp.take(pair.reshape(blocks_here, BLOCK, 2 * width), source, axis=0)
    far = lax.all_to_all(outgoing, "seq", split_axis=0, concat_axis=0, tiled=True)
    others = [before, after, far.reshape(slot_total * BLOCK, 2 * width)]
    key_parts = [part[:, :width] for part in others]
    value_parts = [part[:, width:] for part in others]

    here = jnp.arange(blocks_here, dtype=jnp.int32)[:, None]
    ahead = jnp.where(here == 0, blocks_here, here - 1)
    behind = jnp.where(here == blocks_here - 1, blocks_here + 1, here + 1)
    table = jnp.concatenate(
        [
            ahead,
            here,
            behind,
            jnp.broadcast_to(far_place[None, rand_total:], (blocks_here, GLOB)),
            far_place[:rand_total].reshape(blocks_here, RAND),
        ],
        axis=1,
    )
    landing = (source[:, None] == jnp.arange(blocks_here)[None, :]).astype(jnp.bfloat16)

    def send(grads, earlier):
        own, grad_before, grad_after, grad_far = grads
        last_rim = lax.ppermute(grad_before, "seq", down)
        first_rim = lax.ppermute(grad_after, "seq", up)
        returned = lax.all_to_all(
            grad_far.reshape(slot_total, BLOCK, width),
            "seq", split_axis=0, concat_axis=0, tiled=True,
        )
        return [own, last_rim, first_rim, returned]

    def total(grads):
        own, last_rim, first_rim, returned = grads
        landed = jnp.einsum("sq,sbx->qbx", landing, returned, preferred_element_type=jnp.float32)
        sums = own.reshape(blocks_here, BLOCK, width) + landed
        sums = sums.at[blocks_here - 1].add(last_rim.astype(jnp.float32))
        sums = sums.at[0].add(first_rim.astype(jnp.float32))
        return sums.reshape(tok_rows, width).astype(jnp.bfloat16)

    pool_rows = tok_rows + sum(part.shape[0] for part in key_parts)
    table, *staged, keys, values = stage(
        given_places, (table,), queries, out_grad, keys, values, pool_rows
    )
    out, query_grad, dk, dv = attend(
        table, staged, [keys, *key_parts], [values, *value_parts], send
    )
    return out, query_grad, total(dk), total(dv)


def local(queries, keys, values, out_grad, rand_blocks, global_blocks):
    cycle_size = lax.axis_size("seq")
    blocks_here = queries.shape[0] // BLOCK
    capacity = (RAND * blocks_here + GLOB + cycle_size - 1) // cycle_size
    dense = capacity >= blocks_here and cycle_size == 4
    plan = dense_local if dense else sparse_local
    return plan(queries, keys, values, out_grad, rand_blocks, global_blocks)


def solution(mesh):
    rows = P(("dp", "seq"), None)
    return jax.shard_map(
        local,
        mesh=mesh,
        in_specs=(rows, rows, rows, rows, P("dp", None), P("dp")),
        out_specs=(rows, rows, rows, rows),
        check_vma=False,
    )
```

```python
import functools

import jax
import jax.numpy as jnp
from jax import lax
from jax.experimental import pallas as pl
from jax.experimental.pallas import tpu as pltpu
from jax.sharding import PartitionSpec as P

KVH = 2
HD = 128
BLOCK = 64
GLOB = 2
RAND = 3
GROUP = 4
ENTRIES = 3 + GLOB + RAND
LOG2E = 1.4426950408889634
SCALE = HD ** (-0.5)


NN = (((1,), (0,)), ((), ()))
TN = (((0,), (0,)), ((), ()))
dot = functools.partial(lax.dot_general, preferred_element_type=jnp.float32)

KEYS = ENTRIES * BLOCK
CHUNK = 128
FACTOR = SCALE * LOG2E
ROWS = GROUP * BLOCK


def units(blocks_here):
    return [(b, h, b * KVH + h) for b in range(blocks_here) for h in range(KVH)]


def given_places(lists, blocks_here, b):
    return [lists[0][b, e] for e in range(ENTRIES)]


def dense_offsets(cycle_size, position):
    odd = position & 1
    offsets = list(range(cycle_size))
    offsets[1], offsets[2] = 1 + odd, 2 - odd
    return offsets


def dense_places(cycle_size, lists, blocks_here, b):
    rand_ref, glob_ref = lists
    me = lax.axis_index("seq").astype(jnp.int32)
    odd = lax.axis_index("dp").astype(jnp.int32) & 1

    def place(owner, local):
        offset = owner ^ me
        swapped = (odd == 1) & ((offset == 1) | (offset == 2))
        return jnp.where(swapped, 3 - offset, offset) * blocks_here + local

    def far_place(block):
        return place(lax.div(block, blocks_here), lax.rem(block, blocks_here))

    window = [b - 1, b, b + 1]
    if b == 0:
        window[0] = place(lax.rem(me + cycle_size - 1, cycle_size), blocks_here - 1)
    if b == blocks_here - 1:
        window[2] = place(lax.rem(me + 1, cycle_size), 0)
    far = [glob_ref[i] for i in range(GLOB)] + [rand_ref[i, me * blocks_here + b] for i in range(RAND)]
    return window + [far_place(block) for block in far]


def spans(table, b):
    result = []
    for e in range(ENTRIES):
        near = b + e - 1
        if e < 3 and 0 <= near < table.shape[0]:
            result.append(pl.ds(near * BLOCK, BLOCK))
        else:
            result.append(pl.ds(pl.multiple_of(table[b, e] * BLOCK, BLOCK), BLOCK))
    return result


def picked(pool, places, h):
    return jnp.concatenate([pool[place, h * HD : (h + 1) * HD] for place in places], axis=0)


def unstack(ref, b, h, value):
    for j in range(GROUP):
        c = (h * GROUP + j) * HD
        ref[b * BLOCK : (b + 1) * BLOCK, c : c + HD] = value[j * BLOCK : (j + 1) * BLOCK]


def add_terms(pool, places, h, terms):
    for e, place in enumerate(places):
        pool[place, h * HD : (h + 1) * HD] += terms[e * BLOCK : (e + 1) * BLOCK]


def gather_pool(pool, parts):
    start = 0
    for part in parts:
        pool[start : start + part.shape[0]] = part[...]
        start += part.shape[0]


def split_pool(outs, pool, factor):
    start = 0
    for out in outs:
        total = pool[start : start + out.shape[0]]
        out[...] = (total if factor is None else total * factor).astype(out.dtype)
        start += out.shape[0]


def stage_kernel(locate, count, *refs):
    sources, refs = refs[: count + 4], refs[count + 4 :]
    table, q_rows, g_rows, q_cols, g_cols, dv_pool, dk_pool, k_ref, v_ref, *refs = refs
    lists = refs[:count]
    q_ref, g_ref, sem = refs[count:]
    targets = [*lists, q_ref, g_ref, k_ref, v_ref]
    copies = [
        pltpu.make_async_copy(source, target, sem.at[i])
        for i, (source, target) in enumerate(zip(sources, targets))
    ]
    for copy in copies:
        copy.start()
    dv_pool[...] = jnp.zeros_like(dv_pool)
    dk_pool[...] = jnp.zeros_like(dk_pool)
    for copy in copies[: count + 2]:
        copy.wait()
    for b in range(table.shape[0]):
        for e, place in enumerate(locate(lists, table.shape[0], b)):
            table[b, e] = jnp.int32(place)
    for ref, rows, cols in ((q_ref, q_rows, q_cols), (g_ref, g_rows, g_cols)):
        for b, h, u in units(table.shape[0]):
            heads = [(h * GROUP + j) * HD for j in range(GROUP)]
            unit = jnp.concatenate(
                [ref[b * BLOCK : (b + 1) * BLOCK, c : c + HD] for c in heads], axis=0
            )
            rows[u * ROWS : (u + 1) * ROWS] = unit
            cols[u * HD : (u + 1) * HD] = unit.T
    for copy in copies[count + 2 :]:
        copy.wait()


def probs_kernel(count, table, q_cols, g_rows, cleared, *refs):
    parts = refs[:count][::-1]
    probs_ref, k_pool, dv_pool, *dv_refs = refs[count:]
    gather_pool(k_pool, parts)
    for b, h, u in units(table.shape[0]):
        places = spans(table, b)
        scores = dot(picked(k_pool, places, h), q_cols[u * HD : (u + 1) * HD], NN)
        chunks = [scores[i : i + CHUNK] for i in range(0, KEYS, CHUNK)]
        peaks = [jnp.max(chunk, axis=0, keepdims=True) for chunk in chunks]
        expos = [jnp.exp2((chunk - peak) * FACTOR) for chunk, peak in zip(chunks, peaks)]
        peak = functools.reduce(jnp.maximum, peaks)
        scales = [jnp.exp2((own - peak) * FACTOR) for own in peaks]
        norm = 1.0 / sum(jnp.sum(e, axis=0, keepdims=True) * r for e, r in zip(expos, scales))
        probs = [(e * (r * norm)).astype(jnp.bfloat16) for e, r in zip(expos, scales)]
        probs_b = jnp.concatenate(probs, axis=0)
        probs_ref[u * KEYS : (u + 1) * KEYS] = probs_b
        add_terms(dv_pool, places, h, dot(probs_b, g_rows[u * ROWS : (u + 1) * ROWS], NN))
    split_pool(dv_refs, dv_pool, None)


def dscores_kernel(count, table, q_rows, g_cols, probs_ref, cleared, *refs):
    parts = refs[:count][::-1]
    ds_ref, v_pool, dk_pool, *dk_refs = refs[count:]
    gather_pool(v_pool, parts)
    for b, h, u in units(table.shape[0]):
        places = spans(table, b)
        probs = probs_ref[u * KEYS : (u + 1) * KEYS].astype(jnp.float32)
        dprobs = dot(picked(v_pool, places, h), g_cols[u * HD : (u + 1) * HD], NN)
        delta = jnp.sum(probs * dprobs, axis=0, keepdims=True)
        dscores = (probs * (dprobs - delta)).astype(jnp.bfloat16)
        ds_ref[u * KEYS : (u + 1) * KEYS] = dscores
        add_terms(dk_pool, places, h, dot(dscores, q_rows[u * ROWS : (u + 1) * ROWS], NN))
    split_pool(dk_refs, dk_pool, SCALE)


def rows_kernel(table, probs_ref, ds_ref, k_pool, v_pool, out_any, qgrad_any, out_ref, qgrad_ref, sem):
    copies = []
    for b in range(table.shape[0]):
        places = spans(table, b)
        for h in range(KVH):
            span = slice((b * KVH + h) * KEYS, (b * KVH + h + 1) * KEYS)
            attended = dot(probs_ref[span], picked(v_pool, places, h), TN)
            unstack(out_ref, b, h, attended.astype(jnp.bfloat16))
            qgrad = dot(ds_ref[span], picked(k_pool, places, h), TN) * SCALE
            unstack(qgrad_ref, b, h, qgrad.astype(jnp.bfloat16))
        rows = pl.ds(b * BLOCK, BLOCK)
        for ref, target in ((out_ref, out_any), (qgrad_ref, qgrad_any)):
            copies.append(pltpu.make_async_copy(ref.at[rows], target.at[rows], sem.at[len(copies)]))
            copies[-1].start()
    for copy in copies:
        copy.wait()


SMEM = pl.BlockSpec(memory_space=pltpu.SMEM)
HBM = pl.BlockSpec(memory_space=pltpu.HBM)
VMEM = pl.BlockSpec(memory_space=pltpu.VMEM)


def run_kernel(kernel, operands, in_specs, results, scratch, products, out_spec=VMEM, aliases={}):
    flops = products * 2 * 4 * KVH * ROWS * KEYS * HD
    return pl.pallas_call(
        kernel,
        out_shape=[
            result if hasattr(result, "memory_space") else jax.ShapeDtypeStruct(*result)
            for result in results
        ],
        in_specs=in_specs + [VMEM] * (len(operands) - len(in_specs)),
        out_specs=[SMEM if hasattr(result, "memory_space") else out_spec for result in results],
        scratch_shapes=scratch,
        input_output_aliases=aliases,
        compiler_params=pltpu.CompilerParams(vmem_limit_bytes=32 * 2**20),
        cost_estimate=pl.CostEstimate(
            flops=flops, bytes_accessed=products * 2**20, transcendentals=0
        ),
    )(*operands)


def stage(locate, lists, queries, out_grad, keys, values, pool_rows):
    blocks_here = queries.shape[0] // BLOCK
    half = jnp.bfloat16
    rows = ((blocks_here * KVH * ROWS, HD), half)
    cols = ((blocks_here * KVH * HD, ROWS), half)
    narrow, wide = (keys.shape, half), (queries.shape, half)
    cleared = ((pool_rows, keys.shape[1]), jnp.float32)
    mine = (*lists, queries, out_grad, keys, values)
    return run_kernel(
        functools.partial(stage_kernel, locate, len(lists)),
        [pltpu.with_memory_space_constraint(array, pltpu.HBM) for array in mine],
        [HBM] * len(mine),
        [
            pltpu.SMEM((blocks_here, ENTRIES), jnp.int32),
            rows, rows, cols, cols, cleared, cleared, narrow, narrow,
        ],
        [
            *[pltpu.SMEM(array.shape, array.dtype) for array in lists],
            pltpu.VMEM(*wide), pltpu.VMEM(*wide),
            pltpu.SemaphoreType.DMA((len(mine),)),
        ],
        1,
    )


def attend(table, staged, key_parts, value_parts, send):
    q_rows, g_rows, q_cols, g_cols, dv_pool, dk_pool = staged
    tok_rows, width = key_parts[0].shape
    half, full = jnp.bfloat16, jnp.float32
    wide = ((tok_rows, GROUP * width), half)
    count = len(key_parts)
    pool_rows = sum(part.shape[0] for part in key_parts)
    held = ((table.shape[0] * KVH * KEYS, ROWS), half)
    sums = [(part.shape, half if i else full) for i, part in enumerate(key_parts)]
    pool, cleared = ((pool_rows, width), half), ((pool_rows, width), full)
    probs, k_pool, _, *dv = run_kernel(
        functools.partial(probs_kernel, count),
        (table, q_cols, g_rows, dv_pool, *key_parts[::-1]),
        [SMEM], [held, pool, cleared, *sums], [], 2, aliases={3: 2},
    )
    dv = send(dv, None)
    dscores, v_pool, _, *dk = run_kernel(
        functools.partial(dscores_kernel, count),
        (table, q_rows, g_cols, probs, dk_pool, *value_parts[::-1]),
        [SMEM], [held, pool, cleared, *sums], [], 2, aliases={4: 2},
    )
    dk = send(dk, dv)
    dv[1], table = lax.optimization_barrier((dv[1], table))
    out, query_grad = run_kernel(
        rows_kernel, (table, probs, dscores, k_pool, v_pool), [SMEM], [wide, wide],
        [pltpu.VMEM(*wide)] * 2 + [pltpu.SemaphoreType.DMA((2 * table.shape[0],))], 2, HBM,
    )
    dv[2:], dk[-1], query_grad = lax.optimization_barrier((dv[2:], dk[-1], query_grad))
    return out, query_grad, dk, dv


def dense_local(queries, keys, values, out_grad, rand_blocks, global_blocks):
    cycle_size = lax.axis_size("seq")
    positions = lax.axis_size("dp")

    def swap(array, part):
        pairs = []
        for position in range(positions):
            offset = dense_offsets(cycle_size, position)[part]
            pairs += [(i * positions + position, (i ^ offset) * positions + position) for i in range(cycle_size)]
        return lax.ppermute(array, ("seq", "dp"), pairs)

    def send(grads, earlier):
        own, first, second, far = grads
        far, second = swap(far, 3), swap(second, 2)
        if earlier is not None:
            first, earlier[1] = lax.optimization_barrier((first, earlier[1]))
        return [own, swap(first, 1), second, far]

    def total(grads):
        return sum(grad.astype(jnp.float32) for grad in grads).astype(jnp.bfloat16)

    parts = range(1, cycle_size)
    key_parts = [swap(keys, part) for part in parts]
    table, *staged, keys, values = stage(
        functools.partial(dense_places, cycle_size), (rand_blocks.T, global_blocks),
        queries, out_grad, keys, values, cycle_size * keys.shape[0],
    )
    value_parts = [swap(values, part) for part in parts]
    out, query_grad, dk, dv = attend(
        table, staged, [keys, *key_parts], [values, *value_parts], send
    )
    return out, query_grad, total([dk[0], dk[2], dk[1], dk[3]]), total(dv)


def sparse_local(queries, keys, values, out_grad, rand_blocks, global_blocks):
    cycle_size = lax.axis_size("seq")
    myself = lax.axis_index("seq").astype(jnp.int32)
    tok_rows, width = keys.shape
    blocks_here = tok_rows // BLOCK
    rand_total = RAND * blocks_here
    capacity = (rand_total + GLOB + cycle_size - 1) // cycle_size
    slot_total = cycle_size * capacity
    listed = jnp.concatenate(
        [
            rand_blocks.reshape(cycle_size, rand_total),
            jnp.broadcast_to(global_blocks[None, :], (cycle_size, GLOB)),
        ],
        axis=1,
    )
    entries = listed.shape[1]
    owners = listed // blocks_here
    local_slot = listed % blocks_here
    earlier = jnp.arange(entries)[None, :] < jnp.arange(entries)[:, None]
    same_owner = owners[:, :, None] == owners[:, None, :]
    ranking = jnp.sum(same_owner & earlier[None], axis=2)
    owners_mine = lax.dynamic_index_in_dim(owners, myself, 0, keepdims=False)
    ranking_mine = lax.dynamic_index_in_dim(ranking, myself, 0, keepdims=False)
    far_place = (blocks_here + 2 + owners_mine * capacity + ranking_mine).astype(jnp.int32)
    slot_ids = jnp.arange(slot_total)
    requester = slot_ids // capacity
    position = slot_ids % capacity
    matches = (owners[requester] == myself) & (ranking[requester] == position[:, None])
    source = jnp.sum(jnp.where(matches, local_slot[requester], 0), axis=1)

    up = [(i, (i + 1) % cycle_size) for i in range(cycle_size)]
    down = [(j, i) for i, j in up]
    pair = jnp.concatenate([keys, values], axis=1)
    before = lax.ppermute(pair[tok_rows - BLOCK :], "seq", up)
    after = lax.ppermute(pair[:BLOCK], "seq", down)
    outgoing = jnp.take(pair.reshape(blocks_here, BLOCK, 2 * width), source, axis=0)
    far = lax.all_to_all(outgoing, "seq", split_axis=0, concat_axis=0, tiled=True)
    others = [before, after, far.reshape(slot_total * BLOCK, 2 * width)]
    key_parts = [part[:, :width] for part in others]
    value_parts = [part[:, width:] for part in others]

    here = jnp.arange(blocks_here, dtype=jnp.int32)[:, None]
    ahead = jnp.where(here == 0, blocks_here, here - 1)
    behind = jnp.where(here == blocks_here - 1, blocks_here + 1, here + 1)
    table = jnp.concatenate(
        [
            ahead,
            here,
            behind,
            jnp.broadcast_to(far_place[None, rand_total:], (blocks_here, GLOB)),
            far_place[:rand_total].reshape(blocks_here, RAND),
        ],
        axis=1,
    )
    landing = (source[:, None] == jnp.arange(blocks_here)[None, :]).astype(jnp.bfloat16)

    def send(grads, earlier):
        own, grad_before, grad_after, grad_far = grads
        last_rim = lax.ppermute(grad_before, "seq", down)
        first_rim = lax.ppermute(grad_after, "seq", up)
        returned = lax.all_to_all(
            grad_far.reshape(slot_total, BLOCK, width),
            "seq", split_axis=0, concat_axis=0, tiled=True,
        )
        return [own, last_rim, first_rim, returned]

    def total(grads):
        own, last_rim, first_rim, returned = grads
        landed = jnp.einsum("sq,sbx->qbx", landing, returned, preferred_element_type=jnp.float32)
        sums = own.reshape(blocks_here, BLOCK, width) + landed
        sums = sums.at[blocks_here - 1].add(last_rim.astype(jnp.float32))
        sums = sums.at[0].add(first_rim.astype(jnp.float32))
        return sums.reshape(tok_rows, width).astype(jnp.bfloat16)

    pool_rows = tok_rows + sum(part.shape[0] for part in key_parts)
    table, *staged, keys, values = stage(
        given_places, (table,), queries, out_grad, keys, values, pool_rows
    )
    out, query_grad, dk, dv = attend(
        table, staged, [keys, *key_parts], [values, *value_parts], send
    )
    return out, query_grad, total(dk), total(dv)


def local(queries, keys, values, out_grad, rand_blocks, global_blocks):
    cycle_size = lax.axis_size("seq")
    blocks_here = queries.shape[0] // BLOCK
    capacity = (RAND * blocks_here + GLOB + cycle_size - 1) // cycle_size
    dense = capacity >= blocks_here and cycle_size == 4
    plan = dense_local if dense else sparse_local
    return plan(queries, keys, values, out_grad, rand_blocks, global_blocks)


def solution(mesh):
    rows = P(("dp", "seq"), None)
    return jax.shard_map(
        local,
        mesh=mesh,
        in_specs=(rows, rows, rows, rows, P("dp", None), P("dp")),
        out_specs=(rows, rows, rows, rows),
        check_vma=False,
    )
```

```python
import functools

import jax
import jax.numpy as jnp
from jax import lax
from jax.experimental import pallas as pl
from jax.experimental.pallas import tpu as pltpu
from jax.sharding import PartitionSpec as P

KVH = 2
HD = 128
BLOCK = 64
GLOB = 2
RAND = 3
GROUP = 4
ENTRIES = 3 + GLOB + RAND
LOG2E = 1.4426950408889634
SCALE = HD ** (-0.5)


NN = (((1,), (0,)), ((), ()))
TN = (((0,), (0,)), ((), ()))
dot = functools.partial(lax.dot_general, preferred_element_type=jnp.float32)

KEYS = ENTRIES * BLOCK
CHUNK = 128
FACTOR = SCALE * LOG2E
ROWS = GROUP * BLOCK


def units(blocks_here):
    return [(b, h, b * KVH + h) for b in range(blocks_here) for h in range(KVH)]


def given_places(lists, blocks_here, b):
    return [lists[0][b, e] for e in range(ENTRIES)]


def dense_offsets(cycle_size, position):
    odd = position & 1
    offsets = list(range(cycle_size))
    offsets[1], offsets[2] = 1 + odd, 2 - odd
    return offsets


def dense_places(cycle_size, lists, blocks_here, b):
    rand_ref, glob_ref = lists
    me = lax.axis_index("seq").astype(jnp.int32)
    odd = lax.axis_index("dp").astype(jnp.int32) & 1

    def place(owner, local):
        offset = owner ^ me
        swapped = (odd == 1) & ((offset == 1) | (offset == 2))
        return jnp.where(swapped, 3 - offset, offset) * blocks_here + local

    def far_place(block):
        return place(lax.div(block, blocks_here), lax.rem(block, blocks_here))

    window = [b - 1, b, b + 1]
    if b == 0:
        window[0] = place(lax.rem(me + cycle_size - 1, cycle_size), blocks_here - 1)
    if b == blocks_here - 1:
        window[2] = place(lax.rem(me + 1, cycle_size), 0)
    far = [glob_ref[i] for i in range(GLOB)] + [rand_ref[i, me * blocks_here + b] for i in range(RAND)]
    return window + [far_place(block) for block in far]


def spans(table, b):
    result = []
    for e in range(ENTRIES):
        near = b + e - 1
        if e < 3 and 0 <= near < table.shape[0]:
            result.append(pl.ds(near * BLOCK, BLOCK))
        else:
            result.append(pl.ds(pl.multiple_of(table[b, e] * BLOCK, BLOCK), BLOCK))
    return result


def picked(pool, places, h):
    return jnp.concatenate([pool[place, h * HD : (h + 1) * HD] for place in places], axis=0)


def unstack(ref, b, h, value):
    for j in range(GROUP):
        c = (h * GROUP + j) * HD
        ref[b * BLOCK : (b + 1) * BLOCK, c : c + HD] = value[j * BLOCK : (j + 1) * BLOCK]


def add_terms(pool, places, h, terms):
    for e, place in enumerate(places):
        pool[place, h * HD : (h + 1) * HD] += terms[e * BLOCK : (e + 1) * BLOCK]


def gather_pool(pool, parts):
    start = 0
    for part in parts:
        pool[start : start + part.shape[0]] = part[...]
        start += part.shape[0]


def split_pool(outs, pool, factor):
    start = 0
    for out in outs:
        total = pool[start : start + out.shape[0]]
        out[...] = (total if factor is None else total * factor).astype(out.dtype)
        start += out.shape[0]


def stage_kernel(locate, count, *refs):
    sources, refs = refs[: count + 4], refs[count + 4 :]
    table, q_rows, g_rows, q_cols, g_cols, dv_pool, dk_pool, k_ref, v_ref, *refs = refs
    lists = refs[:count]
    q_ref, g_ref, sem = refs[count:]
    targets = [*lists, q_ref, g_ref, k_ref, v_ref]
    copies = [
        pltpu.make_async_copy(source, target, sem.at[i])
        for i, (source, target) in enumerate(zip(sources, targets))
    ]
    for copy in copies:
        copy.start()
    dv_pool[...] = jnp.zeros_like(dv_pool)
    dk_pool[...] = jnp.zeros_like(dk_pool)
    for copy in copies[: count + 2]:
        copy.wait()
    for b in range(table.shape[0]):
        for e, place in enumerate(locate(lists, table.shape[0], b)):
            table[b, e] = jnp.int32(place)
    for ref, rows, cols in ((q_ref, q_rows, q_cols), (g_ref, g_rows, g_cols)):
        for b, h, u in units(table.shape[0]):
            heads = [(h * GROUP + j) * HD for j in range(GROUP)]
            unit = jnp.concatenate(
                [ref[b * BLOCK : (b + 1) * BLOCK, c : c + HD] for c in heads], axis=0
            )
            rows[u * ROWS : (u + 1) * ROWS] = unit
            cols[u * HD : (u + 1) * HD] = unit.T
    for copy in copies[count + 2 :]:
        copy.wait()


def probs_kernel(count, table, q_cols, g_rows, cleared, *refs):
    parts = [*refs[: count - 2], refs[count - 1], refs[count - 2]]
    probs_ref, k_pool, dv_pool, *dv_refs = refs[count:]
    gather_pool(k_pool, parts)
    for b, h, u in units(table.shape[0]):
        places = spans(table, b)
        scores = dot(picked(k_pool, places, h), q_cols[u * HD : (u + 1) * HD], NN)
        chunks = [scores[i : i + CHUNK] for i in range(0, KEYS, CHUNK)]
        peaks = [jnp.max(chunk, axis=0, keepdims=True) for chunk in chunks]
        expos = [jnp.exp2((chunk - peak) * FACTOR) for chunk, peak in zip(chunks, peaks)]
        peak = functools.reduce(jnp.maximum, peaks)
        scales = [jnp.exp2((own - peak) * FACTOR) for own in peaks]
        norm = 1.0 / sum(jnp.sum(e, axis=0, keepdims=True) * r for e, r in zip(expos, scales))
        probs = [(e * (r * norm)).astype(jnp.bfloat16) for e, r in zip(expos, scales)]
        probs_b = jnp.concatenate(probs, axis=0)
        probs_ref[u * KEYS : (u + 1) * KEYS] = probs_b
        add_terms(dv_pool, places, h, dot(probs_b, g_rows[u * ROWS : (u + 1) * ROWS], NN))
    split_pool(dv_refs, dv_pool, None)


def dscores_kernel(count, table, q_rows, g_cols, probs_ref, cleared, *refs):
    parts = refs[:count][::-1]
    ds_ref, v_pool, dk_pool, *dk_refs = refs[count:]
    gather_pool(v_pool, parts)
    for b, h, u in units(table.shape[0]):
        places = spans(table, b)
        probs = probs_ref[u * KEYS : (u + 1) * KEYS].astype(jnp.float32)
        dprobs = dot(picked(v_pool, places, h), g_cols[u * HD : (u + 1) * HD], NN)
        delta = jnp.sum(probs * dprobs, axis=0, keepdims=True)
        dscores = (probs * (dprobs - delta)).astype(jnp.bfloat16)
        ds_ref[u * KEYS : (u + 1) * KEYS] = dscores
        add_terms(dk_pool, places, h, dot(dscores, q_rows[u * ROWS : (u + 1) * ROWS], NN))
    split_pool(dk_refs, dk_pool, SCALE)


def rows_kernel(table, probs_ref, ds_ref, k_pool, v_pool, out_any, qgrad_any, out_ref, qgrad_ref, sem):
    copies = []
    for b in range(table.shape[0]):
        places = spans(table, b)
        for h in range(KVH):
            span = slice((b * KVH + h) * KEYS, (b * KVH + h + 1) * KEYS)
            attended = dot(probs_ref[span], picked(v_pool, places, h), TN)
            unstack(out_ref, b, h, attended.astype(jnp.bfloat16))
            qgrad = dot(ds_ref[span], picked(k_pool, places, h), TN) * SCALE
            unstack(qgrad_ref, b, h, qgrad.astype(jnp.bfloat16))
        rows = pl.ds(b * BLOCK, BLOCK)
        for ref, target in ((out_ref, out_any), (qgrad_ref, qgrad_any)):
            copies.append(pltpu.make_async_copy(ref.at[rows], target.at[rows], sem.at[len(copies)]))
            copies[-1].start()
    for copy in copies:
        copy.wait()


SMEM = pl.BlockSpec(memory_space=pltpu.SMEM)
HBM = pl.BlockSpec(memory_space=pltpu.HBM)
VMEM = pl.BlockSpec(memory_space=pltpu.VMEM)


def run_kernel(kernel, operands, in_specs, results, scratch, products, out_spec=VMEM, aliases={}):
    flops = products * 2 * 4 * KVH * ROWS * KEYS * HD
    return pl.pallas_call(
        kernel,
        out_shape=[
            result if hasattr(result, "memory_space") else jax.ShapeDtypeStruct(*result)
            for result in results
        ],
        in_specs=in_specs + [VMEM] * (len(operands) - len(in_specs)),
        out_specs=[SMEM if hasattr(result, "memory_space") else out_spec for result in results],
        scratch_shapes=scratch,
        input_output_aliases=aliases,
        compiler_params=pltpu.CompilerParams(vmem_limit_bytes=32 * 2**20),
        cost_estimate=pl.CostEstimate(
            flops=flops, bytes_accessed=products * 2**20, transcendentals=0
        ),
    )(*operands)


def stage(locate, lists, queries, out_grad, keys, values, pool_rows):
    blocks_here = queries.shape[0] // BLOCK
    half = jnp.bfloat16
    rows = ((blocks_here * KVH * ROWS, HD), half)
    cols = ((blocks_here * KVH * HD, ROWS), half)
    narrow, wide = (keys.shape, half), (queries.shape, half)
    cleared = ((pool_rows, keys.shape[1]), jnp.float32)
    mine = (*lists, queries, out_grad, keys, values)
    return run_kernel(
        functools.partial(stage_kernel, locate, len(lists)),
        [pltpu.with_memory_space_constraint(array, pltpu.HBM) for array in mine],
        [HBM] * len(mine),
        [
            pltpu.SMEM((blocks_here, ENTRIES), jnp.int32),
            rows, rows, cols, cols, cleared, cleared, narrow, narrow,
        ],
        [
            *[pltpu.SMEM(array.shape, array.dtype) for array in lists],
            pltpu.VMEM(*wide), pltpu.VMEM(*wide),
            pltpu.SemaphoreType.DMA((len(mine),)),
        ],
        1,
    )


def attend(table, staged, key_parts, value_parts, send):
    q_rows, g_rows, q_cols, g_cols, dv_pool, dk_pool = staged
    tok_rows, width = key_parts[0].shape
    half, full = jnp.bfloat16, jnp.float32
    wide = ((tok_rows, GROUP * width), half)
    count = len(key_parts)
    pool_rows = sum(part.shape[0] for part in key_parts)
    held = ((table.shape[0] * KVH * KEYS, ROWS), half)
    sums = [(part.shape, half if i else full) for i, part in enumerate(key_parts)]
    pool, cleared = ((pool_rows, width), half), ((pool_rows, width), full)
    probs, k_pool, _, *dv = run_kernel(
        functools.partial(probs_kernel, count),
        (table, q_cols, g_rows, dv_pool, *key_parts[:-2], *key_parts[:-3:-1]),
        [SMEM], [held, pool, cleared, *sums], [], 2, aliases={3: 2},
    )
    dv = send(dv, None)
    dscores, v_pool, _, *dk = run_kernel(
        functools.partial(dscores_kernel, count),
        (table, q_rows, g_cols, probs, dk_pool, *value_parts[::-1]),
        [SMEM], [held, pool, cleared, *sums], [], 2, aliases={4: 2},
    )
    dk = send(dk, dv)
    dv[1], table = lax.optimization_barrier((dv[1], table))
    out, query_grad = run_kernel(
        rows_kernel, (table, probs, dscores, k_pool, v_pool), [SMEM], [wide, wide],
        [pltpu.VMEM(*wide)] * 2 + [pltpu.SemaphoreType.DMA((2 * table.shape[0],))], 2, HBM,
    )
    dv[2:], dk[-1], query_grad = lax.optimization_barrier((dv[2:], dk[-1], query_grad))
    return out, query_grad, dk, dv


def dense_local(queries, keys, values, out_grad, rand_blocks, global_blocks):
    cycle_size = lax.axis_size("seq")
    positions = lax.axis_size("dp")

    def swap(array, part):
        pairs = []
        for position in range(positions):
            offset = dense_offsets(cycle_size, position)[part]
            pairs += [(i * positions + position, (i ^ offset) * positions + position) for i in range(cycle_size)]
        return lax.ppermute(array, ("seq", "dp"), pairs)

    def send(grads, earlier):
        sent = [grads[0]] + [None] * (cycle_size - 1)
        sent[-1] = swap(grads[-1], cycle_size - 1)
        near = grads[1:-1]
        if earlier is not None:
            near, earlier[1] = lax.optimization_barrier((near, earlier[1]))
        for part in range(1, cycle_size - 1):
            sent[part] = swap(near[part - 1], part)
        return sent

    def total(grads):
        return sum(grad.astype(jnp.float32) for grad in grads).astype(jnp.bfloat16)

    parts = range(1, cycle_size)
    key_parts = [swap(keys, part) for part in parts]
    table, *staged, keys, values = stage(
        functools.partial(dense_places, cycle_size), (rand_blocks.T, global_blocks),
        queries, out_grad, keys, values, cycle_size * keys.shape[0],
    )
    value_parts = [swap(values, part) for part in parts]
    out, query_grad, dk, dv = attend(
        table, staged, [keys, *key_parts], [values, *value_parts], send
    )
    return out, query_grad, total(dk), total(dv)


def sparse_local(queries, keys, values, out_grad, rand_blocks, global_blocks):
    cycle_size = lax.axis_size("seq")
    myself = lax.axis_index("seq").astype(jnp.int32)
    tok_rows, width = keys.shape
    blocks_here = tok_rows // BLOCK
    rand_total = RAND * blocks_here
    capacity = (rand_total + GLOB + cycle_size - 1) // cycle_size
    slot_total = cycle_size * capacity
    listed = jnp.concatenate(
        [
            rand_blocks.reshape(cycle_size, rand_total),
            jnp.broadcast_to(global_blocks[None, :], (cycle_size, GLOB)),
        ],
        axis=1,
    )
    entries = listed.shape[1]
    owners = listed // blocks_here
    local_slot = listed % blocks_here
    earlier = jnp.arange(entries)[None, :] < jnp.arange(entries)[:, None]
    same_owner = owners[:, :, None] == owners[:, None, :]
    ranking = jnp.sum(same_owner & earlier[None], axis=2)
    owners_mine = lax.dynamic_index_in_dim(owners, myself, 0, keepdims=False)
    ranking_mine = lax.dynamic_index_in_dim(ranking, myself, 0, keepdims=False)
    far_place = (blocks_here + 2 + owners_mine * capacity + ranking_mine).astype(jnp.int32)
    slot_ids = jnp.arange(slot_total)
    requester = slot_ids // capacity
    position = slot_ids % capacity
    matches = (owners[requester] == myself) & (ranking[requester] == position[:, None])
    source = jnp.sum(jnp.where(matches, local_slot[requester], 0), axis=1)

    up = [(i, (i + 1) % cycle_size) for i in range(cycle_size)]
    down = [(j, i) for i, j in up]
    pair = jnp.concatenate([keys, values], axis=1)
    before = lax.ppermute(pair[tok_rows - BLOCK :], "seq", up)
    after = lax.ppermute(pair[:BLOCK], "seq", down)
    outgoing = jnp.take(pair.reshape(blocks_here, BLOCK, 2 * width), source, axis=0)
    far = lax.all_to_all(outgoing, "seq", split_axis=0, concat_axis=0, tiled=True)
    others = [before, after, far.reshape(slot_total * BLOCK, 2 * width)]
    key_parts = [part[:, :width] for part in others]
    value_parts = [part[:, width:] for part in others]

    here = jnp.arange(blocks_here, dtype=jnp.int32)[:, None]
    ahead = jnp.where(here == 0, blocks_here, here - 1)
    behind = jnp.where(here == blocks_here - 1, blocks_here + 1, here + 1)
    table = jnp.concatenate(
        [
            ahead,
            here,
            behind,
            jnp.broadcast_to(far_place[None, rand_total:], (blocks_here, GLOB)),
            far_place[:rand_total].reshape(blocks_here, RAND),
        ],
        axis=1,
    )
    landing = (source[:, None] == jnp.arange(blocks_here)[None, :]).astype(jnp.bfloat16)

    def send(grads, earlier):
        own, grad_before, grad_after, grad_far = grads
        last_rim = lax.ppermute(grad_before, "seq", down)
        first_rim = lax.ppermute(grad_after, "seq", up)
        returned = lax.all_to_all(
            grad_far.reshape(slot_total, BLOCK, width),
            "seq", split_axis=0, concat_axis=0, tiled=True,
        )
        return [own, last_rim, first_rim, returned]

    def total(grads):
        own, last_rim, first_rim, returned = grads
        landed = jnp.einsum("sq,sbx->qbx", landing, returned, preferred_element_type=jnp.float32)
        sums = own.reshape(blocks_here, BLOCK, width) + landed
        sums = sums.at[blocks_here - 1].add(last_rim.astype(jnp.float32))
        sums = sums.at[0].add(first_rim.astype(jnp.float32))
        return sums.reshape(tok_rows, width).astype(jnp.bfloat16)

    pool_rows = tok_rows + sum(part.shape[0] for part in key_parts)
    table, *staged, keys, values = stage(
        given_places, (table,), queries, out_grad, keys, values, pool_rows
    )
    out, query_grad, dk, dv = attend(
        table, staged, [keys, *key_parts], [values, *value_parts], send
    )
    return out, query_grad, total(dk), total(dv)


def local(queries, keys, values, out_grad, rand_blocks, global_blocks):
    cycle_size = lax.axis_size("seq")
    blocks_here = queries.shape[0] // BLOCK
    capacity = (RAND * blocks_here + GLOB + cycle_size - 1) // cycle_size
    dense = capacity >= blocks_here and cycle_size == 4
    plan = dense_local if dense else sparse_local
    return plan(queries, keys, values, out_grad, rand_blocks, global_blocks)


def solution(mesh):
    rows = P(("dp", "seq"), None)
    return jax.shard_map(
        local,
        mesh=mesh,
        in_specs=(rows, rows, rows, rows, P("dp", None), P("dp")),
        out_specs=(rows, rows, rows, rows),
        check_vma=False,
    )
```

```python
import functools

import jax
import jax.numpy as jnp
from jax import lax
from jax.experimental import pallas as pl
from jax.experimental.pallas import tpu as pltpu
from jax.sharding import PartitionSpec as P

KVH = 2
HD = 128
BLOCK = 64
GLOB = 2
RAND = 3
GROUP = 4
ENTRIES = 3 + GLOB + RAND
LOG2E = 1.4426950408889634
SCALE = HD ** (-0.5)


NN = (((1,), (0,)), ((), ()))
TN = (((0,), (0,)), ((), ()))
dot = functools.partial(lax.dot_general, preferred_element_type=jnp.float32)

KEYS = ENTRIES * BLOCK
CHUNK = 128
FACTOR = SCALE * LOG2E
ROWS = GROUP * BLOCK


def units(blocks_here):
    return [(b, h, b * KVH + h) for b in range(blocks_here) for h in range(KVH)]


def given_places(lists, blocks_here, b):
    return [lists[0][b, e] for e in range(ENTRIES)]


def dense_offsets(cycle_size, position):
    odd = position & 1
    offsets = list(range(cycle_size))
    offsets[1], offsets[2] = 1 + odd, 2 - odd
    return offsets


def dense_places(cycle_size, lists, blocks_here, b):
    rand_ref, glob_ref = lists
    me = lax.axis_index("seq").astype(jnp.int32)
    odd = lax.axis_index("dp").astype(jnp.int32) & 1

    def place(owner, local):
        offset = owner ^ me
        swapped = (odd == 1) & ((offset == 1) | (offset == 2))
        return jnp.where(swapped, 3 - offset, offset) * blocks_here + local

    def far_place(block):
        return place(lax.div(block, blocks_here), lax.rem(block, blocks_here))

    window = [b - 1, b, b + 1]
    if b == 0:
        window[0] = place(lax.rem(me + cycle_size - 1, cycle_size), blocks_here - 1)
    if b == blocks_here - 1:
        window[2] = place(lax.rem(me + 1, cycle_size), 0)
    far = [glob_ref[i] for i in range(GLOB)] + [rand_ref[i, me * blocks_here + b] for i in range(RAND)]
    return window + [far_place(block) for block in far]


def spans(table, b):
    result = []
    for e in range(ENTRIES):
        near = b + e - 1
        if e < 3 and 0 <= near < table.shape[0]:
            result.append(pl.ds(near * BLOCK, BLOCK))
        else:
            result.append(pl.ds(pl.multiple_of(table[b, e] * BLOCK, BLOCK), BLOCK))
    return result


def picked(pool, places, h):
    return jnp.concatenate([pool[place, h * HD : (h + 1) * HD] for place in places], axis=0)


def unstack(ref, b, h, value):
    for j in range(GROUP):
        c = (h * GROUP + j) * HD
        ref[b * BLOCK : (b + 1) * BLOCK, c : c + HD] = value[j * BLOCK : (j + 1) * BLOCK]


def add_terms(pool, places, h, terms):
    for e, place in enumerate(places):
        pool[place, h * HD : (h + 1) * HD] += terms[e * BLOCK : (e + 1) * BLOCK]


def gather_pool(pool, parts):
    start = 0
    for part in parts:
        pool[start : start + part.shape[0]] = part[...]
        start += part.shape[0]


def split_pool(outs, pool, factor):
    start = 0
    for out in outs:
        total = pool[start : start + out.shape[0]]
        out[...] = (total if factor is None else total * factor).astype(out.dtype)
        start += out.shape[0]


def stage_kernel(locate, count, *refs):
    sources, refs = refs[: count + 4], refs[count + 4 :]
    table, q_rows, g_rows, q_cols, g_cols, dv_pool, dk_pool, k_ref, v_ref, *refs = refs
    lists = refs[:count]
    q_ref, g_ref, sem = refs[count:]
    targets = [*lists, q_ref, g_ref, k_ref, v_ref]
    copies = [
        pltpu.make_async_copy(source, target, sem.at[i])
        for i, (source, target) in enumerate(zip(sources, targets))
    ]
    for copy in copies:
        copy.start()
    dv_pool[...] = jnp.zeros_like(dv_pool)
    dk_pool[...] = jnp.zeros_like(dk_pool)
    for copy in copies[: count + 2]:
        copy.wait()
    for b in range(table.shape[0]):
        for e, place in enumerate(locate(lists, table.shape[0], b)):
            table[b, e] = jnp.int32(place)
    for ref, rows, cols in ((q_ref, q_rows, q_cols), (g_ref, g_rows, g_cols)):
        for b, h, u in units(table.shape[0]):
            heads = [(h * GROUP + j) * HD for j in range(GROUP)]
            unit = jnp.concatenate(
                [ref[b * BLOCK : (b + 1) * BLOCK, c : c + HD] for c in heads], axis=0
            )
            rows[u * ROWS : (u + 1) * ROWS] = unit
            cols[u * HD : (u + 1) * HD] = unit.T
    for copy in copies[count + 2 :]:
        copy.wait()


def probs_kernel(count, table, q_cols, g_rows, cleared, *refs):
    parts = refs[:count][::-1]
    probs_ref, k_pool, dv_pool, *dv_refs = refs[count:]
    gather_pool(k_pool, parts)
    for b, h, u in units(table.shape[0]):
        places = spans(table, b)
        scores = dot(picked(k_pool, places, h), q_cols[u * HD : (u + 1) * HD], NN)
        chunks = [scores[i : i + CHUNK] for i in range(0, KEYS, CHUNK)]
        peaks = [jnp.max(chunk, axis=0, keepdims=True) for chunk in chunks]
        expos = [jnp.exp2((chunk - peak) * FACTOR) for chunk, peak in zip(chunks, peaks)]
        peak = functools.reduce(jnp.maximum, peaks)
        scales = [jnp.exp2((own - peak) * FACTOR) for own in peaks]
        norm = 1.0 / sum(jnp.sum(e, axis=0, keepdims=True) * r for e, r in zip(expos, scales))
        probs = [(e * (r * norm)).astype(jnp.bfloat16) for e, r in zip(expos, scales)]
        probs_b = jnp.concatenate(probs, axis=0)
        probs_ref[u * KEYS : (u + 1) * KEYS] = probs_b
        add_terms(dv_pool, places, h, dot(probs_b, g_rows[u * ROWS : (u + 1) * ROWS], NN))
    split_pool(dv_refs, dv_pool, None)


def dscores_kernel(count, table, q_rows, g_cols, probs_ref, cleared, *refs):
    parts = refs[:count][::-1]
    ds_ref, v_pool, dk_pool, *dk_refs = refs[count:]
    gather_pool(v_pool, parts)
    for b, h, u in units(table.shape[0]):
        places = spans(table, b)
        probs = probs_ref[u * KEYS : (u + 1) * KEYS].astype(jnp.float32)
        dprobs = dot(picked(v_pool, places, h), g_cols[u * HD : (u + 1) * HD], NN)
        delta = jnp.sum(probs * dprobs, axis=0, keepdims=True)
        dscores = (probs * (dprobs - delta)).astype(jnp.bfloat16)
        ds_ref[u * KEYS : (u + 1) * KEYS] = dscores
        add_terms(dk_pool, places, h, dot(dscores, q_rows[u * ROWS : (u + 1) * ROWS], NN))
    split_pool(dk_refs, dk_pool, SCALE)


def rows_kernel(table, probs_ref, ds_ref, k_pool, v_pool, out_any, qgrad_any, out_ref, qgrad_ref, sem):
    copies = []
    for b in range(table.shape[0]):
        places = spans(table, b)
        for h in range(KVH):
            span = slice((b * KVH + h) * KEYS, (b * KVH + h + 1) * KEYS)
            attended = dot(probs_ref[span], picked(v_pool, places, h), TN)
            unstack(out_ref, b, h, attended.astype(jnp.bfloat16))
            qgrad = dot(ds_ref[span], picked(k_pool, places, h), TN) * SCALE
            unstack(qgrad_ref, b, h, qgrad.astype(jnp.bfloat16))
        rows = pl.ds(b * BLOCK, BLOCK)
        for ref, target in ((out_ref, out_any), (qgrad_ref, qgrad_any)):
            copies.append(pltpu.make_async_copy(ref.at[rows], target.at[rows], sem.at[len(copies)]))
            copies[-1].start()
    for copy in copies:
        copy.wait()


def total_kernel(*refs):
    *parts, out_any, out_ref, sem = refs
    copies = []
    for i in range(0, out_ref.shape[0], BLOCK):
        rows = pl.ds(i, BLOCK)
        total = sum(part[rows].astype(jnp.float32) for part in parts)
        out_ref[rows] = total.astype(out_ref.dtype)
        copies.append(pltpu.make_async_copy(out_ref.at[rows], out_any.at[rows], sem.at[len(copies)]))
        copies[-1].start()
    for copy in copies:
        copy.wait()


SMEM = pl.BlockSpec(memory_space=pltpu.SMEM)
HBM = pl.BlockSpec(memory_space=pltpu.HBM)
VMEM = pl.BlockSpec(memory_space=pltpu.VMEM)


def run_kernel(kernel, operands, in_specs, results, scratch, products, out_spec=VMEM, aliases={}):
    flops = products * 2 * 4 * KVH * ROWS * KEYS * HD
    return pl.pallas_call(
        kernel,
        out_shape=[
            result if hasattr(result, "memory_space") else jax.ShapeDtypeStruct(*result)
            for result in results
        ],
        in_specs=in_specs + [VMEM] * (len(operands) - len(in_specs)),
        out_specs=[SMEM if hasattr(result, "memory_space") else out_spec for result in results],
        scratch_shapes=scratch,
        input_output_aliases=aliases,
        compiler_params=pltpu.CompilerParams(vmem_limit_bytes=32 * 2**20),
        cost_estimate=pl.CostEstimate(
            flops=flops, bytes_accessed=products * 2**20, transcendentals=0
        ),
    )(*operands)


def stage(locate, lists, queries, out_grad, keys, values, pool_rows):
    blocks_here = queries.shape[0] // BLOCK
    half = jnp.bfloat16
    rows = ((blocks_here * KVH * ROWS, HD), half)
    cols = ((blocks_here * KVH * HD, ROWS), half)
    narrow, wide = (keys.shape, half), (queries.shape, half)
    cleared = ((pool_rows, keys.shape[1]), jnp.float32)
    mine = (*lists, queries, out_grad, keys, values)
    return run_kernel(
        functools.partial(stage_kernel, locate, len(lists)),
        [pltpu.with_memory_space_constraint(array, pltpu.HBM) for array in mine],
        [HBM] * len(mine),
        [
            pltpu.SMEM((blocks_here, ENTRIES), jnp.int32),
            rows, rows, cols, cols, cleared, cleared, narrow, narrow,
        ],
        [
            *[pltpu.SMEM(array.shape, array.dtype) for array in lists],
            pltpu.VMEM(*wide), pltpu.VMEM(*wide),
            pltpu.SemaphoreType.DMA((len(mine),)),
        ],
        1,
    )


def attend(table, staged, key_parts, value_parts, send):
    q_rows, g_rows, q_cols, g_cols, dv_pool, dk_pool = staged
    tok_rows, width = key_parts[0].shape
    half, full = jnp.bfloat16, jnp.float32
    wide = ((tok_rows, GROUP * width), half)
    count = len(key_parts)
    pool_rows = sum(part.shape[0] for part in key_parts)
    held = ((table.shape[0] * KVH * KEYS, ROWS), half)
    sums = [(part.shape, half if i else full) for i, part in enumerate(key_parts)]
    pool, cleared = ((pool_rows, width), half), ((pool_rows, width), full)
    probs, k_pool, _, *dv = run_kernel(
        functools.partial(probs_kernel, count),
        (table, q_cols, g_rows, dv_pool, *key_parts[::-1]),
        [SMEM], [held, pool, cleared, *sums], [], 2, aliases={3: 2},
    )
    dv = send(dv, None)
    dscores, v_pool, _, *dk = run_kernel(
        functools.partial(dscores_kernel, count),
        (table, q_rows, g_cols, probs, dk_pool, *value_parts[::-1]),
        [SMEM], [held, pool, cleared, *sums], [], 2, aliases={4: 2},
    )
    dk = send(dk, dv)
    dv[1], table = lax.optimization_barrier((dv[1], table))
    out, query_grad = run_kernel(
        rows_kernel, (table, probs, dscores, k_pool, v_pool), [SMEM], [wide, wide],
        [pltpu.VMEM(*wide)] * 2 + [pltpu.SemaphoreType.DMA((2 * table.shape[0],))], 2, HBM,
    )
    dv[2:], dk[-1], query_grad = lax.optimization_barrier((dv[2:], dk[-1], query_grad))
    return out, query_grad, dk, dv


def dense_local(queries, keys, values, out_grad, rand_blocks, global_blocks):
    cycle_size = lax.axis_size("seq")
    positions = lax.axis_size("dp")

    def swap(array, part):
        pairs = []
        for position in range(positions):
            offset = dense_offsets(cycle_size, position)[part]
            pairs += [(i * positions + position, (i ^ offset) * positions + position) for i in range(cycle_size)]
        return lax.ppermute(array, ("seq", "dp"), pairs)

    def send(grads, earlier):
        sent = [grads[0]] + [None] * (cycle_size - 1)
        sent[-1] = swap(grads[-1], cycle_size - 1)
        near = grads[1:-1]
        if earlier is not None:
            near, earlier[1] = lax.optimization_barrier((near, earlier[1]))
        for part in range(1, cycle_size - 1):
            sent[part] = swap(near[part - 1], part)
        return sent

    def total(grads):
        result = (grads[0].shape, jnp.bfloat16)
        semaphores = pltpu.SemaphoreType.DMA((grads[0].shape[0] // BLOCK,))
        scratch = [pltpu.VMEM(*result), semaphores]
        return run_kernel(total_kernel, grads, [], [result], scratch, 0, HBM)[0]

    parts = range(1, cycle_size)
    key_parts = [swap(keys, part) for part in parts]
    table, *staged, keys, values = stage(
        functools.partial(dense_places, cycle_size), (rand_blocks.T, global_blocks),
        queries, out_grad, keys, values, cycle_size * keys.shape[0],
    )
    value_parts = [swap(values, part) for part in parts]
    out, query_grad, dk, dv = attend(
        table, staged, [keys, *key_parts], [values, *value_parts], send
    )
    return out, query_grad, total(dk), total(dv)


def sparse_local(queries, keys, values, out_grad, rand_blocks, global_blocks):
    cycle_size = lax.axis_size("seq")
    myself = lax.axis_index("seq").astype(jnp.int32)
    tok_rows, width = keys.shape
    blocks_here = tok_rows // BLOCK
    rand_total = RAND * blocks_here
    capacity = (rand_total + GLOB + cycle_size - 1) // cycle_size
    slot_total = cycle_size * capacity
    listed = jnp.concatenate(
        [
            rand_blocks.reshape(cycle_size, rand_total),
            jnp.broadcast_to(global_blocks[None, :], (cycle_size, GLOB)),
        ],
        axis=1,
    )
    entries = listed.shape[1]
    owners = listed // blocks_here
    local_slot = listed % blocks_here
    earlier = jnp.arange(entries)[None, :] < jnp.arange(entries)[:, None]
    same_owner = owners[:, :, None] == owners[:, None, :]
    ranking = jnp.sum(same_owner & earlier[None], axis=2)
    owners_mine = lax.dynamic_index_in_dim(owners, myself, 0, keepdims=False)
    ranking_mine = lax.dynamic_index_in_dim(ranking, myself, 0, keepdims=False)
    far_place = (blocks_here + 2 + owners_mine * capacity + ranking_mine).astype(jnp.int32)
    slot_ids = jnp.arange(slot_total)
    requester = slot_ids // capacity
    position = slot_ids % capacity
    matches = (owners[requester] == myself) & (ranking[requester] == position[:, None])
    source = jnp.sum(jnp.where(matches, local_slot[requester], 0), axis=1)

    up = [(i, (i + 1) % cycle_size) for i in range(cycle_size)]
    down = [(j, i) for i, j in up]
    pair = jnp.concatenate([keys, values], axis=1)
    before = lax.ppermute(pair[tok_rows - BLOCK :], "seq", up)
    after = lax.ppermute(pair[:BLOCK], "seq", down)
    outgoing = jnp.take(pair.reshape(blocks_here, BLOCK, 2 * width), source, axis=0)
    far = lax.all_to_all(outgoing, "seq", split_axis=0, concat_axis=0, tiled=True)
    others = [before, after, far.reshape(slot_total * BLOCK, 2 * width)]
    key_parts = [part[:, :width] for part in others]
    value_parts = [part[:, width:] for part in others]

    here = jnp.arange(blocks_here, dtype=jnp.int32)[:, None]
    ahead = jnp.where(here == 0, blocks_here, here - 1)
    behind = jnp.where(here == blocks_here - 1, blocks_here + 1, here + 1)
    table = jnp.concatenate(
        [
            ahead,
            here,
            behind,
            jnp.broadcast_to(far_place[None, rand_total:], (blocks_here, GLOB)),
            far_place[:rand_total].reshape(blocks_here, RAND),
        ],
        axis=1,
    )
    landing = (source[:, None] == jnp.arange(blocks_here)[None, :]).astype(jnp.bfloat16)

    def send(grads, earlier):
        own, grad_before, grad_after, grad_far = grads
        last_rim = lax.ppermute(grad_before, "seq", down)
        first_rim = lax.ppermute(grad_after, "seq", up)
        returned = lax.all_to_all(
            grad_far.reshape(slot_total, BLOCK, width),
            "seq", split_axis=0, concat_axis=0, tiled=True,
        )
        return [own, last_rim, first_rim, returned]

    def total(grads):
        own, last_rim, first_rim, returned = grads
        landed = jnp.einsum("sq,sbx->qbx", landing, returned, preferred_element_type=jnp.float32)
        sums = own.reshape(blocks_here, BLOCK, width) + landed
        sums = sums.at[blocks_here - 1].add(last_rim.astype(jnp.float32))
        sums = sums.at[0].add(first_rim.astype(jnp.float32))
        return sums.reshape(tok_rows, width).astype(jnp.bfloat16)

    pool_rows = tok_rows + sum(part.shape[0] for part in key_parts)
    table, *staged, keys, values = stage(
        given_places, (table,), queries, out_grad, keys, values, pool_rows
    )
    out, query_grad, dk, dv = attend(
        table, staged, [keys, *key_parts], [values, *value_parts], send
    )
    return out, query_grad, total(dk), total(dv)


def local(queries, keys, values, out_grad, rand_blocks, global_blocks):
    cycle_size = lax.axis_size("seq")
    blocks_here = queries.shape[0] // BLOCK
    capacity = (RAND * blocks_here + GLOB + cycle_size - 1) // cycle_size
    dense = capacity >= blocks_here and cycle_size == 4
    plan = dense_local if dense else sparse_local
    return plan(queries, keys, values, out_grad, rand_blocks, global_blocks)


def solution(mesh):
    rows = P(("dp", "seq"), None)
    return jax.shard_map(
        local,
        mesh=mesh,
        in_specs=(rows, rows, rows, rows, P("dp", None), P("dp")),
        out_specs=(rows, rows, rows, rows),
        check_vma=False,
    )
```

```python
import functools

import jax
import jax.numpy as jnp
from jax import lax
from jax.experimental import pallas as pl
from jax.experimental.pallas import tpu as pltpu
from jax.sharding import PartitionSpec as P

KVH = 2
HD = 128
BLOCK = 64
GLOB = 2
RAND = 3
GROUP = 4
ENTRIES = 3 + GLOB + RAND
LOG2E = 1.4426950408889634
SCALE = HD ** (-0.5)


NN = (((1,), (0,)), ((), ()))
TN = (((0,), (0,)), ((), ()))
dot = functools.partial(lax.dot_general, preferred_element_type=jnp.float32)

KEYS = ENTRIES * BLOCK
CHUNK = 64
FACTOR = SCALE * LOG2E
ROWS = GROUP * BLOCK


def units(blocks_here):
    return [(b, h, b * KVH + h) for b in range(blocks_here) for h in range(KVH)]


def given_places(lists, blocks_here, b):
    return [lists[0][b, e] for e in range(ENTRIES)]


def dense_offsets(cycle_size, position):
    odd = position & 1
    offsets = list(range(cycle_size))
    offsets[1], offsets[2] = 1 + odd, 2 - odd
    return offsets


def dense_places(cycle_size, lists, blocks_here, b):
    rand_ref, glob_ref = lists
    me = lax.axis_index("seq").astype(jnp.int32)
    odd = lax.axis_index("dp").astype(jnp.int32) & 1

    def place(owner, local):
        offset = owner ^ me
        swapped = (odd == 1) & ((offset == 1) | (offset == 2))
        return jnp.where(swapped, 3 - offset, offset) * blocks_here + local

    def far_place(block):
        return place(lax.div(block, blocks_here), lax.rem(block, blocks_here))

    window = [b - 1, b, b + 1]
    if b == 0:
        window[0] = place(lax.rem(me + cycle_size - 1, cycle_size), blocks_here - 1)
    if b == blocks_here - 1:
        window[2] = place(lax.rem(me + 1, cycle_size), 0)
    far = [glob_ref[i] for i in range(GLOB)] + [rand_ref[i, me * blocks_here + b] for i in range(RAND)]
    return window + [far_place(block) for block in far]


def spans(table, b):
    result = []
    for e in range(ENTRIES):
        near = b + e - 1
        if e < 3 and 0 <= near < table.shape[0]:
            result.append(pl.ds(near * BLOCK, BLOCK))
        else:
            result.append(pl.ds(pl.multiple_of(table[b, e] * BLOCK, BLOCK), BLOCK))
    return result


def picked(pool, places, h):
    return jnp.concatenate([pool[place, h * HD : (h + 1) * HD] for place in places], axis=0)


def unstack(ref, b, h, value):
    for j in range(GROUP):
        c = (h * GROUP + j) * HD
        ref[b * BLOCK : (b + 1) * BLOCK, c : c + HD] = value[j * BLOCK : (j + 1) * BLOCK]


def add_terms(pool, places, h, terms):
    for e, place in enumerate(places):
        pool[place, h * HD : (h + 1) * HD] += terms[e * BLOCK : (e + 1) * BLOCK]


def gather_pool(pool, parts):
    start = 0
    for part in parts:
        pool[start : start + part.shape[0]] = part[...]
        start += part.shape[0]


def split_pool(outs, pool, factor):
    start = 0
    for out in outs:
        total = pool[start : start + out.shape[0]]
        out[...] = (total if factor is None else total * factor).astype(out.dtype)
        start += out.shape[0]


def stage_kernel(locate, count, *refs):
    sources, refs = refs[: count + 4], refs[count + 4 :]
    table, q_rows, g_rows, q_cols, g_cols, dv_pool, dk_pool, k_ref, v_ref, *refs = refs
    lists = refs[:count]
    q_ref, g_ref, sem = refs[count:]
    targets = [*lists, q_ref, g_ref, k_ref, v_ref]
    copies = [
        pltpu.make_async_copy(source, target, sem.at[i])
        for i, (source, target) in enumerate(zip(sources, targets))
    ]
    for copy in copies:
        copy.start()
    dv_pool[...] = jnp.zeros_like(dv_pool)
    dk_pool[...] = jnp.zeros_like(dk_pool)
    for copy in copies[: count + 2]:
        copy.wait()
    for b in range(table.shape[0]):
        for e, place in enumerate(locate(lists, table.shape[0], b)):
            table[b, e] = jnp.int32(place)
    for ref, rows, cols in ((q_ref, q_rows, q_cols), (g_ref, g_rows, g_cols)):
        for b, h, u in units(table.shape[0]):
            heads = [(h * GROUP + j) * HD for j in range(GROUP)]
            unit = jnp.concatenate(
                [ref[b * BLOCK : (b + 1) * BLOCK, c : c + HD] for c in heads], axis=0
            )
            rows[u * ROWS : (u + 1) * ROWS] = unit
            cols[u * HD : (u + 1) * HD] = unit.T
    for copy in copies[count + 2 :]:
        copy.wait()


def probs_kernel(count, table, q_cols, g_rows, cleared, *refs):
    parts = refs[:count][::-1]
    probs_ref, k_pool, dv_pool, *dv_refs = refs[count:]
    gather_pool(k_pool, parts)
    for b, h, u in units(table.shape[0]):
        places = spans(table, b)
        scores = dot(picked(k_pool, places, h), q_cols[u * HD : (u + 1) * HD], NN)
        chunks = [scores[i : i + CHUNK] for i in range(0, KEYS, CHUNK)]
        peaks = [jnp.max(chunk, axis=0, keepdims=True) for chunk in chunks]
        expos = [jnp.exp2((chunk - peak) * FACTOR) for chunk, peak in zip(chunks, peaks)]
        peak = functools.reduce(jnp.maximum, peaks)
        scales = [jnp.exp2((own - peak) * FACTOR) for own in peaks]
        norm = 1.0 / sum(jnp.sum(e, axis=0, keepdims=True) * r for e, r in zip(expos, scales))
        probs = [(e * (r * norm)).astype(jnp.bfloat16) for e, r in zip(expos, scales)]
        probs_b = jnp.concatenate(probs, axis=0)
        probs_ref[u * KEYS : (u + 1) * KEYS] = probs_b
        add_terms(dv_pool, places, h, dot(probs_b, g_rows[u * ROWS : (u + 1) * ROWS], NN))
    split_pool(dv_refs, dv_pool, None)


def dscores_kernel(count, table, q_rows, g_cols, probs_ref, cleared, *refs):
    parts = refs[:count][::-1]
    ds_ref, v_pool, dk_pool, *dk_refs = refs[count:]
    gather_pool(v_pool, parts)
    for b, h, u in units(table.shape[0]):
        places = spans(table, b)
        probs = probs_ref[u * KEYS : (u + 1) * KEYS].astype(jnp.float32)
        dprobs = dot(picked(v_pool, places, h), g_cols[u * HD : (u + 1) * HD], NN)
        delta = jnp.sum(probs * dprobs, axis=0, keepdims=True)
        dscores = (probs * (dprobs - delta)).astype(jnp.bfloat16)
        ds_ref[u * KEYS : (u + 1) * KEYS] = dscores
        add_terms(dk_pool, places, h, dot(dscores, q_rows[u * ROWS : (u + 1) * ROWS], NN))
    split_pool(dk_refs, dk_pool, SCALE)


def rows_kernel(table, probs_ref, ds_ref, k_pool, v_pool, out_any, qgrad_any, out_ref, qgrad_ref, sem):
    copies = []
    for b in range(table.shape[0]):
        places = spans(table, b)
        for h in range(KVH):
            span = slice((b * KVH + h) * KEYS, (b * KVH + h + 1) * KEYS)
            attended = dot(probs_ref[span], picked(v_pool, places, h), TN)
            unstack(out_ref, b, h, attended.astype(jnp.bfloat16))
            qgrad = dot(ds_ref[span], picked(k_pool, places, h), TN) * SCALE
            unstack(qgrad_ref, b, h, qgrad.astype(jnp.bfloat16))
        rows = pl.ds(b * BLOCK, BLOCK)
        for ref, target in ((out_ref, out_any), (qgrad_ref, qgrad_any)):
            copies.append(pltpu.make_async_copy(ref.at[rows], target.at[rows], sem.at[len(copies)]))
            copies[-1].start()
    for copy in copies:
        copy.wait()


def total_kernel(*refs):
    *parts, out_any, out_ref, sem = refs
    copies = []
    for i in range(0, out_ref.shape[0], BLOCK):
        rows = pl.ds(i, BLOCK)
        total = sum(part[rows].astype(jnp.float32) for part in parts)
        out_ref[rows] = total.astype(out_ref.dtype)
        copies.append(pltpu.make_async_copy(out_ref.at[rows], out_any.at[rows], sem.at[len(copies)]))
        copies[-1].start()
    for copy in copies:
        copy.wait()


SMEM = pl.BlockSpec(memory_space=pltpu.SMEM)
HBM = pl.BlockSpec(memory_space=pltpu.HBM)
VMEM = pl.BlockSpec(memory_space=pltpu.VMEM)


def run_kernel(kernel, operands, in_specs, results, scratch, products, out_spec=VMEM, aliases={}):
    flops = products * 2 * 4 * KVH * ROWS * KEYS * HD
    return pl.pallas_call(
        kernel,
        out_shape=[
            result if hasattr(result, "memory_space") else jax.ShapeDtypeStruct(*result)
            for result in results
        ],
        in_specs=in_specs + [VMEM] * (len(operands) - len(in_specs)),
        out_specs=[SMEM if hasattr(result, "memory_space") else out_spec for result in results],
        scratch_shapes=scratch,
        input_output_aliases=aliases,
        compiler_params=pltpu.CompilerParams(vmem_limit_bytes=32 * 2**20),
        cost_estimate=pl.CostEstimate(
            flops=flops, bytes_accessed=products * 2**20, transcendentals=0
        ),
    )(*operands)


def stage(locate, lists, queries, out_grad, keys, values, pool_rows):
    blocks_here = queries.shape[0] // BLOCK
    half = jnp.bfloat16
    rows = ((blocks_here * KVH * ROWS, HD), half)
    cols = ((blocks_here * KVH * HD, ROWS), half)
    narrow, wide = (keys.shape, half), (queries.shape, half)
    cleared = ((pool_rows, keys.shape[1]), jnp.float32)
    mine = (*lists, queries, out_grad, keys, values)
    return run_kernel(
        functools.partial(stage_kernel, locate, len(lists)),
        [pltpu.with_memory_space_constraint(array, pltpu.HBM) for array in mine],
        [HBM] * len(mine),
        [
            pltpu.SMEM((blocks_here, ENTRIES), jnp.int32),
            rows, rows, cols, cols, cleared, cleared, narrow, narrow,
        ],
        [
            *[pltpu.SMEM(array.shape, array.dtype) for array in lists],
            pltpu.VMEM(*wide), pltpu.VMEM(*wide),
            pltpu.SemaphoreType.DMA((len(mine),)),
        ],
        1,
    )


def attend(table, staged, key_parts, value_parts, send):
    q_rows, g_rows, q_cols, g_cols, dv_pool, dk_pool = staged
    tok_rows, width = key_parts[0].shape
    half, full = jnp.bfloat16, jnp.float32
    wide = ((tok_rows, GROUP * width), half)
    count = len(key_parts)
    pool_rows = sum(part.shape[0] for part in key_parts)
    held = ((table.shape[0] * KVH * KEYS, ROWS), half)
    sums = [(part.shape, half if i else full) for i, part in enumerate(key_parts)]
    pool, cleared = ((pool_rows, width), half), ((pool_rows, width), full)
    probs, k_pool, _, *dv = run_kernel(
        functools.partial(probs_kernel, count),
        (table, q_cols, g_rows, dv_pool, *key_parts[::-1]),
        [SMEM], [held, pool, cleared, *sums], [], 2, aliases={3: 2},
    )
    dv = send(dv, None)
    dscores, v_pool, _, *dk = run_kernel(
        functools.partial(dscores_kernel, count),
        (table, q_rows, g_cols, probs, dk_pool, *value_parts[::-1]),
        [SMEM], [held, pool, cleared, *sums], [], 2, aliases={4: 2},
    )
    dk = send(dk, dv)
    dv[1], table = lax.optimization_barrier((dv[1], table))
    out, query_grad = run_kernel(
        rows_kernel, (table, probs, dscores, k_pool, v_pool), [SMEM], [wide, wide],
        [pltpu.VMEM(*wide)] * 2 + [pltpu.SemaphoreType.DMA((2 * table.shape[0],))], 2, HBM,
    )
    dv[2:], dk[-1], query_grad = lax.optimization_barrier((dv[2:], dk[-1], query_grad))
    return out, query_grad, dk, dv


def dense_local(queries, keys, values, out_grad, rand_blocks, global_blocks):
    cycle_size = lax.axis_size("seq")
    positions = lax.axis_size("dp")

    def swap(array, part):
        pairs = []
        for position in range(positions):
            offset = dense_offsets(cycle_size, position)[part]
            pairs += [(i * positions + position, (i ^ offset) * positions + position) for i in range(cycle_size)]
        return lax.ppermute(array, ("seq", "dp"), pairs)

    def send(grads, earlier):
        sent = [grads[0]] + [None] * (cycle_size - 1)
        sent[-1] = swap(grads[-1], cycle_size - 1)
        near = grads[1:-1]
        if earlier is not None:
            near, earlier[1] = lax.optimization_barrier((near, earlier[1]))
        for part in range(1, cycle_size - 1):
            sent[part] = swap(near[part - 1], part)
        return sent

    def total(grads):
        result = (grads[0].shape, jnp.bfloat16)
        semaphores = pltpu.SemaphoreType.DMA((grads[0].shape[0] // BLOCK,))
        scratch = [pltpu.VMEM(*result), semaphores]
        return run_kernel(total_kernel, grads, [], [result], scratch, 0, HBM)[0]

    parts = range(1, cycle_size)
    key_parts = [swap(keys, part) for part in parts]
    table, *staged, keys, values = stage(
        functools.partial(dense_places, cycle_size), (rand_blocks.T, global_blocks),
        queries, out_grad, keys, values, cycle_size * keys.shape[0],
    )
    value_parts = [swap(values, part) for part in parts]
    out, query_grad, dk, dv = attend(
        table, staged, [keys, *key_parts], [values, *value_parts], send
    )
    return out, query_grad, total(dk), total(dv)


def sparse_local(queries, keys, values, out_grad, rand_blocks, global_blocks):
    cycle_size = lax.axis_size("seq")
    myself = lax.axis_index("seq").astype(jnp.int32)
    tok_rows, width = keys.shape
    blocks_here = tok_rows // BLOCK
    rand_total = RAND * blocks_here
    capacity = (rand_total + GLOB + cycle_size - 1) // cycle_size
    slot_total = cycle_size * capacity
    listed = jnp.concatenate(
        [
            rand_blocks.reshape(cycle_size, rand_total),
            jnp.broadcast_to(global_blocks[None, :], (cycle_size, GLOB)),
        ],
        axis=1,
    )
    entries = listed.shape[1]
    owners = listed // blocks_here
    local_slot = listed % blocks_here
    earlier = jnp.arange(entries)[None, :] < jnp.arange(entries)[:, None]
    same_owner = owners[:, :, None] == owners[:, None, :]
    ranking = jnp.sum(same_owner & earlier[None], axis=2)
    owners_mine = lax.dynamic_index_in_dim(owners, myself, 0, keepdims=False)
    ranking_mine = lax.dynamic_index_in_dim(ranking, myself, 0, keepdims=False)
    far_place = (blocks_here + 2 + owners_mine * capacity + ranking_mine).astype(jnp.int32)
    slot_ids = jnp.arange(slot_total)
    requester = slot_ids // capacity
    position = slot_ids % capacity
    matches = (owners[requester] == myself) & (ranking[requester] == position[:, None])
    source = jnp.sum(jnp.where(matches, local_slot[requester], 0), axis=1)

    up = [(i, (i + 1) % cycle_size) for i in range(cycle_size)]
    down = [(j, i) for i, j in up]
    pair = jnp.concatenate([keys, values], axis=1)
    before = lax.ppermute(pair[tok_rows - BLOCK :], "seq", up)
    after = lax.ppermute(pair[:BLOCK], "seq", down)
    outgoing = jnp.take(pair.reshape(blocks_here, BLOCK, 2 * width), source, axis=0)
    far = lax.all_to_all(outgoing, "seq", split_axis=0, concat_axis=0, tiled=True)
    others = [before, after, far.reshape(slot_total * BLOCK, 2 * width)]
    key_parts = [part[:, :width] for part in others]
    value_parts = [part[:, width:] for part in others]

    here = jnp.arange(blocks_here, dtype=jnp.int32)[:, None]
    ahead = jnp.where(here == 0, blocks_here, here - 1)
    behind = jnp.where(here == blocks_here - 1, blocks_here + 1, here + 1)
    table = jnp.concatenate(
        [
            ahead,
            here,
            behind,
            jnp.broadcast_to(far_place[None, rand_total:], (blocks_here, GLOB)),
            far_place[:rand_total].reshape(blocks_here, RAND),
        ],
        axis=1,
    )
    landing = (source[:, None] == jnp.arange(blocks_here)[None, :]).astype(jnp.bfloat16)

    def send(grads, earlier):
        own, grad_before, grad_after, grad_far = grads
        last_rim = lax.ppermute(grad_before, "seq", down)
        first_rim = lax.ppermute(grad_after, "seq", up)
        returned = lax.all_to_all(
            grad_far.reshape(slot_total, BLOCK, width),
            "seq", split_axis=0, concat_axis=0, tiled=True,
        )
        return [own, last_rim, first_rim, returned]

    def total(grads):
        own, last_rim, first_rim, returned = grads
        landed = jnp.einsum("sq,sbx->qbx", landing, returned, preferred_element_type=jnp.float32)
        sums = own.reshape(blocks_here, BLOCK, width) + landed
        sums = sums.at[blocks_here - 1].add(last_rim.astype(jnp.float32))
        sums = sums.at[0].add(first_rim.astype(jnp.float32))
        return sums.reshape(tok_rows, width).astype(jnp.bfloat16)

    pool_rows = tok_rows + sum(part.shape[0] for part in key_parts)
    table, *staged, keys, values = stage(
        given_places, (table,), queries, out_grad, keys, values, pool_rows
    )
    out, query_grad, dk, dv = attend(
        table, staged, [keys, *key_parts], [values, *value_parts], send
    )
    return out, query_grad, total(dk), total(dv)


def local(queries, keys, values, out_grad, rand_blocks, global_blocks):
    cycle_size = lax.axis_size("seq")
    blocks_here = queries.shape[0] // BLOCK
    capacity = (RAND * blocks_here + GLOB + cycle_size - 1) // cycle_size
    dense = capacity >= blocks_here and cycle_size == 4
    plan = dense_local if dense else sparse_local
    return plan(queries, keys, values, out_grad, rand_blocks, global_blocks)


def solution(mesh):
    rows = P(("dp", "seq"), None)
    return jax.shard_map(
        local,
        mesh=mesh,
        in_specs=(rows, rows, rows, rows, P("dp", None), P("dp")),
        out_specs=(rows, rows, rows, rows),
        check_vma=False,
    )
```
